32 devices in a mesh: freq: 2 (over x), row: 16 (over z, y, core).
Axes of the slice: x: 2, y: 2, z: 4, core: 2. Of those that a mesh axis runs over, the one named last changes fastest.
Arguments:
- data_real: bfloat16 [16384, 8192], P(('freq', 'row')), parts along dimension 0, may hold values from -6 to 6
- data_imag: bfloat16 [16384, 8192], P(('freq', 'row')), parts along dimension 0, may hold values from -6 to 6
- counts: int32 [8, 8], replicated, may hold values from 0 to 4
- source_cols: int32 [128], replicated, may hold values from 0 to 8191, as said below
Outputs:
- pred_real: float32 [16384, 128], P(('freq', 'row')), parts along dimension 0
- pred_imag: float32 [16384, 128], P(('freq', 'row')), parts along dimension 0
The draws below stay inside these ranges and needn't reach their ends.
There are 2 independent parts, one for each index of `freq`. The reference program is written for one: setup_inputs(seed, part) draws one part's arguments, and reference() takes and returns one part's arrays. A program takes and returns all parts, laid end to end along the dimension named above; an argument that names none is the same for every part. Nothing has to cross between parts.
Inputs may be any that keep to these rules, and one draw needn't show every extreme that they name: `source_cols`: 128 distinct grid points; 0 and 8191 are always among them.
All inputs are finite; a program needn't handle non-finite values.
Results may differ from the reference program's by a relative error of at most 0.0029.
Values may be sent and summed in bfloat16 or wider, within the bound.
No kernel may reach another device: no remote copies, remote signals or barrier semaphores. Data moves between devices by JAX's collectives and lax.ppermute only.
A program may use at most 128 MiB of HBM per device.

```python
import jax
import jax.numpy as jnp
from jax import lax

N = 8192
SRC = 128
TILES = 8


def draw_source_cols(key, part):
    inner = jax.random.permutation(jax.random.fold_in(key, 11), N - 2)[:SRC - 2] + 1
    both = jnp.concatenate([jnp.array([0, N - 1], jnp.int32), inner.astype(jnp.int32)])
    order = jax.random.permutation(jax.random.fold_in(key, 12), SRC)
    return both[order]


def place_ends(values, rng, smallest, largest):
    shape = values.shape
    index_at = [jax.random.randint(jax.random.fold_in(rng, axis), (), 0, shape[axis]) for axis in range(len(shape))]
    values = values.at[tuple(index_at)].set(smallest)
    longest = shape.index(max(shape))
    index_at[longest] = (index_at[longest] + 1) % shape[longest]
    return values.at[tuple(index_at)].set(largest)


def strengthened(drawn, own_key, source, target, blocks, factor):
    def block_of(dim):
        return (jnp.arange(drawn.shape[dim]) // (drawn.shape[dim] // blocks)).reshape((-1,) + (1,) * (drawn.ndim - 1 - dim))

    one_side = jax.random.permutation(own_key, blocks)[block_of(target)]
    far = (block_of(target) + blocks // 2) % blocks
    return jnp.where((block_of(source) == one_side) | (block_of(source) == far), factor * drawn, drawn)


def level_of(own_key, dims, cuts, least, high):
    def one(position, shards_of):
        draws = jax.random.uniform(jax.random.fold_in(jax.random.fold_in(own_key, 6), position), (shards_of,), jnp.float32, least / len(cuts), high / len(cuts))
        return jnp.repeat(jnp.exp(draws), dims[position] // shards_of).reshape((-1,) + (1,) * (len(dims) - position - 1))

    factor_of = one(*cuts[0])
    for cut in cuts[1:]:
        factor_of = factor_of * one(*cut)
    return factor_of


def noise_with(key, shape, deviation, most, pieces, heavy, kind=jnp.bfloat16):
    entries = deviation * jax.random.normal(key, shape, jnp.float32)
    if pieces:
        entries = entries * level_of(key, shape, pieces, -0.22, 0.18)
    return jnp.clip(strengthened(entries, jax.random.fold_in(key, 3), *heavy), -most, most).astype(kind)


def setup_inputs(seed: int = 0, part: int = 0) -> dict:
    streams_of = jax.random.split(jax.random.key(seed), 5)
    part_keys = jax.random.split(jax.random.fold_in(streams_of[4], part), 5)
    data_real = noise_with(part_keys[0], (N, N), 1.0, 6.0, ((0, 16),), (0, 1, 16, 2.0))
    data_imag = noise_with(part_keys[1], (N, N), 1.0, 6.0, ((0, 16),), (0, 1, 16, 2.0))
    counts = place_ends(jax.random.randint(streams_of[2], (TILES, TILES), 0, 5), jax.random.fold_in(streams_of[2], 1), 0, 4).astype(jnp.int32)
    source_cols = draw_source_cols(jax.random.fold_in(streams_of[4], 71), part)
    return {"data_real": data_real, "data_imag": data_imag, "counts": counts, "source_cols": source_cols}


def symmetrize(data_real, data_imag, counts, row_ids):
    width = data_real.shape[1]
    tile = width // TILES
    table = counts.astype(jnp.float32)
    col_tiles = jnp.arange(width, dtype=jnp.int32) // tile
    row_tiles = row_ids // tile
    forward = table[row_tiles][:, col_tiles]
    backward = table.T[row_tiles][:, col_tiles]
    denom = jnp.maximum(forward + backward, 1.0)
    results = []
    for data in (data_real, data_imag):
        own = data[row_ids, :].astype(jnp.float32)
        mirror = data[:, row_ids].T.astype(jnp.float32)
        results.append(((forward * own + backward * mirror) / denom).astype(jnp.bfloat16))
    return (results[0], results[1])

def reference(data_real, data_imag, counts, source_cols):
    width = data_real.shape[0]
    tile = width // TILES
    src_real, src_imag = symmetrize(data_real, data_imag, counts, source_cols.astype(jnp.int32))
    panel_real = src_real.T
    panel_imag = src_imag.T
    factor = -1.0 / jnp.sqrt(jnp.float32(width))

    def block(index):
        row_ids = (index * tile + jnp.arange(tile, dtype=jnp.int32)).astype(jnp.int32)
        sym_real, sym_imag = symmetrize(data_real, data_imag, counts, row_ids)
        real = jnp.dot(sym_real, panel_real, preferred_element_type=jnp.float32) - jnp.dot(sym_imag, panel_imag, preferred_element_type=jnp.float32)
        imag = jnp.dot(sym_real, panel_imag, preferred_element_type=jnp.float32) + jnp.dot(sym_imag, panel_real, preferred_element_type=jnp.float32)
        return (factor * real, factor * imag)
    real, imag = lax.map(block, jnp.arange(TILES, dtype=jnp.int32))
    count = source_cols.shape[0]
    return (real.reshape(width, count), imag.reshape(width, count))
```

```python
import functools
import math

import jax
import jax.numpy as jnp
from jax import lax
from jax.experimental import pallas as pl
from jax.experimental.pallas import tpu as pltpu
from jax.sharding import PartitionSpec as P

TILES = 8
AXIS = "row"
VMEM_LIMIT = 40 * 1024 * 1024
F32 = jnp.float32
BF16 = jnp.bfloat16


def params():
    return pltpu.CompilerParams(vmem_limit_bytes=VMEM_LIMIT)


def whole_vmem():
    return pl.BlockSpec(memory_space=pltpu.VMEM)


def whole_smem():
    return pl.BlockSpec(memory_space=pltpu.SMEM)


def cost(flops, size):
    return pl.CostEstimate(flops=flops, bytes_accessed=size, transcendentals=0)


def dot(left, right):
    return jnp.dot(left, right, preferred_element_type=F32)


def ranks_of(col, rows):
    count = col.shape[0]
    owner = col // rows
    owner_row = jnp.transpose(jnp.broadcast_to(owner.astype(F32), (count, count))).astype(jnp.int32)
    before = lax.broadcasted_iota(jnp.int32, (count, count), 1) < lax.broadcasted_iota(
        jnp.int32, (count, count), 0
    )
    same = (owner_row == owner) & before
    return jnp.sum(same.astype(F32), axis=1, keepdims=True).astype(jnp.int32)


def rows_kernel(cap, round_ref, real_ref, imag_ref, col_ref, out_ref, pick_ref):
    rows, width = real_ref.shape
    count = col_ref.shape[0]
    groups = out_ref.shape[0]

    @pl.when(pl.program_id(0) == 0)
    def _():
        me = lax.axis_index(AXIS)
        col = col_ref[...]
        slot = ranks_of(col, rows) - round_ref[0] * cap
        to_slot = (slot == lax.broadcasted_iota(jnp.int32, (count, cap), 1)).astype(F32)
        local = col - me * rows
        to_row = (local == lax.broadcasted_iota(jnp.int32, (count, rows), 1)).astype(F32)
        pick_ref[...] = dot(jnp.transpose(to_slot).astype(BF16), to_row.astype(BF16)).astype(BF16)

    pick = pick_ref[...]
    for part, ref in enumerate((real_ref, imag_ref)):
        found = dot(pick, ref[...])
        for g in range(groups):
            out_ref[g, part * cap : (part + 1) * cap, :] = found[
                :, g * rows : (g + 1) * rows
            ].astype(BF16)


def own_source_rows(data_real, data_imag, col, which, cap, step):
    rows, width = data_real.shape
    count = col.shape[0]
    block = pl.BlockSpec((rows, step), lambda t: (0, t))
    return pl.pallas_call(
        functools.partial(rows_kernel, cap),
        grid=(width // step,),
        in_specs=[whole_smem(), block, block, whole_vmem()],
        out_specs=pl.BlockSpec((step // rows, 2 * cap, rows), lambda t: (t, 0, 0)),
        out_shape=jax.ShapeDtypeStruct((width // rows, 2 * cap, rows), BF16),
        scratch_shapes=[pltpu.VMEM((cap, rows), BF16)],
        compiler_params=params(),
        cost_estimate=cost(4 * cap * rows * width, 4 * rows * width),
        name="own_source_rows",
    )(which, data_real, data_imag, col)


def cols_kernel(real_ref, imag_ref, row_ref, out_ref, acc_ref):
    rows, step = real_ref.shape
    count = row_ref.shape[1]
    t = pl.program_id(0)

    @pl.when(t == 0)
    def _():
        acc_ref[...] = jnp.zeros_like(acc_ref)

    place = lax.broadcasted_iota(jnp.int32, (step, count), 0) + t * step
    pick = (place == row_ref[...]).astype(F32).astype(BF16)
    acc_ref[:, :count] += dot(real_ref[...], pick)
    acc_ref[:, count:] += dot(imag_ref[...], pick)

    @pl.when(t == pl.num_programs(0) - 1)
    def _():
        out_ref[...] = jnp.transpose(acc_ref[...]).astype(BF16)


def own_source_cols(data_real, data_imag, row, step):
    rows, width = data_real.shape
    count = row.shape[1]
    block = pl.BlockSpec((rows, step), lambda t: (0, t))
    return pl.pallas_call(
        cols_kernel,
        grid=(width // step,),
        in_specs=[block, block, whole_vmem()],
        out_specs=pl.BlockSpec((2 * count, rows), lambda t: (0, 0)),
        out_shape=jax.ShapeDtypeStruct((2 * count, rows), BF16),
        scratch_shapes=[pltpu.VMEM((rows, 2 * count), F32)],
        compiler_params=params(),
        cost_estimate=cost(4 * rows * width * count, 4 * rows * width),
        name="own_source_cols",
    )(data_real, data_imag, row)


def select_kernel(cap, round_ref, got_ref, col_ref, out_ref):
    groups, _, rows = got_ref.shape
    count = col_ref.shape[0]
    col = col_ref[...]
    slot = ranks_of(col, rows) - round_ref[0] * cap
    inside = (slot >= 0) & (slot < cap)
    place = jnp.where(inside, (col // rows) * (2 * cap) + slot, -1)
    lanes = lax.broadcasted_iota(jnp.int32, (count, groups * 2 * cap), 1)
    pick = jnp.concatenate([lanes == place, lanes == jnp.where(inside, place + cap, -1)], axis=0)
    got = got_ref[...].reshape(groups * 2 * cap, rows)
    out_ref[...] = dot(pick.astype(F32).astype(BF16), got).astype(BF16)


def select_rows(got, col, which, cap):
    groups, _, rows = got.shape
    count = col.shape[0]
    return pl.pallas_call(
        functools.partial(select_kernel, cap),
        in_specs=[whole_smem(), whole_vmem(), whole_vmem()],
        out_specs=whole_vmem(),
        out_shape=jax.ShapeDtypeStruct((2 * count, rows), BF16),
        compiler_params=params(),
        cost_estimate=cost(8 * count * groups * cap * rows, 4 * groups * cap * rows),
        name="select_rows",
    )(which, got, col)


def panel_kernel(width, counts_ref, rowpart_ref, colpart_ref, col_ref, panel_ref, panel_t_ref):
    rows = rowpart_ref.shape[1]
    tile = width // TILES
    mine = lax.axis_index(AXIS) * rows // tile
    tiles = col_ref[...] // tile
    forward = jnp.zeros_like(tiles)
    backward = jnp.zeros_like(tiles)
    for t in range(TILES):
        forward = jnp.where(tiles == t, counts_ref[mine, t], forward)
        backward = jnp.where(tiles == t, counts_ref[t, mine], backward)
    forward = jnp.concatenate([forward, forward], axis=0).astype(F32)
    backward = jnp.concatenate([backward, backward], axis=0).astype(F32)
    own = colpart_ref[...].astype(F32)
    mirror = rowpart_ref[...].astype(F32)
    panel = (forward * own + backward * mirror) / jnp.maximum(forward + backward, 1.0)
    panel_t_ref[...] = panel.astype(BF16)
    panel_ref[...] = jnp.transpose(panel).astype(BF16)


def own_panel(counts, rowpart, colpart, col, width):
    double, rows = rowpart.shape
    return pl.pallas_call(
        functools.partial(panel_kernel, width),
        in_specs=[whole_smem(), whole_vmem(), whole_vmem(), whole_vmem()],
        out_specs=[whole_vmem(), whole_vmem()],
        out_shape=[
            jax.ShapeDtypeStruct((rows, double), BF16),
            jax.ShapeDtypeStruct((double, rows), BF16),
        ],
        compiler_params=params(),
        cost_estimate=cost(8 * rows * double, 8 * rows * double),
        name="own_panel",
    )(counts, rowpart, colpart, col)


def weight(counts_ref, mine, other, shape):
    forward = jnp.full(shape, counts_ref[mine, other], jnp.int32).astype(F32)
    backward = jnp.full(shape, counts_ref[other, mine], jnp.int32).astype(F32)
    return forward / jnp.maximum(forward + backward, 1.0)


def mirror_kernel(width, counts_ref, real_ref, imag_ref, panel_t_ref, out_ref):
    rows, step = real_ref.shape
    tile = width // TILES
    count = panel_t_ref.shape[0] // 2
    mine = lax.axis_index(AXIS) * rows // tile
    scale = weight(counts_ref, mine, pl.program_id(0) * step // tile, (1, step))
    panel_t = panel_t_ref[...]
    turned = jnp.concatenate([-panel_t[count:], panel_t[:count]], axis=0)
    found = (dot(panel_t, real_ref[...]) + dot(turned, imag_ref[...])) * scale
    for g in range(out_ref.shape[0]):
        out_ref[g] = found[:, g * rows : (g + 1) * rows]


def mirror_term(counts, data_real, data_imag, panel_t, step):
    rows, width = data_real.shape
    double = panel_t.shape[0]
    block = pl.BlockSpec((rows, step), lambda t: (0, t))
    return pl.pallas_call(
        functools.partial(mirror_kernel, width),
        grid=(width // step,),
        in_specs=[whole_smem(), block, block, whole_vmem()],
        out_specs=pl.BlockSpec((step // rows, double, rows), lambda t: (t, 0, 0)),
        out_shape=jax.ShapeDtypeStruct((width // rows, double, rows), F32),
        compiler_params=params(),
        cost_estimate=cost(4 * rows * width * double, 4 * rows * width + 2 * double * width),
        name="mirror_term",
    )(counts, data_real, data_imag, panel_t)


def direct_kernel(width, counts_ref, real_ref, imag_ref, panel_ref, out_ref):
    rows, step = real_ref.shape
    tile = width // TILES
    t = pl.program_id(0)
    count = panel_ref.shape[1] // 2
    mine = lax.axis_index(AXIS) * rows // tile

    @pl.when(t == 0)
    def _():
        out_ref[...] = jnp.zeros_like(out_ref)

    panel = panel_ref[...]
    turned = jnp.concatenate([-panel[:, count:], panel[:, :count]], axis=1)
    found = dot(real_ref[...], panel) + dot(imag_ref[...], turned)
    out_ref[...] += found * weight(counts_ref, mine, t * step // tile, (1, 2 * count))


def direct_term(counts, data_real, data_imag, panel, step):
    rows, width = data_real.shape
    double = panel.shape[1]
    block = pl.BlockSpec((rows, step), lambda t: (0, t))
    return pl.pallas_call(
        functools.partial(direct_kernel, width),
        grid=(width // step,),
        in_specs=[whole_smem(), block, block, pl.BlockSpec((step, double), lambda t: (t, 0))],
        out_specs=pl.BlockSpec((rows, double), lambda t: (0, 0)),
        out_shape=jax.ShapeDtypeStruct((rows, double), F32),
        compiler_params=params(),
        cost_estimate=cost(4 * rows * width * double, 4 * rows * width + 2 * double * width),
        name="direct_term",
    )(counts, data_real, data_imag, panel)


def block_at(me, span, dz, dy, dc):
    far, near = span
    z, y, c = me // (2 * near), (me // 2) % near, me % 2
    return (((z + dz) % far) * near + (y + dy) % near) * 2 + (c + dc) % 2


def shift(value, span, dz, dy, dc):
    size = 2 * span[0] * span[1]
    return lax.ppermute(value, AXIS, [(i, block_at(i, span, dz, dy, dc)) for i in range(size)])


def mirror_part_kernel(
    width, span, dz, me_ref, counts_ref, real_ref, imag_ref, panel_t_ref, other_ref, own_ref
):
    rows = real_ref.shape[1]
    tile = width // TILES
    count = panel_t_ref.shape[0] // 2
    turn, dy = pl.program_id(0), pl.program_id(1)
    mine = me_ref[0] * rows // tile
    block = block_at(me_ref[0], span, dz, dy, 1 - turn)
    scale = weight(counts_ref, mine, block * rows // tile, (1, rows))
    panel_t = panel_t_ref[...]
    turned = jnp.concatenate([-panel_t[count:], panel_t[:count]], axis=0)
    found = (dot(panel_t, real_ref[...]) + dot(turned, imag_ref[...])) * scale

    @pl.when(turn == 0)
    def _():
        other_ref[0] = found.astype(BF16)

    @pl.when(turn == 1)
    def _():
        own_ref[0] = found


def mirror_part(me, counts, data_real, data_imag, panel_t, span, dz):
    rows, width = data_real.shape
    double = panel_t.shape[0]
    near = span[1]
    block = pl.BlockSpec(
        (rows, rows), lambda turn, dy, me: (0, block_at(me[0], span, dz, dy, 1 - turn))
    )
    spec = pltpu.PrefetchScalarGridSpec(
        num_scalar_prefetch=1,
        grid=(2, near),
        in_specs=[whole_smem(), block, block, whole_vmem()],
        out_specs=[
            pl.BlockSpec(
                (1, double, rows), lambda turn, dy, me: (jnp.where(turn == 0, dy, near - 1), 0, 0)
            ),
            pl.BlockSpec((1, double, rows), lambda turn, dy, me: (jnp.where(turn == 0, 0, dy), 0, 0)),
        ],
    )
    return pl.pallas_call(
        functools.partial(mirror_part_kernel, width, span, dz),
        grid_spec=spec,
        out_shape=[
            jax.ShapeDtypeStruct((near, double, rows), BF16),
            jax.ShapeDtypeStruct((near, double, rows), F32),
        ],
        compiler_params=params(),
        cost_estimate=cost(8 * rows * rows * near * double, 8 * rows * rows * near),
        name="mirror_part",
    )(me, counts, data_real, data_imag, panel_t)


def direct_blocks_kernel(width, span, me_ref, counts_ref, real_ref, imag_ref, *refs):
    panel_refs, out_ref = refs[:-1], refs[-1]
    rows = real_ref.shape[0]
    tile = width // TILES
    count = panel_refs[0].shape[1] // 2
    k = pl.program_id(0)
    mine = me_ref[0] * rows // tile
    block = source_of(me_ref[0], span, k)
    scale = weight(counts_ref, mine, block * rows // tile, (1, 2 * count))

    @pl.when(k == 0)
    def _():
        out_ref[...] = jnp.zeros_like(out_ref)

    for i, ref in enumerate(panel_refs):

        @pl.when(k == i)
        def _(ref=ref):
            panel = ref[...]
            turned = jnp.concatenate([-panel[:, count:], panel[:, :count]], axis=1)
            found = dot(real_ref[...], panel) + dot(imag_ref[...], turned)
            out_ref[...] += found * scale


def source_of(me, span, k):
    far, near = span
    dc, dz, dy = k // (far * near), (k // near) % far, k % near
    return block_at(me, span, far - dz, near - dy, dc)


def direct_blocks(me, counts, data_real, data_imag, panels, span):
    rows, width = data_real.shape
    double = panels[0].shape[1]
    block = pl.BlockSpec((rows, rows), lambda k, me: (0, source_of(me[0], span, k)))
    spec = pltpu.PrefetchScalarGridSpec(
        num_scalar_prefetch=1,
        grid=(len(panels),),
        in_specs=[whole_smem(), block, block] + [whole_vmem()] * len(panels),
        out_specs=pl.BlockSpec((rows, double), lambda k, me: (0, 0)),
    )
    return pl.pallas_call(
        functools.partial(direct_blocks_kernel, width, span),
        grid_spec=spec,
        out_shape=jax.ShapeDtypeStruct((rows, double), F32),
        compiler_params=params(),
        cost_estimate=cost(4 * rows * width * double, 4 * rows * width + 2 * double * width),
        name="direct_blocks",
    )(me, counts, data_real, data_imag, *panels)


def gather_levels(panel, span):
    far, near = span
    along = [panel] + [shift(panel, span, dz, 0, 0) for dz in range(1, far)]
    plane = [
        block if dy == 0 else shift(block, span, 0, dy, 0) for block in along for dy in range(near)
    ]
    return plane + [shift(block, span, 0, 0, 1) for block in plane]


def mirror_levels(me, counts, data_real, data_imag, panel_t, span):
    far, near = span
    terms = []
    for dz in list(range(1, far)) + [0]:
        other, own = mirror_part(me, counts, data_real, data_imag, panel_t, span, dz)
        total = own + shift(other, span, 0, 0, 1).astype(F32)
        held = total[0]
        for dy in range(1, near):
            held = held + shift(total[dy].astype(BF16), span, 0, dy, 0).astype(F32)
        terms.append(held if dz == 0 else shift(held.astype(BF16), span, dz, 0, 0))
    return terms


def finish_kernel(factor, direct_ref, *refs):
    mirror_refs, (real_ref, imag_ref) = refs[:-2], refs[-2:]
    count = real_ref.shape[1]
    mirror = mirror_refs[-1][...].astype(F32)
    for ref in mirror_refs[:-1]:
        mirror += ref[...].astype(F32)
    total = factor * (direct_ref[...] + jnp.transpose(mirror))
    real_ref[...] = total[:, :count]
    imag_ref[...] = total[:, count:]


def finish(direct, mirrors, width):
    rows, double = direct.shape
    shape = jax.ShapeDtypeStruct((rows, double // 2), F32)
    return pl.pallas_call(
        functools.partial(finish_kernel, -1.0 / math.sqrt(width)),
        in_specs=[whole_vmem()] * (1 + len(mirrors)),
        out_specs=[whole_vmem(), whole_vmem()],
        out_shape=[shape, shape],
        compiler_params=params(),
        cost_estimate=cost(4 * rows * double, 10 * rows * double),
        name="finish",
    )(direct, *mirrors)


def shards(data_real, data_imag, counts, source_cols):
    rows, width = data_real.shape
    groups = width // rows
    count = source_cols.shape[0]
    step = width // TILES
    cap = min(rows, count, -(-3 * count // groups // 8) * 8)
    col = source_cols.reshape(count, 1)
    row = source_cols.reshape(1, count)

    def exchange(which):
        sent = own_source_rows(data_real, data_imag, col, which, cap, step)
        return lax.all_to_all(sent, AXIS, split_axis=0, concat_axis=0)

    first = jnp.zeros((1,), jnp.int32)
    got = exchange(first)
    colpart = own_source_cols(data_real, data_imag, row, step)
    rowpart = select_rows(got, col, first, cap)

    owner = source_cols // rows
    most = jnp.max(jnp.sum(owner[:, None] == jnp.arange(groups)[None, :], axis=0, dtype=jnp.int32))

    def more(state):
        return state[0] * cap < most

    def body(state):
        which, held = state
        one = which.reshape(1)
        return which + 1, held + select_rows(exchange(one), col, one, cap)

    _, rowpart = lax.while_loop(more, body, (jnp.int32(1), rowpart))

    panel, panel_t = own_panel(counts, rowpart, colpart, col, width)
    if rows % 128 == 0 and groups <= 16:
        near = 2 ** (((groups // 2).bit_length() - 1) // 2)
        span = (groups // 2 // near, near)
        me = lax.axis_index(AXIS).reshape(1)
        panels = gather_levels(panel, span)
        mirrors = mirror_levels(me, counts, data_real, data_imag, panel_t, span)
        direct = direct_blocks(me, counts, data_real, data_imag, panels, span)
    else:
        full = lax.all_gather(panel, AXIS, axis=0, tiled=True)
        partial = mirror_term(counts, data_real, data_imag, panel_t, step)
        mirrors = [lax.psum_scatter(partial, AXIS, scatter_dimension=0, tiled=False)]
        direct = direct_term(counts, data_real, data_imag, full, step)
    return tuple(finish(direct, mirrors, width))


def solution(mesh):
    placed = (P(("freq", "row"), None), P(("freq", "row"), None), P(), P())
    return jax.shard_map(
        shards,
        mesh=mesh,
        in_specs=placed,
        out_specs=(P(("freq", "row"), None), P(("freq", "row"), None)),
        check_vma=False,
    )
```

```python
import functools
import math

import jax
import jax.numpy as jnp
from jax import lax
from jax.experimental import pallas as pl
from jax.experimental.pallas import tpu as pltpu
from jax.sharding import PartitionSpec as P

TILES = 8
AXIS = "row"
GROUP = 16
PIECE = 1024
F32 = jnp.float32
BF16 = jnp.bfloat16


def params(mib=16):
    return pltpu.CompilerParams(vmem_limit_bytes=mib * 1024 * 1024)


def whole_vmem():
    return pl.BlockSpec(memory_space=pltpu.VMEM)


def whole_smem():
    return pl.BlockSpec(memory_space=pltpu.SMEM)


def cost(flops, size):
    return pl.CostEstimate(flops=flops, bytes_accessed=size, transcendentals=0)


def dot(left, right):
    return jnp.dot(left, right, preferred_element_type=F32)


def ranks_of(col, rows):
    count = col.shape[0]
    owner = col // rows
    owner_row = jnp.transpose(jnp.broadcast_to(owner.astype(F32), (count, count))).astype(jnp.int32)
    before = lax.broadcasted_iota(jnp.int32, (count, count), 1) < lax.broadcasted_iota(
        jnp.int32, (count, count), 0
    )
    same = (owner_row == owner) & before
    return jnp.sum(same.astype(F32), axis=1, keepdims=True).astype(jnp.int32)


def rows_kernel(cap, round_ref, col_ref, real_ref, imag_ref, out_ref, near_ref, held_ref, sems):
    rows, width = real_ref.shape
    groups = out_ref.shape[0]
    count = col_ref.shape[0]
    base = lax.axis_index(AXIS) * rows
    skip = round_ref[0] * cap

    def copies(slot, local):
        group = pl.ds(pl.multiple_of(local // GROUP * GROUP, GROUP), GROUP)
        return [
            pltpu.make_async_copy(ref.at[group], near_ref.at[slot, part], sems.at[slot, part])
            for part, ref in enumerate((real_ref, imag_ref))
        ]

    def each(act):
        def visit(s, found):
            local = col_ref[s] - base
            own = (local >= 0) & (local < rows)
            slot = found - skip

            @pl.when(own & (slot >= 0) & (slot < cap))
            def _():
                act(slot, local)

            return found + own.astype(jnp.int32)

        lax.fori_loop(0, count, visit, jnp.int32(0))

    def begin(slot, local):
        for copy in copies(slot, local):
            copy.start()

    def pick(slot, local):
        chosen = lax.broadcasted_iota(jnp.int32, (GROUP, PIECE), 0) == local % GROUP
        for part, copy in enumerate(copies(slot, local)):
            copy.wait()
            for at in range(0, width, PIECE):
                group = near_ref[slot, part, :, at : at + PIECE].astype(F32)
                held_ref[pl.ds(part * cap + slot, 1), at : at + PIECE] = jnp.sum(
                    jnp.where(chosen, group, 0.0), axis=0, keepdims=True
                )

    each(begin)
    held_ref[...] = jnp.zeros_like(held_ref)
    each(pick)
    for g in range(groups):
        out_ref[g] = held_ref[:, g * rows : (g + 1) * rows].astype(BF16)


def own_source_rows(data_real, data_imag, source_cols, which, cap):
    rows, width = data_real.shape
    anywhere = pl.BlockSpec(memory_space=pl.ANY)
    return pl.pallas_call(
        functools.partial(rows_kernel, cap),
        in_specs=[whole_smem(), whole_smem(), anywhere, anywhere],
        out_specs=whole_vmem(),
        out_shape=jax.ShapeDtypeStruct((width // rows, 2 * cap, rows), BF16),
        scratch_shapes=[
            pltpu.VMEM((cap, 2, GROUP, width), BF16),
            pltpu.VMEM((2 * cap, width), F32),
            pltpu.SemaphoreType.DMA((cap, 2)),
        ],
        compiler_params=params(24),
        cost_estimate=cost(0, 2 * cap * width),
        name="own_source_rows",
    )(which, source_cols, data_real, data_imag)


def cols_kernel(real_ref, imag_ref, row_ref, out_ref, acc_ref):
    rows, step = real_ref.shape
    count = row_ref.shape[1]
    t = pl.program_id(0)

    @pl.when(t == 0)
    def _():
        acc_ref[...] = jnp.zeros_like(acc_ref)

    place = lax.broadcasted_iota(jnp.int32, (step, count), 0) + t * step
    pick = (place == row_ref[...]).astype(F32).astype(BF16)
    acc_ref[:, :count] += dot(real_ref[...], pick)
    acc_ref[:, count:] += dot(imag_ref[...], pick)

    @pl.when(t == pl.num_programs(0) - 1)
    def _():
        out_ref[...] = jnp.transpose(acc_ref[...]).astype(BF16)


def own_source_cols(data_real, data_imag, row, step):
    rows, width = data_real.shape
    count = row.shape[1]
    block = pl.BlockSpec((rows, step), lambda t: (0, t))
    return pl.pallas_call(
        cols_kernel,
        grid=(width // step,),
        in_specs=[block, block, whole_vmem()],
        out_specs=pl.BlockSpec((2 * count, rows), lambda t: (0, 0)),
        out_shape=jax.ShapeDtypeStruct((2 * count, rows), BF16),
        scratch_shapes=[pltpu.VMEM((rows, 2 * count), F32)],
        compiler_params=params(),
        cost_estimate=cost(4 * rows * width * count, 4 * rows * width),
        name="own_source_cols",
    )(data_real, data_imag, row)


def select_kernel(cap, round_ref, got_ref, col_ref, out_ref):
    groups, _, rows = got_ref.shape
    count = col_ref.shape[0]
    col = col_ref[...]
    slot = ranks_of(col, rows) - round_ref[0] * cap
    inside = (slot >= 0) & (slot < cap)
    place = jnp.where(inside, (col // rows) * (2 * cap) + slot, -1)
    lanes = lax.broadcasted_iota(jnp.int32, (count, groups * 2 * cap), 1)
    pick = jnp.concatenate([lanes == place, lanes == jnp.where(inside, place + cap, -1)], axis=0)
    got = got_ref[...].reshape(groups * 2 * cap, rows)
    out_ref[...] = dot(pick.astype(F32).astype(BF16), got).astype(BF16)


def select_rows(got, col, which, cap):
    groups, _, rows = got.shape
    count = col.shape[0]
    return pl.pallas_call(
        functools.partial(select_kernel, cap),
        in_specs=[whole_smem(), whole_vmem(), whole_vmem()],
        out_specs=whole_vmem(),
        out_shape=jax.ShapeDtypeStruct((2 * count, rows), BF16),
        compiler_params=params(),
        cost_estimate=cost(8 * count * groups * cap * rows, 4 * groups * cap * rows),
        name="select_rows",
    )(which, got, col)


def panel_kernel(width, counts_ref, rowpart_ref, colpart_ref, col_ref, panel_ref, panel_t_ref):
    rows = rowpart_ref.shape[1]
    tile = width // TILES
    mine = lax.axis_index(AXIS) * rows // tile
    tiles = col_ref[...] // tile
    forward = jnp.zeros_like(tiles)
    backward = jnp.zeros_like(tiles)
    for t in range(TILES):
        forward = jnp.where(tiles == t, counts_ref[mine, t], forward)
        backward = jnp.where(tiles == t, counts_ref[t, mine], backward)
    forward = jnp.concatenate([forward, forward], axis=0).astype(F32)
    backward = jnp.concatenate([backward, backward], axis=0).astype(F32)
    own = colpart_ref[...].astype(F32)
    mirror = rowpart_ref[...].astype(F32)
    panel = (forward * own + backward * mirror) / jnp.maximum(forward + backward, 1.0)
    panel_t_ref[...] = panel.astype(BF16)
    panel_ref[...] = jnp.transpose(panel).astype(BF16)


def own_panel(counts, rowpart, colpart, col, width):
    double, rows = rowpart.shape
    return pl.pallas_call(
        functools.partial(panel_kernel, width),
        in_specs=[whole_smem(), whole_vmem(), whole_vmem(), whole_vmem()],
        out_specs=[whole_vmem(), whole_vmem()],
        out_shape=[
            jax.ShapeDtypeStruct((rows, double), BF16),
            jax.ShapeDtypeStruct((double, rows), BF16),
        ],
        compiler_params=params(),
        cost_estimate=cost(8 * rows * double, 8 * rows * double),
        name="own_panel",
    )(counts, rowpart, colpart, col)


def weight(counts_ref, mine, other, shape):
    forward = jnp.full(shape, counts_ref[mine, other], jnp.int32).astype(F32)
    backward = jnp.full(shape, counts_ref[other, mine], jnp.int32).astype(F32)
    return forward / jnp.maximum(forward + backward, 1.0)


def mirror_kernel(width, counts_ref, real_ref, imag_ref, panel_t_ref, out_ref):
    rows, step = real_ref.shape
    tile = width // TILES
    count = panel_t_ref.shape[0] // 2
    mine = lax.axis_index(AXIS) * rows // tile
    scale = weight(counts_ref, mine, pl.program_id(0) * step // tile, (1, step))
    panel_t = panel_t_ref[...]
    turned = jnp.concatenate([-panel_t[count:], panel_t[:count]], axis=0)
    found = (dot(panel_t, real_ref[...]) + dot(turned, imag_ref[...])) * scale
    for g in range(out_ref.shape[0]):
        out_ref[g] = found[:, g * rows : (g + 1) * rows]


def mirror_term(counts, data_real, data_imag, panel_t, step):
    rows, width = data_real.shape
    double = panel_t.shape[0]
    block = pl.BlockSpec((rows, step), lambda t: (0, t))
    return pl.pallas_call(
        functools.partial(mirror_kernel, width),
        grid=(width // step,),
        in_specs=[whole_smem(), block, block, whole_vmem()],
        out_specs=pl.BlockSpec((step // rows, double, rows), lambda t: (t, 0, 0)),
        out_shape=jax.ShapeDtypeStruct((width // rows, double, rows), F32),
        compiler_params=params(),
        cost_estimate=cost(4 * rows * width * double, 4 * rows * width + 2 * double * width),
        name="mirror_term",
    )(counts, data_real, data_imag, panel_t)


def direct_kernel(width, counts_ref, real_ref, imag_ref, panel_ref, out_ref):
    rows, step = real_ref.shape
    tile = width // TILES
    t = pl.program_id(0)
    count = panel_ref.shape[1] // 2
    mine = lax.axis_index(AXIS) * rows // tile

    @pl.when(t == 0)
    def _():
        out_ref[...] = jnp.zeros_like(out_ref)

    panel = panel_ref[...]
    turned = jnp.concatenate([-panel[:, count:], panel[:, :count]], axis=1)
    found = dot(real_ref[...], panel) + dot(imag_ref[...], turned)
    out_ref[...] += found * weight(counts_ref, mine, t * step // tile, (1, 2 * count))


def direct_term(counts, data_real, data_imag, panel, step):
    rows, width = data_real.shape
    double = panel.shape[1]
    block = pl.BlockSpec((rows, step), lambda t: (0, t))
    return pl.pallas_call(
        functools.partial(direct_kernel, width),
        grid=(width // step,),
        in_specs=[whole_smem(), block, block, pl.BlockSpec((step, double), lambda t: (t, 0))],
        out_specs=pl.BlockSpec((rows, double), lambda t: (0, 0)),
        out_shape=jax.ShapeDtypeStruct((rows, double), F32),
        compiler_params=params(),
        cost_estimate=cost(4 * rows * width * double, 4 * rows * width + 2 * double * width),
        name="direct_term",
    )(counts, data_real, data_imag, panel)


def block_at(me, span, dz, dy, dc):
    far, near = span
    z, y, c = me // (2 * near), (me // 2) % near, me % 2
    return (((z + dz) % far) * near + (y + dy) % near) * 2 + (c + dc) % 2


def shift(value, span, dz, dy, dc):
    size = 2 * span[0] * span[1]
    return lax.ppermute(value, AXIS, [(i, block_at(i, span, dz, dy, dc)) for i in range(size)])


def mirror_part_kernel(
    width, span, dz, me_ref, counts_ref, real_ref, imag_ref, panel_t_ref, other_ref, own_ref
):
    rows = real_ref.shape[1]
    tile = width // TILES
    count = panel_t_ref.shape[0] // 2
    turn, dy = pl.program_id(0), pl.program_id(1)
    mine = me_ref[0] * rows // tile
    block = block_at(me_ref[0], span, dz, dy, 1 - turn)
    scale = weight(counts_ref, mine, block * rows // tile, (1, rows))
    panel_t = panel_t_ref[...]
    turned = jnp.concatenate([-panel_t[count:], panel_t[:count]], axis=0)
    found = (dot(panel_t, real_ref[...]) + dot(turned, imag_ref[...])) * scale

    @pl.when(turn == 0)
    def _():
        other_ref[0] = found.astype(BF16)

    @pl.when(turn == 1)
    def _():
        own_ref[0] = found


def mirror_part(me, counts, data_real, data_imag, panel_t, span, dz):
    rows, width = data_real.shape
    double = panel_t.shape[0]
    near = span[1]
    block = pl.BlockSpec(
        (rows, rows), lambda turn, dy, me: (0, block_at(me[0], span, dz, dy, 1 - turn))
    )
    spec = pltpu.PrefetchScalarGridSpec(
        num_scalar_prefetch=1,
        grid=(2, near),
        in_specs=[whole_smem(), block, block, whole_vmem()],
        out_specs=[
            pl.BlockSpec(
                (1, double, rows), lambda turn, dy, me: (jnp.where(turn == 0, dy, near - 1), 0, 0)
            ),
            pl.BlockSpec((1, double, rows), lambda turn, dy, me: (jnp.where(turn == 0, 0, dy), 0, 0)),
        ],
    )
    return pl.pallas_call(
        functools.partial(mirror_part_kernel, width, span, dz),
        grid_spec=spec,
        out_shape=[
            jax.ShapeDtypeStruct((near, double, rows), BF16),
            jax.ShapeDtypeStruct((near, double, rows), F32),
        ],
        compiler_params=params(),
        cost_estimate=cost(0, 4 * rows * double),
        name="mirror_part",
    )(me, counts, data_real, data_imag, panel_t)


def direct_part_kernel(width, span, dz, me_ref, counts_ref, real_ref, imag_ref, *refs):
    panel_refs, sum_ref, out_ref = refs[: 2 * span[1]], refs[-2], refs[-1]
    rows = real_ref.shape[0]
    tile = width // TILES
    count = panel_refs[0].shape[1] // 2
    k = pl.program_id(0)
    mine = me_ref[0] * rows // tile
    block = source_of(me_ref[0], span, dz, k)
    scale = weight(counts_ref, mine, block * rows // tile, (1, 2 * count))

    @pl.when(k == 0)
    def _():
        out_ref[...] = jnp.zeros_like(out_ref) if dz == 0 else sum_ref[...]

    for i, ref in enumerate(panel_refs):

        @pl.when(k == i)
        def _(ref=ref):
            panel = ref[...]
            turned = jnp.concatenate([-panel[:, count:], panel[:, :count]], axis=1)
            found = dot(real_ref[...], panel) + dot(imag_ref[...], turned)
            out_ref[...] += found * scale


def source_of(me, span, dz, k):
    far, near = span
    return block_at(me, span, far - dz, near - k % near, k // near)


def direct_part(me, counts, data_real, data_imag, panels, before, span, dz):
    rows, width = data_real.shape
    double = panels[0].shape[1]
    block = pl.BlockSpec((rows, rows), lambda k, me: (0, source_of(me[0], span, dz, k)))
    rest = [whole_vmem()] * len(panels) + ([] if dz == 0 else [whole_vmem()])
    spec = pltpu.PrefetchScalarGridSpec(
        num_scalar_prefetch=1,
        grid=(len(panels),),
        in_specs=[whole_smem(), block, block] + rest,
        out_specs=pl.BlockSpec((rows, double), lambda k, me: (0, 0)),
    )
    return pl.pallas_call(
        functools.partial(direct_part_kernel, width, span, dz),
        grid_spec=spec,
        out_shape=jax.ShapeDtypeStruct((rows, double), F32),
        compiler_params=params(),
        cost_estimate=cost(0, 4 * rows * double),
        name="direct_part",
    )(me, counts, data_real, data_imag, *panels, *([] if dz == 0 else [before]))


def gather_levels(panel, span):
    far, near = span
    along = [panel] + [shift(panel, span, dz, 0, 0) for dz in range(1, far)]
    gathered = []
    for block in along:
        plane = [block] + [shift(block, span, 0, dy, 0) for dy in range(1, near)]
        gathered.append(plane + [shift(each, span, 0, 0, 1) for each in plane])
    return gathered


def mirror_levels(me, counts, data_real, data_imag, panel_t, span):
    far, near = span
    terms = []
    for dz in list(range(1, far)) + [0]:
        other, own = mirror_part(me, counts, data_real, data_imag, panel_t, span, dz)
        total = own + shift(other, span, 0, 0, 1).astype(F32)
        held = total[0]
        for dy in range(1, near):
            held = held + shift(total[dy].astype(BF16), span, 0, dy, 0).astype(F32)
        terms.append(held if dz == 0 else shift(held.astype(BF16), span, dz, 0, 0))
    return terms


def finish_kernel(factor, direct_ref, *refs):
    mirror_refs, (real_ref, imag_ref) = refs[:-2], refs[-2:]
    count = real_ref.shape[1]
    mirror = mirror_refs[-1][...].astype(F32)
    for ref in mirror_refs[:-1]:
        mirror += ref[...].astype(F32)
    total = factor * (direct_ref[...] + jnp.transpose(mirror))
    real_ref[...] = total[:, :count]
    imag_ref[...] = total[:, count:]


def finish(direct, mirrors, width):
    rows, double = direct.shape
    shape = jax.ShapeDtypeStruct((rows, double // 2), F32)
    return pl.pallas_call(
        functools.partial(finish_kernel, -1.0 / math.sqrt(width)),
        in_specs=[whole_vmem()] * (1 + len(mirrors)),
        out_specs=[whole_vmem(), whole_vmem()],
        out_shape=[shape, shape],
        compiler_params=params(),
        cost_estimate=cost(4 * rows * double, 10 * rows * double),
        name="finish",
    )(direct, *mirrors)


def shards(data_real, data_imag, counts, source_cols):
    rows, width = data_real.shape
    groups = width // rows
    count = source_cols.shape[0]
    step = width // TILES
    cap = min(rows, count, -(-2 * count // groups // 8) * 8)
    col = source_cols.reshape(count, 1)
    row = source_cols.reshape(1, count)

    def exchange(which):
        sent = own_source_rows(data_real, data_imag, source_cols, which, cap)
        return lax.all_to_all(sent, AXIS, split_axis=0, concat_axis=0)

    first = jnp.zeros((1,), jnp.int32)
    got = exchange(first)
    colpart = own_source_cols(data_real, data_imag, row, step)
    rowpart = select_rows(got, col, first, cap)

    owner = source_cols // rows
    most = jnp.max(jnp.sum(owner[:, None] == jnp.arange(groups)[None, :], axis=0, dtype=jnp.int32))

    def more(state):
        return state[0] * cap < most

    def body(state):
        which, held = state
        one = which.reshape(1)
        return which + 1, held + select_rows(exchange(one), col, one, cap)

    _, rowpart = lax.while_loop(more, body, (jnp.int32(1), rowpart))

    panel, panel_t = own_panel(counts, rowpart, colpart, col, width)
    if rows % 128 == 0 and groups <= 16:
        near = 2 ** (((groups // 2).bit_length() - 1) // 2)
        span = (groups // 2 // near, near)
        me = lax.axis_index(AXIS).reshape(1)
        panels = gather_levels(panel, span)
        mirrors = mirror_levels(me, counts, data_real, data_imag, panel_t, span)
        direct = None
        for dz, group in enumerate(panels):
            direct = direct_part(me, counts, data_real, data_imag, group, direct, span, dz)
    else:
        full = lax.all_gather(panel, AXIS, axis=0, tiled=True)
        partial = mirror_term(counts, data_real, data_imag, panel_t, step)
        mirrors = [lax.psum_scatter(partial, AXIS, scatter_dimension=0, tiled=False)]
        direct = direct_term(counts, data_real, data_imag, full, step)
    return tuple(finish(direct, mirrors, width))


def solution(mesh):
    placed = (P(("freq", "row"), None), P(("freq", "row"), None), P(), P())
    return jax.shard_map(
        shards,
        mesh=mesh,
        in_specs=placed,
        out_specs=(P(("freq", "row"), None), P(("freq", "row"), None)),
        check_vma=False,
    )
```

```python
import functools
import math

import jax
import jax.numpy as jnp
from jax import lax
from jax.experimental import pallas as pl
from jax.experimental.pallas import tpu as pltpu
from jax.sharding import PartitionSpec as P

TILES = 8
AXIS = "row"
GROUP = 16
PIECE = 1024
F32 = jnp.float32
BF16 = jnp.bfloat16


def params(mib=16):
    return pltpu.CompilerParams(vmem_limit_bytes=mib * 1024 * 1024)


def whole_vmem():
    return pl.BlockSpec(memory_space=pltpu.VMEM)


def whole_smem():
    return pl.BlockSpec(memory_space=pltpu.SMEM)


def cost(flops, size):
    return pl.CostEstimate(flops=flops, bytes_accessed=size, transcendentals=0)


def dot(left, right):
    return jnp.dot(left, right, preferred_element_type=F32)


def ranks_of(col, rows):
    count = col.shape[0]
    owner = col // rows
    owner_row = jnp.transpose(jnp.broadcast_to(owner.astype(F32), (count, count))).astype(jnp.int32)
    before = lax.broadcasted_iota(jnp.int32, (count, count), 1) < lax.broadcasted_iota(
        jnp.int32, (count, count), 0
    )
    same = (owner_row == owner) & before
    return jnp.sum(same.astype(F32), axis=1, keepdims=True).astype(jnp.int32)


def rows_kernel(cap, round_ref, col_ref, real_ref, imag_ref, out_ref, list_ref, near_ref, held_ref, sems):
    rows, width = real_ref.shape
    groups = out_ref.shape[0]
    count = col_ref.shape[0]
    base = lax.axis_index(AXIS) * rows
    skip = round_ref[0] * cap

    def copies(slot, local):
        group = pl.ds(pl.multiple_of(local // GROUP * GROUP, GROUP), GROUP)
        return [
            pltpu.make_async_copy(ref.at[group], near_ref.at[slot, part], sems.at[slot, part])
            for part, ref in enumerate((real_ref, imag_ref))
        ]

    def begin(s, found):
        local = col_ref[s] - base
        own = (local >= 0) & (local < rows)
        slot = found - skip

        @pl.when(own & (slot >= 0) & (slot < cap))
        def _():
            list_ref[slot] = local
            for copy in copies(slot, local):
                copy.start()

        return found + own.astype(jnp.int32)

    def pick(slot, _):
        local = list_ref[slot]
        chosen = lax.broadcasted_iota(jnp.int32, (GROUP, PIECE), 0) == local % GROUP
        for part, copy in enumerate(copies(slot, local)):
            copy.wait()
            for at in range(0, width, PIECE):
                group = near_ref[slot, part, :, at : at + PIECE].astype(F32)
                held_ref[pl.ds(part * cap + slot, 1), at : at + PIECE] = jnp.sum(
                    jnp.where(chosen, group, 0.0), axis=0, keepdims=True
                )
        return 0

    found = lax.fori_loop(0, count, begin, jnp.int32(0))
    held_ref[...] = jnp.zeros_like(held_ref)
    lax.fori_loop(0, jnp.clip(found - skip, 0, cap), pick, 0)
    for g in range(groups):
        out_ref[g] = held_ref[:, g * rows : (g + 1) * rows].astype(BF16)


def own_source_rows(data_real, data_imag, source_cols, which, cap):
    rows, width = data_real.shape
    anywhere = pl.BlockSpec(memory_space=pl.ANY)
    return pl.pallas_call(
        functools.partial(rows_kernel, cap),
        in_specs=[whole_smem(), whole_smem(), anywhere, anywhere],
        out_specs=whole_vmem(),
        out_shape=jax.ShapeDtypeStruct((width // rows, 2 * cap, rows), BF16),
        scratch_shapes=[
            pltpu.SMEM((cap,), jnp.int32),
            pltpu.VMEM((cap, 2, GROUP, width), BF16),
            pltpu.VMEM((2 * cap, width), F32),
            pltpu.SemaphoreType.DMA((cap, 2)),
        ],
        compiler_params=params(24),
        cost_estimate=cost(0, 2 * cap * width),
        name="own_source_rows",
    )(which, source_cols, data_real, data_imag)


def cols_kernel(real_ref, imag_ref, row_ref, out_ref, acc_ref):
    rows, step = real_ref.shape
    count = row_ref.shape[1]
    t = pl.program_id(0)

    @pl.when(t == 0)
    def _():
        acc_ref[...] = jnp.zeros_like(acc_ref)

    place = lax.broadcasted_iota(jnp.int32, (step, count), 0) + t * step
    pick = (place == row_ref[...]).astype(F32).astype(BF16)
    acc_ref[:, :count] += dot(real_ref[...], pick)
    acc_ref[:, count:] += dot(imag_ref[...], pick)

    @pl.when(t == pl.num_programs(0) - 1)
    def _():
        out_ref[...] = jnp.transpose(acc_ref[...]).astype(BF16)


def own_source_cols(data_real, data_imag, row, step):
    rows, width = data_real.shape
    count = row.shape[1]
    block = pl.BlockSpec((rows, step), lambda t: (0, t))
    return pl.pallas_call(
        cols_kernel,
        grid=(width // step,),
        in_specs=[block, block, whole_vmem()],
        out_specs=pl.BlockSpec((2 * count, rows), lambda t: (0, 0)),
        out_shape=jax.ShapeDtypeStruct((2 * count, rows), BF16),
        scratch_shapes=[pltpu.VMEM((rows, 2 * count), F32)],
        compiler_params=params(),
        cost_estimate=cost(4 * rows * width * count, 4 * rows * width),
        name="own_source_cols",
    )(data_real, data_imag, row)


def select_kernel(cap, round_ref, got_ref, col_ref, out_ref):
    groups, _, rows = got_ref.shape
    count = col_ref.shape[0]
    col = col_ref[...]
    slot = ranks_of(col, rows) - round_ref[0] * cap
    inside = (slot >= 0) & (slot < cap)
    place = jnp.where(inside, (col // rows) * (2 * cap) + slot, -1)
    lanes = lax.broadcasted_iota(jnp.int32, (count, groups * 2 * cap), 1)
    pick = jnp.concatenate([lanes == place, lanes == jnp.where(inside, place + cap, -1)], axis=0)
    got = got_ref[...].reshape(groups * 2 * cap, rows)
    out_ref[...] = dot(pick.astype(F32).astype(BF16), got).astype(BF16)


def select_rows(got, col, which, cap):
    groups, _, rows = got.shape
    count = col.shape[0]
    return pl.pallas_call(
        functools.partial(select_kernel, cap),
        in_specs=[whole_smem(), whole_vmem(), whole_vmem()],
        out_specs=whole_vmem(),
        out_shape=jax.ShapeDtypeStruct((2 * count, rows), BF16),
        compiler_params=params(),
        cost_estimate=cost(8 * count * groups * cap * rows, 4 * groups * cap * rows),
        name="select_rows",
    )(which, got, col)


def panel_kernel(width, counts_ref, rowpart_ref, colpart_ref, col_ref, panel_ref, panel_t_ref):
    rows = rowpart_ref.shape[1]
    tile = width // TILES
    mine = lax.axis_index(AXIS) * rows // tile
    tiles = col_ref[...] // tile
    forward = jnp.zeros_like(tiles)
    backward = jnp.zeros_like(tiles)
    for t in range(TILES):
        forward = jnp.where(tiles == t, counts_ref[mine, t], forward)
        backward = jnp.where(tiles == t, counts_ref[t, mine], backward)
    forward = jnp.concatenate([forward, forward], axis=0).astype(F32)
    backward = jnp.concatenate([backward, backward], axis=0).astype(F32)
    own = colpart_ref[...].astype(F32)
    mirror = rowpart_ref[...].astype(F32)
    panel = (forward * own + backward * mirror) / jnp.maximum(forward + backward, 1.0)
    panel_t_ref[...] = panel.astype(BF16)
    panel_ref[...] = jnp.transpose(panel).astype(BF16)


def own_panel(counts, rowpart, colpart, col, width):
    double, rows = rowpart.shape
    return pl.pallas_call(
        functools.partial(panel_kernel, width),
        in_specs=[whole_smem(), whole_vmem(), whole_vmem(), whole_vmem()],
        out_specs=[whole_vmem(), whole_vmem()],
        out_shape=[
            jax.ShapeDtypeStruct((rows, double), BF16),
            jax.ShapeDtypeStruct((double, rows), BF16),
        ],
        compiler_params=params(),
        cost_estimate=cost(8 * rows * double, 8 * rows * double),
        name="own_panel",
    )(counts, rowpart, colpart, col)


def weight(counts_ref, mine, other, shape):
    forward = jnp.full(shape, counts_ref[mine, other], jnp.int32).astype(F32)
    backward = jnp.full(shape, counts_ref[other, mine], jnp.int32).astype(F32)
    return forward / jnp.maximum(forward + backward, 1.0)


def mirror_kernel(width, counts_ref, real_ref, imag_ref, panel_t_ref, out_ref):
    rows, step = real_ref.shape
    tile = width // TILES
    count = panel_t_ref.shape[0] // 2
    mine = lax.axis_index(AXIS) * rows // tile
    scale = weight(counts_ref, mine, pl.program_id(0) * step // tile, (1, step))
    panel_t = panel_t_ref[...]
    turned = jnp.concatenate([-panel_t[count:], panel_t[:count]], axis=0)
    found = (dot(panel_t, real_ref[...]) + dot(turned, imag_ref[...])) * scale
    for g in range(out_ref.shape[0]):
        out_ref[g] = found[:, g * rows : (g + 1) * rows]


def mirror_term(counts, data_real, data_imag, panel_t, step):
    rows, width = data_real.shape
    double = panel_t.shape[0]
    block = pl.BlockSpec((rows, step), lambda t: (0, t))
    return pl.pallas_call(
        functools.partial(mirror_kernel, width),
        grid=(width // step,),
        in_specs=[whole_smem(), block, block, whole_vmem()],
        out_specs=pl.BlockSpec((step // rows, double, rows), lambda t: (t, 0, 0)),
        out_shape=jax.ShapeDtypeStruct((width // rows, double, rows), F32),
        compiler_params=params(),
        cost_estimate=cost(4 * rows * width * double, 4 * rows * width + 2 * double * width),
        name="mirror_term",
    )(counts, data_real, data_imag, panel_t)


def direct_kernel(width, counts_ref, real_ref, imag_ref, panel_ref, out_ref):
    rows, step = real_ref.shape
    tile = width // TILES
    t = pl.program_id(0)
    count = panel_ref.shape[1] // 2
    mine = lax.axis_index(AXIS) * rows // tile

    @pl.when(t == 0)
    def _():
        out_ref[...] = jnp.zeros_like(out_ref)

    panel = panel_ref[...]
    turned = jnp.concatenate([-panel[:, count:], panel[:, :count]], axis=1)
    found = dot(real_ref[...], panel) + dot(imag_ref[...], turned)
    out_ref[...] += found * weight(counts_ref, mine, t * step // tile, (1, 2 * count))


def direct_term(counts, data_real, data_imag, panel, step):
    rows, width = data_real.shape
    double = panel.shape[1]
    block = pl.BlockSpec((rows, step), lambda t: (0, t))
    return pl.pallas_call(
        functools.partial(direct_kernel, width),
        grid=(width // step,),
        in_specs=[whole_smem(), block, block, pl.BlockSpec((step, double), lambda t: (t, 0))],
        out_specs=pl.BlockSpec((rows, double), lambda t: (0, 0)),
        out_shape=jax.ShapeDtypeStruct((rows, double), F32),
        compiler_params=params(),
        cost_estimate=cost(4 * rows * width * double, 4 * rows * width + 2 * double * width),
        name="direct_term",
    )(counts, data_real, data_imag, panel)


def block_at(me, span, dz, dy, dc):
    far, near = span
    z, y, c = me // (2 * near), (me // 2) % near, me % 2
    return (((z + dz) % far) * near + (y + dy) % near) * 2 + (c + dc) % 2


def shift(value, span, dz, dy, dc):
    size = 2 * span[0] * span[1]
    return lax.ppermute(value, AXIS, [(i, block_at(i, span, dz, dy, dc)) for i in range(size)])


def distance(order, i):
    dz = order[0]
    for at in range(1, len(order)):
        dz = jnp.where(i == at, order[at], dz)
    return dz


def mirror_part_kernel(
    width, span, order, me_ref, counts_ref, real_ref, imag_ref, panel_t_ref, other_ref, own_ref
):
    rows = real_ref.shape[1]
    tile = width // TILES
    count = panel_t_ref.shape[0] // 2
    turn, dy, i = pl.program_id(0), pl.program_id(1), pl.program_id(2)
    mine = me_ref[0] * rows // tile
    block = block_at(me_ref[0], span, distance(order, i), dy, 1 - turn)
    scale = weight(counts_ref, mine, block * rows // tile, (1, rows))
    panel_t = panel_t_ref[...]
    turned = jnp.concatenate([-panel_t[count:], panel_t[:count]], axis=0)
    found = (dot(panel_t, real_ref[...]) + dot(turned, imag_ref[...])) * scale

    @pl.when(turn == 0)
    def _():
        other_ref[0] = found.astype(BF16)

    @pl.when(turn == 1)
    def _():
        own_ref[0] = found


def mirror_part(me, counts, data_real, data_imag, panel_t, span, order):
    rows, width = data_real.shape
    double = panel_t.shape[0]
    near, some = span[1], len(order)
    last = near * some - 1
    block = pl.BlockSpec(
        (rows, rows),
        lambda turn, dy, i, me: (0, block_at(me[0], span, distance(order, i), dy, 1 - turn)),
    )
    spec = pltpu.PrefetchScalarGridSpec(
        num_scalar_prefetch=1,
        grid=(2, near, some),
        in_specs=[whole_smem(), block, block, whole_vmem()],
        out_specs=[
            pl.BlockSpec(
                (1, double, rows),
                lambda turn, dy, i, me: (jnp.where(turn == 0, dy * some + i, last), 0, 0),
            ),
            pl.BlockSpec(
                (1, double, rows),
                lambda turn, dy, i, me: (jnp.where(turn == 0, 0, dy * some + i), 0, 0),
            ),
        ],
    )
    return pl.pallas_call(
        functools.partial(mirror_part_kernel, width, span, order),
        grid_spec=spec,
        out_shape=[
            jax.ShapeDtypeStruct((near * some, double, rows), BF16),
            jax.ShapeDtypeStruct((near * some, double, rows), F32),
        ],
        compiler_params=params(),
        cost_estimate=cost(0, 0),
        name="mirror_part",
    )(me, counts, data_real, data_imag, panel_t)


def direct_part_kernel(width, span, way, me_ref, counts_ref, real_ref, imag_ref, panel_ref, *refs):
    out_ref = refs[-1]
    rows = real_ref.shape[0]
    tile = width // TILES
    count = panel_ref.shape[2] // 2
    k = pl.program_id(0)
    mine = me_ref[0] * rows // tile
    block = block_at(me_ref[0], span, span[0] - k, *way)
    scale = weight(counts_ref, mine, block * rows // tile, (1, 2 * count))
    panel = panel_ref[0]
    turned = jnp.concatenate([-panel[:, count:], panel[:, :count]], axis=1)
    found = (dot(real_ref[...], panel) + dot(imag_ref[...], turned)) * scale

    @pl.when(k == 0)
    def _():
        out_ref[...] = found + refs[0][...] if len(refs) == 2 else found

    @pl.when(k > 0)
    def _():
        out_ref[...] += found


def direct_part(me, counts, data_real, data_imag, panels, before, span, way):
    rows, width = data_real.shape
    double = panels.shape[2]
    block = pl.BlockSpec((rows, rows), lambda k, me: (0, block_at(me[0], span, span[0] - k, *way)))
    spec = pltpu.PrefetchScalarGridSpec(
        num_scalar_prefetch=1,
        grid=(panels.shape[0],),
        in_specs=[whole_smem(), block, block, pl.BlockSpec((1, rows, double), lambda k, me: (k, 0, 0))]
        + [whole_vmem()] * len(before),
        out_specs=pl.BlockSpec((rows, double), lambda k, me: (0, 0)),
    )
    return pl.pallas_call(
        functools.partial(direct_part_kernel, width, span, way),
        grid_spec=spec,
        out_shape=jax.ShapeDtypeStruct((rows, double), F32),
        compiler_params=params(),
        cost_estimate=cost(0, 0),
        name="direct_part",
    )(me, counts, data_real, data_imag, panels, *before)


def levels(me, counts, data_real, data_imag, panel, panel_t, span):
    far, near = span
    along = [shift(panel, span, dz, 0, 0) for dz in range(1, far)]
    beside = shift(panel, span, 0, 1, 0)

    def summed(order):
        some = len(order)
        other, own = mirror_part(me, counts, data_real, data_imag, panel_t, span, order)
        total = own + shift(other, span, 0, 0, 1).astype(F32)
        return total[:some] + shift(total[some:].astype(BF16), span, 0, 1, 0).astype(F32)

    half = summed((2, 1))
    mirrors = [shift(half[i].astype(BF16), span, dz, 0, 0) for i, dz in enumerate((2, 1))]
    half = summed((3, 0))
    mirrors += [shift(half[0].astype(BF16), span, 3, 0, 0), half[1]]

    column = jnp.stack([panel] + along)
    next_column = jnp.concatenate([beside[None], shift(jnp.stack(along), span, 0, 1, 0)])
    direct = []
    for way, panels in (
        ((0, 0), column),
        ((0, 1), shift(column, span, 0, 0, 1)),
        ((1, 0), next_column),
        ((1, 1), shift(next_column, span, 0, 0, 1)),
    ):
        direct = [direct_part(me, counts, data_real, data_imag, panels, direct, span, way)]
    return direct[0], mirrors


def finish_kernel(factor, direct_ref, *refs):
    mirror_refs, (real_ref, imag_ref) = refs[:-2], refs[-2:]
    count = real_ref.shape[1]
    mirror = mirror_refs[-1][...].astype(F32)
    for ref in mirror_refs[:-1]:
        mirror += ref[...].astype(F32)
    total = factor * (direct_ref[...] + jnp.transpose(mirror))
    real_ref[...] = total[:, :count]
    imag_ref[...] = total[:, count:]


def finish(direct, mirrors, width):
    rows, double = direct.shape
    shape = jax.ShapeDtypeStruct((rows, double // 2), F32)
    return pl.pallas_call(
        functools.partial(finish_kernel, -1.0 / math.sqrt(width)),
        in_specs=[whole_vmem()] * (1 + len(mirrors)),
        out_specs=[whole_vmem(), whole_vmem()],
        out_shape=[shape, shape],
        compiler_params=params(),
        cost_estimate=cost(4 * rows * double, 10 * rows * double),
        name="finish",
    )(direct, *mirrors)


def shards(data_real, data_imag, counts, source_cols):
    rows, width = data_real.shape
    groups = width // rows
    count = source_cols.shape[0]
    step = width // TILES
    cap = min(rows, count, -(-2 * count // groups // 8) * 8)
    col = source_cols.reshape(count, 1)
    row = source_cols.reshape(1, count)

    def exchange(which):
        sent = own_source_rows(data_real, data_imag, source_cols, which, cap)
        return lax.all_to_all(sent, AXIS, split_axis=0, concat_axis=0)

    first = jnp.zeros((1,), jnp.int32)
    got = exchange(first)
    colpart = own_source_cols(data_real, data_imag, row, step)
    rowpart = select_rows(got, col, first, cap)

    owner = source_cols // rows
    most = jnp.max(jnp.sum(owner[:, None] == jnp.arange(groups)[None, :], axis=0, dtype=jnp.int32))

    def more(state):
        return state[0] * cap < most

    def body(state):
        which, held = state
        one = which.reshape(1)
        return which + 1, held + select_rows(exchange(one), col, one, cap)

    _, rowpart = lax.while_loop(more, body, (jnp.int32(1), rowpart))

    panel, panel_t = own_panel(counts, rowpart, colpart, col, width)
    if rows % 128 == 0 and groups == 16:
        me = lax.axis_index(AXIS).reshape(1)
        direct, mirrors = levels(me, counts, data_real, data_imag, panel, panel_t, (4, 2))
    else:
        full = lax.all_gather(panel, AXIS, axis=0, tiled=True)
        partial = mirror_term(counts, data_real, data_imag, panel_t, step)
        mirrors = [lax.psum_scatter(partial, AXIS, scatter_dimension=0, tiled=False)]
        direct = direct_term(counts, data_real, data_imag, full, step)
    return tuple(finish(direct, mirrors, width))


def solution(mesh):
    placed = (P(("freq", "row"), None), P(("freq", "row"), None), P(), P())
    return jax.shard_map(
        shards,
        mesh=mesh,
        in_specs=placed,
        out_specs=(P(("freq", "row"), None), P(("freq", "row"), None)),
        check_vma=False,
    )
```

```python
import functools
import math

import jax
import jax.numpy as jnp
from jax import lax
from jax.experimental import pallas as pl
from jax.experimental.pallas import tpu as pltpu
from jax.sharding import PartitionSpec as P

TILES = 8
AXIS = "row"
GROUP = 16
PIECE = 1024
F32 = jnp.float32
BF16 = jnp.bfloat16


def params(mib=16):
    return pltpu.CompilerParams(vmem_limit_bytes=mib * 1024 * 1024)


def whole_vmem():
    return pl.BlockSpec(memory_space=pltpu.VMEM)


def anywhere():
    return pl.BlockSpec(memory_space=pl.ANY)


def whole_smem():
    return pl.BlockSpec(memory_space=pltpu.SMEM)


def cost(flops, size):
    return pl.CostEstimate(flops=flops, bytes_accessed=size, transcendentals=0)


def dot(left, right):
    return jnp.dot(left, right, preferred_element_type=F32)


def ranks_of(col, rows):
    count = col.shape[0]
    owner = col // rows
    owner_row = jnp.transpose(jnp.broadcast_to(owner.astype(F32), (count, count))).astype(jnp.int32)
    before = lax.broadcasted_iota(jnp.int32, (count, count), 1) < lax.broadcasted_iota(
        jnp.int32, (count, count), 0
    )
    same = (owner_row == owner) & before
    return jnp.sum(same.astype(F32), axis=1, keepdims=True).astype(jnp.int32)


def rows_kernel(cap, round_ref, col_ref, real_ref, imag_ref, out_ref, list_ref, near_ref, held_ref, sems):
    rows, width = real_ref.shape
    groups = out_ref.shape[0]
    count = col_ref.shape[0]
    base = lax.axis_index(AXIS) * rows
    skip = round_ref[0] * cap

    def copies(slot, local):
        group = pl.ds(pl.multiple_of(local // GROUP * GROUP, GROUP), GROUP)
        return [
            pltpu.make_async_copy(ref.at[group], near_ref.at[slot, part], sems.at[slot, part])
            for part, ref in enumerate((real_ref, imag_ref))
        ]

    def begin(s, found):
        local = col_ref[s] - base
        own = (local >= 0) & (local < rows)
        slot = found - skip

        @pl.when(own & (slot >= 0) & (slot < cap))
        def _():
            list_ref[slot] = local
            for copy in copies(slot, local):
                copy.start()

        return found + own.astype(jnp.int32)

    def pick(slot, _):
        local = list_ref[slot]
        chosen = lax.broadcasted_iota(jnp.int32, (GROUP, PIECE), 0) == local % GROUP
        for part, copy in enumerate(copies(slot, local)):
            copy.wait()
            for at in range(0, width, PIECE):
                group = near_ref[slot, part, :, at : at + PIECE].astype(F32)
                held_ref[pl.ds(part * cap + slot, 1), at : at + PIECE] = jnp.sum(
                    jnp.where(chosen, group, 0.0), axis=0, keepdims=True
                )
        return 0

    found = lax.fori_loop(0, count, begin, jnp.int32(0))
    held_ref[...] = jnp.zeros_like(held_ref)
    lax.fori_loop(0, jnp.clip(found - skip, 0, cap), pick, 0)
    for g in range(groups):
        out_ref[g] = held_ref[:, g * rows : (g + 1) * rows].astype(BF16)


def own_source_rows(data_real, data_imag, source_cols, which, cap):
    rows, width = data_real.shape
    return pl.pallas_call(
        functools.partial(rows_kernel, cap),
        in_specs=[whole_smem(), whole_smem(), anywhere(), anywhere()],
        out_specs=whole_vmem(),
        out_shape=jax.ShapeDtypeStruct((width // rows, 2 * cap, rows), BF16),
        scratch_shapes=[
            pltpu.SMEM((cap,), jnp.int32),
            pltpu.VMEM((cap, 2, GROUP, width), BF16),
            pltpu.VMEM((2 * cap, width), F32),
            pltpu.SemaphoreType.DMA((cap, 2)),
        ],
        compiler_params=params(24),
        cost_estimate=cost(0, 2 * cap * width),
        name="own_source_rows",
    )(which, source_cols, data_real, data_imag)


def cols_kernel(real_ref, imag_ref, row_ref, out_ref, acc_ref):
    rows, step = real_ref.shape
    count = row_ref.shape[1]
    t = pl.program_id(0)

    @pl.when(t == 0)
    def _():
        acc_ref[...] = jnp.zeros_like(acc_ref)

    place = lax.broadcasted_iota(jnp.int32, (step, count), 0) + t * step
    pick = (place == row_ref[...]).astype(F32).astype(BF16)
    acc_ref[:, :count] += dot(real_ref[...], pick)
    acc_ref[:, count:] += dot(imag_ref[...], pick)

    @pl.when(t == pl.num_programs(0) - 1)
    def _():
        out_ref[...] = jnp.transpose(acc_ref[...]).astype(BF16)


def own_source_cols(data_real, data_imag, row, step):
    rows, width = data_real.shape
    count = row.shape[1]
    block = pl.BlockSpec((rows, step), lambda t: (0, t))
    return pl.pallas_call(
        cols_kernel,
        grid=(width // step,),
        in_specs=[block, block, whole_vmem()],
        out_specs=pl.BlockSpec((2 * count, rows), lambda t: (0, 0)),
        out_shape=jax.ShapeDtypeStruct((2 * count, rows), BF16),
        scratch_shapes=[pltpu.VMEM((rows, 2 * count), F32)],
        compiler_params=params(),
        cost_estimate=cost(4 * rows * width * count, 4 * rows * width),
        name="own_source_cols",
    )(data_real, data_imag, row)


def select_kernel(cap, round_ref, got_ref, col_ref, out_ref):
    groups, _, rows = got_ref.shape
    count = col_ref.shape[0]
    col = col_ref[...]
    slot = ranks_of(col, rows) - round_ref[0] * cap
    inside = (slot >= 0) & (slot < cap)
    place = jnp.where(inside, (col // rows) * (2 * cap) + slot, -1)
    lanes = lax.broadcasted_iota(jnp.int32, (count, groups * 2 * cap), 1)
    pick = jnp.concatenate([lanes == place, lanes == jnp.where(inside, place + cap, -1)], axis=0)
    got = got_ref[...].reshape(groups * 2 * cap, rows)
    out_ref[...] = dot(pick.astype(F32).astype(BF16), got).astype(BF16)


def select_rows(got, col, which, cap):
    groups, _, rows = got.shape
    count = col.shape[0]
    return pl.pallas_call(
        functools.partial(select_kernel, cap),
        in_specs=[whole_smem(), whole_vmem(), whole_vmem()],
        out_specs=whole_vmem(),
        out_shape=jax.ShapeDtypeStruct((2 * count, rows), BF16),
        compiler_params=params(),
        cost_estimate=cost(8 * count * groups * cap * rows, 4 * groups * cap * rows),
        name="select_rows",
    )(which, got, col)


def panel_kernel(width, counts_ref, rowpart_ref, colpart_ref, col_ref, panel_ref, panel_t_ref):
    rows = rowpart_ref.shape[1]
    tile = width // TILES
    mine = lax.axis_index(AXIS) * rows // tile
    tiles = col_ref[...] // tile
    forward = jnp.zeros_like(tiles)
    backward = jnp.zeros_like(tiles)
    for t in range(TILES):
        forward = jnp.where(tiles == t, counts_ref[mine, t], forward)
        backward = jnp.where(tiles == t, counts_ref[t, mine], backward)
    forward = jnp.concatenate([forward, forward], axis=0).astype(F32)
    backward = jnp.concatenate([backward, backward], axis=0).astype(F32)
    own = colpart_ref[...].astype(F32)
    mirror = rowpart_ref[...].astype(F32)
    panel = (forward * own + backward * mirror) / jnp.maximum(forward + backward, 1.0)
    panel_t_ref[...] = panel.astype(BF16)
    panel_ref[...] = jnp.transpose(panel).astype(BF16)


def own_panel(counts, rowpart, colpart, col, width):
    double, rows = rowpart.shape
    return pl.pallas_call(
        functools.partial(panel_kernel, width),
        in_specs=[whole_smem(), whole_vmem(), whole_vmem(), whole_vmem()],
        out_specs=[whole_vmem(), whole_vmem()],
        out_shape=[
            jax.ShapeDtypeStruct((rows, double), BF16),
            jax.ShapeDtypeStruct((double, rows), BF16),
        ],
        compiler_params=params(),
        cost_estimate=cost(8 * rows * double, 8 * rows * double),
        name="own_panel",
    )(counts, rowpart, colpart, col)


def weight(counts_ref, mine, other, shape):
    forward = jnp.full(shape, counts_ref[mine, other], jnp.int32).astype(F32)
    backward = jnp.full(shape, counts_ref[other, mine], jnp.int32).astype(F32)
    return forward / jnp.maximum(forward + backward, 1.0)


def mirror_kernel(width, counts_ref, real_ref, imag_ref, panel_t_ref, out_ref):
    rows, step = real_ref.shape
    tile = width // TILES
    count = panel_t_ref.shape[0] // 2
    mine = lax.axis_index(AXIS) * rows // tile
    scale = weight(counts_ref, mine, pl.program_id(0) * step // tile, (1, step))
    panel_t = panel_t_ref[...]
    turned = jnp.concatenate([-panel_t[count:], panel_t[:count]], axis=0)
    found = (dot(panel_t, real_ref[...]) + dot(turned, imag_ref[...])) * scale
    for g in range(out_ref.shape[0]):
        out_ref[g] = found[:, g * rows : (g + 1) * rows]


def mirror_term(counts, data_real, data_imag, panel_t, step):
    rows, width = data_real.shape
    double = panel_t.shape[0]
    block = pl.BlockSpec((rows, step), lambda t: (0, t))
    return pl.pallas_call(
        functools.partial(mirror_kernel, width),
        grid=(width // step,),
        in_specs=[whole_smem(), block, block, whole_vmem()],
        out_specs=pl.BlockSpec((step // rows, double, rows), lambda t: (t, 0, 0)),
        out_shape=jax.ShapeDtypeStruct((width // rows, double, rows), F32),
        compiler_params=params(),
        cost_estimate=cost(4 * rows * width * double, 4 * rows * width + 2 * double * width),
        name="mirror_term",
    )(counts, data_real, data_imag, panel_t)


def direct_kernel(width, counts_ref, real_ref, imag_ref, panel_ref, out_ref):
    rows, step = real_ref.shape
    tile = width // TILES
    t = pl.program_id(0)
    count = panel_ref.shape[1] // 2
    mine = lax.axis_index(AXIS) * rows // tile

    @pl.when(t == 0)
    def _():
        out_ref[...] = jnp.zeros_like(out_ref)

    panel = panel_ref[...]
    turned = jnp.concatenate([-panel[:, count:], panel[:, :count]], axis=1)
    found = dot(real_ref[...], panel) + dot(imag_ref[...], turned)
    out_ref[...] += found * weight(counts_ref, mine, t * step // tile, (1, 2 * count))


def direct_term(counts, data_real, data_imag, panel, step):
    rows, width = data_real.shape
    double = panel.shape[1]
    block = pl.BlockSpec((rows, step), lambda t: (0, t))
    return pl.pallas_call(
        functools.partial(direct_kernel, width),
        grid=(width // step,),
        in_specs=[whole_smem(), block, block, pl.BlockSpec((step, double), lambda t: (t, 0))],
        out_specs=pl.BlockSpec((rows, double), lambda t: (0, 0)),
        out_shape=jax.ShapeDtypeStruct((rows, double), F32),
        compiler_params=params(),
        cost_estimate=cost(4 * rows * width * double, 4 * rows * width + 2 * double * width),
        name="direct_term",
    )(counts, data_real, data_imag, panel)


def block_at(me, span, dz, dy, dc):
    far, near = span
    z, y, c = me // (2 * near), (me // 2) % near, me % 2
    return (((z + dz) % far) * near + (y + dy) % near) * 2 + (c + dc) % 2


def shift(value, span, dz, dy, dc):
    size = 2 * span[0] * span[1]
    return lax.ppermute(value, AXIS, [(i, block_at(i, span, dz, dy, dc)) for i in range(size)])


def distance(order, i):
    dz = order[0]
    for at in range(1, len(order)):
        dz = jnp.where(i == at, order[at], dz)
    return dz


def mirror_part_kernel(
    width, span, order, me_ref, counts_ref, real_ref, imag_ref, panel_t_ref, *refs
):
    other_ref, own_ref = refs[-2:]
    rows = real_ref.shape[1]
    tile = width // TILES
    count = panel_t_ref.shape[0] // 2
    turn, dy, i = pl.program_id(0), pl.program_id(1), pl.program_id(2)
    mine = me_ref[0] * rows // tile
    block = block_at(me_ref[0], span, distance(order, i), dy, 1 - turn)
    scale = weight(counts_ref, mine, block * rows // tile, (1, rows))
    panel_t = panel_t_ref[...]
    turned = jnp.concatenate([-panel_t[count:], panel_t[:count]], axis=0)
    found = (dot(panel_t, real_ref[...]) + dot(turned, imag_ref[...])) * scale

    @pl.when(turn == 0)
    def _():
        other_ref[0] = found.astype(BF16)

    @pl.when(turn == 1)
    def _():
        own_ref[0] = found


def mirror_part(me, counts, data_real, data_imag, panel_t, span, order, after):
    rows, width = data_real.shape
    double = panel_t.shape[0]
    near, some = span[1], len(order)
    last = near * some - 1
    block = pl.BlockSpec(
        (rows, rows),
        lambda turn, dy, i, me: (0, block_at(me[0], span, distance(order, i), dy, 1 - turn)),
    )
    spec = pltpu.PrefetchScalarGridSpec(
        num_scalar_prefetch=1,
        grid=(2, near, some),
        in_specs=[whole_smem(), block, block, whole_vmem()] + [anywhere()] * len(after),
        out_specs=[
            pl.BlockSpec(
                (1, double, rows),
                lambda turn, dy, i, me: (jnp.where(turn == 0, dy * some + i, last), 0, 0),
            ),
            pl.BlockSpec(
                (1, double, rows),
                lambda turn, dy, i, me: (jnp.where(turn == 0, 0, dy * some + i), 0, 0),
            ),
        ],
    )
    return pl.pallas_call(
        functools.partial(mirror_part_kernel, width, span, order),
        grid_spec=spec,
        out_shape=[
            jax.ShapeDtypeStruct((near * some, double, rows), BF16),
            jax.ShapeDtypeStruct((near * some, double, rows), F32),
        ],
        compiler_params=params(),
        cost_estimate=cost(400000000000, 0),
        name="mirror_part",
    )(me, counts, data_real, data_imag, panel_t, *after)


def move(value, span, up, starts):
    far, near = span
    size = 2 * far * near
    pairs = [(i, block_at(i, span, up % far, 0, 0)) for i in range(size) if i // (2 * near) in starts]
    return lax.ppermute(value, AXIS, pairs)


def arrange_kernel(span, me_ref, up_ref, down_ref, up_two_ref, down_two_ref, end_ref, *refs):
    out_ref = refs[-1]
    z = me_ref[0] // (2 * span[1])

    def choose(at, which, yes_ref, no_ref):
        @pl.when(which)
        def _():
            out_ref[at] = yes_ref[...]

        @pl.when(jnp.logical_not(which))
        def _():
            out_ref[at] = no_ref[...]

    choose(0, z > 0, up_ref, end_ref)
    choose(1, z > 1, up_two_ref, down_two_ref)
    choose(2, z < span[0] - 1, down_ref, end_ref)


def arrange(me, blocks, span, after):
    return pl.pallas_call(
        functools.partial(arrange_kernel, span),
        in_specs=[whole_smem()] + [whole_vmem()] * len(blocks) + [anywhere()] * len(after),
        out_specs=whole_vmem(),
        out_shape=jax.ShapeDtypeStruct((span[0] - 1,) + blocks[0].shape, BF16),
        compiler_params=params(),
        cost_estimate=cost(0, 0),
        name="arrange",
    )(me, *blocks, *after)


def stack_kernel(count, *refs):
    out_ref = refs[-1]
    at = 0
    for ref in refs[:count]:
        if len(ref.shape) == 2:
            out_ref[at] = ref[...]
            at += 1
        else:
            out_ref[at : at + ref.shape[0]] = ref[...]
            at += ref.shape[0]


def stack(blocks, after):
    size = sum(1 if len(block.shape) == 2 else block.shape[0] for block in blocks)
    return pl.pallas_call(
        functools.partial(stack_kernel, len(blocks)),
        in_specs=[whole_vmem()] * len(blocks) + [anywhere()] * len(after),
        out_specs=whole_vmem(),
        out_shape=jax.ShapeDtypeStruct((size,) + blocks[0].shape[-2:], BF16),
        compiler_params=params(),
        cost_estimate=cost(0, 0),
        name="stack",
    )(*blocks, *after)


def direct_part_kernel(width, span, way, me_ref, counts_ref, real_ref, imag_ref, panel_ref, *refs):
    out_ref = refs[-1]
    rows = real_ref.shape[0]
    tile = width // TILES
    count = panel_ref.shape[2] // 2
    k = pl.program_id(0)
    mine = me_ref[0] * rows // tile
    block = block_at(me_ref[0], span, span[0] - k, *way)
    scale = weight(counts_ref, mine, block * rows // tile, (1, 2 * count))
    panel = panel_ref[0]
    turned = jnp.concatenate([-panel[:, count:], panel[:, :count]], axis=1)
    found = (dot(real_ref[...], panel) + dot(imag_ref[...], turned)) * scale

    @pl.when(k == 0)
    def _():
        out_ref[...] = found + refs[0][...] if len(refs) == 2 else found

    @pl.when(k > 0)
    def _():
        out_ref[...] += found


def direct_part(me, counts, data_real, data_imag, panels, before, span, way):
    rows, width = data_real.shape
    double = panels.shape[2]
    block = pl.BlockSpec((rows, rows), lambda k, me: (0, block_at(me[0], span, span[0] - k, *way)))
    spec = pltpu.PrefetchScalarGridSpec(
        num_scalar_prefetch=1,
        grid=(panels.shape[0],),
        in_specs=[whole_smem(), block, block, pl.BlockSpec((1, rows, double), lambda k, me: (k, 0, 0))]
        + [whole_vmem()] * len(before),
        out_specs=pl.BlockSpec((rows, double), lambda k, me: (0, 0)),
    )
    return pl.pallas_call(
        functools.partial(direct_part_kernel, width, span, way),
        grid_spec=spec,
        out_shape=jax.ShapeDtypeStruct((rows, double), F32),
        compiler_params=params(),
        cost_estimate=cost(0, 0),
        name="direct_part",
    )(me, counts, data_real, data_imag, panels, *before)


def levels(me, counts, data_real, data_imag, panel, panel_t, span):
    far, near = span
    up = move(panel, span, 1, (0, 1, 2))
    down = move(panel, span, -1, (1, 2, 3))
    beside = shift(panel, span, 0, 1, 0)

    def over_cores(order, after):
        some = len(order)
        other, own = mirror_part(me, counts, data_real, data_imag, panel_t, span, order, after)
        total = own + shift(other, span, 0, 0, 1).astype(F32)
        return total[:some], total[some:].astype(BF16)

    def over_y(kept, sent):
        return kept + shift(sent, span, 0, 1, 0).astype(F32)

    kept, sent = over_cores((2, 1), [])
    last_kept, last_sent = over_cores((3, 0), [up, down, beside])
    up_two = move(up, span, 1, (1, 2))
    down_two = move(down, span, -1, (1, 2))
    lower = me[0] // (2 * near) < far // 2
    carried = jnp.where(lower, down_two, up_two)
    end = lax.ppermute(
        carried,
        AXIS,
        [(i, block_at(i, span, 1, 0, 0)) for i in range(4 * near, 6 * near)]
        + [(i, block_at(i, span, far - 1, 0, 0)) for i in range(2 * near, 4 * near)],
    )
    half = over_y(kept, sent)
    to_z = [half[i].astype(BF16) for i in range(2)]
    mirrors = [shift(to_z[i], span, dz, 0, 0) for i, dz in enumerate((2, 1))]
    half = over_y(last_kept, last_sent)
    last_to_z = half[0].astype(BF16)
    mirrors += [shift(last_to_z, span, 3, 0, 0), half[1]]

    ahead = arrange(me, [up, down, up_two, down_two, end], span, to_z + [last_sent])
    column = stack([panel, ahead], [])
    direct = []

    def add(panels, way):
        direct[:] = [direct_part(me, counts, data_real, data_imag, panels, direct, span, way)]

    add(column, (0, 0))
    add(shift(column, span, 0, 0, 1), (0, 1))
    next_column = stack([beside, shift(ahead, span, 0, 1, 0)], mirrors[:3] + direct)
    add(next_column, (1, 0))
    add(shift(next_column, span, 0, 0, 1), (1, 1))
    return direct[0], mirrors


def finish_kernel(factor, direct_ref, *refs):
    mirror_refs, (real_ref, imag_ref) = refs[:-2], refs[-2:]
    count = real_ref.shape[1]
    mirror = mirror_refs[-1][...].astype(F32)
    for ref in mirror_refs[:-1]:
        mirror += ref[...].astype(F32)
    total = factor * (direct_ref[...] + jnp.transpose(mirror))
    real_ref[...] = total[:, :count]
    imag_ref[...] = total[:, count:]


def finish(direct, mirrors, width):
    rows, double = direct.shape
    shape = jax.ShapeDtypeStruct((rows, double // 2), F32)
    return pl.pallas_call(
        functools.partial(finish_kernel, -1.0 / math.sqrt(width)),
        in_specs=[whole_vmem()] * (1 + len(mirrors)),
        out_specs=[whole_vmem(), whole_vmem()],
        out_shape=[shape, shape],
        compiler_params=params(),
        cost_estimate=cost(4 * rows * double, 10 * rows * double),
        name="finish",
    )(direct, *mirrors)


def shards(data_real, data_imag, counts, source_cols):
    rows, width = data_real.shape
    groups = width // rows
    count = source_cols.shape[0]
    step = width // TILES
    cap = min(rows, count, -(-2 * count // groups // 8) * 8)
    col = source_cols.reshape(count, 1)
    row = source_cols.reshape(1, count)

    def exchange(which):
        sent = own_source_rows(data_real, data_imag, source_cols, which, cap)
        return lax.all_to_all(sent, AXIS, split_axis=0, concat_axis=0)

    first = jnp.zeros((1,), jnp.int32)
    got = exchange(first)
    colpart = own_source_cols(data_real, data_imag, row, step)
    rowpart = select_rows(got, col, first, cap)

    owner = source_cols // rows
    most = jnp.max(jnp.sum(owner[:, None] == jnp.arange(groups)[None, :], axis=0, dtype=jnp.int32))

    def further(rowpart):
        def body(which, held):
            one = which.reshape(1)
            return held + select_rows(exchange(one), col, one, cap)

        return lax.fori_loop(1, (most + cap - 1) // cap, body, rowpart)

    rowpart = lax.cond(most > cap, further, lambda rowpart: rowpart, rowpart)

    panel, panel_t = own_panel(counts, rowpart, colpart, col, width)
    if rows % 128 == 0 and groups == 16:
        me = lax.axis_index(AXIS).reshape(1)
        direct, mirrors = levels(me, counts, data_real, data_imag, panel, panel_t, (4, 2))
    else:
        full = lax.all_gather(panel, AXIS, axis=0, tiled=True)
        partial = mirror_term(counts, data_real, data_imag, panel_t, step)
        mirrors = [lax.psum_scatter(partial, AXIS, scatter_dimension=0, tiled=False)]
        direct = direct_term(counts, data_real, data_imag, full, step)
    return tuple(finish(direct, mirrors, width))


def solution(mesh):
    placed = (P(("freq", "row"), None), P(("freq", "row"), None), P(), P())
    return jax.shard_map(
        shards,
        mesh=mesh,
        in_specs=placed,
        out_specs=(P(("freq", "row"), None), P(("freq", "row"), None)),
        check_vma=False,
    )
```

```python
import functools
import math

import jax
import jax.numpy as jnp
from jax import lax
from jax.experimental import pallas as pl
from jax.experimental.pallas import tpu as pltpu
from jax.sharding import PartitionSpec as P

TILES = 8
AXIS = "row"
GROUP = 16
PIECE = 1024
F32 = jnp.float32
BF16 = jnp.bfloat16


def params(mib=16):
    return pltpu.CompilerParams(vmem_limit_bytes=mib * 1024 * 1024)


def whole_vmem():
    return pl.BlockSpec(memory_space=pltpu.VMEM)


def anywhere():
    return pl.BlockSpec(memory_space=pl.ANY)


def in_vmem(value):
    return pltpu.with_memory_space_constraint(value, pltpu.VMEM)


def whole_smem():
    return pl.BlockSpec(memory_space=pltpu.SMEM)


def cost(flops, size):
    return pl.CostEstimate(flops=flops, bytes_accessed=size, transcendentals=0)


def dot(left, right):
    return jnp.dot(left, right, preferred_element_type=F32)


def ranks_of(col, rows):
    count = col.shape[0]
    owner = col // rows
    owner_row = jnp.transpose(jnp.broadcast_to(owner.astype(F32), (count, count))).astype(jnp.int32)
    before = lax.broadcasted_iota(jnp.int32, (count, count), 1) < lax.broadcasted_iota(
        jnp.int32, (count, count), 0
    )
    same = (owner_row == owner) & before
    return jnp.sum(same.astype(F32), axis=1, keepdims=True).astype(jnp.int32)


def rows_kernel(cap, round_ref, col_ref, real_ref, imag_ref, out_ref, list_ref, near_ref, held_ref, sems):
    rows, width = real_ref.shape
    groups = out_ref.shape[0]
    count = col_ref.shape[0]
    base = lax.axis_index(AXIS) * rows
    skip = round_ref[0] * cap

    def copies(slot, local):
        group = pl.ds(pl.multiple_of(local // GROUP * GROUP, GROUP), GROUP)
        return [
            pltpu.make_async_copy(ref.at[group], near_ref.at[slot, part], sems.at[slot, part])
            for part, ref in enumerate((real_ref, imag_ref))
        ]

    def begin(s, found):
        local = col_ref[s] - base
        own = (local >= 0) & (local < rows)
        slot = found - skip

        @pl.when(own & (slot >= 0) & (slot < cap))
        def _():
            list_ref[slot] = local
            for copy in copies(slot, local):
                copy.start()

        return found + own.astype(jnp.int32)

    def pick(slot, _):
        local = list_ref[slot]
        chosen = lax.broadcasted_iota(jnp.int32, (GROUP, PIECE), 0) == local % GROUP
        for part, copy in enumerate(copies(slot, local)):
            copy.wait()
            for at in range(0, width, PIECE):
                group = near_ref[slot, part, :, at : at + PIECE].astype(F32)
                held_ref[pl.ds(part * cap + slot, 1), at : at + PIECE] = jnp.sum(
                    jnp.where(chosen, group, 0.0), axis=0, keepdims=True
                )
        return 0

    found = lax.fori_loop(0, count, begin, jnp.int32(0))
    held_ref[...] = jnp.zeros_like(held_ref)
    lax.fori_loop(0, jnp.clip(found - skip, 0, cap), pick, 0)
    for g in range(groups):
        out_ref[g] = held_ref[:, g * rows : (g + 1) * rows].astype(BF16)


def own_source_rows(data_real, data_imag, source_cols, which, cap):
    rows, width = data_real.shape
    return pl.pallas_call(
        functools.partial(rows_kernel, cap),
        in_specs=[whole_smem(), whole_smem(), anywhere(), anywhere()],
        out_specs=whole_vmem(),
        out_shape=jax.ShapeDtypeStruct((width // rows, 2 * cap, rows), BF16),
        scratch_shapes=[
            pltpu.SMEM((cap,), jnp.int32),
            pltpu.VMEM((cap, 2, GROUP, width), BF16),
            pltpu.VMEM((2 * cap, width), F32),
            pltpu.SemaphoreType.DMA((cap, 2)),
        ],
        compiler_params=params(24),
        cost_estimate=cost(0, 2 * cap * width),
        name="own_source_rows",
    )(which, source_cols, data_real, data_imag)


def hold_kernel(real_ref, imag_ref, row_ref, held_ref, cols_ref, acc_ref, sems):
    rows, width = real_ref.shape
    count = row_ref.shape[1]
    step = width // sems.shape[1]

    def copy(part, t):
        ref = (real_ref, imag_ref)[part]
        there = held_ref.at[pl.ds(part * rows, rows), pl.ds(t * step, step)]
        return pltpu.make_async_copy(ref.at[:, pl.ds(t * step, step)], there, sems.at[part, t])

    steps = [(part, t) for t in range(sems.shape[1]) for part in range(2)]
    for part, t in steps:
        copy(part, t).start()
    acc_ref[...] = jnp.zeros_like(acc_ref)
    for t in range(sems.shape[1]):
        place = lax.broadcasted_iota(jnp.int32, (step, count), 0) + t * step
        pick = (place == row_ref[...]).astype(F32).astype(BF16)
        for part in range(2):
            copy(part, t).wait()
        acc_ref[...] += dot(held_ref[:, t * step : (t + 1) * step], pick)
    cols_ref[:count] = jnp.transpose(acc_ref[:rows]).astype(BF16)
    cols_ref[count:] = jnp.transpose(acc_ref[rows:]).astype(BF16)


def hold(data_real, data_imag, row):
    rows, width = data_real.shape
    count = row.shape[1]
    return pl.pallas_call(
        hold_kernel,
        in_specs=[anywhere(), anywhere(), whole_vmem()],
        out_specs=[whole_vmem(), whole_vmem()],
        out_shape=[pltpu.VMEM((2 * rows, width), BF16), pltpu.VMEM((2 * count, rows), BF16)],
        scratch_shapes=[
            pltpu.VMEM((2 * rows, count), F32),
            pltpu.SemaphoreType.DMA((2, TILES)),
        ],
        compiler_params=params(),
        cost_estimate=cost(4 * rows * width * count, 4 * rows * width),
        name="hold",
    )(data_real, data_imag, row)


def select_kernel(cap, round_ref, got_ref, col_ref, out_ref):
    out_ref[...] = pick_rows(cap, round_ref[0], got_ref, col_ref).astype(BF16)


def select_rows(got, col, which, cap):
    groups, _, rows = got.shape
    count = col.shape[0]
    return pl.pallas_call(
        functools.partial(select_kernel, cap),
        in_specs=[whole_smem(), whole_vmem(), whole_vmem()],
        out_specs=whole_vmem(),
        out_shape=jax.ShapeDtypeStruct((2 * count, rows), BF16),
        compiler_params=params(),
        cost_estimate=cost(8 * count * groups * cap * rows, 4 * groups * cap * rows),
        name="select_rows",
    )(which, got, col)


def pick_rows(cap, which, got_ref, col_ref):
    groups, _, rows = got_ref.shape
    count = col_ref.shape[0]
    col = col_ref[...]
    slot = ranks_of(col, rows) - which * cap
    inside = (slot >= 0) & (slot < cap)
    place = jnp.where(inside, (col // rows) * (2 * cap) + slot, -1)
    lanes = lax.broadcasted_iota(jnp.int32, (count, groups * 2 * cap), 1)
    pick = jnp.concatenate([lanes == place, lanes == jnp.where(inside, place + cap, -1)], axis=0)
    got = got_ref[...].reshape(groups * 2 * cap, rows)
    return dot(pick.astype(F32).astype(BF16), got)


def panel_kernel(
    width, cap, counts_ref, got_ref, more_ref, colpart_ref, col_ref, panel_ref, panel_t_ref
):
    double, rows = colpart_ref.shape
    count = double // 2
    tile = width // TILES
    mine = lax.axis_index(AXIS) * rows // tile
    tiles = col_ref[...] // tile
    forward = jnp.zeros_like(tiles)
    backward = jnp.zeros_like(tiles)
    for t in range(TILES):
        forward = jnp.where(tiles == t, counts_ref[mine, t], forward)
        backward = jnp.where(tiles == t, counts_ref[t, mine], backward)
    forward = jnp.concatenate([forward, forward], axis=0).astype(F32)
    backward = jnp.concatenate([backward, backward], axis=0).astype(F32)
    own = colpart_ref[...].astype(F32)
    mirror = pick_rows(cap, 0, got_ref, col_ref) + more_ref[...].astype(F32)
    panel = (forward * own + backward * mirror) / jnp.maximum(forward + backward, 1.0)
    panel_t_ref[:, :rows] = panel.astype(BF16)
    panel_t_ref[:count, rows:] = (-panel[count:]).astype(BF16)
    panel_t_ref[count:, rows:] = panel[:count].astype(BF16)
    panel_ref[...] = jnp.transpose(panel).astype(BF16)


def own_panel(counts, got, more, colpart, col, width, cap):
    double, rows = colpart.shape
    return pl.pallas_call(
        functools.partial(panel_kernel, width, cap),
        in_specs=[whole_smem(), whole_vmem(), whole_vmem(), whole_vmem(), whole_vmem()],
        out_specs=[whole_vmem(), whole_vmem()],
        out_shape=[pltpu.VMEM((rows, double), BF16), pltpu.VMEM((double, 2 * rows), BF16)],
        compiler_params=params(),
        cost_estimate=cost(8 * rows * double, 8 * rows * double),
        name="own_panel",
    )(counts, in_vmem(got), more, colpart, col)


def weight(counts_ref, mine, other, shape):
    forward = jnp.full(shape, counts_ref[mine, other], jnp.int32).astype(F32)
    backward = jnp.full(shape, counts_ref[other, mine], jnp.int32).astype(F32)
    return forward / jnp.maximum(forward + backward, 1.0)


def mirror_kernel(width, counts_ref, held_ref, panel_t_ref, out_ref):
    rows = held_ref.shape[0] // 2
    tile = width // TILES
    mine = lax.axis_index(AXIS) * rows // tile
    panel_t = panel_t_ref[...]
    for t in range(TILES):
        found = dot(panel_t, held_ref[:, t * tile : (t + 1) * tile])
        found = found * weight(counts_ref, mine, t, (1, tile))
        for g in range(tile // rows):
            out_ref[t * (tile // rows) + g] = found[:, g * rows : (g + 1) * rows]


def mirror_term(counts, held, panel_t):
    rows, width = held.shape[0] // 2, held.shape[1]
    double = panel_t.shape[0]
    return pl.pallas_call(
        functools.partial(mirror_kernel, width),
        in_specs=[whole_smem(), whole_vmem(), whole_vmem()],
        out_specs=whole_vmem(),
        out_shape=jax.ShapeDtypeStruct((width // rows, double, rows), F32),
        compiler_params=params(32),
        cost_estimate=cost(4 * rows * width * double, 4 * rows * width + 2 * double * width),
        name="mirror_term",
    )(counts, held, panel_t)


def direct_kernel(width, counts_ref, held_ref, panel_ref, out_ref):
    rows = held_ref.shape[0] // 2
    tile = width // TILES
    mine = lax.axis_index(AXIS) * rows // tile
    total = jnp.zeros(out_ref.shape, F32)
    for t in range(TILES):
        columns = slice(t * tile, (t + 1) * tile)
        found = block_product(held_ref, columns, panel_ref[columns, :])
        total += found * weight(counts_ref, mine, t, (1, out_ref.shape[1]))
    out_ref[...] = total


def block_product(held_ref, columns, panel):
    rows = held_ref.shape[0] // 2
    count = panel.shape[1] // 2
    turned = jnp.concatenate([-panel[:, count:], panel[:, :count]], axis=1)
    return dot(held_ref[:rows, columns], panel) + dot(held_ref[rows:, columns], turned)


def direct_term(counts, held, panel):
    rows, width = held.shape[0] // 2, held.shape[1]
    double = panel.shape[1]
    return pl.pallas_call(
        functools.partial(direct_kernel, width),
        in_specs=[whole_smem(), whole_vmem(), whole_vmem()],
        out_specs=whole_vmem(),
        out_shape=jax.ShapeDtypeStruct((rows, double), F32),
        compiler_params=params(32),
        cost_estimate=cost(4 * rows * width * double, 4 * rows * width + 2 * double * width),
        name="direct_term",
    )(counts, held, panel)


def block_at(me, span, dz, dy, dc):
    far, near = span
    z, y, c = me // (2 * near), (me // 2) % near, me % 2
    return (((z + dz) % far) * near + (y + dy) % near) * 2 + (c + dc) % 2


def shift(value, span, dz, dy, dc):
    size = 2 * span[0] * span[1]
    return lax.ppermute(value, AXIS, [(i, block_at(i, span, dz, dy, dc)) for i in range(size)])


def mirror_part_kernel(
    width, span, order, me_ref, counts_ref, held_ref, panel_t_ref, *refs
):
    other_ref, own_ref = refs[-2:]
    rows = held_ref.shape[0] // 2
    tile = width // TILES
    me = me_ref[0]
    mine = me * rows // tile
    panel_t = panel_t_ref[...]
    for dy in range(span[1]):
        for i, dz in enumerate(order):
            for turn in range(2):
                block = block_at(me, span, dz, dy, 1 - turn)
                scale = weight(counts_ref, mine, block * rows // tile, (1, rows))
                columns = pl.ds(pl.multiple_of(block * rows, rows), rows)
                found = dot(panel_t, held_ref[:, columns]) * scale
                if turn == 0:
                    other_ref[dy * len(order) + i] = found.astype(BF16)
                else:
                    own_ref[dy * len(order) + i] = found


def mirror_part(me, counts, held, panel_t, span, order, after):
    rows, width = held.shape[0] // 2, held.shape[1]
    double = panel_t.shape[0]
    blocks = span[1] * len(order)
    return pl.pallas_call(
        functools.partial(mirror_part_kernel, width, span, order),
        in_specs=[whole_smem(), whole_smem(), whole_vmem(), whole_vmem()] + [anywhere()] * len(after),
        out_specs=[whole_vmem(), whole_vmem()],
        out_shape=[
            pltpu.VMEM((blocks, double, rows), BF16),
            pltpu.VMEM((blocks, double, rows), F32),
        ],
        compiler_params=params(),
        cost_estimate=cost(400000000000, 0),
        name="mirror_part",
    )(me, counts, held, panel_t, *after)


def move(value, span, up, starts):
    far, near = span
    size = 2 * far * near
    pairs = [(i, block_at(i, span, up % far, 0, 0)) for i in range(size) if i // (2 * near) in starts]
    return lax.ppermute(value, AXIS, pairs)


def arrange_kernel(span, me_ref, up_ref, down_ref, up_two_ref, down_two_ref, end_ref, *refs):
    out_ref = refs[-1]
    z = me_ref[0] // (2 * span[1])

    def choose(at, which, yes_ref, no_ref):
        @pl.when(which)
        def _():
            out_ref[at] = yes_ref[...]

        @pl.when(jnp.logical_not(which))
        def _():
            out_ref[at] = no_ref[...]

    choose(0, z > 0, up_ref, end_ref)
    choose(1, z > 1, up_two_ref, down_two_ref)
    choose(2, z < span[0] - 1, down_ref, end_ref)


def arrange(me, blocks, span, after):
    return pl.pallas_call(
        functools.partial(arrange_kernel, span),
        in_specs=[whole_smem()] + [whole_vmem()] * len(blocks) + [anywhere()] * len(after),
        out_specs=whole_vmem(),
        out_shape=pltpu.VMEM((span[0] - 1,) + blocks[0].shape, BF16),
        compiler_params=params(),
        cost_estimate=cost(0, 0),
        name="arrange",
    )(me, *[in_vmem(block) for block in blocks], *after)


def stack_kernel(count, *refs):
    out_ref = refs[-1]
    at = 0
    for ref in refs[:count]:
        if len(ref.shape) == 2:
            out_ref[at] = ref[...]
            at += 1
        else:
            out_ref[at : at + ref.shape[0]] = ref[...]
            at += ref.shape[0]


def stack(blocks, after):
    size = sum(1 if len(block.shape) == 2 else block.shape[0] for block in blocks)
    return pl.pallas_call(
        functools.partial(stack_kernel, len(blocks)),
        in_specs=[whole_vmem()] * len(blocks) + [anywhere()] * len(after),
        out_specs=whole_vmem(),
        out_shape=pltpu.VMEM((size,) + blocks[0].shape[-2:], BF16),
        compiler_params=params(),
        cost_estimate=cost(0, 0),
        name="stack",
    )(*[in_vmem(block) for block in blocks], *after)


def direct_part_kernel(width, span, way, me_ref, counts_ref, held_ref, panel_ref, *refs):
    out_ref = refs[-1]
    rows = held_ref.shape[0] // 2
    tile = width // TILES
    me = me_ref[0]
    mine = me * rows // tile
    total = refs[0][...] if len(refs) == 2 else jnp.zeros(out_ref.shape, F32)
    for k in range(panel_ref.shape[0]):
        block = block_at(me, span, span[0] - k, *way)
        columns = pl.ds(pl.multiple_of(block * rows, rows), rows)
        scale = weight(counts_ref, mine, block * rows // tile, (1, out_ref.shape[1]))
        total += block_product(held_ref, columns, panel_ref[k]) * scale
    out_ref[...] = total


def direct_part(me, counts, held, panels, before, span, way):
    rows, width = held.shape[0] // 2, held.shape[1]
    double = panels.shape[2]
    return pl.pallas_call(
        functools.partial(direct_part_kernel, width, span, way),
        in_specs=[whole_smem(), whole_smem()] + [whole_vmem()] * (2 + len(before)),
        out_specs=whole_vmem(),
        out_shape=pltpu.VMEM((rows, double), F32),
        compiler_params=params(),
        cost_estimate=cost(0, 0),
        name="direct_part",
    )(me, counts, held, in_vmem(panels), *before)


def levels(me, counts, held, panel, panel_t, span):
    far, near = span
    up = move(panel, span, 1, (0, 1, 2))
    down = move(panel, span, -1, (1, 2, 3))
    beside = shift(panel, span, 0, 1, 0)

    def over_cores(order, after):
        some = len(order)
        other, own = mirror_part(me, counts, held, panel_t, span, order, after)
        total = own + shift(other, span, 0, 0, 1).astype(F32)
        return total[:some], total[some:].astype(BF16)

    def over_y(kept, sent):
        return kept + shift(sent, span, 0, 1, 0).astype(F32)

    kept, sent = over_cores((2, 1), [])
    last_kept, last_sent = over_cores((3, 0), [up, down, beside])
    up_two = move(up, span, 1, (1, 2))
    down_two = move(down, span, -1, (1, 2))
    lower = me[0] // (2 * near) < far // 2
    carried = jnp.where(lower, down_two, up_two)
    end = lax.ppermute(
        carried,
        AXIS,
        [(i, block_at(i, span, 1, 0, 0)) for i in range(4 * near, 6 * near)]
        + [(i, block_at(i, span, far - 1, 0, 0)) for i in range(2 * near, 4 * near)],
    )
    half = over_y(kept, sent)
    to_z = [half[i].astype(BF16) for i in range(2)]
    mirrors = [shift(to_z[i], span, dz, 0, 0) for i, dz in enumerate((2, 1))]
    half = over_y(last_kept, last_sent)
    last_to_z = half[0].astype(BF16)
    mirrors += [shift(last_to_z, span, 3, 0, 0), half[1]]

    ahead = arrange(me, [up, down, up_two, down_two, end], span, to_z + [last_sent])
    column = stack([panel, ahead], [])
    direct = []

    def add(panels, way):
        direct[:] = [direct_part(me, counts, held, panels, direct, span, way)]

    add(column, (0, 0))
    add(shift(column, span, 0, 0, 1), (0, 1))
    next_column = stack([beside, shift(ahead, span, 0, 1, 0)], mirrors[:3] + direct)
    add(next_column, (1, 0))
    add(shift(next_column, span, 0, 0, 1), (1, 1))
    return direct[0], mirrors


def finish_kernel(factor, direct_ref, *refs):
    mirror_refs, (real_ref, imag_ref) = refs[:-2], refs[-2:]
    count = real_ref.shape[1]
    mirror = mirror_refs[-1][...].astype(F32)
    for ref in mirror_refs[:-1]:
        mirror += ref[...].astype(F32)
    total = factor * (direct_ref[...] + jnp.transpose(mirror))
    real_ref[...] = total[:, :count]
    imag_ref[...] = total[:, count:]


def finish(direct, mirrors, width):
    rows, double = direct.shape
    shape = jax.ShapeDtypeStruct((rows, double // 2), F32)
    return pl.pallas_call(
        functools.partial(finish_kernel, -1.0 / math.sqrt(width)),
        in_specs=[whole_vmem()] * (1 + len(mirrors)),
        out_specs=[whole_vmem(), whole_vmem()],
        out_shape=[shape, shape],
        compiler_params=params(),
        cost_estimate=cost(4 * rows * double, 10 * rows * double),
        name="finish",
    )(in_vmem(direct), *[in_vmem(mirror) for mirror in mirrors])


def shards(data_real, data_imag, counts, source_cols):
    rows, width = data_real.shape
    groups = width // rows
    count = source_cols.shape[0]
    cap = min(rows, count, -(-2 * count // groups // 8) * 8)
    col = source_cols.reshape(count, 1)
    row = source_cols.reshape(1, count)

    def exchange(which):
        sent = own_source_rows(data_real, data_imag, source_cols, which, cap)
        return lax.all_to_all(sent, AXIS, split_axis=0, concat_axis=0)

    first = jnp.zeros((1,), jnp.int32)
    got = exchange(first)
    held, colpart = hold(data_real, data_imag, row)

    owner = source_cols // rows
    most = jnp.max(jnp.sum(owner[:, None] == jnp.arange(groups)[None, :], axis=0, dtype=jnp.int32))

    def further():
        def body(which, found):
            one = which.reshape(1)
            return found + select_rows(exchange(one), col, one, cap)

        return lax.fori_loop(1, (most + cap - 1) // cap, body, nothing())

    def nothing():
        return jnp.zeros((2 * count, rows), BF16)

    more = lax.cond(most > cap, further, nothing)
    panel, panel_t = own_panel(counts, got, more, colpart, col, width, cap)
    if rows % 128 == 0 and groups == 16:
        me = lax.axis_index(AXIS).reshape(1)
        direct, mirrors = levels(me, counts, held, panel, panel_t, (4, 2))
    else:
        full = lax.all_gather(panel, AXIS, axis=0, tiled=True)
        partial = mirror_term(counts, held, panel_t)
        mirrors = [lax.psum_scatter(partial, AXIS, scatter_dimension=0, tiled=False)]
        direct = direct_term(counts, held, full)
    return tuple(finish(direct, mirrors, width))


def solution(mesh):
    placed = (P(("freq", "row"), None), P(("freq", "row"), None), P(), P())
    return jax.shard_map(
        shards,
        mesh=mesh,
        in_specs=placed,
        out_specs=(P(("freq", "row"), None), P(("freq", "row"), None)),
        check_vma=False,
    )
```

```python
import functools
import math

import jax
import jax.numpy as jnp
from jax import lax
from jax.experimental import pallas as pl
from jax.experimental.pallas import tpu as pltpu
from jax.sharding import PartitionSpec as P

TILES = 8
AXIS = "row"
GROUP = 16
PIECE = 1024
F32 = jnp.float32
BF16 = jnp.bfloat16


def params(mib=16):
    return pltpu.CompilerParams(vmem_limit_bytes=mib * 1024 * 1024)


def whole_vmem():
    return pl.BlockSpec(memory_space=pltpu.VMEM)


def anywhere():
    return pl.BlockSpec(memory_space=pl.ANY)


def in_vmem(value):
    return pltpu.with_memory_space_constraint(value, pltpu.VMEM)


def whole_smem():
    return pl.BlockSpec(memory_space=pltpu.SMEM)


def cost(flops, size):
    return pl.CostEstimate(flops=flops, bytes_accessed=size, transcendentals=0)


def dot(left, right):
    return jnp.dot(left, right, preferred_element_type=F32)


def ranks_of(col, rows):
    count = col.shape[0]
    owner = col // rows
    owner_row = jnp.transpose(jnp.broadcast_to(owner.astype(F32), (count, count))).astype(jnp.int32)
    before = lax.broadcasted_iota(jnp.int32, (count, count), 1) < lax.broadcasted_iota(
        jnp.int32, (count, count), 0
    )
    same = (owner_row == owner) & before
    return jnp.sum(same.astype(F32), axis=1, keepdims=True).astype(jnp.int32)


def rows_kernel(cap, round_ref, me_ref, col_ref, real_ref, imag_ref, out_ref, list_ref, near_ref, held_ref, sems):
    rows, width = real_ref.shape
    groups = out_ref.shape[0]
    count = col_ref.shape[0]
    base = me_ref[0] * rows
    skip = round_ref[0] * cap

    def copies(slot, local):
        group = pl.ds(pl.multiple_of(local // GROUP * GROUP, GROUP), GROUP)
        return [
            pltpu.make_async_copy(ref.at[group], near_ref.at[slot, part], sems.at[slot, part])
            for part, ref in enumerate((real_ref, imag_ref))
        ]

    def begin(s, found):
        local = col_ref[s] - base
        own = (local >= 0) & (local < rows)
        slot = found - skip

        @pl.when(own & (slot >= 0) & (slot < cap))
        def _():
            list_ref[slot] = local
            for copy in copies(slot, local):
                copy.start()

        return found + own.astype(jnp.int32)

    def pick(slot, _):
        local = list_ref[slot]
        chosen = lax.broadcasted_iota(jnp.int32, (GROUP, PIECE), 0) == local % GROUP
        for part, copy in enumerate(copies(slot, local)):
            copy.wait()
            for at in range(0, width, PIECE):
                group = near_ref[slot, part, :, at : at + PIECE].astype(F32)
                held_ref[pl.ds(part * cap + slot, 1), at : at + PIECE] = jnp.sum(
                    jnp.where(chosen, group, 0.0), axis=0, keepdims=True
                )
        return 0

    found = lax.fori_loop(0, count, begin, jnp.int32(0))
    held_ref[...] = jnp.zeros_like(held_ref)
    lax.fori_loop(0, jnp.clip(found - skip, 0, cap), pick, 0)
    for g in range(groups):
        out_ref[g] = held_ref[:, g * rows : (g + 1) * rows].astype(BF16)


def own_source_rows(me, data_real, data_imag, source_cols, which, cap):
    rows, width = data_real.shape
    return pl.pallas_call(
        functools.partial(rows_kernel, cap),
        in_specs=[whole_smem()] * 3 + [anywhere()] * 2,
        out_specs=whole_vmem(),
        out_shape=jax.ShapeDtypeStruct((width // rows, 2 * cap, rows), BF16),
        scratch_shapes=[
            pltpu.SMEM((cap,), jnp.int32),
            pltpu.VMEM((cap, 2, GROUP, width), BF16),
            pltpu.VMEM((2 * cap, width), F32),
            pltpu.SemaphoreType.DMA((cap, 2)),
        ],
        compiler_params=params(24),
        cost_estimate=cost(0, 2 * cap * width),
        name="own_source_rows",
    )(which, me, source_cols, data_real, data_imag)


def hold_kernel(
    real_ref, imag_ref, row_ref, col_ref, held_ref, cols_ref, most_ref, acc_ref, sems
):
    rows, width = real_ref.shape
    count = row_ref.shape[1]
    step = width // sems.shape[1]

    def copy(part, t):
        ref = (real_ref, imag_ref)[part]
        there = held_ref.at[pl.ds(part * rows, rows), pl.ds(t * step, step)]
        return pltpu.make_async_copy(ref.at[:, pl.ds(t * step, step)], there, sems.at[part, t])

    steps = [(part, t) for t in range(sems.shape[1]) for part in range(2)]
    for part, t in steps:
        copy(part, t).start()
    acc_ref[...] = jnp.zeros_like(acc_ref)
    most_ref[0] = jnp.max(ranks_of(col_ref[...], rows)) + 1
    for t in range(sems.shape[1]):
        place = lax.broadcasted_iota(jnp.int32, (step, count), 0) + t * step
        pick = (place == row_ref[...]).astype(F32).astype(BF16)
        for part in range(2):
            copy(part, t).wait()
        acc_ref[...] += dot(held_ref[:, t * step : (t + 1) * step], pick)
    cols_ref[:count] = jnp.transpose(acc_ref[:rows]).astype(BF16)
    cols_ref[count:] = jnp.transpose(acc_ref[rows:]).astype(BF16)


def hold(data_real, data_imag, row, col):
    rows, width = data_real.shape
    count = row.shape[1]
    return pl.pallas_call(
        hold_kernel,
        in_specs=[anywhere(), anywhere(), whole_vmem(), whole_vmem()],
        out_specs=[whole_vmem(), whole_vmem(), whole_smem()],
        out_shape=[
            pltpu.VMEM((2 * rows, width), BF16),
            pltpu.VMEM((2 * count, rows), BF16),
            jax.ShapeDtypeStruct((1,), jnp.int32),
        ],
        scratch_shapes=[
            pltpu.VMEM((2 * rows, count), F32),
            pltpu.SemaphoreType.DMA((2, TILES)),
        ],
        compiler_params=params(),
        cost_estimate=cost(4 * rows * width * count, 4 * rows * width),
        name="hold",
    )(data_real, data_imag, row, col)


def select_kernel(cap, round_ref, got_ref, col_ref, out_ref):
    out_ref[...] = pick_rows(cap, round_ref[0], got_ref, col_ref).astype(BF16)


def select_rows(got, col, which, cap):
    groups, _, rows = got.shape
    count = col.shape[0]
    return pl.pallas_call(
        functools.partial(select_kernel, cap),
        in_specs=[whole_smem(), whole_vmem(), whole_vmem()],
        out_specs=whole_vmem(),
        out_shape=jax.ShapeDtypeStruct((2 * count, rows), BF16),
        compiler_params=params(),
        cost_estimate=cost(8 * count * groups * cap * rows, 4 * groups * cap * rows),
        name="select_rows",
    )(which, got, col)


def pick_rows(cap, which, got_ref, col_ref):
    groups, _, rows = got_ref.shape
    count = col_ref.shape[0]
    col = col_ref[...]
    slot = ranks_of(col, rows) - which * cap
    inside = (slot >= 0) & (slot < cap)
    place = jnp.where(inside, (col // rows) * (2 * cap) + slot, -1)
    lanes = lax.broadcasted_iota(jnp.int32, (count, groups * 2 * cap), 1)
    pick = jnp.concatenate([lanes == place, lanes == jnp.where(inside, place + cap, -1)], axis=0)
    got = got_ref[...].reshape(groups * 2 * cap, rows)
    return dot(pick.astype(F32).astype(BF16), got)


def panel_kernel(
    width, cap, me_ref, counts_ref, got_ref, more_ref, colpart_ref, col_ref, panel_ref, panel_t_ref
):
    double, rows = colpart_ref.shape
    count = double // 2
    tile = width // TILES
    mine = me_ref[0] * rows // tile
    tiles = col_ref[...] // tile
    forward = jnp.zeros_like(tiles)
    backward = jnp.zeros_like(tiles)
    for t in range(TILES):
        forward = jnp.where(tiles == t, counts_ref[mine, t], forward)
        backward = jnp.where(tiles == t, counts_ref[t, mine], backward)
    forward = jnp.concatenate([forward, forward], axis=0).astype(F32)
    backward = jnp.concatenate([backward, backward], axis=0).astype(F32)
    own = colpart_ref[...].astype(F32)
    mirror = pick_rows(cap, 0, got_ref, col_ref) + more_ref[...].astype(F32)
    panel = (forward * own + backward * mirror) / jnp.maximum(forward + backward, 1.0)
    panel_t_ref[:, :rows] = panel.astype(BF16)
    panel_t_ref[:count, rows:] = (-panel[count:]).astype(BF16)
    panel_t_ref[count:, rows:] = panel[:count].astype(BF16)
    panel_ref[...] = jnp.transpose(panel).astype(BF16)


def own_panel(me, counts, got, more, colpart, col, width, cap):
    double, rows = colpart.shape
    return pl.pallas_call(
        functools.partial(panel_kernel, width, cap),
        in_specs=[whole_smem()] * 2 + [whole_vmem()] * 4,
        out_specs=[whole_vmem()] * 2,
        out_shape=[pltpu.VMEM((rows, double), BF16), pltpu.VMEM((double, 2 * rows), BF16)],
        compiler_params=params(),
        cost_estimate=cost(8 * rows * double, 8 * rows * double),
        name="own_panel",
    )(me, counts, in_vmem(got), more, colpart, col)


def weight(counts_ref, mine, other, shape):
    forward = jnp.full(shape, counts_ref[mine, other], jnp.int32).astype(F32)
    backward = jnp.full(shape, counts_ref[other, mine], jnp.int32).astype(F32)
    return forward / jnp.maximum(forward + backward, 1.0)


def mirror_block(held_ref, columns, panel_t):
    return dot(panel_t, held_ref[:, columns])


def direct_block(held_ref, columns, panel):
    count = panel.shape[1] // 2
    turned = jnp.concatenate([-panel[:, count:], panel[:, :count]], axis=1)
    rows = held_ref.shape[0] // 2
    return dot(held_ref[:rows, columns], panel) + dot(held_ref[rows:, columns], turned)


def mirror_kernel(width, me_ref, counts_ref, held_ref, panel_t_ref, out_ref):
    rows = held_ref.shape[0] // 2
    tile = width // TILES
    mine = me_ref[0] * rows // tile
    for t in range(TILES):
        found = mirror_block(held_ref, slice(t * tile, (t + 1) * tile), panel_t_ref[...])
        found = found * weight(counts_ref, mine, t, (1, tile))
        for g in range(tile // rows):
            out_ref[t * (tile // rows) + g] = found[:, g * rows : (g + 1) * rows]


def mirror_term(me, counts, held, panel_t):
    rows, width = held.shape[0] // 2, held.shape[1]
    double = panel_t.shape[0]
    return pl.pallas_call(
        functools.partial(mirror_kernel, width),
        in_specs=[whole_smem()] * 2 + [whole_vmem()] * 2,
        out_specs=whole_vmem(),
        out_shape=jax.ShapeDtypeStruct((width // rows, double, rows), F32),
        compiler_params=params(40),
        cost_estimate=cost(4 * rows * width * double, 4 * rows * width + 2 * double * width),
        name="mirror_term",
    )(me, counts, held, panel_t)


def direct_kernel(width, me_ref, counts_ref, held_ref, panel_ref, out_ref):
    rows = held_ref.shape[0] // 2
    tile = width // TILES
    mine = me_ref[0] * rows // tile
    total = jnp.zeros(out_ref.shape, F32)
    for t in range(TILES):
        columns = slice(t * tile, (t + 1) * tile)
        found = direct_block(held_ref, columns, panel_ref[columns, :])
        total += found * weight(counts_ref, mine, t, (1, out_ref.shape[1]))
    out_ref[...] = total


def direct_term(me, counts, held, panel):
    rows, width = held.shape[0] // 2, held.shape[1]
    double = panel.shape[1]
    return pl.pallas_call(
        functools.partial(direct_kernel, width),
        in_specs=[whole_smem()] * 2 + [whole_vmem()] * 2,
        out_specs=whole_vmem(),
        out_shape=jax.ShapeDtypeStruct((rows, double), F32),
        compiler_params=params(40),
        cost_estimate=cost(4 * rows * width * double, 4 * rows * width + 2 * double * width),
        name="direct_term",
    )(me, counts, held, panel)


def block_at(me, span, dz, dy, dc):
    far, near = span
    z, y, c = me // (2 * near), (me // 2) % near, me % 2
    return (((z + dz) % far) * near + (y + dy) % near) * 2 + (c + dc) % 2


def shift(value, span, dz, dy, dc):
    size = 2 * span[0] * span[1]
    return lax.ppermute(value, AXIS, [(i, block_at(i, span, dz, dy, dc)) for i in range(size)])


def mirror_part_kernel(
    width, span, order, me_ref, counts_ref, held_ref, panel_t_ref, *refs
):
    other_ref, own_ref = refs[-2:]
    rows = held_ref.shape[0] // 2
    tile = width // TILES
    me = me_ref[0]
    mine = me * rows // tile
    for dy in range(span[1]):
        for i, dz in enumerate(order):
            for turn in range(2):
                block = block_at(me, span, dz, dy, 1 - turn)
                scale = weight(counts_ref, mine, block * rows // tile, (1, rows))
                columns = pl.ds(pl.multiple_of(block * rows, rows), rows)
                found = mirror_block(held_ref, columns, panel_t_ref[...]) * scale
                if turn == 0:
                    other_ref[dy * len(order) + i] = found.astype(BF16)
                else:
                    own_ref[dy * len(order) + i] = found


def mirror_part(me, counts, held, panel_t, span, order, after):
    rows, width = held.shape[0] // 2, held.shape[1]
    double = panel_t.shape[0]
    blocks = span[1] * len(order)
    return pl.pallas_call(
        functools.partial(mirror_part_kernel, width, span, order),
        in_specs=[whole_smem()] * 2 + [whole_vmem()] * 2 + [anywhere()] * len(after),
        out_specs=[whole_vmem(), whole_vmem()],
        out_shape=[
            pltpu.VMEM((blocks, double, rows), BF16),
            pltpu.VMEM((blocks, double, rows), F32),
        ],
        compiler_params=params(),
        cost_estimate=cost(400000000000, 0),
        name="mirror_part",
    )(me, counts, held, panel_t, *after)


def over_cores_kernel(own_ref, got_ref, *refs):
    kept_ref, sent_ref = refs[-2:]
    some = kept_ref.shape[0]
    for i in range(some):
        kept_ref[i] = own_ref[i] + got_ref[i].astype(F32)
        sent_ref[i] = (own_ref[some + i] + got_ref[some + i].astype(F32)).astype(BF16)


def over_cores(own, got, after):
    some = own.shape[0] // 2
    shape = (some,) + own.shape[1:]
    return pl.pallas_call(
        over_cores_kernel,
        in_specs=[whole_vmem()] * 2 + [anywhere()] * len(after),
        out_specs=[whole_vmem()] * 2,
        out_shape=[pltpu.VMEM(shape, F32), pltpu.VMEM(shape, BF16)],
        compiler_params=params(),
        cost_estimate=cost(0, 0),
        name="over_cores",
    )(own, in_vmem(got), *after)


def over_y_kernel(kept_ref, got_ref, *out_refs):
    for i, out_ref in enumerate(out_refs):
        out_ref[...] = (kept_ref[i] + got_ref[i].astype(F32)).astype(BF16)


def over_y(kept, got):
    some = kept.shape[0]
    return pl.pallas_call(
        over_y_kernel,
        in_specs=[whole_vmem()] * 2,
        out_specs=[whole_vmem()] * some,
        out_shape=[pltpu.VMEM(kept.shape[1:], BF16)] * some,
        compiler_params=params(),
        cost_estimate=cost(0, 0),
        name="over_y",
    )(kept, in_vmem(got))


def stack_kernel(count, *refs):
    out_ref = refs[-1]
    at = 0
    for ref in refs[:count]:
        if len(ref.shape) == 2:
            out_ref[at] = ref[...]
            at += 1
        else:
            out_ref[at : at + ref.shape[0]] = ref[...]
            at += ref.shape[0]


def stack(blocks, after):
    size = sum(1 if len(block.shape) == 2 else block.shape[0] for block in blocks)
    return pl.pallas_call(
        functools.partial(stack_kernel, len(blocks)),
        in_specs=[whole_vmem()] * len(blocks) + [anywhere()] * len(after),
        out_specs=whole_vmem(),
        out_shape=pltpu.VMEM((size,) + blocks[0].shape[-2:], BF16),
        compiler_params=params(),
        cost_estimate=cost(0, 0),
        name="stack",
    )(*[in_vmem(block) for block in blocks], *after)


def direct_part_kernel(
    width, span, way, first, me_ref, counts_ref, held_ref, panel_ref, *refs
):
    out_ref = refs[-1]
    rows = held_ref.shape[0] // 2
    tile = width // TILES
    me = me_ref[0]
    mine = me * rows // tile
    total = jnp.zeros(out_ref.shape, F32) if first else refs[0][...]
    for k in range(panel_ref.shape[0]):
        block = block_at(me, span, span[0] - k, *way)
        columns = pl.ds(pl.multiple_of(block * rows, rows), rows)
        scale = weight(counts_ref, mine, block * rows // tile, (1, out_ref.shape[1]))
        total += direct_block(held_ref, columns, panel_ref[k]) * scale
    out_ref[...] = total


def direct_part(me, counts, held, panels, before, span, way, flops=0):
    rows, width = held.shape[0] // 2, held.shape[1]
    double = panels.shape[2]
    return pl.pallas_call(
        functools.partial(direct_part_kernel, width, span, way, not before),
        in_specs=[whole_smem()] * 2 + [whole_vmem()] * (2 + len(before)),
        out_specs=whole_vmem(),
        out_shape=pltpu.VMEM((rows, double), F32),
        compiler_params=params(),
        cost_estimate=cost(flops, 0),
        name="direct_part",
    )(me, counts, held, in_vmem(panels), *before)


def levels(me, counts, held, panel, panel_t, span):
    far, near = span
    along = [shift(panel, span, dz, 0, 0) for dz in range(1, far)]
    beside = shift(panel, span, 0, 1, 0)

    away = (2, 1, 3)
    other, own = mirror_part(me, counts, held, panel_t, span, away, [])
    other_here, own_here = mirror_part(me, counts, held, panel_t, span, (0,), [beside])
    kept, sent = over_cores(own, shift(other, span, 0, 0, 1), [])
    to_z = over_y(kept, shift(sent, span, 0, 1, 0))
    mirrors = [shift(term, span, dz, 0, 0) for term, dz in zip(to_z, away)]

    ahead = stack(along, [sent, own_here])
    column = stack([panel, ahead], [])
    direct = [direct_part(me, counts, held, column, [], span, (0, 0), 400000000000)]

    def add(panels, way):
        direct[:] = [direct_part(me, counts, held, panels, direct, span, way)]

    other_here = stack([other_here], [ahead])
    kept, sent = over_cores(own_here, shift(other_here, span, 0, 0, 1), direct)
    mirrors += [kept.reshape(kept.shape[1:]), shift(sent, span, 0, 1, 0).reshape(kept.shape[1:])]
    add(shift(column, span, 0, 0, 1), (0, 1))
    next_column = stack([beside, shift(ahead, span, 0, 1, 0)], direct + mirrors[:3] + [sent])
    add(next_column, (1, 0))
    add(shift(next_column, span, 0, 0, 1), (1, 1))
    return direct[0], mirrors


def finish_kernel(factor, direct_ref, *refs):
    mirror_refs, (real_ref, imag_ref) = refs[:-2], refs[-2:]
    count = real_ref.shape[1]
    mirror = mirror_refs[-1][...].astype(F32)
    for ref in mirror_refs[:-1]:
        mirror += ref[...].astype(F32)
    total = factor * (direct_ref[...] + jnp.transpose(mirror))
    real_ref[...] = total[:, :count]
    imag_ref[...] = total[:, count:]


def finish(direct, mirrors, width):
    rows, double = direct.shape
    shape = jax.ShapeDtypeStruct((rows, double // 2), F32)
    return pl.pallas_call(
        functools.partial(finish_kernel, -1.0 / math.sqrt(width)),
        in_specs=[whole_vmem()] * (1 + len(mirrors)),
        out_specs=[whole_vmem(), whole_vmem()],
        out_shape=[shape, shape],
        compiler_params=params(),
        cost_estimate=cost(4 * rows * double, 10 * rows * double),
        name="finish",
    )(in_vmem(direct), *[in_vmem(mirror) for mirror in mirrors])


def shards(data_real, data_imag, counts, source_cols):
    rows, width = data_real.shape
    groups = width // rows
    count = source_cols.shape[0]
    cap = min(rows, count, -(-2 * count // groups // 8) * 8)
    col = source_cols.reshape(count, 1)
    row = source_cols.reshape(1, count)
    me = lax.axis_index(AXIS).reshape(1)

    def exchange(which):
        sent = own_source_rows(me, data_real, data_imag, source_cols, which, cap)
        return lax.all_to_all(sent, AXIS, split_axis=0, concat_axis=0)

    got = exchange(jnp.zeros((1,), jnp.int32))
    held, colpart, most = hold(data_real, data_imag, row, col)

    def further():
        def body(which, found):
            one = which.reshape(1)
            return found + select_rows(exchange(one), col, one, cap)

        return lax.fori_loop(1, (most[0] + cap - 1) // cap, body, nothing())

    def nothing():
        return jnp.zeros((2 * count, rows), BF16)

    more = lax.cond(most[0] > cap, further, nothing)
    panel, panel_t = own_panel(me, counts, got, more, colpart, col, width, cap)
    if rows % 128 == 0 and groups == 16:
        direct, mirrors = levels(me, counts, held, panel, panel_t, (4, 2))
    else:
        full = lax.all_gather(panel, AXIS, axis=0, tiled=True)
        partial = mirror_term(me, counts, held, panel_t)
        mirrors = [lax.psum_scatter(partial, AXIS, scatter_dimension=0, tiled=False)]
        direct = direct_term(me, counts, held, full)
    return tuple(finish(direct, mirrors, width))


def solution(mesh):
    placed = (P(("freq", "row"), None), P(("freq", "row"), None), P(), P())
    return jax.shard_map(
        shards,
        mesh=mesh,
        in_specs=placed,
        out_specs=(P(("freq", "row"), None), P(("freq", "row"), None)),
        check_vma=False,
    )
```

```python
import functools
import math

import jax
import jax.numpy as jnp
from jax import lax
from jax.experimental import pallas as pl
from jax.experimental.pallas import tpu as pltpu
from jax.sharding import PartitionSpec as P

TILES = 8
AXIS = "row"
GROUP = 16
PIECE = 1024
F32 = jnp.float32
BF16 = jnp.bfloat16


def params(mib=16):
    return pltpu.CompilerParams(vmem_limit_bytes=mib * 1024 * 1024)


def whole_vmem():
    return pl.BlockSpec(memory_space=pltpu.VMEM)


def anywhere():
    return pl.BlockSpec(memory_space=pl.ANY)


def whole_smem():
    return pl.BlockSpec(memory_space=pltpu.SMEM)


def cost(flops, size):
    return pl.CostEstimate(flops=flops, bytes_accessed=size, transcendentals=0)


def dot(left, right):
    return jnp.dot(left, right, preferred_element_type=F32)


def ranks_of(col, rows):
    count = col.shape[0]
    owner = col // rows
    owner_row = jnp.transpose(jnp.broadcast_to(owner.astype(F32), (count, count))).astype(jnp.int32)
    before = lax.broadcasted_iota(jnp.int32, (count, count), 1) < lax.broadcasted_iota(
        jnp.int32, (count, count), 0
    )
    same = (owner_row == owner) & before
    return jnp.sum(same.astype(F32), axis=1, keepdims=True).astype(jnp.int32)


def rows_kernel(cap, round_ref, me_ref, col_ref, real_ref, imag_ref, out_ref, list_ref, near_ref, held_ref, sems):
    rows, width = real_ref.shape
    groups = out_ref.shape[0]
    count = col_ref.shape[0]
    base = me_ref[0] * rows
    skip = round_ref[0] * cap

    def copies(slot, local):
        group = pl.ds(pl.multiple_of(local // GROUP * GROUP, GROUP), GROUP)
        return [
            pltpu.make_async_copy(ref.at[group], near_ref.at[slot, part], sems.at[slot, part])
            for part, ref in enumerate((real_ref, imag_ref))
        ]

    def begin(s, found):
        local = col_ref[s] - base
        own = (local >= 0) & (local < rows)
        slot = found - skip

        @pl.when(own & (slot >= 0) & (slot < cap))
        def _():
            list_ref[slot] = local
            for copy in copies(slot, local):
                copy.start()

        return found + own.astype(jnp.int32)

    def pick(slot, _):
        local = list_ref[slot]
        chosen = lax.broadcasted_iota(jnp.int32, (GROUP, PIECE), 0) == local % GROUP
        for part, copy in enumerate(copies(slot, local)):
            copy.wait()
            for at in range(0, width, PIECE):
                group = near_ref[slot, part, :, at : at + PIECE].astype(F32)
                held_ref[pl.ds(part * cap + slot, 1), at : at + PIECE] = jnp.sum(
                    jnp.where(chosen, group, 0.0), axis=0, keepdims=True
                )
        return 0

    found = lax.fori_loop(0, count, begin, jnp.int32(0))
    held_ref[...] = jnp.zeros_like(held_ref)
    lax.fori_loop(0, jnp.clip(found - skip, 0, cap), pick, 0)
    for g in range(groups):
        out_ref[g] = held_ref[:, g * rows : (g + 1) * rows].astype(BF16)


def own_source_rows(me, data_real, data_imag, source_cols, which, cap):
    rows, width = data_real.shape
    return pl.pallas_call(
        functools.partial(rows_kernel, cap),
        in_specs=[whole_smem()] * 3 + [anywhere()] * 2,
        out_specs=whole_vmem(),
        out_shape=jax.ShapeDtypeStruct((width // rows, 2 * cap, rows), BF16),
        scratch_shapes=[
            pltpu.SMEM((cap,), jnp.int32),
            pltpu.VMEM((cap, 2, GROUP, width), BF16),
            pltpu.VMEM((2 * cap, width), F32),
            pltpu.SemaphoreType.DMA((cap, 2)),
        ],
        compiler_params=params(24),
        cost_estimate=cost(0, 2 * cap * width),
        name="own_source_rows",
    )(which, me, source_cols, data_real, data_imag)


def cols_kernel(real_ref, imag_ref, row_ref, out_ref, acc_ref):
    rows, step = real_ref.shape
    count = row_ref.shape[1]
    t = pl.program_id(0)

    @pl.when(t == 0)
    def _():
        acc_ref[...] = jnp.zeros_like(acc_ref)

    place = lax.broadcasted_iota(jnp.int32, (step, count), 0) + t * step
    pick = (place == row_ref[...]).astype(F32).astype(BF16)
    acc_ref[:, :count] += dot(real_ref[...], pick)
    acc_ref[:, count:] += dot(imag_ref[...], pick)

    @pl.when(t == pl.num_programs(0) - 1)
    def _():
        out_ref[...] = jnp.transpose(acc_ref[...]).astype(BF16)


def own_source_cols(data_real, data_imag, row, step):
    rows, width = data_real.shape
    count = row.shape[1]
    block = pl.BlockSpec((rows, step), lambda t: (0, t))
    return pl.pallas_call(
        cols_kernel,
        grid=(width // step,),
        in_specs=[block, block, whole_vmem()],
        out_specs=pl.BlockSpec((2 * count, rows), lambda t: (0, 0)),
        out_shape=jax.ShapeDtypeStruct((2 * count, rows), BF16),
        scratch_shapes=[pltpu.VMEM((rows, 2 * count), F32)],
        compiler_params=params(),
        cost_estimate=cost(4 * rows * width * count, 4 * rows * width),
        name="own_source_cols",
    )(data_real, data_imag, row)


def select_kernel(cap, round_ref, got_ref, col_ref, out_ref):
    out_ref[...] = pick_rows(cap, round_ref[0], got_ref, col_ref).astype(BF16)


def select_rows(got, col, which, cap):
    groups, _, rows = got.shape
    count = col.shape[0]
    return pl.pallas_call(
        functools.partial(select_kernel, cap),
        in_specs=[whole_smem(), whole_vmem(), whole_vmem()],
        out_specs=whole_vmem(),
        out_shape=jax.ShapeDtypeStruct((2 * count, rows), BF16),
        compiler_params=params(),
        cost_estimate=cost(8 * count * groups * cap * rows, 4 * groups * cap * rows),
        name="select_rows",
    )(which, got, col)


def pick_rows(cap, which, got_ref, col_ref):
    groups, _, rows = got_ref.shape
    count = col_ref.shape[0]
    col = col_ref[...]
    slot = ranks_of(col, rows) - which * cap
    inside = (slot >= 0) & (slot < cap)
    place = jnp.where(inside, (col // rows) * (2 * cap) + slot, -1)
    lanes = lax.broadcasted_iota(jnp.int32, (count, groups * 2 * cap), 1)
    pick = jnp.concatenate([lanes == place, lanes == jnp.where(inside, place + cap, -1)], axis=0)
    got = got_ref[...].reshape(groups * 2 * cap, rows)
    return dot(pick.astype(F32).astype(BF16), got)


def panel_kernel(width, me_ref, counts_ref, rowpart_ref, colpart_ref, col_ref, panel_ref, panel_t_ref):
    double, rows = colpart_ref.shape
    count = double // 2
    tile = width // TILES
    mine = me_ref[0] * rows // tile
    tiles = col_ref[...] // tile
    forward = jnp.zeros_like(tiles)
    backward = jnp.zeros_like(tiles)
    for t in range(TILES):
        forward = jnp.where(tiles == t, counts_ref[mine, t], forward)
        backward = jnp.where(tiles == t, counts_ref[t, mine], backward)
    forward = jnp.concatenate([forward, forward], axis=0).astype(F32)
    backward = jnp.concatenate([backward, backward], axis=0).astype(F32)
    own = colpart_ref[...].astype(F32)
    mirror = rowpart_ref[...].astype(F32)
    panel = (forward * own + backward * mirror) / jnp.maximum(forward + backward, 1.0)
    panel_t_ref[:, :rows] = panel.astype(BF16)
    panel_t_ref[:count, rows:] = (-panel[count:]).astype(BF16)
    panel_t_ref[count:, rows:] = panel[:count].astype(BF16)
    panel_ref[...] = jnp.transpose(panel).astype(BF16)


def own_panel(me, counts, rowpart, colpart, col, width):
    double, rows = colpart.shape
    return pl.pallas_call(
        functools.partial(panel_kernel, width),
        in_specs=[whole_smem()] * 2 + [whole_vmem()] * 3,
        out_specs=[whole_vmem()] * 2,
        out_shape=[
            jax.ShapeDtypeStruct((rows, double), BF16),
            jax.ShapeDtypeStruct((double, 2 * rows), BF16),
        ],
        compiler_params=params(),
        cost_estimate=cost(8 * rows * double, 8 * rows * double),
        name="own_panel",
    )(me, counts, rowpart, colpart, col)


def weight(counts_ref, mine, other, shape):
    forward = jnp.full(shape, counts_ref[mine, other], jnp.int32).astype(F32)
    backward = jnp.full(shape, counts_ref[other, mine], jnp.int32).astype(F32)
    return forward / jnp.maximum(forward + backward, 1.0)


def mirror_block(real, imag, panel_t):
    rows = real.shape[0]
    return dot(panel_t[:, :rows], real) + dot(panel_t[:, rows:], imag)


def direct_block(real, imag, panel):
    count = panel.shape[1] // 2
    turned = jnp.concatenate([-panel[:, count:], panel[:, :count]], axis=1)
    return dot(real, panel) + dot(imag, turned)


def mirror_kernel(width, me_ref, counts_ref, real_ref, imag_ref, panel_t_ref, out_ref):
    rows, tile = real_ref.shape
    mine = me_ref[0] * rows // tile
    found = mirror_block(real_ref[...], imag_ref[...], panel_t_ref[...])
    found = found * weight(counts_ref, mine, pl.program_id(0), (1, tile))
    for g in range(out_ref.shape[0]):
        out_ref[g] = found[:, g * rows : (g + 1) * rows]


def mirror_term(me, counts, data_real, data_imag, panel_t):
    rows, width = data_real.shape
    double = panel_t.shape[0]
    tile = width // TILES
    block = pl.BlockSpec((rows, tile), lambda t: (0, t))
    return pl.pallas_call(
        functools.partial(mirror_kernel, width),
        grid=(TILES,),
        in_specs=[whole_smem()] * 2 + [block, block, whole_vmem()],
        out_specs=pl.BlockSpec((tile // rows, double, rows), lambda t: (t, 0, 0)),
        out_shape=jax.ShapeDtypeStruct((width // rows, double, rows), F32),
        compiler_params=params(32),
        cost_estimate=cost(4 * rows * width * double, 4 * rows * width + 2 * double * width),
        name="mirror_term",
    )(me, counts, data_real, data_imag, panel_t)


def direct_kernel(width, me_ref, counts_ref, real_ref, imag_ref, panel_ref, out_ref):
    rows, tile = real_ref.shape
    mine = me_ref[0] * rows // tile
    t = pl.program_id(0)

    @pl.when(t == 0)
    def _():
        out_ref[...] = jnp.zeros_like(out_ref)

    found = direct_block(real_ref[...], imag_ref[...], panel_ref[...])
    out_ref[...] += found * weight(counts_ref, mine, t, (1, out_ref.shape[1]))


def direct_term(me, counts, data_real, data_imag, panel):
    rows, width = data_real.shape
    double = panel.shape[1]
    tile = width // TILES
    block = pl.BlockSpec((rows, tile), lambda t: (0, t))
    return pl.pallas_call(
        functools.partial(direct_kernel, width),
        grid=(TILES,),
        in_specs=[whole_smem()] * 2 + [block, block, pl.BlockSpec((tile, double), lambda t: (t, 0))],
        out_specs=pl.BlockSpec((rows, double), lambda t: (0, 0)),
        out_shape=jax.ShapeDtypeStruct((rows, double), F32),
        compiler_params=params(),
        cost_estimate=cost(4 * rows * width * double, 4 * rows * width + 2 * double * width),
        name="direct_term",
    )(me, counts, data_real, data_imag, panel)


def block_at(me, span, dz, dy, dc):
    far, near = span
    z, y, c = me // (2 * near), (me // 2) % near, me % 2
    return (((z + dz) % far) * near + (y + dy) % near) * 2 + (c + dc) % 2


def shift(value, span, dz, dy, dc):
    size = 2 * span[0] * span[1]
    return lax.ppermute(value, AXIS, [(i, block_at(i, span, dz, dy, dc)) for i in range(size)])


def distance(order, i):
    dz = order[0]
    for at in range(1, len(order)):
        dz = jnp.where(i == at, order[at], dz)
    return dz


def mirror_part_kernel(
    width, span, order, me_ref, counts_ref, real_ref, imag_ref, panel_t_ref, *refs
):
    other_ref, own_ref = refs[-2:]
    rows = real_ref.shape[0]
    tile = width // TILES
    turn, dy, i = pl.program_id(0), pl.program_id(1), pl.program_id(2)
    mine = me_ref[0] * rows // tile
    block = block_at(me_ref[0], span, distance(order, i), dy, 1 - turn)
    scale = weight(counts_ref, mine, block * rows // tile, (1, rows))
    found = mirror_block(real_ref[...], imag_ref[...], panel_t_ref[...]) * scale

    @pl.when(turn == 0)
    def _():
        other_ref[0] = found.astype(BF16)

    @pl.when(turn == 1)
    def _():
        own_ref[0] = found


def mirror_part(me, counts, data_real, data_imag, panel_t, span, order, after):
    rows, width = data_real.shape
    double = panel_t.shape[0]
    near, some = span[1], len(order)
    last = near * some - 1
    block = pl.BlockSpec(
        (rows, rows),
        lambda turn, dy, i, me: (0, block_at(me[0], span, distance(order, i), dy, 1 - turn)),
    )
    spec = pltpu.PrefetchScalarGridSpec(
        num_scalar_prefetch=1,
        grid=(2, near, some),
        in_specs=[whole_smem(), block, block, whole_vmem()] + [anywhere()] * len(after),
        out_specs=[
            pl.BlockSpec(
                (1, double, rows),
                lambda turn, dy, i, me: (jnp.where(turn == 0, dy * some + i, last), 0, 0),
            ),
            pl.BlockSpec(
                (1, double, rows),
                lambda turn, dy, i, me: (jnp.where(turn == 0, 0, dy * some + i), 0, 0),
            ),
        ],
    )
    return pl.pallas_call(
        functools.partial(mirror_part_kernel, width, span, order),
        grid_spec=spec,
        out_shape=[
            jax.ShapeDtypeStruct((near * some, double, rows), BF16),
            jax.ShapeDtypeStruct((near * some, double, rows), F32),
        ],
        compiler_params=params(),
        cost_estimate=cost(400000000000, 0),
        name="mirror_part",
    )(me, counts, data_real, data_imag, panel_t, *after)


def ordered(value, after):
    return lax.optimization_barrier((value, after))[0]


def direct_part_kernel(
    width, span, way, first, me_ref, counts_ref, real_ref, imag_ref, panel_ref, *refs
):
    out_ref = refs[-1]
    rows = real_ref.shape[0]
    tile = width // TILES
    k = pl.program_id(0)
    mine = me_ref[0] * rows // tile
    block = block_at(me_ref[0], span, span[0] - k, *way)
    scale = weight(counts_ref, mine, block * rows // tile, (1, out_ref.shape[1]))
    found = direct_block(real_ref[...], imag_ref[...], panel_ref[0]) * scale

    @pl.when(k == 0)
    def _():
        out_ref[...] = found if first else found + refs[0][...]

    @pl.when(k > 0)
    def _():
        out_ref[...] += found


def direct_part(me, counts, data_real, data_imag, panels, before, span, way, flops=0):
    rows, width = data_real.shape
    double = panels.shape[2]
    block = pl.BlockSpec((rows, rows), lambda k, me: (0, block_at(me[0], span, span[0] - k, *way)))
    spec = pltpu.PrefetchScalarGridSpec(
        num_scalar_prefetch=1,
        grid=(panels.shape[0],),
        in_specs=[whole_smem(), block, block, pl.BlockSpec((1, rows, double), lambda k, me: (k, 0, 0))]
        + [whole_vmem()] * len(before),
        out_specs=pl.BlockSpec((rows, double), lambda k, me: (0, 0)),
    )
    return pl.pallas_call(
        functools.partial(direct_part_kernel, width, span, way, not before),
        grid_spec=spec,
        out_shape=jax.ShapeDtypeStruct((rows, double), F32),
        compiler_params=params(),
        cost_estimate=cost(flops, 0),
        name="direct_part",
    )(me, counts, data_real, data_imag, panels, *before)


def levels(me, counts, data_real, data_imag, panel, panel_t, span):
    far, near = span
    data = (data_real, data_imag)
    along = [shift(panel, span, dz, 0, 0) for dz in range(1, far)]
    beside = shift(panel, span, 0, 1, 0)

    away = (2, 1, 3)
    some = len(away)
    other, own = mirror_part(me, counts, *data, panel_t, span, away, [])
    other_here, own_here = mirror_part(me, counts, *data, panel_t, span, (0,), [beside])
    total = own + shift(other, span, 0, 0, 1).astype(F32)
    sent = total[some:].astype(BF16)
    total = total[:some] + shift(sent, span, 0, 1, 0).astype(F32)
    mirrors = [shift(total[i].astype(BF16), span, dz, 0, 0) for i, dz in enumerate(away)]

    ahead = jnp.stack(ordered(along, [sent, own_here]))
    column = jnp.concatenate([panel[None], ahead])
    direct = [direct_part(me, counts, *data, column, [], span, (0, 0), 400000000000)]

    def add(panels, way):
        direct[:] = [direct_part(me, counts, *data, panels, direct, span, way)]

    other_here = ordered(other_here, ahead)
    total = own_here + ordered(shift(other_here, span, 0, 0, 1), direct).astype(F32)
    sent = total[1].astype(BF16)
    mirrors += [total[0], shift(sent, span, 0, 1, 0)]
    add(shift(column, span, 0, 0, 1), (0, 1))
    arrived = ordered(shift(ahead, span, 0, 1, 0), direct + mirrors[:3] + [sent])
    next_column = jnp.concatenate([beside[None], arrived])
    add(next_column, (1, 0))
    add(shift(next_column, span, 0, 0, 1), (1, 1))
    return direct[0], mirrors


def finish_kernel(factor, direct_ref, *refs):
    mirror_refs, (real_ref, imag_ref) = refs[:-2], refs[-2:]
    count = real_ref.shape[1]
    mirror = mirror_refs[-1][...].astype(F32)
    for ref in mirror_refs[:-1]:
        mirror += ref[...].astype(F32)
    total = factor * (direct_ref[...] + jnp.transpose(mirror))
    real_ref[...] = total[:, :count]
    imag_ref[...] = total[:, count:]


def finish(direct, mirrors, width):
    rows, double = direct.shape
    shape = jax.ShapeDtypeStruct((rows, double // 2), F32)
    return pl.pallas_call(
        functools.partial(finish_kernel, -1.0 / math.sqrt(width)),
        in_specs=[whole_vmem()] * (1 + len(mirrors)),
        out_specs=[whole_vmem(), whole_vmem()],
        out_shape=[shape, shape],
        compiler_params=params(),
        cost_estimate=cost(4 * rows * double, 10 * rows * double),
        name="finish",
    )(direct, *mirrors)


def shards(data_real, data_imag, counts, source_cols):
    rows, width = data_real.shape
    groups = width // rows
    count = source_cols.shape[0]
    cap = min(rows, count, -(-2 * count // groups // 8) * 8)
    col = source_cols.reshape(count, 1)
    row = source_cols.reshape(1, count)
    me = lax.axis_index(AXIS).reshape(1)

    def exchange(which):
        sent = own_source_rows(me, data_real, data_imag, source_cols, which, cap)
        return lax.all_to_all(sent, AXIS, split_axis=0, concat_axis=0)

    first = jnp.zeros((1,), jnp.int32)
    got = exchange(first)
    colpart = own_source_cols(data_real, data_imag, row, width // TILES)
    rowpart = select_rows(got, col, first, cap)

    owner = source_cols // rows
    most = jnp.max(jnp.sum(owner[:, None] == jnp.arange(groups)[None, :], axis=0, dtype=jnp.int32))

    def further(rowpart):
        def body(which, held):
            one = which.reshape(1)
            return held + select_rows(exchange(one), col, one, cap)

        return lax.fori_loop(1, (most + cap - 1) // cap, body, rowpart)

    rowpart = lax.cond(most > cap, further, lambda rowpart: rowpart, rowpart)
    panel, panel_t = own_panel(me, counts, rowpart, colpart, col, width)
    if rows % 128 == 0 and groups == 16:
        direct, mirrors = levels(me, counts, data_real, data_imag, panel, panel_t, (4, 2))
    else:
        full = lax.all_gather(panel, AXIS, axis=0, tiled=True)
        partial = mirror_term(me, counts, data_real, data_imag, panel_t)
        mirrors = [lax.psum_scatter(partial, AXIS, scatter_dimension=0, tiled=False)]
        direct = direct_term(me, counts, data_real, data_imag, full)
    return tuple(finish(direct, mirrors, width))


def solution(mesh):
    placed = (P(("freq", "row"), None), P(("freq", "row"), None), P(), P())
    return jax.shard_map(
        shards,
        mesh=mesh,
        in_specs=placed,
        out_specs=(P(("freq", "row"), None), P(("freq", "row"), None)),
        check_vma=False,
    )
```

```python
import functools
import math

import jax
import jax.numpy as jnp
from jax import lax
from jax.experimental import pallas as pl
from jax.experimental.pallas import tpu as pltpu
from jax.sharding import PartitionSpec as P

TILES = 8
AXIS = "row"
GROUP = 16
PIECE = 1024
F32 = jnp.float32
BF16 = jnp.bfloat16


def params(mib=16):
    return pltpu.CompilerParams(vmem_limit_bytes=mib * 1024 * 1024)


def whole_vmem():
    return pl.BlockSpec(memory_space=pltpu.VMEM)


def anywhere():
    return pl.BlockSpec(memory_space=pl.ANY)


def in_hbm(value):
    return pltpu.with_memory_space_constraint(value, pltpu.HBM)


def whole_smem():
    return pl.BlockSpec(memory_space=pltpu.SMEM)


def cost(flops, size):
    return pl.CostEstimate(flops=flops, bytes_accessed=size, transcendentals=0)


def dot(left, right):
    return jnp.dot(left, right, preferred_element_type=F32)


def ranks_of(col, rows):
    count = col.shape[0]
    owner = col // rows
    owner_row = jnp.transpose(jnp.broadcast_to(owner.astype(F32), (count, count))).astype(jnp.int32)
    before = lax.broadcasted_iota(jnp.int32, (count, count), 1) < lax.broadcasted_iota(
        jnp.int32, (count, count), 0
    )
    same = (owner_row == owner) & before
    return jnp.sum(same.astype(F32), axis=1, keepdims=True).astype(jnp.int32)


def rows_kernel(cap, round_ref, me_ref, col_ref, real_ref, imag_ref, out_ref, list_ref, near_ref, held_ref, sems):
    rows, width = real_ref.shape
    groups = out_ref.shape[0]
    count = col_ref.shape[0]
    base = me_ref[0] * rows
    skip = round_ref[0] * cap

    def copies(slot, local):
        group = pl.ds(pl.multiple_of(local // GROUP * GROUP, GROUP), GROUP)
        return [
            pltpu.make_async_copy(ref.at[group], near_ref.at[slot, part], sems.at[slot, part])
            for part, ref in enumerate((real_ref, imag_ref))
        ]

    def begin(s, found):
        local = col_ref[s] - base
        own = (local >= 0) & (local < rows)
        slot = found - skip

        @pl.when(own & (slot >= 0) & (slot < cap))
        def _():
            list_ref[slot] = local
            for copy in copies(slot, local):
                copy.start()

        return found + own.astype(jnp.int32)

    def pick(slot, _):
        local = list_ref[slot]
        chosen = lax.broadcasted_iota(jnp.int32, (GROUP, PIECE), 0) == local % GROUP
        for part, copy in enumerate(copies(slot, local)):
            copy.wait()
            for at in range(0, width, PIECE):
                group = near_ref[slot, part, :, at : at + PIECE].astype(F32)
                held_ref[pl.ds(part * cap + slot, 1), at : at + PIECE] = jnp.sum(
                    jnp.where(chosen, group, 0.0), axis=0, keepdims=True
                )
        return 0

    found = lax.fori_loop(0, count, begin, jnp.int32(0))
    held_ref[...] = jnp.zeros_like(held_ref)
    lax.fori_loop(0, jnp.clip(found - skip, 0, cap), pick, 0)
    for g in range(groups):
        out_ref[g] = held_ref[:, g * rows : (g + 1) * rows].astype(BF16)


def own_source_rows(me, data_real, data_imag, source_cols, which, cap):
    rows, width = data_real.shape
    return pl.pallas_call(
        functools.partial(rows_kernel, cap),
        in_specs=[whole_smem()] * 3 + [anywhere()] * 2,
        out_specs=whole_vmem(),
        out_shape=jax.ShapeDtypeStruct((width // rows, 2 * cap, rows), BF16),
        scratch_shapes=[
            pltpu.SMEM((cap,), jnp.int32),
            pltpu.VMEM((cap, 2, GROUP, width), BF16),
            pltpu.VMEM((2 * cap, width), F32),
            pltpu.SemaphoreType.DMA((cap, 2)),
        ],
        compiler_params=params(24),
        cost_estimate=cost(0, 2 * cap * width),
        name="own_source_rows",
    )(which, me, source_cols, data_real, data_imag)


def cols_kernel(real_ref, imag_ref, row_ref, out_ref, acc_ref):
    rows, step = real_ref.shape
    count = row_ref.shape[1]
    t = pl.program_id(0)

    @pl.when(t == 0)
    def _():
        acc_ref[...] = jnp.zeros_like(acc_ref)

    place = lax.broadcasted_iota(jnp.int32, (step, count), 0) + t * step
    pick = (place == row_ref[...]).astype(F32).astype(BF16)
    acc_ref[:, :count] += dot(real_ref[...], pick)
    acc_ref[:, count:] += dot(imag_ref[...], pick)

    @pl.when(t == pl.num_programs(0) - 1)
    def _():
        out_ref[...] = jnp.transpose(acc_ref[...]).astype(BF16)


def own_source_cols(data_real, data_imag, row, step):
    rows, width = data_real.shape
    count = row.shape[1]
    block = pl.BlockSpec((rows, step), lambda t: (0, t))
    return pl.pallas_call(
        cols_kernel,
        grid=(width // step,),
        in_specs=[block, block, whole_vmem()],
        out_specs=pl.BlockSpec((2 * count, rows), lambda t: (0, 0)),
        out_shape=jax.ShapeDtypeStruct((2 * count, rows), BF16),
        scratch_shapes=[pltpu.VMEM((rows, 2 * count), F32)],
        compiler_params=params(),
        cost_estimate=cost(4 * rows * width * count, 4 * rows * width),
        name="own_source_cols",
    )(data_real, data_imag, row)


def select_kernel(cap, round_ref, got_ref, col_ref, out_ref):
    out_ref[...] = pick_rows(cap, round_ref[0], got_ref, col_ref).astype(BF16)


def select_rows(got, col, which, cap):
    groups, _, rows = got.shape
    count = col.shape[0]
    return pl.pallas_call(
        functools.partial(select_kernel, cap),
        in_specs=[whole_smem(), whole_vmem(), whole_vmem()],
        out_specs=whole_vmem(),
        out_shape=jax.ShapeDtypeStruct((2 * count, rows), BF16),
        compiler_params=params(),
        cost_estimate=cost(8 * count * groups * cap * rows, 4 * groups * cap * rows),
        name="select_rows",
    )(which, got, col)


def pick_rows(cap, which, got_ref, col_ref):
    groups, _, rows = got_ref.shape
    count = col_ref.shape[0]
    col = col_ref[...]
    slot = ranks_of(col, rows) - which * cap
    inside = (slot >= 0) & (slot < cap)
    place = jnp.where(inside, (col // rows) * (2 * cap) + slot, -1)
    lanes = lax.broadcasted_iota(jnp.int32, (count, groups * 2 * cap), 1)
    pick = jnp.concatenate([lanes == place, lanes == jnp.where(inside, place + cap, -1)], axis=0)
    got = got_ref[...].reshape(groups * 2 * cap, rows)
    return dot(pick.astype(F32).astype(BF16), got)


def panel_kernel(width, me_ref, counts_ref, rowpart_ref, colpart_ref, col_ref, panel_ref, panel_t_ref):
    double, rows = colpart_ref.shape
    count = double // 2
    tile = width // TILES
    mine = me_ref[0] * rows // tile
    tiles = col_ref[...] // tile
    forward = jnp.zeros_like(tiles)
    backward = jnp.zeros_like(tiles)
    for t in range(TILES):
        forward = jnp.where(tiles == t, counts_ref[mine, t], forward)
        backward = jnp.where(tiles == t, counts_ref[t, mine], backward)
    forward = jnp.concatenate([forward, forward], axis=0).astype(F32)
    backward = jnp.concatenate([backward, backward], axis=0).astype(F32)
    own = colpart_ref[...].astype(F32)
    mirror = rowpart_ref[...].astype(F32)
    panel = (forward * own + backward * mirror) / jnp.maximum(forward + backward, 1.0)
    panel_t_ref[:, :rows] = panel.astype(BF16)
    panel_t_ref[:count, rows:] = (-panel[count:]).astype(BF16)
    panel_t_ref[count:, rows:] = panel[:count].astype(BF16)
    panel_ref[...] = jnp.transpose(panel).astype(BF16)


def own_panel(me, counts, rowpart, colpart, col, width):
    double, rows = colpart.shape
    return pl.pallas_call(
        functools.partial(panel_kernel, width),
        in_specs=[whole_smem()] * 2 + [whole_vmem()] * 3,
        out_specs=[whole_vmem()] * 2,
        out_shape=[
            jax.ShapeDtypeStruct((rows, double), BF16),
            jax.ShapeDtypeStruct((double, 2 * rows), BF16),
        ],
        compiler_params=params(),
        cost_estimate=cost(8 * rows * double, 8 * rows * double),
        name="own_panel",
    )(me, counts, rowpart, colpart, col)


def weight(counts_ref, mine, other, shape):
    forward = jnp.full(shape, counts_ref[mine, other], jnp.int32).astype(F32)
    backward = jnp.full(shape, counts_ref[other, mine], jnp.int32).astype(F32)
    return forward / jnp.maximum(forward + backward, 1.0)


def mirror_block(real, imag, panel_t):
    rows = real.shape[0]
    return dot(panel_t[:, :rows], real) + dot(panel_t[:, rows:], imag)


def direct_block(real, imag, panel):
    count = panel.shape[1] // 2
    turned = jnp.concatenate([-panel[:, count:], panel[:, :count]], axis=1)
    return dot(real, panel) + dot(imag, turned)


def mirror_kernel(width, me_ref, counts_ref, real_ref, imag_ref, panel_t_ref, out_ref):
    rows, tile = real_ref.shape
    mine = me_ref[0] * rows // tile
    found = mirror_block(real_ref[...], imag_ref[...], panel_t_ref[...])
    found = found * weight(counts_ref, mine, pl.program_id(0), (1, tile))
    for g in range(out_ref.shape[0]):
        out_ref[g] = found[:, g * rows : (g + 1) * rows]


def mirror_term(me, counts, data_real, data_imag, panel_t):
    rows, width = data_real.shape
    double = panel_t.shape[0]
    tile = width // TILES
    block = pl.BlockSpec((rows, tile), lambda t: (0, t))
    return pl.pallas_call(
        functools.partial(mirror_kernel, width),
        grid=(TILES,),
        in_specs=[whole_smem()] * 2 + [block, block, whole_vmem()],
        out_specs=pl.BlockSpec((tile // rows, double, rows), lambda t: (t, 0, 0)),
        out_shape=jax.ShapeDtypeStruct((width // rows, double, rows), F32),
        compiler_params=params(32),
        cost_estimate=cost(4 * rows * width * double, 4 * rows * width + 2 * double * width),
        name="mirror_term",
    )(me, counts, data_real, data_imag, panel_t)


def direct_kernel(width, me_ref, counts_ref, real_ref, imag_ref, panel_ref, out_ref):
    rows, tile = real_ref.shape
    mine = me_ref[0] * rows // tile
    t = pl.program_id(0)

    @pl.when(t == 0)
    def _():
        out_ref[...] = jnp.zeros_like(out_ref)

    found = direct_block(real_ref[...], imag_ref[...], panel_ref[...])
    out_ref[...] += found * weight(counts_ref, mine, t, (1, out_ref.shape[1]))


def direct_term(me, counts, data_real, data_imag, panel):
    rows, width = data_real.shape
    double = panel.shape[1]
    tile = width // TILES
    block = pl.BlockSpec((rows, tile), lambda t: (0, t))
    return pl.pallas_call(
        functools.partial(direct_kernel, width),
        grid=(TILES,),
        in_specs=[whole_smem()] * 2 + [block, block, pl.BlockSpec((tile, double), lambda t: (t, 0))],
        out_specs=pl.BlockSpec((rows, double), lambda t: (0, 0)),
        out_shape=jax.ShapeDtypeStruct((rows, double), F32),
        compiler_params=params(),
        cost_estimate=cost(4 * rows * width * double, 4 * rows * width + 2 * double * width),
        name="direct_term",
    )(me, counts, data_real, data_imag, panel)


def block_at(me, span, dz, dy, dc):
    far, near = span
    z, y, c = me // (2 * near), (me // 2) % near, me % 2
    return (((z + dz) % far) * near + (y + dy) % near) * 2 + (c + dc) % 2


def shift(value, span, dz, dy, dc):
    size = 2 * span[0] * span[1]
    return lax.ppermute(value, AXIS, [(i, block_at(i, span, dz, dy, dc)) for i in range(size)])


def distance(order, i):
    dz = order[0]
    for at in range(1, len(order)):
        dz = jnp.where(i == at, order[at], dz)
    return dz


def mirror_part_kernel(
    width, span, order, me_ref, counts_ref, real_ref, imag_ref, panel_t_ref, *refs
):
    other_ref, own_ref = refs[-2:]
    rows = real_ref.shape[0]
    tile = width // TILES
    turn, dy, i = pl.program_id(0), pl.program_id(1), pl.program_id(2)
    mine = me_ref[0] * rows // tile
    block = block_at(me_ref[0], span, distance(order, i), dy, 1 - turn)
    scale = weight(counts_ref, mine, block * rows // tile, (1, rows))
    found = mirror_block(real_ref[...], imag_ref[...], panel_t_ref[...]) * scale

    @pl.when(turn == 0)
    def _():
        other_ref[0] = found.astype(BF16)

    @pl.when(turn == 1)
    def _():
        own_ref[0] = found


def mirror_part(me, counts, data_real, data_imag, panel_t, span, order, after):
    rows, width = data_real.shape
    double = panel_t.shape[0]
    near, some = span[1], len(order)
    last = near * some - 1
    block = pl.BlockSpec(
        (rows, rows),
        lambda turn, dy, i, me: (0, block_at(me[0], span, distance(order, i), dy, 1 - turn)),
    )
    spec = pltpu.PrefetchScalarGridSpec(
        num_scalar_prefetch=1,
        grid=(2, near, some),
        in_specs=[whole_smem(), block, block, whole_vmem()] + [anywhere()] * len(after),
        out_specs=[
            pl.BlockSpec(
                (1, double, rows),
                lambda turn, dy, i, me: (jnp.where(turn == 0, dy * some + i, last), 0, 0),
            ),
            pl.BlockSpec(
                (1, double, rows),
                lambda turn, dy, i, me: (jnp.where(turn == 0, 0, dy * some + i), 0, 0),
            ),
        ],
    )
    return pl.pallas_call(
        functools.partial(mirror_part_kernel, width, span, order),
        grid_spec=spec,
        out_shape=[
            jax.ShapeDtypeStruct((near * some, double, rows), BF16),
            jax.ShapeDtypeStruct((near * some, double, rows), F32),
        ],
        compiler_params=params(),
        cost_estimate=cost(400000000000, 0),
        name="mirror_part",
    )(me, counts, data_real, data_imag, panel_t, *after)


def ordered(value, after):
    return lax.optimization_barrier((value, after))[0]


def direct_part_kernel(
    width, span, way, first, me_ref, counts_ref, real_ref, imag_ref, panel_ref, *refs
):
    out_ref = refs[-1]
    rows = real_ref.shape[0]
    tile = width // TILES
    k = pl.program_id(0)
    mine = me_ref[0] * rows // tile
    block = block_at(me_ref[0], span, span[0] - k, *way)
    scale = weight(counts_ref, mine, block * rows // tile, (1, out_ref.shape[1]))
    found = direct_block(real_ref[...], imag_ref[...], panel_ref[0]) * scale

    @pl.when(k == 0)
    def _():
        out_ref[...] = found if first else found + refs[0][...]

    @pl.when(k > 0)
    def _():
        out_ref[...] += found


def direct_part(me, counts, data_real, data_imag, panels, before, span, way, flops=0):
    rows, width = data_real.shape
    double = panels.shape[2]
    block = pl.BlockSpec((rows, rows), lambda k, me: (0, block_at(me[0], span, span[0] - k, *way)))
    spec = pltpu.PrefetchScalarGridSpec(
        num_scalar_prefetch=1,
        grid=(panels.shape[0],),
        in_specs=[whole_smem(), block, block, pl.BlockSpec((1, rows, double), lambda k, me: (k, 0, 0))]
        + [whole_vmem()] * len(before),
        out_specs=pl.BlockSpec((rows, double), lambda k, me: (0, 0)),
    )
    return pl.pallas_call(
        functools.partial(direct_part_kernel, width, span, way, not before),
        grid_spec=spec,
        out_shape=jax.ShapeDtypeStruct((rows, double), F32),
        compiler_params=params(),
        cost_estimate=cost(flops, 0),
        name="direct_part",
    )(me, counts, data_real, data_imag, panels, *before)


def levels(me, counts, data_real, data_imag, panel, panel_t, span):
    far, near = span
    data = (in_hbm(data_real), in_hbm(data_imag))
    along = [shift(panel, span, dz, 0, 0) for dz in range(1, far)]
    beside = shift(panel, span, 0, 1, 0)

    def part(order, after):
        other, own = mirror_part(me, counts, *data, panel_t, span, order, after)
        return own, other

    def over_cores(own, other):
        total = own + shift(other, span, 0, 0, 1).astype(F32)
        some = own.shape[0] // near
        return total[:some], total[some:].astype(BF16)

    def over_y(kept, sent, order):
        total = kept + shift(sent, span, 0, 1, 0).astype(F32)
        return [shift(total[i].astype(BF16), span, dz, 0, 0) for i, dz in enumerate(order)]

    first, rest = (2,), (1, 3)
    kept, sent = over_cores(*part(first, []))
    own, other = part(rest, [sent])
    own_here, other_here = part((0,), [beside])
    mirrors = over_y(kept, sent, first)
    kept, sent = over_cores(own, other)
    mirrors += over_y(kept, sent, rest)

    ahead = jnp.stack(ordered(along, [sent, own_here]))
    column = jnp.concatenate([panel[None], ahead])
    direct = [direct_part(me, counts, *data, column, [], span, (0, 0), 400000000000)]

    def add(panels, way):
        direct[:] = [direct_part(me, counts, *data, panels, direct, span, way)]

    other_here = ordered(other_here, ahead)
    total = own_here + ordered(shift(other_here, span, 0, 0, 1), direct).astype(F32)
    sent = total[1].astype(BF16)
    mirrors += [total[0], shift(sent, span, 0, 1, 0)]
    add(shift(column, span, 0, 0, 1), (0, 1))
    arrived = ordered(shift(ahead, span, 0, 1, 0), direct + mirrors[:3] + [sent])
    next_column = jnp.concatenate([beside[None], arrived])
    add(next_column, (1, 0))
    add(shift(next_column, span, 0, 0, 1), (1, 1))
    return direct[0], mirrors


def finish_kernel(factor, direct_ref, *refs):
    mirror_refs, (real_ref, imag_ref) = refs[:-2], refs[-2:]
    count = real_ref.shape[1]
    mirror = mirror_refs[-1][...].astype(F32)
    for ref in mirror_refs[:-1]:
        mirror += ref[...].astype(F32)
    total = factor * (direct_ref[...] + jnp.transpose(mirror))
    real_ref[...] = total[:, :count]
    imag_ref[...] = total[:, count:]


def finish(direct, mirrors, width):
    rows, double = direct.shape
    shape = jax.ShapeDtypeStruct((rows, double // 2), F32)
    return pl.pallas_call(
        functools.partial(finish_kernel, -1.0 / math.sqrt(width)),
        in_specs=[whole_vmem()] * (1 + len(mirrors)),
        out_specs=[whole_vmem(), whole_vmem()],
        out_shape=[shape, shape],
        compiler_params=params(),
        cost_estimate=cost(4 * rows * double, 10 * rows * double),
        name="finish",
    )(direct, *mirrors)


def shards(data_real, data_imag, counts, source_cols):
    rows, width = data_real.shape
    groups = width // rows
    count = source_cols.shape[0]
    cap = min(rows, count, -(-2 * count // groups // 8) * 8)
    col = source_cols.reshape(count, 1)
    row = source_cols.reshape(1, count)
    me = lax.axis_index(AXIS).reshape(1)

    def exchange(which):
        sent = own_source_rows(me, data_real, data_imag, source_cols, which, cap)
        return lax.all_to_all(sent, AXIS, split_axis=0, concat_axis=0)

    first = jnp.zeros((1,), jnp.int32)
    got = exchange(first)
    colpart = own_source_cols(data_real, data_imag, row, width // TILES)
    rowpart = select_rows(got, col, first, cap)

    owner = source_cols // rows
    most = jnp.max(jnp.sum(owner[:, None] == jnp.arange(groups)[None, :], axis=0, dtype=jnp.int32))

    def further(rowpart):
        def body(which, held):
            one = which.reshape(1)
            return held + select_rows(exchange(one), col, one, cap)

        return lax.fori_loop(1, (most + cap - 1) // cap, body, rowpart)

    rowpart = lax.cond(most > cap, further, lambda rowpart: rowpart, rowpart)
    panel, panel_t = own_panel(me, counts, rowpart, colpart, col, width)
    if rows % 128 == 0 and groups == 16:
        direct, mirrors = levels(me, counts, data_real, data_imag, panel, panel_t, (4, 2))
    else:
        full = lax.all_gather(panel, AXIS, axis=0, tiled=True)
        partial = mirror_term(me, counts, data_real, data_imag, panel_t)
        mirrors = [lax.psum_scatter(partial, AXIS, scatter_dimension=0, tiled=False)]
        direct = direct_term(me, counts, data_real, data_imag, full)
    return tuple(finish(direct, mirrors, width))


def solution(mesh):
    placed = (P(("freq", "row"), None), P(("freq", "row"), None), P(), P())
    return jax.shard_map(
        shards,
        mesh=mesh,
        in_specs=placed,
        out_specs=(P(("freq", "row"), None), P(("freq", "row"), None)),
        check_vma=False,
    )
```

```python
import functools
import math

import jax
import jax.numpy as jnp
from jax import lax
from jax.experimental import pallas as pl
from jax.experimental.pallas import tpu as pltpu
from jax.sharding import PartitionSpec as P

TILES = 8
AXIS = "row"
GROUP = 16
PIECE = 1024
F32 = jnp.float32
BF16 = jnp.bfloat16


def params(mib=16):
    return pltpu.CompilerParams(vmem_limit_bytes=mib * 1024 * 1024)


def whole_vmem():
    return pl.BlockSpec(memory_space=pltpu.VMEM)


def anywhere():
    return pl.BlockSpec(memory_space=pl.ANY)


def in_hbm(value):
    return pltpu.with_memory_space_constraint(value, pltpu.HBM)


def whole_smem():
    return pl.BlockSpec(memory_space=pltpu.SMEM)


def cost(flops, size):
    return pl.CostEstimate(flops=flops, bytes_accessed=size, transcendentals=0)


def dot(left, right):
    return jnp.dot(left, right, preferred_element_type=F32)


def ranks_of(col, rows):
    count = col.shape[0]
    owner = col // rows
    owner_row = jnp.transpose(jnp.broadcast_to(owner.astype(F32), (count, count))).astype(jnp.int32)
    before = lax.broadcasted_iota(jnp.int32, (count, count), 1) < lax.broadcasted_iota(
        jnp.int32, (count, count), 0
    )
    same = (owner_row == owner) & before
    return jnp.sum(same.astype(F32), axis=1, keepdims=True).astype(jnp.int32)


def rows_kernel(cap, round_ref, me_ref, col_ref, real_ref, imag_ref, out_ref, list_ref, near_ref, held_ref, sems):
    rows, width = real_ref.shape
    groups = out_ref.shape[0]
    count = col_ref.shape[0]
    base = me_ref[0] * rows
    skip = round_ref[0] * cap

    def copies(slot, local):
        group = pl.ds(pl.multiple_of(local // GROUP * GROUP, GROUP), GROUP)
        return [
            pltpu.make_async_copy(ref.at[group], near_ref.at[slot, part], sems.at[slot, part])
            for part, ref in enumerate((real_ref, imag_ref))
        ]

    def begin(s, found):
        local = col_ref[s] - base
        own = (local >= 0) & (local < rows)
        slot = found - skip

        @pl.when(own & (slot >= 0) & (slot < cap))
        def _():
            list_ref[slot] = local
            for copy in copies(slot, local):
                copy.start()

        return found + own.astype(jnp.int32)

    def pick(slot, _):
        local = list_ref[slot]
        chosen = lax.broadcasted_iota(jnp.int32, (GROUP, PIECE), 0) == local % GROUP
        for part, copy in enumerate(copies(slot, local)):
            copy.wait()
            for at in range(0, width, PIECE):
                group = near_ref[slot, part, :, at : at + PIECE].astype(F32)
                held_ref[pl.ds(part * cap + slot, 1), at : at + PIECE] = jnp.sum(
                    jnp.where(chosen, group, 0.0), axis=0, keepdims=True
                )
        return 0

    found = lax.fori_loop(0, count, begin, jnp.int32(0))
    held_ref[...] = jnp.zeros_like(held_ref)
    lax.fori_loop(0, jnp.clip(found - skip, 0, cap), pick, 0)
    for g in range(groups):
        out_ref[g] = held_ref[:, g * rows : (g + 1) * rows].astype(BF16)


def own_source_rows(me, data_real, data_imag, source_cols, which, cap):
    rows, width = data_real.shape
    return pl.pallas_call(
        functools.partial(rows_kernel, cap),
        in_specs=[whole_smem()] * 3 + [anywhere()] * 2,
        out_specs=whole_vmem(),
        out_shape=jax.ShapeDtypeStruct((width // rows, 2 * cap, rows), BF16),
        scratch_shapes=[
            pltpu.SMEM((cap,), jnp.int32),
            pltpu.VMEM((cap, 2, GROUP, width), BF16),
            pltpu.VMEM((2 * cap, width), F32),
            pltpu.SemaphoreType.DMA((cap, 2)),
        ],
        compiler_params=params(24),
        cost_estimate=cost(0, 2 * cap * width),
        name="own_source_rows",
    )(which, me, source_cols, data_real, data_imag)


def cols_kernel(real_ref, imag_ref, row_ref, out_ref, acc_ref):
    rows, step = real_ref.shape
    count = row_ref.shape[1]
    t = pl.program_id(0)

    @pl.when(t == 0)
    def _():
        acc_ref[...] = jnp.zeros_like(acc_ref)

    place = lax.broadcasted_iota(jnp.int32, (step, count), 0) + t * step
    pick = (place == row_ref[...]).astype(F32).astype(BF16)
    acc_ref[:, :count] += dot(real_ref[...], pick)
    acc_ref[:, count:] += dot(imag_ref[...], pick)

    @pl.when(t == pl.num_programs(0) - 1)
    def _():
        out_ref[...] = jnp.transpose(acc_ref[...]).astype(BF16)


def own_source_cols(data_real, data_imag, row, step):
    rows, width = data_real.shape
    count = row.shape[1]
    block = pl.BlockSpec((rows, step), lambda t: (0, t))
    return pl.pallas_call(
        cols_kernel,
        grid=(width // step,),
        in_specs=[block, block, whole_vmem()],
        out_specs=pl.BlockSpec((2 * count, rows), lambda t: (0, 0)),
        out_shape=jax.ShapeDtypeStruct((2 * count, rows), BF16),
        scratch_shapes=[pltpu.VMEM((rows, 2 * count), F32)],
        compiler_params=params(),
        cost_estimate=cost(4 * rows * width * count, 4 * rows * width),
        name="own_source_cols",
    )(data_real, data_imag, row)


def select_kernel(cap, round_ref, got_ref, col_ref, out_ref):
    out_ref[...] = pick_rows(cap, round_ref[0], got_ref, col_ref).astype(BF16)


def select_rows(got, col, which, cap):
    groups, _, rows = got.shape
    count = col.shape[0]
    return pl.pallas_call(
        functools.partial(select_kernel, cap),
        in_specs=[whole_smem(), whole_vmem(), whole_vmem()],
        out_specs=whole_vmem(),
        out_shape=jax.ShapeDtypeStruct((2 * count, rows), BF16),
        compiler_params=params(),
        cost_estimate=cost(8 * count * groups * cap * rows, 4 * groups * cap * rows),
        name="select_rows",
    )(which, got, col)


def pick_rows(cap, which, got_ref, col_ref):
    groups, _, rows = got_ref.shape
    count = col_ref.shape[0]
    col = col_ref[...]
    slot = ranks_of(col, rows) - which * cap
    inside = (slot >= 0) & (slot < cap)
    place = jnp.where(inside, (col // rows) * (2 * cap) + slot, -1)
    lanes = lax.broadcasted_iota(jnp.int32, (count, groups * 2 * cap), 1)
    pick = jnp.concatenate([lanes == place, lanes == jnp.where(inside, place + cap, -1)], axis=0)
    got = got_ref[...].reshape(groups * 2 * cap, rows)
    return dot(pick.astype(F32).astype(BF16), got)


def panel_kernel(width, me_ref, counts_ref, rowpart_ref, colpart_ref, col_ref, panel_ref, panel_t_ref):
    double, rows = colpart_ref.shape
    count = double // 2
    tile = width // TILES
    mine = me_ref[0] * rows // tile
    tiles = col_ref[...] // tile
    forward = jnp.zeros_like(tiles)
    backward = jnp.zeros_like(tiles)
    for t in range(TILES):
        forward = jnp.where(tiles == t, counts_ref[mine, t], forward)
        backward = jnp.where(tiles == t, counts_ref[t, mine], backward)
    forward = jnp.concatenate([forward, forward], axis=0).astype(F32)
    backward = jnp.concatenate([backward, backward], axis=0).astype(F32)
    own = colpart_ref[...].astype(F32)
    mirror = rowpart_ref[...].astype(F32)
    panel = (forward * own + backward * mirror) / jnp.maximum(forward + backward, 1.0)
    panel_t_ref[:, :rows] = panel.astype(BF16)
    panel_t_ref[:count, rows:] = (-panel[count:]).astype(BF16)
    panel_t_ref[count:, rows:] = panel[:count].astype(BF16)
    panel_ref[...] = jnp.transpose(panel).astype(BF16)


def own_panel(me, counts, rowpart, colpart, col, width):
    double, rows = colpart.shape
    return pl.pallas_call(
        functools.partial(panel_kernel, width),
        in_specs=[whole_smem()] * 2 + [whole_vmem()] * 3,
        out_specs=[whole_vmem()] * 2,
        out_shape=[
            jax.ShapeDtypeStruct((rows, double), BF16),
            jax.ShapeDtypeStruct((double, 2 * rows), BF16),
        ],
        compiler_params=params(),
        cost_estimate=cost(8 * rows * double, 8 * rows * double),
        name="own_panel",
    )(me, counts, rowpart, colpart, col)


def weight(counts_ref, mine, other, shape):
    forward = jnp.full(shape, counts_ref[mine, other], jnp.int32).astype(F32)
    backward = jnp.full(shape, counts_ref[other, mine], jnp.int32).astype(F32)
    return forward / jnp.maximum(forward + backward, 1.0)


def mirror_block(real, imag, panel_t):
    rows = real.shape[0]
    return dot(panel_t[:, :rows], real) + dot(panel_t[:, rows:], imag)


def direct_block(real, imag, panel):
    count = panel.shape[1] // 2
    turned = jnp.concatenate([-panel[:, count:], panel[:, :count]], axis=1)
    return dot(real, panel) + dot(imag, turned)


def mirror_kernel(width, me_ref, counts_ref, real_ref, imag_ref, panel_t_ref, out_ref):
    rows, tile = real_ref.shape
    mine = me_ref[0] * rows // tile
    found = mirror_block(real_ref[...], imag_ref[...], panel_t_ref[...])
    found = found * weight(counts_ref, mine, pl.program_id(0), (1, tile))
    for g in range(out_ref.shape[0]):
        out_ref[g] = found[:, g * rows : (g + 1) * rows]


def mirror_term(me, counts, data_real, data_imag, panel_t):
    rows, width = data_real.shape
    double = panel_t.shape[0]
    tile = width // TILES
    block = pl.BlockSpec((rows, tile), lambda t: (0, t))
    return pl.pallas_call(
        functools.partial(mirror_kernel, width),
        grid=(TILES,),
        in_specs=[whole_smem()] * 2 + [block, block, whole_vmem()],
        out_specs=pl.BlockSpec((tile // rows, double, rows), lambda t: (t, 0, 0)),
        out_shape=jax.ShapeDtypeStruct((width // rows, double, rows), F32),
        compiler_params=params(32),
        cost_estimate=cost(4 * rows * width * double, 4 * rows * width + 2 * double * width),
        name="mirror_term",
    )(me, counts, data_real, data_imag, panel_t)


def direct_kernel(width, me_ref, counts_ref, real_ref, imag_ref, panel_ref, out_ref):
    rows, tile = real_ref.shape
    mine = me_ref[0] * rows // tile
    t = pl.program_id(0)

    @pl.when(t == 0)
    def _():
        out_ref[...] = jnp.zeros_like(out_ref)

    found = direct_block(real_ref[...], imag_ref[...], panel_ref[...])
    out_ref[...] += found * weight(counts_ref, mine, t, (1, out_ref.shape[1]))


def direct_term(me, counts, data_real, data_imag, panel):
    rows, width = data_real.shape
    double = panel.shape[1]
    tile = width // TILES
    block = pl.BlockSpec((rows, tile), lambda t: (0, t))
    return pl.pallas_call(
        functools.partial(direct_kernel, width),
        grid=(TILES,),
        in_specs=[whole_smem()] * 2 + [block, block, pl.BlockSpec((tile, double), lambda t: (t, 0))],
        out_specs=pl.BlockSpec((rows, double), lambda t: (0, 0)),
        out_shape=jax.ShapeDtypeStruct((rows, double), F32),
        compiler_params=params(),
        cost_estimate=cost(4 * rows * width * double, 4 * rows * width + 2 * double * width),
        name="direct_term",
    )(me, counts, data_real, data_imag, panel)


def block_at(me, span, dz, dy, dc):
    far, near = span
    z, y, c = me // (2 * near), (me // 2) % near, me % 2
    return (((z + dz) % far) * near + (y + dy) % near) * 2 + (c + dc) % 2


def shift(value, span, dz, dy, dc):
    size = 2 * span[0] * span[1]
    return lax.ppermute(value, AXIS, [(i, block_at(i, span, dz, dy, dc)) for i in range(size)])


def distance(order, i):
    dz = order[0]
    for at in range(1, len(order)):
        dz = jnp.where(i == at, order[at], dz)
    return dz


def mirror_part_kernel(
    width, span, order, me_ref, counts_ref, real_ref, imag_ref, panel_t_ref, *refs
):
    other_ref, near_ref, far_ref = refs[-3:]
    rows = real_ref.shape[0]
    tile = width // TILES
    me = me_ref[0]
    dy, i = pl.program_id(0), pl.program_id(1)
    mine = me * rows // tile
    panel_t = panel_t_ref[...]

    def term(turn):
        block = block_at(me, span, distance(order, i), dy, turn)
        scale = weight(counts_ref, mine, block * rows // tile, (1, rows))
        columns = pl.ds(pl.multiple_of((me + turn) % 2 * rows, rows), rows)
        return mirror_block(real_ref[:, columns], imag_ref[:, columns], panel_t) * scale

    other_ref[0] = term(1).astype(BF16)

    @pl.when(dy == 0)
    def _():
        near_ref[0] = term(0)

    @pl.when(dy == 1)
    def _():
        far_ref[0] = term(0)


def mirror_part(me, counts, data_real, data_imag, panel_t, span, order, after):
    rows, width = data_real.shape
    double = panel_t.shape[0]
    some = len(order)
    block = pl.BlockSpec(
        (rows, 2 * rows),
        lambda dy, i, me: (0, block_at(me[0], span, distance(order, i), dy, 0) // 2),
    )
    shape = (1, double, rows)
    spec = pltpu.PrefetchScalarGridSpec(
        num_scalar_prefetch=1,
        grid=(2, some),
        in_specs=[whole_smem(), block, block, whole_vmem()] + [anywhere()] * len(after),
        out_specs=[
            pl.BlockSpec(shape, lambda dy, i, me: (dy * some + i, 0, 0)),
            pl.BlockSpec(shape, lambda dy, i, me: (jnp.where(dy == 0, i, some - 1), 0, 0)),
            pl.BlockSpec(shape, lambda dy, i, me: (jnp.where(dy == 0, 0, i), 0, 0)),
        ],
    )
    return pl.pallas_call(
        functools.partial(mirror_part_kernel, width, span, order),
        grid_spec=spec,
        out_shape=[
            jax.ShapeDtypeStruct((2 * some, double, rows), BF16),
            jax.ShapeDtypeStruct((some, double, rows), F32),
            jax.ShapeDtypeStruct((some, double, rows), F32),
        ],
        compiler_params=params(),
        cost_estimate=cost(400000000000, 0),
        name="mirror_part",
    )(me, counts, data_real, data_imag, panel_t, *after)


def ordered(value, after):
    return lax.optimization_barrier((value, after))[0]


def direct_part_kernel(
    width, span, back, way, first, me_ref, counts_ref, real_ref, imag_ref, panel_ref, *refs
):
    out_ref = refs[-1]
    rows = real_ref.shape[0]
    tile = width // TILES
    k = pl.program_id(0)
    mine = me_ref[0] * rows // tile
    block = block_at(me_ref[0], span, span[0] - distance(back, k), *way)
    scale = weight(counts_ref, mine, block * rows // tile, (1, out_ref.shape[1]))
    found = direct_block(real_ref[...], imag_ref[...], panel_ref[0]) * scale

    @pl.when(k == 0)
    def _():
        out_ref[...] = found if first else found + refs[0][...]

    @pl.when(k > 0)
    def _():
        out_ref[...] += found


def direct_part(me, counts, data_real, data_imag, panels, before, span, back, way, flops=0):
    rows, width = data_real.shape
    double = panels.shape[2]
    block = pl.BlockSpec(
        (rows, rows),
        lambda k, me: (0, block_at(me[0], span, span[0] - distance(back, k), *way)),
    )
    spec = pltpu.PrefetchScalarGridSpec(
        num_scalar_prefetch=1,
        grid=(panels.shape[0],),
        in_specs=[whole_smem(), block, block, pl.BlockSpec((1, rows, double), lambda k, me: (k, 0, 0))]
        + [whole_vmem()] * len(before),
        out_specs=pl.BlockSpec((rows, double), lambda k, me: (0, 0)),
    )
    return pl.pallas_call(
        functools.partial(direct_part_kernel, width, span, back, way, not before),
        grid_spec=spec,
        out_shape=jax.ShapeDtypeStruct((rows, double), F32),
        compiler_params=params(),
        cost_estimate=cost(flops, 0),
        name="direct_part",
    )(me, counts, data_real, data_imag, panels, *before)


def levels(me, counts, data_real, data_imag, panel, panel_t, span):
    far, near = span
    data = (in_hbm(data_real), in_hbm(data_imag))
    along = [shift(panel, span, dz, 0, 0) for dz in range(1, far)]
    beside = shift(panel, span, 0, 1, 0)

    def part(order, after):
        return mirror_part(me, counts, *data, panel_t, span, order, after)

    def to_y(other, own):
        got = shift(other, span, 0, 0, 1)
        some = own.shape[0]
        return (own + got[some:].astype(F32)).astype(BF16), got[:some]

    def to_z(sent, own, got, order):
        total = own + got.astype(F32) + shift(sent, span, 0, 1, 0).astype(F32)
        return [shift(total[i].astype(BF16), span, dz, 0, 0) for i, dz in enumerate(order)]

    first, rest = (2,), (1, 3)
    other, own, own_far = part(first, [])
    sent, got = to_y(other, own_far)
    other_rest, own_rest, own_rest_far = part(rest, [sent])
    other_here, own_here, own_here_far = part((0,), [beside])
    mirrors = to_z(sent, own, got, first)
    sent, got = to_y(other_rest, own_rest_far)
    mirrors += to_z(sent, own_rest, got, rest)

    along = ordered(along, [sent, own_here])
    column = jnp.stack([panel] + along)
    direct = []

    def add(panels, back, way, flops=0):
        direct[:] = [direct_part(me, counts, *data, panels, direct, span, back, way, flops)]

    add(column, (0, 1, 2, 3), (0, 0), 400000000000)
    sent, got = to_y(ordered(other_here, along), ordered(own_here_far, direct))
    mirrors += [own_here[0], got[0], shift(sent[0], span, 0, 1, 0)]
    add(shift(column, span, 0, 0, 1), (0, 1, 2, 3), (0, 1))

    early = jnp.stack([beside, shift(along[0], span, 0, 1, 0)])
    late = shift(jnp.stack(along[1:]), span, 0, 1, 0)
    early = ordered(early, direct)
    add(early, (0, 1), (1, 0))
    add(shift(early, span, 0, 0, 1), (0, 1), (1, 1))
    late = ordered(late, direct + mirrors[:3] + [sent])
    add(late, (2, 3), (1, 0))
    add(shift(late, span, 0, 0, 1), (2, 3), (1, 1))
    return direct[0], mirrors


def finish_kernel(factor, direct_ref, *refs):
    mirror_refs, (real_ref, imag_ref) = refs[:-2], refs[-2:]
    count = real_ref.shape[1]
    mirror = mirror_refs[-1][...].astype(F32)
    for ref in mirror_refs[:-1]:
        mirror += ref[...].astype(F32)
    total = factor * (direct_ref[...] + jnp.transpose(mirror))
    real_ref[...] = total[:, :count]
    imag_ref[...] = total[:, count:]


def finish(direct, mirrors, width):
    rows, double = direct.shape
    shape = jax.ShapeDtypeStruct((rows, double // 2), F32)
    return pl.pallas_call(
        functools.partial(finish_kernel, -1.0 / math.sqrt(width)),
        in_specs=[whole_vmem()] * (1 + len(mirrors)),
        out_specs=[whole_vmem(), whole_vmem()],
        out_shape=[shape, shape],
        compiler_params=params(),
        cost_estimate=cost(4 * rows * double, 10 * rows * double),
        name="finish",
    )(direct, *mirrors)


def shards(data_real, data_imag, counts, source_cols):
    rows, width = data_real.shape
    groups = width // rows
    count = source_cols.shape[0]
    cap = min(rows, count, -(-2 * count // groups // 8) * 8)
    col = source_cols.reshape(count, 1)
    row = source_cols.reshape(1, count)
    me = lax.axis_index(AXIS).reshape(1)

    def exchange(which):
        sent = own_source_rows(me, data_real, data_imag, source_cols, which, cap)
        return lax.all_to_all(sent, AXIS, split_axis=0, concat_axis=0)

    first = jnp.zeros((1,), jnp.int32)
    got = exchange(first)
    colpart = own_source_cols(data_real, data_imag, row, width // TILES)
    rowpart = select_rows(got, col, first, cap)

    owner = source_cols // rows
    most = jnp.max(jnp.sum(owner[:, None] == jnp.arange(groups)[None, :], axis=0, dtype=jnp.int32))

    def further(rowpart):
        def body(which, held):
            one = which.reshape(1)
            return held + select_rows(exchange(one), col, one, cap)

        return lax.fori_loop(1, (most + cap - 1) // cap, body, rowpart)

    rowpart = lax.cond(most > cap, further, lambda rowpart: rowpart, rowpart)
    panel, panel_t = own_panel(me, counts, rowpart, colpart, col, width)
    if rows % 128 == 0 and groups == 16:
        direct, mirrors = levels(me, counts, data_real, data_imag, panel, panel_t, (4, 2))
    else:
        full = lax.all_gather(panel, AXIS, axis=0, tiled=True)
        partial = mirror_term(me, counts, data_real, data_imag, panel_t)
        mirrors = [lax.psum_scatter(partial, AXIS, scatter_dimension=0, tiled=False)]
        direct = direct_term(me, counts, data_real, data_imag, full)
    return tuple(finish(direct, mirrors, width))


def solution(mesh):
    placed = (P(("freq", "row"), None), P(("freq", "row"), None), P(), P())
    return jax.shard_map(
        shards,
        mesh=mesh,
        in_specs=placed,
        out_specs=(P(("freq", "row"), None), P(("freq", "row"), None)),
        check_vma=False,
    )
```

```python
import functools
import math

import jax
import jax.numpy as jnp
from jax import lax
from jax.experimental import pallas as pl
from jax.experimental.pallas import tpu as pltpu
from jax.sharding import PartitionSpec as P

TILES = 8
AXIS = "row"
CORE, Y, LOW, HIGH = 1, 2, 4, 8
GROUP = 16
PIECE = 1024
F32 = jnp.float32
BF16 = jnp.bfloat16


def params(mib=16):
    return pltpu.CompilerParams(vmem_limit_bytes=mib * 1024 * 1024)


def whole_vmem():
    return pl.BlockSpec(memory_space=pltpu.VMEM)


def anywhere():
    return pl.BlockSpec(memory_space=pl.ANY)


def in_hbm(value):
    return pltpu.with_memory_space_constraint(value, pltpu.HBM)


def whole_smem():
    return pl.BlockSpec(memory_space=pltpu.SMEM)


def cost(flops, size):
    return pl.CostEstimate(flops=flops, bytes_accessed=size, transcendentals=0)


def dot(left, right):
    return jnp.dot(left, right, preferred_element_type=F32)


def ranks_of(col, rows):
    count = col.shape[0]
    owner = col // rows
    owner_row = jnp.transpose(jnp.broadcast_to(owner.astype(F32), (count, count))).astype(jnp.int32)
    before = lax.broadcasted_iota(jnp.int32, (count, count), 1) < lax.broadcasted_iota(
        jnp.int32, (count, count), 0
    )
    same = (owner_row == owner) & before
    return jnp.sum(same.astype(F32), axis=1, keepdims=True).astype(jnp.int32)


def rows_kernel(cap, round_ref, me_ref, col_ref, real_ref, imag_ref, out_ref, list_ref, near_ref, held_ref, sems):
    rows, width = real_ref.shape
    groups = out_ref.shape[0]
    count = col_ref.shape[0]
    base = me_ref[0] * rows
    skip = round_ref[0] * cap

    def copies(slot, local):
        group = pl.ds(pl.multiple_of(local // GROUP * GROUP, GROUP), GROUP)
        return [
            pltpu.make_async_copy(ref.at[group], near_ref.at[slot, part], sems.at[slot, part])
            for part, ref in enumerate((real_ref, imag_ref))
        ]

    def begin(s, found):
        local = col_ref[s] - base
        own = (local >= 0) & (local < rows)
        slot = found - skip

        @pl.when(own & (slot >= 0) & (slot < cap))
        def _():
            list_ref[slot] = local
            for copy in copies(slot, local):
                copy.start()

        return found + own.astype(jnp.int32)

    def pick(slot, _):
        local = list_ref[slot]
        chosen = lax.broadcasted_iota(jnp.int32, (GROUP, PIECE), 0) == local % GROUP
        for part, copy in enumerate(copies(slot, local)):
            copy.wait()
            for at in range(0, width, PIECE):
                group = near_ref[slot, part, :, at : at + PIECE].astype(F32)
                held_ref[pl.ds(part * cap + slot, 1), at : at + PIECE] = jnp.sum(
                    jnp.where(chosen, group, 0.0), axis=0, keepdims=True
                )
        return 0

    found = lax.fori_loop(0, count, begin, jnp.int32(0))
    held_ref[...] = jnp.zeros_like(held_ref)
    lax.fori_loop(0, jnp.clip(found - skip, 0, cap), pick, 0)
    for g in range(groups):
        out_ref[g] = held_ref[:, g * rows : (g + 1) * rows].astype(BF16)


def own_source_rows(me, data_real, data_imag, source_cols, which, cap):
    rows, width = data_real.shape
    return pl.pallas_call(
        functools.partial(rows_kernel, cap),
        in_specs=[whole_smem()] * 3 + [anywhere()] * 2,
        out_specs=whole_vmem(),
        out_shape=jax.ShapeDtypeStruct((width // rows, 2 * cap, rows), BF16),
        scratch_shapes=[
            pltpu.SMEM((cap,), jnp.int32),
            pltpu.VMEM((cap, 2, GROUP, width), BF16),
            pltpu.VMEM((2 * cap, width), F32),
            pltpu.SemaphoreType.DMA((cap, 2)),
        ],
        compiler_params=params(24),
        cost_estimate=cost(0, 2 * cap * width),
        name="own_source_rows",
    )(which, me, source_cols, data_real, data_imag)


def cols_kernel(real_ref, imag_ref, row_ref, out_ref, acc_ref):
    rows, step = real_ref.shape
    count = row_ref.shape[1]
    t = pl.program_id(0)

    @pl.when(t == 0)
    def _():
        acc_ref[...] = jnp.zeros_like(acc_ref)

    place = lax.broadcasted_iota(jnp.int32, (step, count), 0) + t * step
    pick = (place == row_ref[...]).astype(F32).astype(BF16)
    acc_ref[:, :count] += dot(real_ref[...], pick)
    acc_ref[:, count:] += dot(imag_ref[...], pick)

    @pl.when(t == pl.num_programs(0) - 1)
    def _():
        out_ref[...] = jnp.transpose(acc_ref[...]).astype(BF16)


def own_source_cols(data_real, data_imag, row, step):
    rows, width = data_real.shape
    count = row.shape[1]
    block = pl.BlockSpec((rows, step), lambda t: (0, t))
    return pl.pallas_call(
        cols_kernel,
        grid=(width // step,),
        in_specs=[block, block, whole_vmem()],
        out_specs=pl.BlockSpec((2 * count, rows), lambda t: (0, 0)),
        out_shape=jax.ShapeDtypeStruct((2 * count, rows), BF16),
        scratch_shapes=[pltpu.VMEM((rows, 2 * count), F32)],
        compiler_params=params(),
        cost_estimate=cost(4 * rows * width * count, 4 * rows * width),
        name="own_source_cols",
    )(data_real, data_imag, row)


def select_kernel(cap, round_ref, got_ref, col_ref, out_ref):
    out_ref[...] = pick_rows(cap, round_ref[0], got_ref, col_ref).astype(BF16)


def select_rows(got, col, which, cap):
    groups, _, rows = got.shape
    count = col.shape[0]
    return pl.pallas_call(
        functools.partial(select_kernel, cap),
        in_specs=[whole_smem(), whole_vmem(), whole_vmem()],
        out_specs=whole_vmem(),
        out_shape=jax.ShapeDtypeStruct((2 * count, rows), BF16),
        compiler_params=params(),
        cost_estimate=cost(8 * count * groups * cap * rows, 4 * groups * cap * rows),
        name="select_rows",
    )(which, got, col)


def pick_rows(cap, which, got_ref, col_ref):
    groups, _, rows = got_ref.shape
    count = col_ref.shape[0]
    col = col_ref[...]
    slot = ranks_of(col, rows) - which * cap
    inside = (slot >= 0) & (slot < cap)
    place = jnp.where(inside, (col // rows) * (2 * cap) + slot, -1)
    lanes = lax.broadcasted_iota(jnp.int32, (count, groups * 2 * cap), 1)
    pick = jnp.concatenate([lanes == place, lanes == jnp.where(inside, place + cap, -1)], axis=0)
    got = got_ref[...].reshape(groups * 2 * cap, rows)
    return dot(pick.astype(F32).astype(BF16), got)


def panel_kernel(width, me_ref, counts_ref, rowpart_ref, colpart_ref, col_ref, panel_ref, panel_t_ref):
    double, rows = colpart_ref.shape
    count = double // 2
    tile = width // TILES
    mine = me_ref[0] * rows // tile
    tiles = col_ref[...] // tile
    forward = jnp.zeros_like(tiles)
    backward = jnp.zeros_like(tiles)
    for t in range(TILES):
        forward = jnp.where(tiles == t, counts_ref[mine, t], forward)
        backward = jnp.where(tiles == t, counts_ref[t, mine], backward)
    forward = jnp.concatenate([forward, forward], axis=0).astype(F32)
    backward = jnp.concatenate([backward, backward], axis=0).astype(F32)
    own = colpart_ref[...].astype(F32)
    mirror = rowpart_ref[...].astype(F32)
    panel = (forward * own + backward * mirror) / jnp.maximum(forward + backward, 1.0)
    panel_t_ref[:, :rows] = panel.astype(BF16)
    panel_t_ref[:count, rows:] = (-panel[count:]).astype(BF16)
    panel_t_ref[count:, rows:] = panel[:count].astype(BF16)
    panel_ref[...] = jnp.transpose(panel).astype(BF16)


def own_panel(me, counts, rowpart, colpart, col, width):
    double, rows = colpart.shape
    return pl.pallas_call(
        functools.partial(panel_kernel, width),
        in_specs=[whole_smem()] * 2 + [whole_vmem()] * 3,
        out_specs=[whole_vmem()] * 2,
        out_shape=[
            jax.ShapeDtypeStruct((rows, double), BF16),
            jax.ShapeDtypeStruct((double, 2 * rows), BF16),
        ],
        compiler_params=params(),
        cost_estimate=cost(8 * rows * double, 8 * rows * double),
        name="own_panel",
    )(me, counts, rowpart, colpart, col)


def weight(counts_ref, mine, other, shape):
    forward = jnp.full(shape, counts_ref[mine, other], jnp.int32).astype(F32)
    backward = jnp.full(shape, counts_ref[other, mine], jnp.int32).astype(F32)
    return forward / jnp.maximum(forward + backward, 1.0)


def mirror_block(real, imag, panel_t):
    rows = real.shape[0]
    return dot(panel_t[:, :rows], real) + dot(panel_t[:, rows:], imag)


def direct_block(real, imag, panel):
    count = panel.shape[1] // 2
    turned = jnp.concatenate([-panel[:, count:], panel[:, :count]], axis=1)
    return dot(real, panel) + dot(imag, turned)


def mirror_kernel(width, me_ref, counts_ref, real_ref, imag_ref, panel_t_ref, out_ref):
    rows, tile = real_ref.shape
    mine = me_ref[0] * rows // tile
    found = mirror_block(real_ref[...], imag_ref[...], panel_t_ref[...])
    found = found * weight(counts_ref, mine, pl.program_id(0), (1, tile))
    for g in range(out_ref.shape[0]):
        out_ref[g] = found[:, g * rows : (g + 1) * rows]


def mirror_term(me, counts, data_real, data_imag, panel_t):
    rows, width = data_real.shape
    double = panel_t.shape[0]
    tile = width // TILES
    block = pl.BlockSpec((rows, tile), lambda t: (0, t))
    return pl.pallas_call(
        functools.partial(mirror_kernel, width),
        grid=(TILES,),
        in_specs=[whole_smem()] * 2 + [block, block, whole_vmem()],
        out_specs=pl.BlockSpec((tile // rows, double, rows), lambda t: (t, 0, 0)),
        out_shape=jax.ShapeDtypeStruct((width // rows, double, rows), F32),
        compiler_params=params(32),
        cost_estimate=cost(4 * rows * width * double, 4 * rows * width + 2 * double * width),
        name="mirror_term",
    )(me, counts, data_real, data_imag, panel_t)


def direct_kernel(width, me_ref, counts_ref, real_ref, imag_ref, panel_ref, out_ref):
    rows, tile = real_ref.shape
    mine = me_ref[0] * rows // tile
    t = pl.program_id(0)

    @pl.when(t == 0)
    def _():
        out_ref[...] = jnp.zeros_like(out_ref)

    found = direct_block(real_ref[...], imag_ref[...], panel_ref[...])
    out_ref[...] += found * weight(counts_ref, mine, t, (1, out_ref.shape[1]))


def direct_term(me, counts, data_real, data_imag, panel):
    rows, width = data_real.shape
    double = panel.shape[1]
    tile = width // TILES
    block = pl.BlockSpec((rows, tile), lambda t: (0, t))
    return pl.pallas_call(
        functools.partial(direct_kernel, width),
        grid=(TILES,),
        in_specs=[whole_smem()] * 2 + [block, block, pl.BlockSpec((tile, double), lambda t: (t, 0))],
        out_specs=pl.BlockSpec((rows, double), lambda t: (0, 0)),
        out_shape=jax.ShapeDtypeStruct((rows, double), F32),
        compiler_params=params(),
        cost_estimate=cost(4 * rows * width * double, 4 * rows * width + 2 * double * width),
        name="direct_term",
    )(me, counts, data_real, data_imag, panel)


def swap(value, mask):
    return lax.ppermute(value, AXIS, [(i, i ^ mask) for i in range(lax.axis_size(AXIS))])


def picked(masks, i):
    mask = masks[0]
    for at in range(1, len(masks)):
        mask = jnp.where(i == at, masks[at], mask)
    return mask


def mirror_part_kernel(width, masks, me_ref, counts_ref, real_ref, imag_ref, panel_t_ref, *refs):
    other_ref, near_ref, far_ref, held_ref, sems = refs[-5:]
    rows = real_ref.shape[0]
    tile = width // TILES
    me = me_ref[0]
    dy, i = pl.program_id(0), pl.program_id(1)
    some = len(masks)
    mine = me * rows // tile
    panel_t = panel_t_ref[...]

    def copies(at, mask):
        columns = pl.ds(pl.multiple_of((me ^ mask) // 2 * (2 * rows), 2 * rows), 2 * rows)
        return [
            pltpu.make_async_copy(
                ref.at[:, columns], held_ref.at[at, pl.ds(part * rows, rows)], sems.at[at, part]
            )
            for part, ref in enumerate((real_ref, imag_ref))
        ]

    @pl.when((dy == 0) & (i == 0))
    def _():
        for at in range(2 * some):
            for copy in copies(at, masks[at % some] ^ (2 * (at // some))):
                copy.start()

    at = dy * some + i
    mask = picked(masks, i) ^ (2 * dy)
    for copy in copies(at, mask):
        copy.wait()

    def term(turn):
        block = me ^ mask ^ turn
        scale = weight(counts_ref, mine, block * rows // tile, (1, rows))
        columns = pl.ds(pl.multiple_of(block % 2 * rows, rows), rows)
        return dot(panel_t, held_ref[at, :, columns]) * scale

    other_ref[0] = term(1).astype(BF16)

    @pl.when(dy == 0)
    def _():
        near_ref[0] = term(0)

    @pl.when(dy == 1)
    def _():
        far_ref[0] = term(0)


def mirror_part(me, counts, data_real, data_imag, panel_t, masks, after):
    rows, width = data_real.shape
    double = panel_t.shape[0]
    some = len(masks)
    shape = (1, double, rows)
    spec = pltpu.PrefetchScalarGridSpec(
        num_scalar_prefetch=1,
        grid=(2, some),
        in_specs=[whole_smem(), anywhere(), anywhere(), whole_vmem()] + [anywhere()] * len(after),
        out_specs=[
            pl.BlockSpec(shape, lambda dy, i, me: (dy * some + i, 0, 0)),
            pl.BlockSpec(shape, lambda dy, i, me: (jnp.where(dy == 0, i, some - 1), 0, 0)),
            pl.BlockSpec(shape, lambda dy, i, me: (jnp.where(dy == 0, 0, i), 0, 0)),
        ],
        scratch_shapes=[
            pltpu.VMEM((2 * some, 2 * rows, 2 * rows), BF16),
            pltpu.SemaphoreType.DMA((2 * some, 2)),
        ],
    )
    return pl.pallas_call(
        functools.partial(mirror_part_kernel, width, masks),
        grid_spec=spec,
        out_shape=[
            jax.ShapeDtypeStruct((2 * some, double, rows), BF16),
            jax.ShapeDtypeStruct((some, double, rows), F32),
            jax.ShapeDtypeStruct((some, double, rows), F32),
        ],
        compiler_params=params(24),
        cost_estimate=cost(400000000000, 0),
        name="mirror_part",
    )(me, counts, data_real, data_imag, panel_t, *after)


def ordered(value, after):
    return lax.optimization_barrier((value, after))[0]


def direct_part_kernel(
    width, masks, first, me_ref, counts_ref, real_ref, imag_ref, panel_ref, *refs
):
    out_ref, held_ref, sems = refs[-3:]
    rows = real_ref.shape[0]
    tile = width // TILES
    me = me_ref[0]
    mine = me * rows // tile

    def copies(k):
        columns = pl.ds(pl.multiple_of((me ^ masks[k]) * rows, rows), rows)
        return [
            pltpu.make_async_copy(ref.at[:, columns], held_ref.at[k, part], sems.at[k, part])
            for part, ref in enumerate((real_ref, imag_ref))
        ]

    for k in range(len(masks)):
        for copy in copies(k):
            copy.start()
    total = jnp.zeros(out_ref.shape, F32) if first else refs[0][...]
    for k in range(len(masks)):
        for copy in copies(k):
            copy.wait()
        scale = weight(counts_ref, mine, (me ^ masks[k]) * rows // tile, (1, out_ref.shape[1]))
        total += direct_block(held_ref[k, 0], held_ref[k, 1], panel_ref[k]) * scale
    out_ref[...] = total


def direct_part(me, counts, data_real, data_imag, panels, before, masks, flops=0):
    rows, width = data_real.shape
    double = panels.shape[2]
    return pl.pallas_call(
        functools.partial(direct_part_kernel, width, masks, not before),
        in_specs=[whole_smem()] * 2 + [anywhere()] * 2 + [whole_vmem()] * (1 + len(before)),
        out_specs=whole_vmem(),
        out_shape=jax.ShapeDtypeStruct((rows, double), F32),
        scratch_shapes=[
            pltpu.VMEM((len(masks), 2, rows, rows), BF16),
            pltpu.SemaphoreType.DMA((len(masks), 2)),
        ],
        compiler_params=params(),
        cost_estimate=cost(flops, 0),
        name="direct_part",
    )(me, counts, data_real, data_imag, panels, *before)


def levels(me, counts, data_real, data_imag, panel, panel_t):
    data = (in_hbm(data_real), in_hbm(data_imag))
    high, low, beside = swap(panel, HIGH), swap(panel, LOW), swap(panel, Y)

    def to_y(other, own):
        got = swap(other, CORE)
        some = own.shape[0]
        return (own + got[some:].astype(F32)).astype(BF16), got[:some]

    def over_y(sent, own, got):
        return own + got.astype(F32) + swap(sent, Y).astype(F32)

    other, own, own_far = mirror_part(me, counts, *data, panel_t, (HIGH, HIGH | LOW), [])
    other_here, own_here, own_here_far = mirror_part(me, counts, *data, panel_t, (0, LOW), [beside])
    sent, got = to_y(other, own_far)
    total = over_y(sent, own, got)
    total = total[0] + swap(total[1].astype(BF16), LOW).astype(F32)
    mirrors = [swap(total.astype(BF16), HIGH)]

    low, high = ordered([low, high], [sent, own_here])
    both = swap(high, LOW)
    column = jnp.stack([panel, low, high, both])
    direct = []

    def add(panels, masks, flops=0):
        direct[:] = [direct_part(me, counts, *data, panels, direct, masks, flops)]

    add(column, (0, LOW, HIGH, HIGH | LOW), 400000000000)
    sent, got = to_y(ordered(other_here, high), ordered(own_here_far, high))
    total = over_y(sent, own_here, got)
    mirrors += [total[0], swap(total[1].astype(BF16), LOW)]
    add(swap(column, CORE), (CORE, CORE | LOW, CORE | HIGH, CORE | HIGH | LOW))

    early = jnp.stack([beside, swap(low, Y)])
    late = swap(jnp.stack([high, both]), Y)
    early = ordered(early, direct)
    add(early, (Y, Y | LOW))
    add(swap(early, CORE), (Y | CORE, Y | CORE | LOW))
    late = ordered(late, direct + mirrors)
    add(late, (Y | HIGH, Y | HIGH | LOW))
    add(swap(late, CORE), (Y | CORE | HIGH, Y | CORE | HIGH | LOW))
    return direct[0], mirrors


def finish_kernel(factor, direct_ref, *refs):
    mirror_refs, (real_ref, imag_ref) = refs[:-2], refs[-2:]
    count = real_ref.shape[1]
    mirror = mirror_refs[-1][...].astype(F32)
    for ref in mirror_refs[:-1]:
        mirror += ref[...].astype(F32)
    total = factor * (direct_ref[...] + jnp.transpose(mirror))
    real_ref[...] = total[:, :count]
    imag_ref[...] = total[:, count:]


def finish(direct, mirrors, width):
    rows, double = direct.shape
    shape = jax.ShapeDtypeStruct((rows, double // 2), F32)
    return pl.pallas_call(
        functools.partial(finish_kernel, -1.0 / math.sqrt(width)),
        in_specs=[whole_vmem()] * (1 + len(mirrors)),
        out_specs=[whole_vmem(), whole_vmem()],
        out_shape=[shape, shape],
        compiler_params=params(),
        cost_estimate=cost(4 * rows * double, 10 * rows * double),
        name="finish",
    )(direct, *mirrors)


def shards(data_real, data_imag, counts, source_cols):
    rows, width = data_real.shape
    groups = width // rows
    count = source_cols.shape[0]
    cap = min(rows, count, -(-2 * count // groups // 8) * 8)
    col = source_cols.reshape(count, 1)
    row = source_cols.reshape(1, count)
    me = lax.axis_index(AXIS).reshape(1)

    def exchange(which):
        sent = own_source_rows(me, data_real, data_imag, source_cols, which, cap)
        return lax.all_to_all(sent, AXIS, split_axis=0, concat_axis=0)

    first = jnp.zeros((1,), jnp.int32)
    got = exchange(first)
    colpart = own_source_cols(data_real, data_imag, row, width // TILES)
    rowpart = select_rows(got, col, first, cap)

    owner = source_cols // rows
    most = jnp.max(jnp.sum(owner[:, None] == jnp.arange(groups)[None, :], axis=0, dtype=jnp.int32))

    def further(rowpart):
        def body(which, held):
            one = which.reshape(1)
            return held + select_rows(exchange(one), col, one, cap)

        return lax.fori_loop(1, (most + cap - 1) // cap, body, rowpart)

    rowpart = lax.cond(most > cap, further, lambda rowpart: rowpart, rowpart)
    panel, panel_t = own_panel(me, counts, rowpart, colpart, col, width)
    if rows % 128 == 0 and groups == 16:
        direct, mirrors = levels(me, counts, data_real, data_imag, panel, panel_t)
    else:
        full = lax.all_gather(panel, AXIS, axis=0, tiled=True)
        partial = mirror_term(me, counts, data_real, data_imag, panel_t)
        mirrors = [lax.psum_scatter(partial, AXIS, scatter_dimension=0, tiled=False)]
        direct = direct_term(me, counts, data_real, data_imag, full)
    return tuple(finish(direct, mirrors, width))


def solution(mesh):
    placed = (P(("freq", "row"), None), P(("freq", "row"), None), P(), P())
    return jax.shard_map(
        shards,
        mesh=mesh,
        in_specs=placed,
        out_specs=(P(("freq", "row"), None), P(("freq", "row"), None)),
        check_vma=False,
    )
```

```python
import functools
import math

import jax
import jax.numpy as jnp
from jax import lax
from jax.experimental import pallas as pl
from jax.experimental.pallas import tpu as pltpu
from jax.sharding import PartitionSpec as P

TILES = 8
AXIS = "row"
CORE, Y, LOW, HIGH = 1, 2, 4, 8
GROUP = 16
MIRROR_COST = 10000000000
DIRECT_COST = 2000000000
PIECE = 1024
F32 = jnp.float32
BF16 = jnp.bfloat16


def params(mib=16):
    return pltpu.CompilerParams(vmem_limit_bytes=mib * 1024 * 1024)


def whole_vmem():
    return pl.BlockSpec(memory_space=pltpu.VMEM)


def anywhere():
    return pl.BlockSpec(memory_space=pl.ANY)


def in_hbm(value):
    return pltpu.with_memory_space_constraint(value, pltpu.HBM)


def whole_smem():
    return pl.BlockSpec(memory_space=pltpu.SMEM)


def cost(flops, size):
    return pl.CostEstimate(flops=flops, bytes_accessed=size, transcendentals=0)


def dot(left, right):
    return jnp.dot(left, right, preferred_element_type=F32)


def ranks_of(col, rows):
    count = col.shape[0]
    owner = col // rows
    owner_row = jnp.transpose(jnp.broadcast_to(owner.astype(F32), (count, count))).astype(jnp.int32)
    before = lax.broadcasted_iota(jnp.int32, (count, count), 1) < lax.broadcasted_iota(
        jnp.int32, (count, count), 0
    )
    same = (owner_row == owner) & before
    return jnp.sum(same.astype(F32), axis=1, keepdims=True).astype(jnp.int32)


def rows_kernel(cap, round_ref, me_ref, col_ref, real_ref, imag_ref, out_ref, list_ref, near_ref, held_ref, sems):
    rows, width = real_ref.shape
    groups = out_ref.shape[0]
    count = col_ref.shape[0]
    base = me_ref[0] * rows
    skip = round_ref[0] * cap

    def copies(slot, local):
        group = pl.ds(pl.multiple_of(local // GROUP * GROUP, GROUP), GROUP)
        return [
            pltpu.make_async_copy(ref.at[group], near_ref.at[slot, part], sems.at[slot, part])
            for part, ref in enumerate((real_ref, imag_ref))
        ]

    def begin(s, found):
        local = col_ref[s] - base
        own = (local >= 0) & (local < rows)
        slot = found - skip

        @pl.when(own & (slot >= 0) & (slot < cap))
        def _():
            list_ref[slot] = local
            for copy in copies(slot, local):
                copy.start()

        return found + own.astype(jnp.int32)

    def pick(slot, _):
        local = list_ref[slot]
        chosen = lax.broadcasted_iota(jnp.int32, (GROUP, PIECE), 0) == local % GROUP
        for part, copy in enumerate(copies(slot, local)):
            copy.wait()
            for at in range(0, width, PIECE):
                group = near_ref[slot, part, :, at : at + PIECE].astype(F32)
                held_ref[pl.ds(part * cap + slot, 1), at : at + PIECE] = jnp.sum(
                    jnp.where(chosen, group, 0.0), axis=0, keepdims=True
                )
        return 0

    found = lax.fori_loop(0, count, begin, jnp.int32(0))
    held_ref[...] = jnp.zeros_like(held_ref)
    lax.fori_loop(0, jnp.clip(found - skip, 0, cap), pick, 0)
    for g in range(groups):
        out_ref[g] = held_ref[:, g * rows : (g + 1) * rows].astype(BF16)


def own_source_rows(me, data_real, data_imag, source_cols, which, cap):
    rows, width = data_real.shape
    return pl.pallas_call(
        functools.partial(rows_kernel, cap),
        in_specs=[whole_smem()] * 3 + [anywhere()] * 2,
        out_specs=whole_vmem(),
        out_shape=jax.ShapeDtypeStruct((width // rows, 2 * cap, rows), BF16),
        scratch_shapes=[
            pltpu.SMEM((cap,), jnp.int32),
            pltpu.VMEM((cap, 2, GROUP, width), BF16),
            pltpu.VMEM((2 * cap, width), F32),
            pltpu.SemaphoreType.DMA((cap, 2)),
        ],
        compiler_params=params(24),
        cost_estimate=cost(0, 2 * cap * width),
        name="own_source_rows",
    )(which, me, source_cols, data_real, data_imag)


def cols_kernel(real_ref, imag_ref, row_ref, out_ref, acc_ref):
    rows, step = real_ref.shape
    count = row_ref.shape[1]
    t = pl.program_id(0)

    @pl.when(t == 0)
    def _():
        acc_ref[...] = jnp.zeros_like(acc_ref)

    place = lax.broadcasted_iota(jnp.int32, (step, count), 0) + t * step
    pick = (place == row_ref[...]).astype(F32).astype(BF16)
    acc_ref[:, :count] += dot(real_ref[...], pick)
    acc_ref[:, count:] += dot(imag_ref[...], pick)

    @pl.when(t == pl.num_programs(0) - 1)
    def _():
        out_ref[...] = jnp.transpose(acc_ref[...]).astype(BF16)


def own_source_cols(data_real, data_imag, row, step):
    rows, width = data_real.shape
    count = row.shape[1]
    block = pl.BlockSpec((rows, step), lambda t: (0, t))
    return pl.pallas_call(
        cols_kernel,
        grid=(width // step,),
        in_specs=[block, block, whole_vmem()],
        out_specs=pl.BlockSpec((2 * count, rows), lambda t: (0, 0)),
        out_shape=jax.ShapeDtypeStruct((2 * count, rows), BF16),
        scratch_shapes=[pltpu.VMEM((rows, 2 * count), F32)],
        compiler_params=params(),
        cost_estimate=cost(4 * rows * width * count, 4 * rows * width),
        name="own_source_cols",
    )(data_real, data_imag, row)


def select_kernel(cap, round_ref, got_ref, col_ref, out_ref):
    out_ref[...] = pick_rows(cap, round_ref[0], got_ref, col_ref).astype(BF16)


def select_rows(got, col, which, cap):
    groups, _, rows = got.shape
    count = col.shape[0]
    return pl.pallas_call(
        functools.partial(select_kernel, cap),
        in_specs=[whole_smem(), whole_vmem(), whole_vmem()],
        out_specs=whole_vmem(),
        out_shape=jax.ShapeDtypeStruct((2 * count, rows), BF16),
        compiler_params=params(),
        cost_estimate=cost(8 * count * groups * cap * rows, 4 * groups * cap * rows),
        name="select_rows",
    )(which, got, col)


def pick_rows(cap, which, got_ref, col_ref):
    groups, _, rows = got_ref.shape
    count = col_ref.shape[0]
    col = col_ref[...]
    slot = ranks_of(col, rows) - which * cap
    inside = (slot >= 0) & (slot < cap)
    place = jnp.where(inside, (col // rows) * (2 * cap) + slot, -1)
    lanes = lax.broadcasted_iota(jnp.int32, (count, groups * 2 * cap), 1)
    pick = jnp.concatenate([lanes == place, lanes == jnp.where(inside, place + cap, -1)], axis=0)
    got = got_ref[...].reshape(groups * 2 * cap, rows)
    return dot(pick.astype(F32).astype(BF16), got)


def panel_kernel(width, me_ref, counts_ref, rowpart_ref, colpart_ref, col_ref, panel_ref, panel_t_ref):
    double, rows = colpart_ref.shape
    count = double // 2
    tile = width // TILES
    mine = me_ref[0] * rows // tile
    tiles = col_ref[...] // tile
    forward = jnp.zeros_like(tiles)
    backward = jnp.zeros_like(tiles)
    for t in range(TILES):
        forward = jnp.where(tiles == t, counts_ref[mine, t], forward)
        backward = jnp.where(tiles == t, counts_ref[t, mine], backward)
    forward = jnp.concatenate([forward, forward], axis=0).astype(F32)
    backward = jnp.concatenate([backward, backward], axis=0).astype(F32)
    own = colpart_ref[...].astype(F32)
    mirror = rowpart_ref[...].astype(F32)
    panel = (forward * own + backward * mirror) / jnp.maximum(forward + backward, 1.0)
    panel_t_ref[:, :rows] = panel.astype(BF16)
    panel_t_ref[:count, rows:] = (-panel[count:]).astype(BF16)
    panel_t_ref[count:, rows:] = panel[:count].astype(BF16)
    panel_ref[...] = jnp.transpose(panel).astype(BF16)


def own_panel(me, counts, rowpart, colpart, col, width):
    double, rows = colpart.shape
    return pl.pallas_call(
        functools.partial(panel_kernel, width),
        in_specs=[whole_smem()] * 2 + [whole_vmem()] * 3,
        out_specs=[whole_vmem()] * 2,
        out_shape=[
            jax.ShapeDtypeStruct((rows, double), BF16),
            jax.ShapeDtypeStruct((double, 2 * rows), BF16),
        ],
        compiler_params=params(),
        cost_estimate=cost(8 * rows * double, 8 * rows * double),
        name="own_panel",
    )(me, counts, rowpart, colpart, col)


def weight(counts_ref, mine, other, shape):
    forward = jnp.full(shape, counts_ref[mine, other], jnp.int32).astype(F32)
    backward = jnp.full(shape, counts_ref[other, mine], jnp.int32).astype(F32)
    return forward / jnp.maximum(forward + backward, 1.0)


def mirror_block(real, imag, panel_t):
    rows = real.shape[0]
    return dot(panel_t[:, :rows], real) + dot(panel_t[:, rows:], imag)


def direct_block(real, imag, panel):
    count = panel.shape[1] // 2
    turned = jnp.concatenate([-panel[:, count:], panel[:, :count]], axis=1)
    return dot(real, panel) + dot(imag, turned)


def mirror_kernel(width, me_ref, counts_ref, real_ref, imag_ref, panel_t_ref, out_ref):
    rows, tile = real_ref.shape
    mine = me_ref[0] * rows // tile
    found = mirror_block(real_ref[...], imag_ref[...], panel_t_ref[...])
    found = found * weight(counts_ref, mine, pl.program_id(0), (1, tile))
    for g in range(out_ref.shape[0]):
        out_ref[g] = found[:, g * rows : (g + 1) * rows]


def mirror_term(me, counts, data_real, data_imag, panel_t):
    rows, width = data_real.shape
    double = panel_t.shape[0]
    tile = width // TILES
    block = pl.BlockSpec((rows, tile), lambda t: (0, t))
    return pl.pallas_call(
        functools.partial(mirror_kernel, width),
        grid=(TILES,),
        in_specs=[whole_smem()] * 2 + [block, block, whole_vmem()],
        out_specs=pl.BlockSpec((tile // rows, double, rows), lambda t: (t, 0, 0)),
        out_shape=jax.ShapeDtypeStruct((width // rows, double, rows), F32),
        compiler_params=params(32),
        cost_estimate=cost(4 * rows * width * double, 4 * rows * width + 2 * double * width),
        name="mirror_term",
    )(me, counts, data_real, data_imag, panel_t)


def direct_kernel(width, me_ref, counts_ref, real_ref, imag_ref, panel_ref, out_ref):
    rows, tile = real_ref.shape
    mine = me_ref[0] * rows // tile
    t = pl.program_id(0)

    @pl.when(t == 0)
    def _():
        out_ref[...] = jnp.zeros_like(out_ref)

    found = direct_block(real_ref[...], imag_ref[...], panel_ref[...])
    out_ref[...] += found * weight(counts_ref, mine, t, (1, out_ref.shape[1]))


def direct_term(me, counts, data_real, data_imag, panel):
    rows, width = data_real.shape
    double = panel.shape[1]
    tile = width // TILES
    block = pl.BlockSpec((rows, tile), lambda t: (0, t))
    return pl.pallas_call(
        functools.partial(direct_kernel, width),
        grid=(TILES,),
        in_specs=[whole_smem()] * 2 + [block, block, pl.BlockSpec((tile, double), lambda t: (t, 0))],
        out_specs=pl.BlockSpec((rows, double), lambda t: (0, 0)),
        out_shape=jax.ShapeDtypeStruct((rows, double), F32),
        compiler_params=params(),
        cost_estimate=cost(4 * rows * width * double, 4 * rows * width + 2 * double * width),
        name="direct_term",
    )(me, counts, data_real, data_imag, panel)


def swap(value, mask):
    return lax.ppermute(value, AXIS, [(i, i ^ mask) for i in range(lax.axis_size(AXIS))])


def picked(masks, i):
    mask = masks[0]
    for at in range(1, len(masks)):
        mask = jnp.where(i == at, masks[at], mask)
    return mask


def mirror_part_kernel(width, masks, me_ref, counts_ref, real_ref, imag_ref, panel_t_ref, *refs):
    other_ref, near_ref, far_ref, held_ref, sems = refs[-5:]
    rows = real_ref.shape[0]
    tile = width // TILES
    me = me_ref[0]
    dy, i = pl.program_id(0), pl.program_id(1)
    some = len(masks)
    mine = me * rows // tile
    panel_t = panel_t_ref[...]

    def copies(at, mask):
        columns = pl.ds(pl.multiple_of((me ^ mask) // 2 * (2 * rows), 2 * rows), 2 * rows)
        return [
            pltpu.make_async_copy(
                ref.at[:, columns], held_ref.at[at, pl.ds(part * rows, rows)], sems.at[at, part]
            )
            for part, ref in enumerate((real_ref, imag_ref))
        ]

    @pl.when((dy == 0) & (i == 0))
    def _():
        for at in range(2 * some):
            for copy in copies(at, masks[at % some] ^ (2 * (at // some))):
                copy.start()

    at = dy * some + i
    mask = picked(masks, i) ^ (2 * dy)
    for copy in copies(at, mask):
        copy.wait()

    def term(turn):
        block = me ^ mask ^ turn
        scale = weight(counts_ref, mine, block * rows // tile, (1, rows))
        columns = pl.ds(pl.multiple_of(block % 2 * rows, rows), rows)
        return dot(panel_t, held_ref[at, :, columns]) * scale

    other_ref[0] = term(1).astype(BF16)

    @pl.when(dy == 0)
    def _():
        near_ref[0] = term(0)

    @pl.when(dy == 1)
    def _():
        far_ref[0] = term(0)


def mirror_part(me, counts, data_real, data_imag, panel_t, masks, after):
    rows, width = data_real.shape
    double = panel_t.shape[0]
    some = len(masks)
    shape = (1, double, rows)
    spec = pltpu.PrefetchScalarGridSpec(
        num_scalar_prefetch=1,
        grid=(2, some),
        in_specs=[whole_smem(), anywhere(), anywhere(), whole_vmem()] + [anywhere()] * len(after),
        out_specs=[
            pl.BlockSpec(shape, lambda dy, i, me: (dy * some + i, 0, 0)),
            pl.BlockSpec(shape, lambda dy, i, me: (jnp.where(dy == 0, i, some - 1), 0, 0)),
            pl.BlockSpec(shape, lambda dy, i, me: (jnp.where(dy == 0, 0, i), 0, 0)),
        ],
        scratch_shapes=[
            pltpu.VMEM((2 * some, 2 * rows, 2 * rows), BF16),
            pltpu.SemaphoreType.DMA((2 * some, 2)),
        ],
    )
    return pl.pallas_call(
        functools.partial(mirror_part_kernel, width, masks),
        grid_spec=spec,
        out_shape=[
            jax.ShapeDtypeStruct((2 * some, double, rows), BF16),
            jax.ShapeDtypeStruct((some, double, rows), F32),
            jax.ShapeDtypeStruct((some, double, rows), F32),
        ],
        compiler_params=params(24),
        cost_estimate=cost(MIRROR_COST, 0),
        name="mirror_part",
    )(me, counts, data_real, data_imag, panel_t, *after)


def ordered(value, after):
    return lax.optimization_barrier((value, after))[0]


def direct_part_kernel(
    width, masks, first, me_ref, counts_ref, real_ref, imag_ref, panel_ref, *refs
):
    out_ref = refs[-1]
    rows = real_ref.shape[0]
    tile = width // TILES
    k = pl.program_id(0)
    mine = me_ref[0] * rows // tile
    block = me_ref[0] ^ picked(masks, k)
    scale = weight(counts_ref, mine, block * rows // tile, (1, out_ref.shape[1]))
    found = direct_block(real_ref[...], imag_ref[...], panel_ref[0]) * scale

    @pl.when(k == 0)
    def _():
        out_ref[...] = found if first else found + refs[0][...]

    @pl.when(k > 0)
    def _():
        out_ref[...] += found


def direct_part(me, counts, data_real, data_imag, panels, before, masks):
    rows, width = data_real.shape
    double = panels.shape[2]
    block = pl.BlockSpec((rows, rows), lambda k, me: (0, me[0] ^ picked(masks, k)))
    spec = pltpu.PrefetchScalarGridSpec(
        num_scalar_prefetch=1,
        grid=(len(masks),),
        in_specs=[whole_smem(), block, block, pl.BlockSpec((1, rows, double), lambda k, me: (k, 0, 0))]
        + [whole_vmem()] * len(before),
        out_specs=pl.BlockSpec((rows, double), lambda k, me: (0, 0)),
    )
    return pl.pallas_call(
        functools.partial(direct_part_kernel, width, masks, not before),
        grid_spec=spec,
        out_shape=jax.ShapeDtypeStruct((rows, double), F32),
        compiler_params=params(),
        cost_estimate=cost(DIRECT_COST, 0),
        name="direct_part",
    )(me, counts, data_real, data_imag, panels, *before)


def levels(me, counts, data_real, data_imag, panel, panel_t):
    data = (in_hbm(data_real), in_hbm(data_imag))
    high, low, beside = swap(panel, HIGH), swap(panel, LOW), swap(panel, Y)

    def to_y(other, own):
        got = swap(other, CORE)
        some = own.shape[0]
        return (own + got[some:].astype(F32)).astype(BF16), got[:some]

    def over_y(sent, own, got):
        return own + got.astype(F32) + swap(sent, Y).astype(F32)

    other, own, own_far = mirror_part(me, counts, *data, panel_t, (HIGH, HIGH | LOW), [])
    sent, got = to_y(other, own_far)
    other_here, own_here, own_here_far = mirror_part(me, counts, *data, panel_t, (0, LOW), [sent])
    total = over_y(sent, own, got)
    total = total[0] + swap(total[1].astype(BF16), LOW).astype(F32)
    mirrors = [swap(total.astype(BF16), HIGH)]

    low, high = ordered([low, high], [sent, own_here])
    both = swap(high, LOW)
    direct = []

    def add(panels, masks):
        direct[:] = [direct_part(me, counts, *data, panels, direct, masks)]

    add(jnp.stack([panel, low, high]), (0, LOW, HIGH))
    sent, got = to_y(ordered(other_here, high), ordered(own_here_far, high))
    total = over_y(sent, own_here, got)
    mirrors += [total[0], swap(total[1].astype(BF16), LOW)]
    column = jnp.stack([panel, low, high, both])
    add(swap(column, CORE), (CORE, CORE | LOW, CORE | HIGH, CORE | HIGH | LOW))

    early = jnp.stack([both, beside, swap(low, Y)])
    late = swap(ordered(jnp.stack([high, both]), [sent]), Y)
    early = ordered(early, direct)
    add(early, (HIGH | LOW, Y, Y | LOW))
    add(swap(early[1:], CORE), (Y | CORE, Y | CORE | LOW))
    late = ordered(late, direct + mirrors[:1])
    add(late, (Y | HIGH, Y | HIGH | LOW))
    add(swap(late, CORE), (Y | CORE | HIGH, Y | CORE | HIGH | LOW))
    return direct[0], mirrors


def finish_kernel(factor, direct_ref, *refs):
    mirror_refs, (real_ref, imag_ref) = refs[:-2], refs[-2:]
    count = real_ref.shape[1]
    mirror = mirror_refs[-1][...].astype(F32)
    for ref in mirror_refs[:-1]:
        mirror += ref[...].astype(F32)
    total = factor * (direct_ref[...] + jnp.transpose(mirror))
    real_ref[...] = total[:, :count]
    imag_ref[...] = total[:, count:]


def finish(direct, mirrors, width):
    rows, double = direct.shape
    shape = jax.ShapeDtypeStruct((rows, double // 2), F32)
    return pl.pallas_call(
        functools.partial(finish_kernel, -1.0 / math.sqrt(width)),
        in_specs=[whole_vmem()] * (1 + len(mirrors)),
        out_specs=[whole_vmem(), whole_vmem()],
        out_shape=[shape, shape],
        compiler_params=params(),
        cost_estimate=cost(4 * rows * double, 10 * rows * double),
        name="finish",
    )(direct, *mirrors)


def shards(data_real, data_imag, counts, source_cols):
    rows, width = data_real.shape
    groups = width // rows
    count = source_cols.shape[0]
    cap = min(rows, count, -(-2 * count // groups // 8) * 8)
    col = source_cols.reshape(count, 1)
    row = source_cols.reshape(1, count)
    me = lax.axis_index(AXIS).reshape(1)

    def exchange(which):
        sent = own_source_rows(me, data_real, data_imag, source_cols, which, cap)
        return lax.all_to_all(sent, AXIS, split_axis=0, concat_axis=0)

    first = jnp.zeros((1,), jnp.int32)
    got = exchange(first)
    colpart = own_source_cols(data_real, data_imag, row, width // TILES)
    rowpart = select_rows(got, col, first, cap)

    owner = source_cols // rows
    most = jnp.max(jnp.sum(owner[:, None] == jnp.arange(groups)[None, :], axis=0, dtype=jnp.int32))

    def further(rowpart):
        def body(which, held):
            one = which.reshape(1)
            return held + select_rows(exchange(one), col, one, cap)

        return lax.fori_loop(1, (most + cap - 1) // cap, body, rowpart)

    rowpart = lax.cond(most > cap, further, lambda rowpart: rowpart, rowpart)
    panel, panel_t = own_panel(me, counts, rowpart, colpart, col, width)
    if rows % 128 == 0 and groups == 16:
        direct, mirrors = levels(me, counts, data_real, data_imag, panel, panel_t)
    else:
        full = lax.all_gather(panel, AXIS, axis=0, tiled=True)
        partial = mirror_term(me, counts, data_real, data_imag, panel_t)
        mirrors = [lax.psum_scatter(partial, AXIS, scatter_dimension=0, tiled=False)]
        direct = direct_term(me, counts, data_real, data_imag, full)
    return tuple(finish(direct, mirrors, width))


def solution(mesh):
    placed = (P(("freq", "row"), None), P(("freq", "row"), None), P(), P())
    return jax.shard_map(
        shards,
        mesh=mesh,
        in_specs=placed,
        out_specs=(P(("freq", "row"), None), P(("freq", "row"), None)),
        check_vma=False,
    )
```

```python
import functools
import math

import jax
import jax.numpy as jnp
from jax import lax
from jax.experimental import pallas as pl
from jax.experimental.pallas import tpu as pltpu
from jax.sharding import PartitionSpec as P

TILES = 8
AXIS = "row"
CORE, Y, LOW, HIGH = 1, 2, 4, 8
GROUP = 16
MIRROR_COST = 10000000000
DIRECT_COST = 2000000000
PIECE = 1024
F32 = jnp.float32
BF16 = jnp.bfloat16


def params(mib=16):
    return pltpu.CompilerParams(vmem_limit_bytes=mib * 1024 * 1024)


def whole_vmem():
    return pl.BlockSpec(memory_space=pltpu.VMEM)


def anywhere():
    return pl.BlockSpec(memory_space=pl.ANY)


def in_hbm(value):
    return pltpu.with_memory_space_constraint(value, pltpu.HBM)


def whole_smem():
    return pl.BlockSpec(memory_space=pltpu.SMEM)


def cost(flops, size):
    return pl.CostEstimate(flops=flops, bytes_accessed=size, transcendentals=0)


def dot(left, right):
    return jnp.dot(left, right, preferred_element_type=F32)


def ranks_of(col, rows):
    count = col.shape[0]
    owner = col // rows
    owner_row = jnp.transpose(jnp.broadcast_to(owner.astype(F32), (count, count))).astype(jnp.int32)
    before = lax.broadcasted_iota(jnp.int32, (count, count), 1) < lax.broadcasted_iota(
        jnp.int32, (count, count), 0
    )
    same = (owner_row == owner) & before
    return jnp.sum(same.astype(F32), axis=1, keepdims=True).astype(jnp.int32)


def rows_kernel(cap, round_ref, me_ref, col_ref, real_ref, imag_ref, out_ref, list_ref, near_ref, held_ref, sems):
    rows, width = real_ref.shape
    groups = out_ref.shape[0]
    count = col_ref.shape[0]
    base = me_ref[0] * rows
    skip = round_ref[0] * cap

    def copies(slot, local):
        group = pl.ds(pl.multiple_of(local // GROUP * GROUP, GROUP), GROUP)
        return [
            pltpu.make_async_copy(ref.at[group], near_ref.at[slot, part], sems.at[slot, part])
            for part, ref in enumerate((real_ref, imag_ref))
        ]

    def begin(s, found):
        local = col_ref[s] - base
        own = (local >= 0) & (local < rows)
        slot = found - skip

        @pl.when(own & (slot >= 0) & (slot < cap))
        def _():
            list_ref[slot] = local
            for copy in copies(slot, local):
                copy.start()

        return found + own.astype(jnp.int32)

    def pick(slot, _):
        local = list_ref[slot]
        chosen = lax.broadcasted_iota(jnp.int32, (GROUP, PIECE), 0) == local % GROUP
        for part, copy in enumerate(copies(slot, local)):
            copy.wait()
            for at in range(0, width, PIECE):
                group = near_ref[slot, part, :, at : at + PIECE].astype(F32)
                held_ref[pl.ds(part * cap + slot, 1), at : at + PIECE] = jnp.sum(
                    jnp.where(chosen, group, 0.0), axis=0, keepdims=True
                )
        return 0

    found = lax.fori_loop(0, count, begin, jnp.int32(0))
    held_ref[...] = jnp.zeros_like(held_ref)
    lax.fori_loop(0, jnp.clip(found - skip, 0, cap), pick, 0)
    for g in range(groups):
        out_ref[g] = held_ref[:, g * rows : (g + 1) * rows].astype(BF16)


def own_source_rows(me, data_real, data_imag, source_cols, which, cap):
    rows, width = data_real.shape
    return pl.pallas_call(
        functools.partial(rows_kernel, cap),
        in_specs=[whole_smem()] * 3 + [anywhere()] * 2,
        out_specs=whole_vmem(),
        out_shape=jax.ShapeDtypeStruct((width // rows, 2 * cap, rows), BF16),
        scratch_shapes=[
            pltpu.SMEM((cap,), jnp.int32),
            pltpu.VMEM((cap, 2, GROUP, width), BF16),
            pltpu.VMEM((2 * cap, width), F32),
            pltpu.SemaphoreType.DMA((cap, 2)),
        ],
        compiler_params=params(24),
        cost_estimate=cost(0, 2 * cap * width),
        name="own_source_rows",
    )(which, me, source_cols, data_real, data_imag)


def cols_kernel(real_ref, imag_ref, row_ref, out_ref, acc_ref):
    rows, step = real_ref.shape
    count = row_ref.shape[1]
    t = pl.program_id(0)

    @pl.when(t == 0)
    def _():
        acc_ref[...] = jnp.zeros_like(acc_ref)

    place = lax.broadcasted_iota(jnp.int32, (step, count), 0) + t * step
    pick = (place == row_ref[...]).astype(F32).astype(BF16)
    acc_ref[:, :count] += dot(real_ref[...], pick)
    acc_ref[:, count:] += dot(imag_ref[...], pick)

    @pl.when(t == pl.num_programs(0) - 1)
    def _():
        out_ref[...] = jnp.transpose(acc_ref[...]).astype(BF16)


def own_source_cols(data_real, data_imag, row, step):
    rows, width = data_real.shape
    count = row.shape[1]
    block = pl.BlockSpec((rows, step), lambda t: (0, t))
    return pl.pallas_call(
        cols_kernel,
        grid=(width // step,),
        in_specs=[block, block, whole_vmem()],
        out_specs=pl.BlockSpec((2 * count, rows), lambda t: (0, 0)),
        out_shape=jax.ShapeDtypeStruct((2 * count, rows), BF16),
        scratch_shapes=[pltpu.VMEM((rows, 2 * count), F32)],
        compiler_params=params(),
        cost_estimate=cost(4 * rows * width * count, 4 * rows * width),
        name="own_source_cols",
    )(data_real, data_imag, row)


def select_kernel(cap, round_ref, got_ref, col_ref, out_ref):
    out_ref[...] = pick_rows(cap, round_ref[0], got_ref, col_ref).astype(BF16)


def select_rows(got, col, which, cap):
    groups, _, rows = got.shape
    count = col.shape[0]
    return pl.pallas_call(
        functools.partial(select_kernel, cap),
        in_specs=[whole_smem(), whole_vmem(), whole_vmem()],
        out_specs=whole_vmem(),
        out_shape=jax.ShapeDtypeStruct((2 * count, rows), BF16),
        compiler_params=params(),
        cost_estimate=cost(8 * count * groups * cap * rows, 4 * groups * cap * rows),
        name="select_rows",
    )(which, got, col)


def pick_rows(cap, which, got_ref, col_ref):
    groups, _, rows = got_ref.shape
    count = col_ref.shape[0]
    col = col_ref[...]
    slot = ranks_of(col, rows) - which * cap
    inside = (slot >= 0) & (slot < cap)
    place = jnp.where(inside, (col // rows) * (2 * cap) + slot, -1)
    lanes = lax.broadcasted_iota(jnp.int32, (count, groups * 2 * cap), 1)
    pick = jnp.concatenate([lanes == place, lanes == jnp.where(inside, place + cap, -1)], axis=0)
    got = got_ref[...].reshape(groups * 2 * cap, rows)
    return dot(pick.astype(F32).astype(BF16), got)


def panel_kernel(width, me_ref, counts_ref, rowpart_ref, colpart_ref, col_ref, panel_ref, panel_t_ref):
    double, rows = colpart_ref.shape
    count = double // 2
    tile = width // TILES
    mine = me_ref[0] * rows // tile
    tiles = col_ref[...] // tile
    forward = jnp.zeros_like(tiles)
    backward = jnp.zeros_like(tiles)
    for t in range(TILES):
        forward = jnp.where(tiles == t, counts_ref[mine, t], forward)
        backward = jnp.where(tiles == t, counts_ref[t, mine], backward)
    forward = jnp.concatenate([forward, forward], axis=0).astype(F32)
    backward = jnp.concatenate([backward, backward], axis=0).astype(F32)
    own = colpart_ref[...].astype(F32)
    mirror = rowpart_ref[...].astype(F32)
    panel = (forward * own + backward * mirror) / jnp.maximum(forward + backward, 1.0)
    panel_t_ref[:, :rows] = panel.astype(BF16)
    panel_t_ref[:count, rows:] = (-panel[count:]).astype(BF16)
    panel_t_ref[count:, rows:] = panel[:count].astype(BF16)
    panel_ref[...] = jnp.transpose(panel).astype(BF16)


def own_panel(me, counts, rowpart, colpart, col, width):
    double, rows = colpart.shape
    return pl.pallas_call(
        functools.partial(panel_kernel, width),
        in_specs=[whole_smem()] * 2 + [whole_vmem()] * 3,
        out_specs=[whole_vmem()] * 2,
        out_shape=[
            jax.ShapeDtypeStruct((rows, double), BF16),
            jax.ShapeDtypeStruct((double, 2 * rows), BF16),
        ],
        compiler_params=params(),
        cost_estimate=cost(8 * rows * double, 8 * rows * double),
        name="own_panel",
    )(me, counts, rowpart, colpart, col)


def weight(counts_ref, mine, other, shape):
    forward = jnp.full(shape, counts_ref[mine, other], jnp.int32).astype(F32)
    backward = jnp.full(shape, counts_ref[other, mine], jnp.int32).astype(F32)
    return forward / jnp.maximum(forward + backward, 1.0)


def mirror_block(real, imag, panel_t):
    rows = real.shape[0]
    return dot(panel_t[:, :rows], real) + dot(panel_t[:, rows:], imag)


def direct_block(real, imag, panel):
    count = panel.shape[1] // 2
    turned = jnp.concatenate([-panel[:, count:], panel[:, :count]], axis=1)
    return dot(real, panel) + dot(imag, turned)


def mirror_kernel(width, me_ref, counts_ref, real_ref, imag_ref, panel_t_ref, out_ref):
    rows, tile = real_ref.shape
    mine = me_ref[0] * rows // tile
    found = mirror_block(real_ref[...], imag_ref[...], panel_t_ref[...])
    found = found * weight(counts_ref, mine, pl.program_id(0), (1, tile))
    for g in range(out_ref.shape[0]):
        out_ref[g] = found[:, g * rows : (g + 1) * rows]


def mirror_term(me, counts, data_real, data_imag, panel_t):
    rows, width = data_real.shape
    double = panel_t.shape[0]
    tile = width // TILES
    block = pl.BlockSpec((rows, tile), lambda t: (0, t))
    return pl.pallas_call(
        functools.partial(mirror_kernel, width),
        grid=(TILES,),
        in_specs=[whole_smem()] * 2 + [block, block, whole_vmem()],
        out_specs=pl.BlockSpec((tile // rows, double, rows), lambda t: (t, 0, 0)),
        out_shape=jax.ShapeDtypeStruct((width // rows, double, rows), F32),
        compiler_params=params(32),
        cost_estimate=cost(4 * rows * width * double, 4 * rows * width + 2 * double * width),
        name="mirror_term",
    )(me, counts, data_real, data_imag, panel_t)


def direct_kernel(width, me_ref, counts_ref, real_ref, imag_ref, panel_ref, out_ref):
    rows, tile = real_ref.shape
    mine = me_ref[0] * rows // tile
    t = pl.program_id(0)

    @pl.when(t == 0)
    def _():
        out_ref[...] = jnp.zeros_like(out_ref)

    found = direct_block(real_ref[...], imag_ref[...], panel_ref[...])
    out_ref[...] += found * weight(counts_ref, mine, t, (1, out_ref.shape[1]))


def direct_term(me, counts, data_real, data_imag, panel):
    rows, width = data_real.shape
    double = panel.shape[1]
    tile = width // TILES
    block = pl.BlockSpec((rows, tile), lambda t: (0, t))
    return pl.pallas_call(
        functools.partial(direct_kernel, width),
        grid=(TILES,),
        in_specs=[whole_smem()] * 2 + [block, block, pl.BlockSpec((tile, double), lambda t: (t, 0))],
        out_specs=pl.BlockSpec((rows, double), lambda t: (0, 0)),
        out_shape=jax.ShapeDtypeStruct((rows, double), F32),
        compiler_params=params(),
        cost_estimate=cost(4 * rows * width * double, 4 * rows * width + 2 * double * width),
        name="direct_term",
    )(me, counts, data_real, data_imag, panel)


def swap(value, mask):
    return lax.ppermute(value, AXIS, [(i, i ^ mask) for i in range(lax.axis_size(AXIS))])


def picked(masks, i):
    mask = masks[0]
    for at in range(1, len(masks)):
        mask = jnp.where(i == at, masks[at], mask)
    return mask


def mirror_part_kernel(width, masks, me_ref, counts_ref, real_ref, imag_ref, panel_t_ref, *refs):
    other_ref, near_ref, far_ref, held_ref, sems = refs[-5:]
    rows = real_ref.shape[0]
    tile = width // TILES
    me = me_ref[0]
    dy, i = pl.program_id(0), pl.program_id(1)
    some = len(masks)
    mine = me * rows // tile
    panel_t = panel_t_ref[...]

    def copies(at, mask):
        columns = pl.ds(pl.multiple_of((me ^ mask) // 2 * (2 * rows), 2 * rows), 2 * rows)
        return [
            pltpu.make_async_copy(
                ref.at[:, columns], held_ref.at[at, pl.ds(part * rows, rows)], sems.at[at, part]
            )
            for part, ref in enumerate((real_ref, imag_ref))
        ]

    @pl.when((dy == 0) & (i == 0))
    def _():
        for at in range(2 * some):
            for copy in copies(at, masks[at % some] ^ (2 * (at // some))):
                copy.start()

    at = dy * some + i
    mask = picked(masks, i) ^ (2 * dy)
    for copy in copies(at, mask):
        copy.wait()

    def term(turn):
        block = me ^ mask ^ turn
        scale = weight(counts_ref, mine, block * rows // tile, (1, rows))
        columns = pl.ds(pl.multiple_of(block % 2 * rows, rows), rows)
        return dot(panel_t, held_ref[at, :, columns]) * scale

    other_ref[0] = term(1).astype(BF16)

    @pl.when(dy == 0)
    def _():
        near_ref[0] = term(0)

    @pl.when(dy == 1)
    def _():
        far_ref[0] = term(0)


def mirror_part(me, counts, data_real, data_imag, panel_t, masks, after):
    rows, width = data_real.shape
    double = panel_t.shape[0]
    some = len(masks)
    shape = (1, double, rows)
    spec = pltpu.PrefetchScalarGridSpec(
        num_scalar_prefetch=1,
        grid=(2, some),
        in_specs=[whole_smem(), anywhere(), anywhere(), whole_vmem()] + [anywhere()] * len(after),
        out_specs=[
            pl.BlockSpec(shape, lambda dy, i, me: (dy * some + i, 0, 0)),
            pl.BlockSpec(shape, lambda dy, i, me: (jnp.where(dy == 0, i, some - 1), 0, 0)),
            pl.BlockSpec(shape, lambda dy, i, me: (jnp.where(dy == 0, 0, i), 0, 0)),
        ],
        scratch_shapes=[
            pltpu.VMEM((2 * some, 2 * rows, 2 * rows), BF16),
            pltpu.SemaphoreType.DMA((2 * some, 2)),
        ],
    )
    return pl.pallas_call(
        functools.partial(mirror_part_kernel, width, masks),
        grid_spec=spec,
        out_shape=[
            jax.ShapeDtypeStruct((2 * some, double, rows), BF16),
            jax.ShapeDtypeStruct((some, double, rows), F32),
            jax.ShapeDtypeStruct((some, double, rows), F32),
        ],
        compiler_params=params(24),
        cost_estimate=cost(MIRROR_COST, 0),
        name="mirror_part",
    )(me, counts, data_real, data_imag, panel_t, *after)


def ordered(value, after):
    return lax.optimization_barrier((value, after))[0]


def direct_part_kernel(
    width, masks, first, me_ref, counts_ref, real_ref, imag_ref, panel_ref, *refs
):
    out_ref = refs[-1]
    rows = real_ref.shape[0]
    tile = width // TILES
    k = pl.program_id(0)
    mine = me_ref[0] * rows // tile
    block = me_ref[0] ^ picked(masks, k)
    scale = weight(counts_ref, mine, block * rows // tile, (1, out_ref.shape[1]))
    found = direct_block(real_ref[...], imag_ref[...], panel_ref[0]) * scale

    @pl.when(k == 0)
    def _():
        out_ref[...] = found if first else found + refs[0][...]

    @pl.when(k > 0)
    def _():
        out_ref[...] += found


def direct_part(me, counts, data_real, data_imag, panels, before, masks):
    rows, width = data_real.shape
    double = panels.shape[2]
    block = pl.BlockSpec((rows, rows), lambda k, me: (0, me[0] ^ picked(masks, k)))
    spec = pltpu.PrefetchScalarGridSpec(
        num_scalar_prefetch=1,
        grid=(len(masks),),
        in_specs=[whole_smem(), block, block, pl.BlockSpec((1, rows, double), lambda k, me: (k, 0, 0))]
        + [whole_vmem()] * len(before),
        out_specs=pl.BlockSpec((rows, double), lambda k, me: (0, 0)),
    )
    return pl.pallas_call(
        functools.partial(direct_part_kernel, width, masks, not before),
        grid_spec=spec,
        out_shape=jax.ShapeDtypeStruct((rows, double), F32),
        compiler_params=params(),
        cost_estimate=cost(DIRECT_COST, 0),
        name="direct_part",
    )(me, counts, data_real, data_imag, panels, *before)


def levels(me, counts, data_real, data_imag, panel, panel_t):
    data = (in_hbm(data_real), in_hbm(data_imag))
    high, low, beside = swap(panel, HIGH), swap(panel, LOW), swap(panel, Y)

    def to_y(other, own):
        got = swap(other, CORE)
        some = own.shape[0]
        return (own + got[some:].astype(F32)).astype(BF16), got[:some]

    def over_y(sent, own, got):
        return own + got.astype(F32) + swap(sent, Y).astype(F32)

    other, own, own_far = mirror_part(me, counts, *data, panel_t, (HIGH, HIGH | LOW), [])
    sent, got = to_y(other, own_far)
    other_here, own_here, own_here_far = mirror_part(me, counts, *data, panel_t, (0, LOW), [sent])
    total = over_y(sent, own, got)
    to_low = total[1].astype(BF16)
    total = total[0] + swap(to_low, LOW).astype(F32)
    mirrors = [swap(total.astype(BF16), HIGH)]

    low, high, beside = ordered([low, high, beside], [sent, own_here])
    direct = []

    def add(panels, masks):
        direct[:] = [direct_part(me, counts, *data, panels, direct, masks)]

    add(ordered(panel[None], high), (0,))
    sent, got = to_y(ordered(other_here, high), ordered(own_here_far, high))
    total = over_y(sent, own_here, got)
    mirrors += [total[0], swap(total[1].astype(BF16), LOW)]

    low_beside = swap(low, Y)
    both = ordered(swap(high, LOW), [sent, to_low])
    column = jnp.stack([panel, low, high, both])
    late = swap(ordered(jnp.stack([high, both]), [sent]), Y)
    add(column[1:], (LOW, HIGH, HIGH | LOW))
    add(swap(column, CORE), (CORE, CORE | LOW, CORE | HIGH, CORE | HIGH | LOW))
    early = jnp.stack([beside, ordered(low_beside, direct)])
    add(early, (Y, Y | LOW))
    add(swap(early, CORE), (Y | CORE, Y | CORE | LOW))
    late = ordered(late, direct + mirrors)
    add(late, (Y | HIGH, Y | HIGH | LOW))
    add(swap(late, CORE), (Y | CORE | HIGH, Y | CORE | HIGH | LOW))
    return direct[0], mirrors


def finish_kernel(factor, direct_ref, *refs):
    mirror_refs, (real_ref, imag_ref) = refs[:-2], refs[-2:]
    count = real_ref.shape[1]
    mirror = mirror_refs[-1][...].astype(F32)
    for ref in mirror_refs[:-1]:
        mirror += ref[...].astype(F32)
    total = factor * (direct_ref[...] + jnp.transpose(mirror))
    real_ref[...] = total[:, :count]
    imag_ref[...] = total[:, count:]


def finish(direct, mirrors, width):
    rows, double = direct.shape
    shape = jax.ShapeDtypeStruct((rows, double // 2), F32)
    return pl.pallas_call(
        functools.partial(finish_kernel, -1.0 / math.sqrt(width)),
        in_specs=[whole_vmem()] * (1 + len(mirrors)),
        out_specs=[whole_vmem(), whole_vmem()],
        out_shape=[shape, shape],
        compiler_params=params(),
        cost_estimate=cost(4 * rows * double, 10 * rows * double),
        name="finish",
    )(direct, *mirrors)


def shards(data_real, data_imag, counts, source_cols):
    rows, width = data_real.shape
    groups = width // rows
    count = source_cols.shape[0]
    cap = min(rows, count, -(-2 * count // groups // 8) * 8)
    col = source_cols.reshape(count, 1)
    row = source_cols.reshape(1, count)
    me = lax.axis_index(AXIS).reshape(1)

    def exchange(which):
        sent = own_source_rows(me, data_real, data_imag, source_cols, which, cap)
        return lax.all_to_all(sent, AXIS, split_axis=0, concat_axis=0)

    first = jnp.zeros((1,), jnp.int32)
    got = exchange(first)
    colpart = own_source_cols(data_real, data_imag, row, width // TILES)
    rowpart = select_rows(got, col, first, cap)

    owner = source_cols // rows
    most = jnp.max(jnp.sum(owner[:, None] == jnp.arange(groups)[None, :], axis=0, dtype=jnp.int32))

    def further(rowpart):
        def body(which, held):
            one = which.reshape(1)
            return held + select_rows(exchange(one), col, one, cap)

        return lax.fori_loop(1, (most + cap - 1) // cap, body, rowpart)

    rowpart = lax.cond(most > cap, further, lambda rowpart: rowpart, rowpart)
    panel, panel_t = own_panel(me, counts, rowpart, colpart, col, width)
    if rows % 128 == 0 and groups == 16:
        direct, mirrors = levels(me, counts, data_real, data_imag, panel, panel_t)
    else:
        full = lax.all_gather(panel, AXIS, axis=0, tiled=True)
        partial = mirror_term(me, counts, data_real, data_imag, panel_t)
        mirrors = [lax.psum_scatter(partial, AXIS, scatter_dimension=0, tiled=False)]
        direct = direct_term(me, counts, data_real, data_imag, full)
    return tuple(finish(direct, mirrors, width))


def solution(mesh):
    placed = (P(("freq", "row"), None), P(("freq", "row"), None), P(), P())
    return jax.shard_map(
        shards,
        mesh=mesh,
        in_specs=placed,
        out_specs=(P(("freq", "row"), None), P(("freq", "row"), None)),
        check_vma=False,
    )
```

```python
import functools
import math

import jax
import jax.numpy as jnp
from jax import lax
from jax.experimental import pallas as pl
from jax.experimental.pallas import tpu as pltpu
from jax.sharding import PartitionSpec as P

TILES = 8
AXIS = "row"
CORE, Y, LOW, HIGH = 1, 2, 4, 8
GROUP = 16
MIRROR_COST = 10000000000
DIRECT_COST = 2000000000
PIECE = 1024
F32 = jnp.float32
BF16 = jnp.bfloat16


def params(mib=16):
    return pltpu.CompilerParams(vmem_limit_bytes=mib * 1024 * 1024)


def whole_vmem():
    return pl.BlockSpec(memory_space=pltpu.VMEM)


def anywhere():
    return pl.BlockSpec(memory_space=pl.ANY)


def in_hbm(value):
    return pltpu.with_memory_space_constraint(value, pltpu.HBM)


def whole_smem():
    return pl.BlockSpec(memory_space=pltpu.SMEM)


def cost(flops, size):
    return pl.CostEstimate(flops=flops, bytes_accessed=size, transcendentals=0)


def dot(left, right):
    return jnp.dot(left, right, preferred_element_type=F32)


def ranks_of(col, rows):
    count = col.shape[0]
    owner = col // rows
    owner_row = jnp.transpose(jnp.broadcast_to(owner.astype(F32), (count, count))).astype(jnp.int32)
    before = lax.broadcasted_iota(jnp.int32, (count, count), 1) < lax.broadcasted_iota(
        jnp.int32, (count, count), 0
    )
    same = (owner_row == owner) & before
    return jnp.sum(same.astype(F32), axis=1, keepdims=True).astype(jnp.int32)


def rows_kernel(cap, round_ref, me_ref, col_ref, real_ref, imag_ref, out_ref, list_ref, near_ref, held_ref, sems):
    rows, width = real_ref.shape
    groups = out_ref.shape[0]
    count = col_ref.shape[0]
    base = me_ref[0] * rows
    skip = round_ref[0] * cap

    def copies(slot, local):
        group = pl.ds(pl.multiple_of(local // GROUP * GROUP, GROUP), GROUP)
        return [
            pltpu.make_async_copy(ref.at[group], near_ref.at[slot, part], sems.at[slot, part])
            for part, ref in enumerate((real_ref, imag_ref))
        ]

    def begin(s, found):
        local = col_ref[s] - base
        own = (local >= 0) & (local < rows)
        slot = found - skip

        @pl.when(own & (slot >= 0) & (slot < cap))
        def _():
            list_ref[slot] = local
            for copy in copies(slot, local):
                copy.start()

        return found + own.astype(jnp.int32)

    def pick(slot, _):
        local = list_ref[slot]
        chosen = lax.broadcasted_iota(jnp.int32, (GROUP, PIECE), 0) == local % GROUP
        for part, copy in enumerate(copies(slot, local)):
            copy.wait()
            for at in range(0, width, PIECE):
                group = near_ref[slot, part, :, at : at + PIECE].astype(F32)
                held_ref[pl.ds(part * cap + slot, 1), at : at + PIECE] = jnp.sum(
                    jnp.where(chosen, group, 0.0), axis=0, keepdims=True
                )
        return 0

    found = lax.fori_loop(0, count, begin, jnp.int32(0))
    held_ref[...] = jnp.zeros_like(held_ref)
    lax.fori_loop(0, jnp.clip(found - skip, 0, cap), pick, 0)
    for g in range(groups):
        out_ref[g] = held_ref[:, g * rows : (g + 1) * rows].astype(BF16)


def own_source_rows(me, data_real, data_imag, source_cols, which, cap):
    rows, width = data_real.shape
    return pl.pallas_call(
        functools.partial(rows_kernel, cap),
        in_specs=[whole_smem()] * 3 + [anywhere()] * 2,
        out_specs=whole_vmem(),
        out_shape=jax.ShapeDtypeStruct((width // rows, 2 * cap, rows), BF16),
        scratch_shapes=[
            pltpu.SMEM((cap,), jnp.int32),
            pltpu.VMEM((cap, 2, GROUP, width), BF16),
            pltpu.VMEM((2 * cap, width), F32),
            pltpu.SemaphoreType.DMA((cap, 2)),
        ],
        compiler_params=params(24),
        cost_estimate=cost(0, 2 * cap * width),
        name="own_source_rows",
    )(which, me, source_cols, data_real, data_imag)


def cols_kernel(real_ref, imag_ref, row_ref, out_ref, acc_ref):
    rows, step = real_ref.shape
    count = row_ref.shape[1]
    t = pl.program_id(0)

    @pl.when(t == 0)
    def _():
        acc_ref[...] = jnp.zeros_like(acc_ref)

    place = lax.broadcasted_iota(jnp.int32, (step, count), 0) + t * step
    pick = (place == row_ref[...]).astype(F32).astype(BF16)
    acc_ref[:, :count] += dot(real_ref[...], pick)
    acc_ref[:, count:] += dot(imag_ref[...], pick)

    @pl.when(t == pl.num_programs(0) - 1)
    def _():
        out_ref[...] = jnp.transpose(acc_ref[...]).astype(BF16)


def own_source_cols(data_real, data_imag, row, step):
    rows, width = data_real.shape
    count = row.shape[1]
    block = pl.BlockSpec((rows, step), lambda t: (0, t))
    return pl.pallas_call(
        cols_kernel,
        grid=(width // step,),
        in_specs=[block, block, whole_vmem()],
        out_specs=pl.BlockSpec((2 * count, rows), lambda t: (0, 0)),
        out_shape=jax.ShapeDtypeStruct((2 * count, rows), BF16),
        scratch_shapes=[pltpu.VMEM((rows, 2 * count), F32)],
        compiler_params=params(),
        cost_estimate=cost(4 * rows * width * count, 4 * rows * width),
        name="own_source_cols",
    )(data_real, data_imag, row)


def select_kernel(cap, round_ref, got_ref, col_ref, out_ref):
    out_ref[...] = pick_rows(cap, round_ref[0], got_ref, col_ref).astype(BF16)


def select_rows(got, col, which, cap):
    groups, _, rows = got.shape
    count = col.shape[0]
    return pl.pallas_call(
        functools.partial(select_kernel, cap),
        in_specs=[whole_smem(), whole_vmem(), whole_vmem()],
        out_specs=whole_vmem(),
        out_shape=jax.ShapeDtypeStruct((2 * count, rows), BF16),
        compiler_params=params(),
        cost_estimate=cost(8 * count * groups * cap * rows, 4 * groups * cap * rows),
        name="select_rows",
    )(which, got, col)


def pick_rows(cap, which, got_ref, col_ref):
    groups, _, rows = got_ref.shape
    count = col_ref.shape[0]
    col = col_ref[...]
    slot = ranks_of(col, rows) - which * cap
    inside = (slot >= 0) & (slot < cap)
    place = jnp.where(inside, (col // rows) * (2 * cap) + slot, -1)
    lanes = lax.broadcasted_iota(jnp.int32, (count, groups * 2 * cap), 1)
    pick = jnp.concatenate([lanes == place, lanes == jnp.where(inside, place + cap, -1)], axis=0)
    got = got_ref[...].reshape(groups * 2 * cap, rows)
    return dot(pick.astype(F32).astype(BF16), got)


def panel_kernel(width, me_ref, counts_ref, rowpart_ref, colpart_ref, col_ref, panel_ref, panel_t_ref):
    double, rows = colpart_ref.shape
    count = double // 2
    tile = width // TILES
    mine = me_ref[0] * rows // tile
    tiles = col_ref[...] // tile
    forward = jnp.zeros_like(tiles)
    backward = jnp.zeros_like(tiles)
    for t in range(TILES):
        forward = jnp.where(tiles == t, counts_ref[mine, t], forward)
        backward = jnp.where(tiles == t, counts_ref[t, mine], backward)
    forward = jnp.concatenate([forward, forward], axis=0).astype(F32)
    backward = jnp.concatenate([backward, backward], axis=0).astype(F32)
    own = colpart_ref[...].astype(F32)
    mirror = rowpart_ref[...].astype(F32)
    panel = (forward * own + backward * mirror) / jnp.maximum(forward + backward, 1.0)
    panel_t_ref[:, :rows] = panel.astype(BF16)
    panel_t_ref[:count, rows:] = (-panel[count:]).astype(BF16)
    panel_t_ref[count:, rows:] = panel[:count].astype(BF16)
    panel_ref[...] = jnp.transpose(panel).astype(BF16)


def own_panel(me, counts, rowpart, colpart, col, width):
    double, rows = colpart.shape
    return pl.pallas_call(
        functools.partial(panel_kernel, width),
        in_specs=[whole_smem()] * 2 + [whole_vmem()] * 3,
        out_specs=[whole_vmem()] * 2,
        out_shape=[
            jax.ShapeDtypeStruct((rows, double), BF16),
            jax.ShapeDtypeStruct((double, 2 * rows), BF16),
        ],
        compiler_params=params(),
        cost_estimate=cost(8 * rows * double, 8 * rows * double),
        name="own_panel",
    )(me, counts, rowpart, colpart, col)


def weight(counts_ref, mine, other, shape):
    forward = jnp.full(shape, counts_ref[mine, other], jnp.int32).astype(F32)
    backward = jnp.full(shape, counts_ref[other, mine], jnp.int32).astype(F32)
    return forward / jnp.maximum(forward + backward, 1.0)


def mirror_block(real, imag, panel_t):
    rows = real.shape[0]
    return dot(panel_t[:, :rows], real) + dot(panel_t[:, rows:], imag)


def direct_block(real, imag, panel):
    count = panel.shape[1] // 2
    turned = jnp.concatenate([-panel[:, count:], panel[:, :count]], axis=1)
    return dot(real, panel) + dot(imag, turned)


def mirror_kernel(width, me_ref, counts_ref, real_ref, imag_ref, panel_t_ref, out_ref):
    rows, tile = real_ref.shape
    mine = me_ref[0] * rows // tile
    found = mirror_block(real_ref[...], imag_ref[...], panel_t_ref[...])
    found = found * weight(counts_ref, mine, pl.program_id(0), (1, tile))
    for g in range(out_ref.shape[0]):
        out_ref[g] = found[:, g * rows : (g + 1) * rows]


def mirror_term(me, counts, data_real, data_imag, panel_t):
    rows, width = data_real.shape
    double = panel_t.shape[0]
    tile = width // TILES
    block = pl.BlockSpec((rows, tile), lambda t: (0, t))
    return pl.pallas_call(
        functools.partial(mirror_kernel, width),
        grid=(TILES,),
        in_specs=[whole_smem()] * 2 + [block, block, whole_vmem()],
        out_specs=pl.BlockSpec((tile // rows, double, rows), lambda t: (t, 0, 0)),
        out_shape=jax.ShapeDtypeStruct((width // rows, double, rows), F32),
        compiler_params=params(32),
        cost_estimate=cost(4 * rows * width * double, 4 * rows * width + 2 * double * width),
        name="mirror_term",
    )(me, counts, data_real, data_imag, panel_t)


def direct_kernel(width, me_ref, counts_ref, real_ref, imag_ref, panel_ref, out_ref):
    rows, tile = real_ref.shape
    mine = me_ref[0] * rows // tile
    t = pl.program_id(0)

    @pl.when(t == 0)
    def _():
        out_ref[...] = jnp.zeros_like(out_ref)

    found = direct_block(real_ref[...], imag_ref[...], panel_ref[...])
    out_ref[...] += found * weight(counts_ref, mine, t, (1, out_ref.shape[1]))


def direct_term(me, counts, data_real, data_imag, panel):
    rows, width = data_real.shape
    double = panel.shape[1]
    tile = width // TILES
    block = pl.BlockSpec((rows, tile), lambda t: (0, t))
    return pl.pallas_call(
        functools.partial(direct_kernel, width),
        grid=(TILES,),
        in_specs=[whole_smem()] * 2 + [block, block, pl.BlockSpec((tile, double), lambda t: (t, 0))],
        out_specs=pl.BlockSpec((rows, double), lambda t: (0, 0)),
        out_shape=jax.ShapeDtypeStruct((rows, double), F32),
        compiler_params=params(),
        cost_estimate=cost(4 * rows * width * double, 4 * rows * width + 2 * double * width),
        name="direct_term",
    )(me, counts, data_real, data_imag, panel)


def swap(value, mask):
    return lax.ppermute(value, AXIS, [(i, i ^ mask) for i in range(lax.axis_size(AXIS))])


def picked(masks, i):
    mask = masks[0]
    for at in range(1, len(masks)):
        mask = jnp.where(i == at, masks[at], mask)
    return mask


def mirror_part_kernel(width, masks, me_ref, counts_ref, real_ref, imag_ref, panel_t_ref, *refs):
    other_ref, near_ref, far_ref, held_ref, sems = refs[-5:]
    rows = real_ref.shape[0]
    tile = width // TILES
    me = me_ref[0]
    dy, i = pl.program_id(0), pl.program_id(1)
    some = len(masks)
    mine = me * rows // tile
    panel_t = panel_t_ref[...]

    def copies(at, mask):
        columns = pl.ds(pl.multiple_of((me ^ mask) // 2 * (2 * rows), 2 * rows), 2 * rows)
        return [
            pltpu.make_async_copy(
                ref.at[:, columns], held_ref.at[at, pl.ds(part * rows, rows)], sems.at[at, part]
            )
            for part, ref in enumerate((real_ref, imag_ref))
        ]

    @pl.when((dy == 0) & (i == 0))
    def _():
        for at in range(2 * some):
            for copy in copies(at, masks[at % some] ^ (2 * (at // some))):
                copy.start()

    at = dy * some + i
    mask = picked(masks, i) ^ (2 * dy)
    for copy in copies(at, mask):
        copy.wait()

    def term(turn):
        block = me ^ mask ^ turn
        scale = weight(counts_ref, mine, block * rows // tile, (1, rows))
        columns = pl.ds(pl.multiple_of(block % 2 * rows, rows), rows)
        return dot(panel_t, held_ref[at, :, columns]) * scale

    other_ref[0] = term(1).astype(BF16)

    @pl.when(dy == 0)
    def _():
        near_ref[0] = term(0)

    @pl.when(dy == 1)
    def _():
        far_ref[0] = term(0)


def mirror_part(me, counts, data_real, data_imag, panel_t, masks, after):
    rows, width = data_real.shape
    double = panel_t.shape[0]
    some = len(masks)
    shape = (1, double, rows)
    spec = pltpu.PrefetchScalarGridSpec(
        num_scalar_prefetch=1,
        grid=(2, some),
        in_specs=[whole_smem(), anywhere(), anywhere(), whole_vmem()] + [anywhere()] * len(after),
        out_specs=[
            pl.BlockSpec(shape, lambda dy, i, me: (dy * some + i, 0, 0)),
            pl.BlockSpec(shape, lambda dy, i, me: (jnp.where(dy == 0, i, some - 1), 0, 0)),
            pl.BlockSpec(shape, lambda dy, i, me: (jnp.where(dy == 0, 0, i), 0, 0)),
        ],
        scratch_shapes=[
            pltpu.VMEM((2 * some, 2 * rows, 2 * rows), BF16),
            pltpu.SemaphoreType.DMA((2 * some, 2)),
        ],
    )
    return pl.pallas_call(
        functools.partial(mirror_part_kernel, width, masks),
        grid_spec=spec,
        out_shape=[
            jax.ShapeDtypeStruct((2 * some, double, rows), BF16),
            jax.ShapeDtypeStruct((some, double, rows), F32),
            jax.ShapeDtypeStruct((some, double, rows), F32),
        ],
        compiler_params=params(24),
        cost_estimate=cost(MIRROR_COST, 0),
        name="mirror_part",
    )(me, counts, data_real, data_imag, panel_t, *after)


def ordered(value, after):
    return lax.optimization_barrier((value, after))[0]


def direct_part_kernel(
    width, masks, first, me_ref, counts_ref, real_ref, imag_ref, panel_ref, *refs
):
    out_ref = refs[-1]
    rows = real_ref.shape[0]
    tile = width // TILES
    k = pl.program_id(0)
    mine = me_ref[0] * rows // tile
    block = me_ref[0] ^ picked(masks, k)
    scale = weight(counts_ref, mine, block * rows // tile, (1, out_ref.shape[1]))
    found = direct_block(real_ref[...], imag_ref[...], panel_ref[0]) * scale

    @pl.when(k == 0)
    def _():
        out_ref[...] = found if first else found + refs[0][...]

    @pl.when(k > 0)
    def _():
        out_ref[...] += found


def direct_part(me, counts, data_real, data_imag, panels, before, masks):
    rows, width = data_real.shape
    double = panels.shape[2]
    block = pl.BlockSpec((rows, rows), lambda k, me: (0, me[0] ^ picked(masks, k)))
    spec = pltpu.PrefetchScalarGridSpec(
        num_scalar_prefetch=1,
        grid=(len(masks),),
        in_specs=[whole_smem(), block, block, pl.BlockSpec((1, rows, double), lambda k, me: (k, 0, 0))]
        + [whole_vmem()] * len(before),
        out_specs=pl.BlockSpec((rows, double), lambda k, me: (0, 0)),
    )
    return pl.pallas_call(
        functools.partial(direct_part_kernel, width, masks, not before),
        grid_spec=spec,
        out_shape=jax.ShapeDtypeStruct((rows, double), F32),
        compiler_params=params(),
        cost_estimate=cost(DIRECT_COST, 0),
        name="direct_part",
    )(me, counts, data_real, data_imag, panels, *before)


def levels(me, counts, data_real, data_imag, panel, panel_t):
    data = (in_hbm(data_real), in_hbm(data_imag))
    high, low, beside = swap(panel, HIGH), swap(panel, LOW), swap(panel, Y)

    def to_y(other, own):
        got = swap(other, CORE)
        some = own.shape[0]
        return (own + got[some:].astype(F32)).astype(BF16), got[:some]

    def over_y(sent, own, got):
        return own + got.astype(F32) + swap(sent, Y).astype(F32)

    other, own, own_far = mirror_part(me, counts, *data, panel_t, (HIGH, HIGH | LOW), [])
    sent, got = to_y(other, own_far)
    other_here, own_here, own_here_far = mirror_part(me, counts, *data, panel_t, (0, LOW), [sent])
    total = over_y(sent, own, got)
    to_low = total[1].astype(BF16)
    total = total[0] + swap(to_low, LOW).astype(F32)
    mirrors = [swap(total.astype(BF16), HIGH)]

    low, high, beside = ordered([low, high, beside], [sent, own_here])
    direct = []

    def add(panels, masks):
        direct[:] = [direct_part(me, counts, *data, panels, direct, masks)]

    add(ordered(panel[None], high), (0,))
    sent, got = to_y(ordered(other_here, high), ordered(own_here_far, high))
    total = over_y(sent, own_here, got)
    here_to_low = total[1].astype(BF16)
    mirrors += [total[0], swap(here_to_low, LOW)]

    low_beside = swap(low, Y)
    both = ordered(swap(high, LOW), [sent, to_low])
    column = jnp.stack([panel, low, high, both])
    late = swap(ordered(jnp.stack([high, both]), [sent]), Y)
    add(column[1:], (LOW, HIGH, HIGH | LOW))
    early = jnp.stack([beside, ordered(low_beside, direct)])
    add(early, (Y, Y | LOW))
    add(swap(early, CORE), (Y | CORE, Y | CORE | LOW))
    turned = ordered(swap(column, CORE), direct + [here_to_low])
    add(turned, (CORE, CORE | LOW, CORE | HIGH, CORE | HIGH | LOW))
    late = ordered(late, direct + mirrors)
    add(late, (Y | HIGH, Y | HIGH | LOW))
    add(swap(late, CORE), (Y | CORE | HIGH, Y | CORE | HIGH | LOW))
    return direct[0], mirrors


def finish_kernel(factor, direct_ref, *refs):
    mirror_refs, (real_ref, imag_ref) = refs[:-2], refs[-2:]
    count = real_ref.shape[1]
    mirror = mirror_refs[-1][...].astype(F32)
    for ref in mirror_refs[:-1]:
        mirror += ref[...].astype(F32)
    total = factor * (direct_ref[...] + jnp.transpose(mirror))
    real_ref[...] = total[:, :count]
    imag_ref[...] = total[:, count:]


def finish(direct, mirrors, width):
    rows, double = direct.shape
    shape = jax.ShapeDtypeStruct((rows, double // 2), F32)
    return pl.pallas_call(
        functools.partial(finish_kernel, -1.0 / math.sqrt(width)),
        in_specs=[whole_vmem()] * (1 + len(mirrors)),
        out_specs=[whole_vmem(), whole_vmem()],
        out_shape=[shape, shape],
        compiler_params=params(),
        cost_estimate=cost(4 * rows * double, 10 * rows * double),
        name="finish",
    )(direct, *mirrors)


def shards(data_real, data_imag, counts, source_cols):
    rows, width = data_real.shape
    groups = width // rows
    count = source_cols.shape[0]
    cap = min(rows, count, -(-2 * count // groups // 8) * 8)
    col = source_cols.reshape(count, 1)
    row = source_cols.reshape(1, count)
    me = lax.axis_index(AXIS).reshape(1)

    def exchange(which):
        sent = own_source_rows(me, data_real, data_imag, source_cols, which, cap)
        return lax.all_to_all(sent, AXIS, split_axis=0, concat_axis=0)

    first = jnp.zeros((1,), jnp.int32)
    got = exchange(first)
    colpart = own_source_cols(data_real, data_imag, row, width // TILES)
    rowpart = select_rows(got, col, first, cap)

    owner = source_cols // rows
    most = jnp.max(jnp.sum(owner[:, None] == jnp.arange(groups)[None, :], axis=0, dtype=jnp.int32))

    def further(rowpart):
        def body(which, held):
            one = which.reshape(1)
            return held + select_rows(exchange(one), col, one, cap)

        return lax.fori_loop(1, (most + cap - 1) // cap, body, rowpart)

    rowpart = lax.cond(most > cap, further, lambda rowpart: rowpart, rowpart)
    panel, panel_t = own_panel(me, counts, rowpart, colpart, col, width)
    if rows % 128 == 0 and groups == 16:
        direct, mirrors = levels(me, counts, data_real, data_imag, panel, panel_t)
    else:
        full = lax.all_gather(panel, AXIS, axis=0, tiled=True)
        partial = mirror_term(me, counts, data_real, data_imag, panel_t)
        mirrors = [lax.psum_scatter(partial, AXIS, scatter_dimension=0, tiled=False)]
        direct = direct_term(me, counts, data_real, data_imag, full)
    return tuple(finish(direct, mirrors, width))


def solution(mesh):
    placed = (P(("freq", "row"), None), P(("freq", "row"), None), P(), P())
    return jax.shard_map(
        shards,
        mesh=mesh,
        in_specs=placed,
        out_specs=(P(("freq", "row"), None), P(("freq", "row"), None)),
        check_vma=False,
    )
```

```python
import functools
import math

import jax
import jax.numpy as jnp
from jax import lax
from jax.experimental import pallas as pl
from jax.experimental.pallas import tpu as pltpu
from jax.sharding import PartitionSpec as P

TILES = 8
AXIS = "row"
CORE, Y, LOW, HIGH = 1, 2, 4, 8
GROUP = 16
MIRROR_COST = 10000000000
DIRECT_COST = 2000000000
PIECE = 1024
F32 = jnp.float32
BF16 = jnp.bfloat16


def params(mib=16):
    return pltpu.CompilerParams(vmem_limit_bytes=mib * 1024 * 1024)


def whole_vmem():
    return pl.BlockSpec(memory_space=pltpu.VMEM)


def anywhere():
    return pl.BlockSpec(memory_space=pl.ANY)


def in_hbm(value):
    return pltpu.with_memory_space_constraint(value, pltpu.HBM)


def whole_smem():
    return pl.BlockSpec(memory_space=pltpu.SMEM)


def cost(flops, size):
    return pl.CostEstimate(flops=flops, bytes_accessed=size, transcendentals=0)


def dot(left, right):
    return jnp.dot(left, right, preferred_element_type=F32)


def ranks_of(col, rows):
    count = col.shape[0]
    owner = col // rows
    owner_row = jnp.transpose(jnp.broadcast_to(owner.astype(F32), (count, count))).astype(jnp.int32)
    before = lax.broadcasted_iota(jnp.int32, (count, count), 1) < lax.broadcasted_iota(
        jnp.int32, (count, count), 0
    )
    same = (owner_row == owner) & before
    return jnp.sum(same.astype(F32), axis=1, keepdims=True).astype(jnp.int32)


def rows_kernel(cap, round_ref, me_ref, col_ref, real_ref, imag_ref, out_ref, list_ref, near_ref, held_ref, sems):
    rows, width = real_ref.shape
    groups = out_ref.shape[0]
    count = col_ref.shape[0]
    base = me_ref[0] * rows
    skip = round_ref[0] * cap

    def copies(slot, local):
        group = pl.ds(pl.multiple_of(local // GROUP * GROUP, GROUP), GROUP)
        return [
            pltpu.make_async_copy(ref.at[group], near_ref.at[slot, part], sems.at[slot, part])
            for part, ref in enumerate((real_ref, imag_ref))
        ]

    def begin(s, found):
        local = col_ref[s] - base
        own = (local >= 0) & (local < rows)
        slot = found - skip

        @pl.when(own & (slot >= 0) & (slot < cap))
        def _():
            list_ref[slot] = local
            for copy in copies(slot, local):
                copy.start()

        return found + own.astype(jnp.int32)

    def pick(slot, _):
        local = list_ref[slot]
        chosen = lax.broadcasted_iota(jnp.int32, (GROUP, PIECE), 0) == local % GROUP
        for part, copy in enumerate(copies(slot, local)):
            copy.wait()
            for at in range(0, width, PIECE):
                group = near_ref[slot, part, :, at : at + PIECE].astype(F32)
                held_ref[pl.ds(part * cap + slot, 1), at : at + PIECE] = jnp.sum(
                    jnp.where(chosen, group, 0.0), axis=0, keepdims=True
                )
        return 0

    found = lax.fori_loop(0, count, begin, jnp.int32(0))
    held_ref[...] = jnp.zeros_like(held_ref)
    lax.fori_loop(0, jnp.clip(found - skip, 0, cap), pick, 0)
    for g in range(groups):
        out_ref[g] = held_ref[:, g * rows : (g + 1) * rows].astype(BF16)


def own_source_rows(me, data_real, data_imag, source_cols, which, cap):
    rows, width = data_real.shape
    return pl.pallas_call(
        functools.partial(rows_kernel, cap),
        in_specs=[whole_smem()] * 3 + [anywhere()] * 2,
        out_specs=whole_vmem(),
        out_shape=jax.ShapeDtypeStruct((width // rows, 2 * cap, rows), BF16),
        scratch_shapes=[
            pltpu.SMEM((cap,), jnp.int32),
            pltpu.VMEM((cap, 2, GROUP, width), BF16),
            pltpu.VMEM((2 * cap, width), F32),
            pltpu.SemaphoreType.DMA((cap, 2)),
        ],
        compiler_params=params(24),
        cost_estimate=cost(0, 2 * cap * width),
        name="own_source_rows",
    )(which, me, source_cols, data_real, data_imag)


def cols_kernel(real_ref, imag_ref, row_ref, out_ref, acc_ref):
    rows, step = real_ref.shape
    count = row_ref.shape[1]
    t = pl.program_id(0)

    @pl.when(t == 0)
    def _():
        acc_ref[...] = jnp.zeros_like(acc_ref)

    place = lax.broadcasted_iota(jnp.int32, (step, count), 0) + t * step
    pick = (place == row_ref[...]).astype(F32).astype(BF16)
    acc_ref[:, :count] += dot(real_ref[...], pick)
    acc_ref[:, count:] += dot(imag_ref[...], pick)

    @pl.when(t == pl.num_programs(0) - 1)
    def _():
        out_ref[...] = jnp.transpose(acc_ref[...]).astype(BF16)


def own_source_cols(data_real, data_imag, row, step):
    rows, width = data_real.shape
    count = row.shape[1]
    block = pl.BlockSpec((rows, step), lambda t: (0, t))
    return pl.pallas_call(
        cols_kernel,
        grid=(width // step,),
        in_specs=[block, block, whole_vmem()],
        out_specs=pl.BlockSpec((2 * count, rows), lambda t: (0, 0)),
        out_shape=jax.ShapeDtypeStruct((2 * count, rows), BF16),
        scratch_shapes=[pltpu.VMEM((rows, 2 * count), F32)],
        compiler_params=params(),
        cost_estimate=cost(4 * rows * width * count, 4 * rows * width),
        name="own_source_cols",
    )(data_real, data_imag, row)


def select_kernel(cap, round_ref, got_ref, col_ref, out_ref):
    out_ref[...] = pick_rows(cap, round_ref[0], got_ref, col_ref).astype(BF16)


def select_rows(got, col, which, cap):
    groups, _, rows = got.shape
    count = col.shape[0]
    return pl.pallas_call(
        functools.partial(select_kernel, cap),
        in_specs=[whole_smem(), whole_vmem(), whole_vmem()],
        out_specs=whole_vmem(),
        out_shape=jax.ShapeDtypeStruct((2 * count, rows), BF16),
        compiler_params=params(),
        cost_estimate=cost(8 * count * groups * cap * rows, 4 * groups * cap * rows),
        name="select_rows",
    )(which, got, col)


def pick_rows(cap, which, got_ref, col_ref):
    groups, _, rows = got_ref.shape
    count = col_ref.shape[0]
    col = col_ref[...]
    slot = ranks_of(col, rows) - which * cap
    inside = (slot >= 0) & (slot < cap)
    place = jnp.where(inside, (col // rows) * (2 * cap) + slot, -1)
    lanes = lax.broadcasted_iota(jnp.int32, (count, groups * 2 * cap), 1)
    pick = jnp.concatenate([lanes == place, lanes == jnp.where(inside, place + cap, -1)], axis=0)
    got = got_ref[...].reshape(groups * 2 * cap, rows)
    return dot(pick.astype(F32).astype(BF16), got)


def own_panel(width, mine, counts_ref, rowpart_ref, colpart_ref, col_ref):
    tile = width // TILES
    tiles = col_ref[...] // tile
    forward = jnp.zeros_like(tiles)
    backward = jnp.zeros_like(tiles)
    for t in range(TILES):
        forward = jnp.where(tiles == t, counts_ref[mine, t], forward)
        backward = jnp.where(tiles == t, counts_ref[t, mine], backward)
    forward = jnp.concatenate([forward, forward], axis=0).astype(F32)
    backward = jnp.concatenate([backward, backward], axis=0).astype(F32)
    own = colpart_ref[...].astype(F32)
    mirror = rowpart_ref[...].astype(F32)
    return (forward * own + backward * mirror) / jnp.maximum(forward + backward, 1.0)


def store_panel(panel, panel_ref, panel_t_ref):
    double, rows = panel.shape
    count = double // 2
    panel_t_ref[:, :rows] = panel.astype(BF16)
    panel_t_ref[:count, rows:] = (-panel[count:]).astype(BF16)
    panel_t_ref[count:, rows:] = panel[:count].astype(BF16)
    panel_ref[...] = jnp.transpose(panel).astype(BF16)


def panel_kernel(
    width, me_ref, counts_ref, rowpart_ref, colpart_ref, col_ref, panel_ref, panel_t_ref
):
    mine = me_ref[0] * rowpart_ref.shape[1] // (width // TILES)
    panel = own_panel(width, mine, counts_ref, rowpart_ref, colpart_ref, col_ref)
    store_panel(panel, panel_ref, panel_t_ref)


def panel_only(me, counts, rowpart, colpart, col, width):
    double, rows = colpart.shape
    return pl.pallas_call(
        functools.partial(panel_kernel, width),
        in_specs=[whole_smem()] * 2 + [whole_vmem()] * 3,
        out_specs=[whole_vmem()] * 2,
        out_shape=[
            jax.ShapeDtypeStruct((rows, double), BF16),
            jax.ShapeDtypeStruct((double, 2 * rows), BF16),
        ],
        compiler_params=params(),
        cost_estimate=cost(8 * rows * double, 8 * rows * double),
        name="panel_only",
    )(me, counts, rowpart, colpart, col)


def weight(counts_ref, mine, other, shape):
    forward = jnp.full(shape, counts_ref[mine, other], jnp.int32).astype(F32)
    backward = jnp.full(shape, counts_ref[other, mine], jnp.int32).astype(F32)
    return forward / jnp.maximum(forward + backward, 1.0)


def mirror_block(real, imag, panel_t):
    rows = real.shape[0]
    return dot(panel_t[:, :rows], real) + dot(panel_t[:, rows:], imag)


def direct_block(real, imag, panel):
    count = panel.shape[1] // 2
    turned = jnp.concatenate([-panel[:, count:], panel[:, :count]], axis=1)
    return dot(real, panel) + dot(imag, turned)


def mirror_kernel(width, me_ref, counts_ref, real_ref, imag_ref, panel_t_ref, out_ref):
    rows, tile = real_ref.shape
    mine = me_ref[0] * rows // tile
    found = mirror_block(real_ref[...], imag_ref[...], panel_t_ref[...])
    found = found * weight(counts_ref, mine, pl.program_id(0), (1, tile))
    for g in range(out_ref.shape[0]):
        out_ref[g] = found[:, g * rows : (g + 1) * rows]


def mirror_term(me, counts, data_real, data_imag, panel_t):
    rows, width = data_real.shape
    double = panel_t.shape[0]
    tile = width // TILES
    block = pl.BlockSpec((rows, tile), lambda t: (0, t))
    return pl.pallas_call(
        functools.partial(mirror_kernel, width),
        grid=(TILES,),
        in_specs=[whole_smem()] * 2 + [block, block, whole_vmem()],
        out_specs=pl.BlockSpec((tile // rows, double, rows), lambda t: (t, 0, 0)),
        out_shape=jax.ShapeDtypeStruct((width // rows, double, rows), F32),
        compiler_params=params(32),
        cost_estimate=cost(4 * rows * width * double, 4 * rows * width + 2 * double * width),
        name="mirror_term",
    )(me, counts, data_real, data_imag, panel_t)


def direct_kernel(width, me_ref, counts_ref, real_ref, imag_ref, panel_ref, out_ref):
    rows, tile = real_ref.shape
    mine = me_ref[0] * rows // tile
    t = pl.program_id(0)

    @pl.when(t == 0)
    def _():
        out_ref[...] = jnp.zeros_like(out_ref)

    found = direct_block(real_ref[...], imag_ref[...], panel_ref[...])
    out_ref[...] += found * weight(counts_ref, mine, t, (1, out_ref.shape[1]))


def direct_term(me, counts, data_real, data_imag, panel):
    rows, width = data_real.shape
    double = panel.shape[1]
    tile = width // TILES
    block = pl.BlockSpec((rows, tile), lambda t: (0, t))
    return pl.pallas_call(
        functools.partial(direct_kernel, width),
        grid=(TILES,),
        in_specs=[whole_smem()] * 2 + [block, block, pl.BlockSpec((tile, double), lambda t: (t, 0))],
        out_specs=pl.BlockSpec((rows, double), lambda t: (0, 0)),
        out_shape=jax.ShapeDtypeStruct((rows, double), F32),
        compiler_params=params(),
        cost_estimate=cost(4 * rows * width * double, 4 * rows * width + 2 * double * width),
        name="direct_term",
    )(me, counts, data_real, data_imag, panel)


def swap(value, mask):
    return lax.ppermute(value, AXIS, [(i, i ^ mask) for i in range(lax.axis_size(AXIS))])


def picked(masks, i):
    mask = masks[0]
    for at in range(1, len(masks)):
        mask = jnp.where(i == at, masks[at], mask)
    return mask


def mirror_part_kernel(width, masks, first, me_ref, counts_ref, real_ref, imag_ref, *refs):
    other_ref, near_ref, far_ref, held_ref, sems = refs[-5:]
    panel_t_ref = refs[4] if first else refs[0]
    rows = real_ref.shape[0]
    tile = width // TILES
    me = me_ref[0]
    dy, i = pl.program_id(0), pl.program_id(1)
    some = len(masks)
    mine = me * rows // tile

    def copies(at, mask):
        columns = pl.ds(pl.multiple_of((me ^ mask) // 2 * (2 * rows), 2 * rows), 2 * rows)
        return [
            pltpu.make_async_copy(
                ref.at[:, columns], held_ref.at[at, pl.ds(part * rows, rows)], sems.at[at, part]
            )
            for part, ref in enumerate((real_ref, imag_ref))
        ]

    @pl.when((dy == 0) & (i == 0))
    def _():
        for at in range(2 * some):
            for copy in copies(at, masks[at % some] ^ (2 * (at // some))):
                copy.start()
        if first:
            store_panel(own_panel(width, mine, counts_ref, *refs[:3]), refs[3], panel_t_ref)

    panel_t = panel_t_ref[...]
    at = dy * some + i
    mask = picked(masks, i) ^ (2 * dy)
    for copy in copies(at, mask):
        copy.wait()

    def term(turn):
        block = me ^ mask ^ turn
        scale = weight(counts_ref, mine, block * rows // tile, (1, rows))
        columns = pl.ds(pl.multiple_of(block % 2 * rows, rows), rows)
        return dot(panel_t, held_ref[at, :, columns]) * scale

    other_ref[0] = term(1).astype(BF16)

    @pl.when(dy == 0)
    def _():
        near_ref[0] = term(0)

    @pl.when(dy == 1)
    def _():
        far_ref[0] = term(0)


def mirror_part(me, counts, data_real, data_imag, panel, masks, after):
    rows, width = data_real.shape
    first = len(panel) == 3
    double = panel[0].shape[0]
    some = len(masks)
    shape = (1, double, rows)
    whole = lambda *dims: pl.BlockSpec(dims, lambda dy, i, me: (0,) * len(dims))
    spec = pltpu.PrefetchScalarGridSpec(
        num_scalar_prefetch=1,
        grid=(2, some),
        in_specs=[whole_smem(), anywhere(), anywhere()]
        + [whole_vmem()] * len(panel)
        + [anywhere()] * len(after),
        out_specs=([whole(rows, double), whole(double, 2 * rows)] if first else [])
        + [
            pl.BlockSpec(shape, lambda dy, i, me: (dy * some + i, 0, 0)),
            pl.BlockSpec(shape, lambda dy, i, me: (jnp.where(dy == 0, i, some - 1), 0, 0)),
            pl.BlockSpec(shape, lambda dy, i, me: (jnp.where(dy == 0, 0, i), 0, 0)),
        ],
        scratch_shapes=[
            pltpu.VMEM((2 * some, 2 * rows, 2 * rows), BF16),
            pltpu.SemaphoreType.DMA((2 * some, 2)),
        ],
    )
    panel_shapes = [
        jax.ShapeDtypeStruct((rows, double), BF16),
        jax.ShapeDtypeStruct((double, 2 * rows), BF16),
    ]
    return pl.pallas_call(
        functools.partial(mirror_part_kernel, width, masks, first),
        grid_spec=spec,
        out_shape=(panel_shapes if first else [])
        + [
            jax.ShapeDtypeStruct((2 * some, double, rows), BF16),
            jax.ShapeDtypeStruct((some, double, rows), F32),
            jax.ShapeDtypeStruct((some, double, rows), F32),
        ],
        compiler_params=params(24),
        cost_estimate=cost(MIRROR_COST, 0),
        name="mirror_part",
    )(me, counts, data_real, data_imag, *panel, *after)


def ordered(value, after):
    return lax.optimization_barrier((value, after))[0]


def direct_part_kernel(
    width, masks, mirrors, me_ref, counts_ref, real_ref, imag_ref, panel_ref, *refs
):
    rows = real_ref.shape[0]
    tile = width // TILES
    k = pl.program_id(0)
    mine = me_ref[0] * rows // tile
    block = me_ref[0] ^ picked(masks, k)
    scale = weight(counts_ref, mine, block * rows // tile, (1, panel_ref.shape[2]))
    found = direct_block(real_ref[...], imag_ref[...], panel_ref[0]) * scale
    sum_refs, (total_ref, *out_refs) = (refs[:-3], refs[-1:] + refs[-3:-1]) if mirrors else (
        refs[:-1],
        refs[-1:],
    )

    @pl.when(k == 0)
    def _():
        total = found
        if mirrors:
            mirror = sum_refs[-1][...].astype(F32)
            for ref in sum_refs[1:-1]:
                mirror += ref[...].astype(F32)
            total += jnp.transpose(mirror)
        total_ref[...] = total + sum_refs[0][...] if sum_refs else total

    @pl.when(k > 0)
    def _():
        total_ref[...] += found

    if mirrors:
        factor = -1.0 / math.sqrt(width)
        count = panel_ref.shape[2] // 2

        @pl.when(k == len(masks) - 1)
        def _():
            out_refs[0][...] = factor * total_ref[:, :count]
            out_refs[1][...] = factor * total_ref[:, count:]


def direct_part(me, counts, data_real, data_imag, panels, before, masks, mirrors=()):
    rows, width = data_real.shape
    double = panels.shape[2]
    block = pl.BlockSpec((rows, rows), lambda k, me: (0, me[0] ^ picked(masks, k)))
    outs = [(rows, double // 2)] * 2 if mirrors else [(rows, double)]
    spec = pltpu.PrefetchScalarGridSpec(
        num_scalar_prefetch=1,
        grid=(len(masks),),
        in_specs=[whole_smem(), block, block, pl.BlockSpec((1, rows, double), lambda k, me: (k, 0, 0))]
        + [whole_vmem()] * (len(before) + len(mirrors)),
        out_specs=[pl.BlockSpec(shape, lambda k, me: (0, 0)) for shape in outs],
        scratch_shapes=[pltpu.VMEM((rows, double), F32)] if mirrors else [],
    )
    return pl.pallas_call(
        functools.partial(direct_part_kernel, width, masks, bool(mirrors)),
        grid_spec=spec,
        out_shape=[jax.ShapeDtypeStruct(shape, F32) for shape in outs],
        compiler_params=params(),
        cost_estimate=cost(DIRECT_COST, 0),
        name="direct_part",
    )(me, counts, data_real, data_imag, panels, *before, *mirrors)


def levels(me, counts, data_real, data_imag, rowpart, colpart, col):
    data = (in_hbm(data_real), in_hbm(data_imag))
    panel, panel_t, other, own, own_far = mirror_part(
        me, counts, *data, [rowpart, colpart, col], (HIGH, HIGH | LOW), []
    )
    high, low, beside = swap(panel, HIGH), swap(panel, LOW), swap(panel, Y)

    def to_y(other, own):
        got = swap(other, CORE)
        some = own.shape[0]
        return (own + got[some:].astype(F32)).astype(BF16), got[:some]

    def over_y(sent, own, got):
        return own + got.astype(F32) + swap(sent, Y).astype(F32)

    sent, got = to_y(other, own_far)
    other_here, own_here, own_here_far = mirror_part(me, counts, *data, [panel_t], (0, LOW), [sent])
    total = over_y(sent, own, got)
    to_low = total[1].astype(BF16)
    total = total[0] + swap(to_low, LOW).astype(F32)
    mirrors = [swap(total.astype(BF16), HIGH)]

    low, high, beside = ordered([low, high, beside], [sent, own_here])
    direct = []

    def add(panels, masks, mirrors=()):
        direct[:] = direct_part(me, counts, *data, panels, direct, masks, mirrors)

    add(ordered(panel[None], high), (0,))
    sent, got = to_y(ordered(other_here, high), ordered(own_here_far, high))
    total = over_y(sent, own_here, got)
    mirrors += [total[0], swap(total[1].astype(BF16), LOW)]

    low_beside = swap(low, Y)
    both = ordered(swap(high, LOW), [sent, to_low])
    column = jnp.stack([panel, low, high, both])
    late = swap(ordered(jnp.stack([high, both]), [sent]), Y)
    add(column[1:], (LOW, HIGH, HIGH | LOW))
    add(swap(column, CORE), (CORE, CORE | LOW, CORE | HIGH, CORE | HIGH | LOW))
    early = jnp.stack([beside, ordered(low_beside, direct)])
    add(early, (Y, Y | LOW))
    add(swap(early, CORE), (Y | CORE, Y | CORE | LOW))
    late = ordered(late, direct + mirrors)
    add(late, (Y | HIGH, Y | HIGH | LOW))
    add(swap(late, CORE), (Y | CORE | HIGH, Y | CORE | HIGH | LOW), mirrors)
    return tuple(direct)


def finish_kernel(factor, direct_ref, mirror_ref, real_ref, imag_ref):
    count = real_ref.shape[1]
    total = factor * (direct_ref[...] + jnp.transpose(mirror_ref[...]))
    real_ref[...] = total[:, :count]
    imag_ref[...] = total[:, count:]


def finish(direct, mirror, width):
    rows, double = direct.shape
    shape = jax.ShapeDtypeStruct((rows, double // 2), F32)
    return pl.pallas_call(
        functools.partial(finish_kernel, -1.0 / math.sqrt(width)),
        in_specs=[whole_vmem()] * 2,
        out_specs=[whole_vmem()] * 2,
        out_shape=[shape, shape],
        compiler_params=params(),
        cost_estimate=cost(4 * rows * double, 10 * rows * double),
        name="finish",
    )(direct, mirror)


def shards(data_real, data_imag, counts, source_cols):
    rows, width = data_real.shape
    groups = width // rows
    count = source_cols.shape[0]
    cap = min(rows, count, -(-2 * count // groups // 8) * 8)
    col = source_cols.reshape(count, 1)
    row = source_cols.reshape(1, count)
    me = lax.axis_index(AXIS).reshape(1)

    def exchange(which):
        sent = own_source_rows(me, data_real, data_imag, source_cols, which, cap)
        return lax.all_to_all(sent, AXIS, split_axis=0, concat_axis=0)

    first = jnp.zeros((1,), jnp.int32)
    got = exchange(first)
    colpart = own_source_cols(data_real, data_imag, row, width // TILES)
    rowpart = select_rows(got, col, first, cap)

    owner = source_cols // rows
    most = jnp.max(jnp.sum(owner[:, None] == jnp.arange(groups)[None, :], axis=0, dtype=jnp.int32))

    def further(rowpart):
        def body(which, held):
            one = which.reshape(1)
            return held + select_rows(exchange(one), col, one, cap)

        return lax.fori_loop(1, (most + cap - 1) // cap, body, rowpart)

    rowpart = lax.cond(most > cap, further, lambda rowpart: rowpart, rowpart)
    if rows % 128 == 0 and groups == 16:
        return levels(me, counts, data_real, data_imag, rowpart, colpart, col)
    panel, panel_t = panel_only(me, counts, rowpart, colpart, col, width)
    full = lax.all_gather(panel, AXIS, axis=0, tiled=True)
    partial = mirror_term(me, counts, data_real, data_imag, panel_t)
    mirror = lax.psum_scatter(partial, AXIS, scatter_dimension=0, tiled=False)
    direct = direct_term(me, counts, data_real, data_imag, full)
    return tuple(finish(direct, mirror, width))


def solution(mesh):
    placed = (P(("freq", "row"), None), P(("freq", "row"), None), P(), P())
    return jax.shard_map(
        shards,
        mesh=mesh,
        in_specs=placed,
        out_specs=(P(("freq", "row"), None), P(("freq", "row"), None)),
        check_vma=False,
    )
```

```python
import functools
import math

import jax
import jax.numpy as jnp
from jax import lax
from jax.experimental import pallas as pl
from jax.experimental.pallas import tpu as pltpu
from jax.sharding import PartitionSpec as P

TILES = 8
AXIS = "row"
CORE, Y, LOW, HIGH = 1, 2, 4, 8
GROUP = 16
MIRROR_COST = 10000000000
DIRECT_COST = 2000000000
PIECE = 1024
F32 = jnp.float32
BF16 = jnp.bfloat16


def params(mib=16):
    return pltpu.CompilerParams(vmem_limit_bytes=mib * 1024 * 1024)


def whole_vmem():
    return pl.BlockSpec(memory_space=pltpu.VMEM)


def anywhere():
    return pl.BlockSpec(memory_space=pl.ANY)


def in_hbm(value):
    return pltpu.with_memory_space_constraint(value, pltpu.HBM)


def whole_smem():
    return pl.BlockSpec(memory_space=pltpu.SMEM)


def cost(flops, size):
    return pl.CostEstimate(flops=flops, bytes_accessed=size, transcendentals=0)


def dot(left, right):
    return jnp.dot(left, right, preferred_element_type=F32)


def ranks_of(col, rows):
    count = col.shape[0]
    owner = col // rows
    owner_row = jnp.transpose(jnp.broadcast_to(owner.astype(F32), (count, count))).astype(jnp.int32)
    before = lax.broadcasted_iota(jnp.int32, (count, count), 1) < lax.broadcasted_iota(
        jnp.int32, (count, count), 0
    )
    same = (owner_row == owner) & before
    return jnp.sum(same.astype(F32), axis=1, keepdims=True).astype(jnp.int32)


def rows_kernel(cap, round_ref, me_ref, col_ref, real_ref, imag_ref, out_ref, list_ref, near_ref, held_ref, sems):
    rows, width = real_ref.shape
    groups = out_ref.shape[0]
    count = col_ref.shape[0]
    base = me_ref[0] * rows
    skip = round_ref[0] * cap

    def copies(slot, local):
        group = pl.ds(pl.multiple_of(local // GROUP * GROUP, GROUP), GROUP)
        return [
            pltpu.make_async_copy(ref.at[group], near_ref.at[slot, part], sems.at[slot, part])
            for part, ref in enumerate((real_ref, imag_ref))
        ]

    def begin(s, found):
        local = col_ref[s] - base
        own = (local >= 0) & (local < rows)
        slot = found - skip

        @pl.when(own & (slot >= 0) & (slot < cap))
        def _():
            list_ref[slot] = local
            for copy in copies(slot, local):
                copy.start()

        return found + own.astype(jnp.int32)

    def pick(slot, _):
        local = list_ref[slot]
        chosen = lax.broadcasted_iota(jnp.int32, (GROUP, PIECE), 0) == local % GROUP
        for part, copy in enumerate(copies(slot, local)):
            copy.wait()
            for at in range(0, width, PIECE):
                group = near_ref[slot, part, :, at : at + PIECE].astype(F32)
                held_ref[pl.ds(part * cap + slot, 1), at : at + PIECE] = jnp.sum(
                    jnp.where(chosen, group, 0.0), axis=0, keepdims=True
                )
        return 0

    found = lax.fori_loop(0, count, begin, jnp.int32(0))
    held_ref[...] = jnp.zeros_like(held_ref)
    lax.fori_loop(0, jnp.clip(found - skip, 0, cap), pick, 0)
    for g in range(groups):
        out_ref[g] = held_ref[:, g * rows : (g + 1) * rows].astype(BF16)


def own_source_rows(me, data_real, data_imag, source_cols, which, cap):
    rows, width = data_real.shape
    return pl.pallas_call(
        functools.partial(rows_kernel, cap),
        in_specs=[whole_smem()] * 3 + [anywhere()] * 2,
        out_specs=whole_vmem(),
        out_shape=jax.ShapeDtypeStruct((width // rows, 2 * cap, rows), BF16),
        scratch_shapes=[
            pltpu.SMEM((cap,), jnp.int32),
            pltpu.VMEM((cap, 2, GROUP, width), BF16),
            pltpu.VMEM((2 * cap, width), F32),
            pltpu.SemaphoreType.DMA((cap, 2)),
        ],
        compiler_params=params(24),
        cost_estimate=cost(0, 2 * cap * width),
        name="own_source_rows",
    )(which, me, source_cols, data_real, data_imag)


def cols_kernel(real_ref, imag_ref, row_ref, out_ref, acc_ref):
    rows, step = real_ref.shape
    count = row_ref.shape[1]
    t = pl.program_id(0)

    @pl.when(t == 0)
    def _():
        acc_ref[...] = jnp.zeros_like(acc_ref)

    place = lax.broadcasted_iota(jnp.int32, (step, count), 0) + t * step
    pick = (place == row_ref[...]).astype(F32).astype(BF16)
    acc_ref[:, :count] += dot(real_ref[...], pick)
    acc_ref[:, count:] += dot(imag_ref[...], pick)

    @pl.when(t == pl.num_programs(0) - 1)
    def _():
        out_ref[...] = jnp.transpose(acc_ref[...]).astype(BF16)


def own_source_cols(data_real, data_imag, row, step):
    rows, width = data_real.shape
    count = row.shape[1]
    block = pl.BlockSpec((rows, step), lambda t: (0, t))
    return pl.pallas_call(
        cols_kernel,
        grid=(width // step,),
        in_specs=[block, block, whole_vmem()],
        out_specs=pl.BlockSpec((2 * count, rows), lambda t: (0, 0)),
        out_shape=jax.ShapeDtypeStruct((2 * count, rows), BF16),
        scratch_shapes=[pltpu.VMEM((rows, 2 * count), F32)],
        compiler_params=params(),
        cost_estimate=cost(4 * rows * width * count, 4 * rows * width),
        name="own_source_cols",
    )(data_real, data_imag, row)


def select_kernel(cap, round_ref, got_ref, col_ref, out_ref):
    out_ref[...] = pick_rows(cap, round_ref[0], got_ref, col_ref).astype(BF16)


def select_rows(got, col, which, cap):
    groups, _, rows = got.shape
    count = col.shape[0]
    return pl.pallas_call(
        functools.partial(select_kernel, cap),
        in_specs=[whole_smem(), whole_vmem(), whole_vmem()],
        out_specs=whole_vmem(),
        out_shape=jax.ShapeDtypeStruct((2 * count, rows), BF16),
        compiler_params=params(),
        cost_estimate=cost(8 * count * groups * cap * rows, 4 * groups * cap * rows),
        name="select_rows",
    )(which, got, col)


def pick_rows(cap, which, got_ref, col_ref):
    groups, _, rows = got_ref.shape
    count = col_ref.shape[0]
    col = col_ref[...]
    slot = ranks_of(col, rows) - which * cap
    inside = (slot >= 0) & (slot < cap)
    place = jnp.where(inside, (col // rows) * (2 * cap) + slot, -1)
    lanes = lax.broadcasted_iota(jnp.int32, (count, groups * 2 * cap), 1)
    pick = jnp.concatenate([lanes == place, lanes == jnp.where(inside, place + cap, -1)], axis=0)
    got = got_ref[...].reshape(groups * 2 * cap, rows)
    return dot(pick.astype(F32).astype(BF16), got)


def own_panel(width, mine, counts_ref, rowpart_ref, colpart_ref, col_ref):
    tile = width // TILES
    tiles = col_ref[...] // tile
    forward = jnp.zeros_like(tiles)
    backward = jnp.zeros_like(tiles)
    for t in range(TILES):
        forward = jnp.where(tiles == t, counts_ref[mine, t], forward)
        backward = jnp.where(tiles == t, counts_ref[t, mine], backward)
    forward = jnp.concatenate([forward, forward], axis=0).astype(F32)
    backward = jnp.concatenate([backward, backward], axis=0).astype(F32)
    own = colpart_ref[...].astype(F32)
    mirror = rowpart_ref[...].astype(F32)
    return (forward * own + backward * mirror) / jnp.maximum(forward + backward, 1.0)


def store_panel(panel, panel_ref, panel_t_ref):
    double, rows = panel.shape
    count = double // 2
    panel_t_ref[:, :rows] = panel.astype(BF16)
    panel_t_ref[:count, rows:] = (-panel[count:]).astype(BF16)
    panel_t_ref[count:, rows:] = panel[:count].astype(BF16)
    panel_ref[...] = jnp.transpose(panel).astype(BF16)


def panel_kernel(
    width, me_ref, counts_ref, rowpart_ref, colpart_ref, col_ref, panel_ref, panel_t_ref
):
    mine = me_ref[0] * rowpart_ref.shape[1] // (width // TILES)
    panel = own_panel(width, mine, counts_ref, rowpart_ref, colpart_ref, col_ref)
    store_panel(panel, panel_ref, panel_t_ref)


def panel_only(me, counts, rowpart, colpart, col, width):
    double, rows = colpart.shape
    return pl.pallas_call(
        functools.partial(panel_kernel, width),
        in_specs=[whole_smem()] * 2 + [whole_vmem()] * 3,
        out_specs=[whole_vmem()] * 2,
        out_shape=[
            jax.ShapeDtypeStruct((rows, double), BF16),
            jax.ShapeDtypeStruct((double, 2 * rows), BF16),
        ],
        compiler_params=params(),
        cost_estimate=cost(8 * rows * double, 8 * rows * double),
        name="panel_only",
    )(me, counts, rowpart, colpart, col)


def weight(counts_ref, mine, other, shape):
    forward = jnp.full(shape, counts_ref[mine, other], jnp.int32).astype(F32)
    backward = jnp.full(shape, counts_ref[other, mine], jnp.int32).astype(F32)
    return forward / jnp.maximum(forward + backward, 1.0)


def mirror_block(real, imag, panel_t):
    rows = real.shape[0]
    return dot(panel_t[:, :rows], real) + dot(panel_t[:, rows:], imag)


def direct_block(real, imag, panel):
    count = panel.shape[1] // 2
    turned = jnp.concatenate([-panel[:, count:], panel[:, :count]], axis=1)
    return dot(real, panel) + dot(imag, turned)


def mirror_kernel(width, me_ref, counts_ref, real_ref, imag_ref, panel_t_ref, out_ref):
    rows, tile = real_ref.shape
    mine = me_ref[0] * rows // tile
    found = mirror_block(real_ref[...], imag_ref[...], panel_t_ref[...])
    found = found * weight(counts_ref, mine, pl.program_id(0), (1, tile))
    for g in range(out_ref.shape[0]):
        out_ref[g] = found[:, g * rows : (g + 1) * rows]


def mirror_term(me, counts, data_real, data_imag, panel_t):
    rows, width = data_real.shape
    double = panel_t.shape[0]
    tile = width // TILES
    block = pl.BlockSpec((rows, tile), lambda t: (0, t))
    return pl.pallas_call(
        functools.partial(mirror_kernel, width),
        grid=(TILES,),
        in_specs=[whole_smem()] * 2 + [block, block, whole_vmem()],
        out_specs=pl.BlockSpec((tile // rows, double, rows), lambda t: (t, 0, 0)),
        out_shape=jax.ShapeDtypeStruct((width // rows, double, rows), F32),
        compiler_params=params(32),
        cost_estimate=cost(4 * rows * width * double, 4 * rows * width + 2 * double * width),
        name="mirror_term",
    )(me, counts, data_real, data_imag, panel_t)


def direct_kernel(width, me_ref, counts_ref, real_ref, imag_ref, panel_ref, out_ref):
    rows, tile = real_ref.shape
    mine = me_ref[0] * rows // tile
    t = pl.program_id(0)

    @pl.when(t == 0)
    def _():
        out_ref[...] = jnp.zeros_like(out_ref)

    found = direct_block(real_ref[...], imag_ref[...], panel_ref[...])
    out_ref[...] += found * weight(counts_ref, mine, t, (1, out_ref.shape[1]))


def direct_term(me, counts, data_real, data_imag, panel):
    rows, width = data_real.shape
    double = panel.shape[1]
    tile = width // TILES
    block = pl.BlockSpec((rows, tile), lambda t: (0, t))
    return pl.pallas_call(
        functools.partial(direct_kernel, width),
        grid=(TILES,),
        in_specs=[whole_smem()] * 2 + [block, block, pl.BlockSpec((tile, double), lambda t: (t, 0))],
        out_specs=pl.BlockSpec((rows, double), lambda t: (0, 0)),
        out_shape=jax.ShapeDtypeStruct((rows, double), F32),
        compiler_params=params(),
        cost_estimate=cost(4 * rows * width * double, 4 * rows * width + 2 * double * width),
        name="direct_term",
    )(me, counts, data_real, data_imag, panel)


def swap(value, mask):
    return lax.ppermute(value, AXIS, [(i, i ^ mask) for i in range(lax.axis_size(AXIS))])


def picked(masks, i):
    mask = masks[0]
    for at in range(1, len(masks)):
        mask = jnp.where(i == at, masks[at], mask)
    return mask


def mirror_part_kernel(width, masks, first, me_ref, counts_ref, real_ref, imag_ref, *refs):
    other_ref, near_ref, far_ref, held_ref, sems = refs[-5:]
    panel_t_ref = refs[4] if first else refs[0]
    rows = real_ref.shape[0]
    tile = width // TILES
    me = me_ref[0]
    dy, i = pl.program_id(0), pl.program_id(1)
    some = len(masks)
    mine = me * rows // tile

    def copies(at, mask):
        columns = pl.ds(pl.multiple_of((me ^ mask) // 2 * (2 * rows), 2 * rows), 2 * rows)
        return [
            pltpu.make_async_copy(
                ref.at[:, columns], held_ref.at[at, pl.ds(part * rows, rows)], sems.at[at, part]
            )
            for part, ref in enumerate((real_ref, imag_ref))
        ]

    @pl.when((dy == 0) & (i == 0))
    def _():
        for at in range(2 * some):
            for copy in copies(at, masks[at % some] ^ (2 * (at // some))):
                copy.start()
        if first:
            store_panel(own_panel(width, mine, counts_ref, *refs[:3]), refs[3], panel_t_ref)

    panel_t = panel_t_ref[...]
    at = dy * some + i
    mask = picked(masks, i) ^ (2 * dy)
    for copy in copies(at, mask):
        copy.wait()

    def term(turn):
        block = me ^ mask ^ turn
        scale = weight(counts_ref, mine, block * rows // tile, (1, rows))
        columns = pl.ds(pl.multiple_of(block % 2 * rows, rows), rows)
        return dot(panel_t, held_ref[at, :, columns]) * scale

    other_ref[0] = term(1).astype(BF16)

    @pl.when(dy == 0)
    def _():
        near_ref[0] = term(0)

    @pl.when(dy == 1)
    def _():
        far_ref[0] = term(0)


def mirror_part(me, counts, data_real, data_imag, panel, masks, after):
    rows, width = data_real.shape
    first = len(panel) == 3
    double = panel[0].shape[0]
    some = len(masks)
    shape = (1, double, rows)
    whole = lambda *dims: pl.BlockSpec(dims, lambda dy, i, me: (0,) * len(dims))
    spec = pltpu.PrefetchScalarGridSpec(
        num_scalar_prefetch=1,
        grid=(2, some),
        in_specs=[whole_smem(), anywhere(), anywhere()]
        + [whole_vmem()] * len(panel)
        + [anywhere()] * len(after),
        out_specs=([whole(rows, double), whole(double, 2 * rows)] if first else [])
        + [
            pl.BlockSpec(shape, lambda dy, i, me: (dy * some + i, 0, 0)),
            pl.BlockSpec(shape, lambda dy, i, me: (jnp.where(dy == 0, i, some - 1), 0, 0)),
            pl.BlockSpec(shape, lambda dy, i, me: (jnp.where(dy == 0, 0, i), 0, 0)),
        ],
        scratch_shapes=[
            pltpu.VMEM((2 * some, 2 * rows, 2 * rows), BF16),
            pltpu.SemaphoreType.DMA((2 * some, 2)),
        ],
    )
    panel_shapes = [
        jax.ShapeDtypeStruct((rows, double), BF16),
        jax.ShapeDtypeStruct((double, 2 * rows), BF16),
    ]
    return pl.pallas_call(
        functools.partial(mirror_part_kernel, width, masks, first),
        grid_spec=spec,
        out_shape=(panel_shapes if first else [])
        + [
            jax.ShapeDtypeStruct((2 * some, double, rows), BF16),
            jax.ShapeDtypeStruct((some, double, rows), F32),
            jax.ShapeDtypeStruct((some, double, rows), F32),
        ],
        compiler_params=params(24),
        cost_estimate=cost(MIRROR_COST, 0),
        name="mirror_part",
    )(me, counts, data_real, data_imag, *panel, *after)


def ordered(value, after):
    return lax.optimization_barrier((value, after))[0]


def direct_part_kernel(
    width, masks, mirrors, me_ref, counts_ref, real_ref, imag_ref, panel_ref, *refs
):
    rows = real_ref.shape[0]
    tile = width // TILES
    k = pl.program_id(0)
    mine = me_ref[0] * rows // tile
    block = me_ref[0] ^ picked(masks, k)
    scale = weight(counts_ref, mine, block * rows // tile, (1, panel_ref.shape[2]))
    found = direct_block(real_ref[...], imag_ref[...], panel_ref[0]) * scale
    sum_refs, (total_ref, *out_refs) = (refs[:-3], refs[-1:] + refs[-3:-1]) if mirrors else (
        refs[:-1],
        refs[-1:],
    )

    @pl.when(k == 0)
    def _():
        total = found
        if mirrors:
            mirror = sum_refs[-1][...].astype(F32)
            for ref in sum_refs[1:-1]:
                mirror += ref[...].astype(F32)
            total += jnp.transpose(mirror)
        total_ref[...] = total + sum_refs[0][...] if sum_refs else total

    @pl.when(k > 0)
    def _():
        total_ref[...] += found

    if mirrors:
        factor = -1.0 / math.sqrt(width)
        count = panel_ref.shape[2] // 2

        @pl.when(k == len(masks) - 1)
        def _():
            out_refs[0][...] = factor * total_ref[:, :count]
            out_refs[1][...] = factor * total_ref[:, count:]


def direct_part(me, counts, data_real, data_imag, panels, before, masks, mirrors=()):
    rows, width = data_real.shape
    double = panels.shape[2]
    block = pl.BlockSpec((rows, rows), lambda k, me: (0, me[0] ^ picked(masks, k)))
    outs = [(rows, double // 2)] * 2 if mirrors else [(rows, double)]
    spec = pltpu.PrefetchScalarGridSpec(
        num_scalar_prefetch=1,
        grid=(len(masks),),
        in_specs=[whole_smem(), block, block, pl.BlockSpec((1, rows, double), lambda k, me: (k, 0, 0))]
        + [whole_vmem()] * (len(before) + len(mirrors)),
        out_specs=[pl.BlockSpec(shape, lambda k, me: (0, 0)) for shape in outs],
        scratch_shapes=[pltpu.VMEM((rows, double), F32)] if mirrors else [],
    )
    return pl.pallas_call(
        functools.partial(direct_part_kernel, width, masks, bool(mirrors)),
        grid_spec=spec,
        out_shape=[jax.ShapeDtypeStruct(shape, F32) for shape in outs],
        compiler_params=params(),
        cost_estimate=cost(DIRECT_COST, 0),
        name="direct_part",
    )(me, counts, data_real, data_imag, panels, *before, *mirrors)


def levels(me, counts, data_real, data_imag, rowpart, colpart, col):
    data = (in_hbm(data_real), in_hbm(data_imag))
    panel, panel_t, other, own, own_far = mirror_part(
        me, counts, *data, [rowpart, colpart, col], (HIGH, HIGH | LOW), []
    )
    high, low, beside = swap(panel, HIGH), swap(panel, LOW), swap(panel, Y)

    def to_y(other, own):
        got = swap(other, CORE)
        some = own.shape[0]
        return (own + got[some:].astype(F32)).astype(BF16), got[:some]

    def over_y(sent, own, got):
        return own + got.astype(F32) + swap(sent, Y).astype(F32)

    sent, got = to_y(other, own_far)
    other_here, own_here, own_here_far = mirror_part(me, counts, *data, [panel_t], (0, LOW), [sent])
    total = over_y(sent, own, got)
    to_low = total[1].astype(BF16)
    total = total[0] + swap(to_low, LOW).astype(F32)
    mirrors = [swap(total.astype(BF16), HIGH)]

    low, high, beside = ordered([low, high, beside], [sent, own_here])
    direct = []

    def add(panels, masks, mirrors=()):
        direct[:] = direct_part(me, counts, *data, panels, direct, masks, mirrors)

    add(ordered(panel[None], high), (0,))
    sent, got = to_y(ordered(other_here, high), ordered(own_here_far, high))
    low_beside = swap(low, Y)
    both = ordered(swap(high, LOW), [sent, to_low])
    column = jnp.stack([panel, low, high, both])
    late = swap(ordered(jnp.stack([high, both]), [sent]), Y)
    arrived = swap(sent, Y)
    early = jnp.stack([beside, low_beside])
    add(jnp.concatenate([column[1:], early]), (LOW, HIGH, HIGH | LOW, Y, Y | LOW))
    add(swap(column, CORE), (CORE, CORE | LOW, CORE | HIGH, CORE | HIGH | LOW))
    total = own_here + got.astype(F32) + arrived.astype(F32)
    mirrors += [total[0], swap(total[1].astype(BF16), LOW)]
    add(swap(early, CORE), (Y | CORE, Y | CORE | LOW))
    late = ordered(late, direct + mirrors)
    add(late, (Y | HIGH, Y | HIGH | LOW))
    add(swap(late, CORE), (Y | CORE | HIGH, Y | CORE | HIGH | LOW), mirrors)
    return tuple(direct)


def finish_kernel(factor, direct_ref, mirror_ref, real_ref, imag_ref):
    count = real_ref.shape[1]
    total = factor * (direct_ref[...] + jnp.transpose(mirror_ref[...]))
    real_ref[...] = total[:, :count]
    imag_ref[...] = total[:, count:]


def finish(direct, mirror, width):
    rows, double = direct.shape
    shape = jax.ShapeDtypeStruct((rows, double // 2), F32)
    return pl.pallas_call(
        functools.partial(finish_kernel, -1.0 / math.sqrt(width)),
        in_specs=[whole_vmem()] * 2,
        out_specs=[whole_vmem()] * 2,
        out_shape=[shape, shape],
        compiler_params=params(),
        cost_estimate=cost(4 * rows * double, 10 * rows * double),
        name="finish",
    )(direct, mirror)


def shards(data_real, data_imag, counts, source_cols):
    rows, width = data_real.shape
    groups = width // rows
    count = source_cols.shape[0]
    cap = min(rows, count, -(-2 * count // groups // 8) * 8)
    col = source_cols.reshape(count, 1)
    row = source_cols.reshape(1, count)
    me = lax.axis_index(AXIS).reshape(1)

    def exchange(which):
        sent = own_source_rows(me, data_real, data_imag, source_cols, which, cap)
        return lax.all_to_all(sent, AXIS, split_axis=0, concat_axis=0)

    first = jnp.zeros((1,), jnp.int32)
    got = exchange(first)
    colpart = own_source_cols(data_real, data_imag, row, width // TILES)
    rowpart = select_rows(got, col, first, cap)

    owner = source_cols // rows
    most = jnp.max(jnp.sum(owner[:, None] == jnp.arange(groups)[None, :], axis=0, dtype=jnp.int32))

    def further(rowpart):
        def body(which, held):
            one = which.reshape(1)
            return held + select_rows(exchange(one), col, one, cap)

        return lax.fori_loop(1, (most + cap - 1) // cap, body, rowpart)

    rowpart = lax.cond(most > cap, further, lambda rowpart: rowpart, rowpart)
    if rows % 128 == 0 and groups == 16:
        return levels(me, counts, data_real, data_imag, rowpart, colpart, col)
    panel, panel_t = panel_only(me, counts, rowpart, colpart, col, width)
    full = lax.all_gather(panel, AXIS, axis=0, tiled=True)
    partial = mirror_term(me, counts, data_real, data_imag, panel_t)
    mirror = lax.psum_scatter(partial, AXIS, scatter_dimension=0, tiled=False)
    direct = direct_term(me, counts, data_real, data_imag, full)
    return tuple(finish(direct, mirror, width))


def solution(mesh):
    placed = (P(("freq", "row"), None), P(("freq", "row"), None), P(), P())
    return jax.shard_map(
        shards,
        mesh=mesh,
        in_specs=placed,
        out_specs=(P(("freq", "row"), None), P(("freq", "row"), None)),
        check_vma=False,
    )
```

```python
import functools
import math

import jax
import jax.numpy as jnp
from jax import lax
from jax.experimental import pallas as pl
from jax.experimental.pallas import tpu as pltpu
from jax.sharding import PartitionSpec as P

TILES = 8
AXIS = "row"
CORE, Y, LOW, HIGH = 1, 2, 4, 8
GROUP = 16
MIRROR_COST = 10000000000
DIRECT_COST = 2000000000
PIECE = 1024
F32 = jnp.float32
BF16 = jnp.bfloat16


def params(mib=16):
    return pltpu.CompilerParams(vmem_limit_bytes=mib * 1024 * 1024)


def whole_vmem():
    return pl.BlockSpec(memory_space=pltpu.VMEM)


def anywhere():
    return pl.BlockSpec(memory_space=pl.ANY)


def in_hbm(value):
    return pltpu.with_memory_space_constraint(value, pltpu.HBM)


def whole_smem():
    return pl.BlockSpec(memory_space=pltpu.SMEM)


def cost(flops, size):
    return pl.CostEstimate(flops=flops, bytes_accessed=size, transcendentals=0)


def dot(left, right):
    return jnp.dot(left, right, preferred_element_type=F32)


def ranks_of(col, rows):
    count = col.shape[0]
    owner = col // rows
    owner_row = jnp.transpose(jnp.broadcast_to(owner.astype(F32), (count, count))).astype(jnp.int32)
    before = lax.broadcasted_iota(jnp.int32, (count, count), 1) < lax.broadcasted_iota(
        jnp.int32, (count, count), 0
    )
    same = (owner_row == owner) & before
    return jnp.sum(same.astype(F32), axis=1, keepdims=True).astype(jnp.int32)


def rows_kernel(cap, round_ref, me_ref, col_ref, real_ref, imag_ref, out_ref, list_ref, near_ref, held_ref, sems):
    rows, width = real_ref.shape
    groups = out_ref.shape[0]
    count = col_ref.shape[0]
    base = me_ref[0] * rows
    skip = round_ref[0] * cap

    def copies(slot, local):
        group = pl.ds(pl.multiple_of(local // GROUP * GROUP, GROUP), GROUP)
        return [
            pltpu.make_async_copy(ref.at[group], near_ref.at[slot, part], sems.at[slot, part])
            for part, ref in enumerate((real_ref, imag_ref))
        ]

    def begin(s, found):
        local = col_ref[s] - base
        own = (local >= 0) & (local < rows)
        slot = found - skip

        @pl.when(own & (slot >= 0) & (slot < cap))
        def _():
            list_ref[slot] = local
            for copy in copies(slot, local):
                copy.start()

        return found + own.astype(jnp.int32)

    def pick(slot, _):
        local = list_ref[slot]
        chosen = lax.broadcasted_iota(jnp.int32, (GROUP, PIECE), 0) == local % GROUP
        for part, copy in enumerate(copies(slot, local)):
            copy.wait()
            for at in range(0, width, PIECE):
                group = near_ref[slot, part, :, at : at + PIECE].astype(F32)
                held_ref[pl.ds(part * cap + slot, 1), at : at + PIECE] = jnp.sum(
                    jnp.where(chosen, group, 0.0), axis=0, keepdims=True
                )
        return 0

    found = lax.fori_loop(0, count, begin, jnp.int32(0))
    held_ref[...] = jnp.zeros_like(held_ref)
    lax.fori_loop(0, jnp.clip(found - skip, 0, cap), pick, 0)
    for g in range(groups):
        out_ref[g] = held_ref[:, g * rows : (g + 1) * rows].astype(BF16)


def own_source_rows(me, data_real, data_imag, source_cols, which, cap):
    rows, width = data_real.shape
    return pl.pallas_call(
        functools.partial(rows_kernel, cap),
        in_specs=[whole_smem()] * 3 + [anywhere()] * 2,
        out_specs=whole_vmem(),
        out_shape=jax.ShapeDtypeStruct((width // rows, 2 * cap, rows), BF16),
        scratch_shapes=[
            pltpu.SMEM((cap,), jnp.int32),
            pltpu.VMEM((cap, 2, GROUP, width), BF16),
            pltpu.VMEM((2 * cap, width), F32),
            pltpu.SemaphoreType.DMA((cap, 2)),
        ],
        compiler_params=params(24),
        cost_estimate=cost(0, 2 * cap * width),
        name="own_source_rows",
    )(which, me, source_cols, data_real, data_imag)


def cols_kernel(real_ref, imag_ref, row_ref, out_ref, acc_ref):
    rows, step = real_ref.shape
    count = row_ref.shape[1]
    t = pl.program_id(0)

    @pl.when(t == 0)
    def _():
        acc_ref[...] = jnp.zeros_like(acc_ref)

    place = lax.broadcasted_iota(jnp.int32, (step, count), 0) + t * step
    pick = (place == row_ref[...]).astype(F32).astype(BF16)
    acc_ref[:, :count] += dot(real_ref[...], pick)
    acc_ref[:, count:] += dot(imag_ref[...], pick)

    @pl.when(t == pl.num_programs(0) - 1)
    def _():
        out_ref[...] = jnp.transpose(acc_ref[...]).astype(BF16)


def own_source_cols(data_real, data_imag, row, step):
    rows, width = data_real.shape
    count = row.shape[1]
    block = pl.BlockSpec((rows, step), lambda t: (0, t))
    return pl.pallas_call(
        cols_kernel,
        grid=(width // step,),
        in_specs=[block, block, whole_vmem()],
        out_specs=pl.BlockSpec((2 * count, rows), lambda t: (0, 0)),
        out_shape=jax.ShapeDtypeStruct((2 * count, rows), BF16),
        scratch_shapes=[pltpu.VMEM((rows, 2 * count), F32)],
        compiler_params=params(),
        cost_estimate=cost(4 * rows * width * count, 4 * rows * width),
        name="own_source_cols",
    )(data_real, data_imag, row)


def select_kernel(cap, round_ref, got_ref, col_ref, out_ref):
    out_ref[...] = pick_rows(cap, round_ref[0], got_ref, col_ref).astype(BF16)


def select_rows(got, col, which, cap):
    groups, _, rows = got.shape
    count = col.shape[0]
    return pl.pallas_call(
        functools.partial(select_kernel, cap),
        in_specs=[whole_smem(), whole_vmem(), whole_vmem()],
        out_specs=whole_vmem(),
        out_shape=jax.ShapeDtypeStruct((2 * count, rows), BF16),
        compiler_params=params(),
        cost_estimate=cost(8 * count * groups * cap * rows, 4 * groups * cap * rows),
        name="select_rows",
    )(which, got, col)


def pick_rows(cap, which, got_ref, col_ref):
    groups, _, rows = got_ref.shape
    count = col_ref.shape[0]
    col = col_ref[...]
    slot = ranks_of(col, rows) - which * cap
    inside = (slot >= 0) & (slot < cap)
    place = jnp.where(inside, (col // rows) * (2 * cap) + slot, -1)
    lanes = lax.broadcasted_iota(jnp.int32, (count, groups * 2 * cap), 1)
    pick = jnp.concatenate([lanes == place, lanes == jnp.where(inside, place + cap, -1)], axis=0)
    got = got_ref[...].reshape(groups * 2 * cap, rows)
    return dot(pick.astype(F32).astype(BF16), got)


def own_panel(width, mine, counts_ref, rowpart_ref, colpart_ref, col_ref):
    tile = width // TILES
    tiles = col_ref[...] // tile
    forward = jnp.zeros_like(tiles)
    backward = jnp.zeros_like(tiles)
    for t in range(TILES):
        forward = jnp.where(tiles == t, counts_ref[mine, t], forward)
        backward = jnp.where(tiles == t, counts_ref[t, mine], backward)
    forward = jnp.concatenate([forward, forward], axis=0).astype(F32)
    backward = jnp.concatenate([backward, backward], axis=0).astype(F32)
    own = colpart_ref[...].astype(F32)
    mirror = rowpart_ref[...].astype(F32)
    return (forward * own + backward * mirror) / jnp.maximum(forward + backward, 1.0)


def store_panel(panel, panel_ref, panel_t_ref):
    double, rows = panel.shape
    count = double // 2
    panel_t_ref[:, :rows] = panel.astype(BF16)
    panel_t_ref[:count, rows:] = (-panel[count:]).astype(BF16)
    panel_t_ref[count:, rows:] = panel[:count].astype(BF16)
    panel_ref[...] = jnp.transpose(panel).astype(BF16)


def panel_kernel(
    width, me_ref, counts_ref, rowpart_ref, colpart_ref, col_ref, panel_ref, panel_t_ref
):
    mine = me_ref[0] * rowpart_ref.shape[1] // (width // TILES)
    panel = own_panel(width, mine, counts_ref, rowpart_ref, colpart_ref, col_ref)
    store_panel(panel, panel_ref, panel_t_ref)


def panel_only(me, counts, rowpart, colpart, col, width):
    double, rows = colpart.shape
    return pl.pallas_call(
        functools.partial(panel_kernel, width),
        in_specs=[whole_smem()] * 2 + [whole_vmem()] * 3,
        out_specs=[whole_vmem()] * 2,
        out_shape=[
            jax.ShapeDtypeStruct((rows, double), BF16),
            jax.ShapeDtypeStruct((double, 2 * rows), BF16),
        ],
        compiler_params=params(),
        cost_estimate=cost(8 * rows * double, 8 * rows * double),
        name="panel_only",
    )(me, counts, rowpart, colpart, col)


def weight(counts_ref, mine, other, shape):
    forward = jnp.full(shape, counts_ref[mine, other], jnp.int32).astype(F32)
    backward = jnp.full(shape, counts_ref[other, mine], jnp.int32).astype(F32)
    return forward / jnp.maximum(forward + backward, 1.0)


def mirror_block(real, imag, panel_t):
    rows = real.shape[0]
    return dot(panel_t[:, :rows], real) + dot(panel_t[:, rows:], imag)


def direct_block(real, imag, panel):
    count = panel.shape[1] // 2
    turned = jnp.concatenate([-panel[:, count:], panel[:, :count]], axis=1)
    return dot(real, panel) + dot(imag, turned)


def mirror_kernel(width, me_ref, counts_ref, real_ref, imag_ref, panel_t_ref, out_ref):
    rows, tile = real_ref.shape
    mine = me_ref[0] * rows // tile
    found = mirror_block(real_ref[...], imag_ref[...], panel_t_ref[...])
    found = found * weight(counts_ref, mine, pl.program_id(0), (1, tile))
    for g in range(out_ref.shape[0]):
        out_ref[g] = found[:, g * rows : (g + 1) * rows]


def mirror_term(me, counts, data_real, data_imag, panel_t):
    rows, width = data_real.shape
    double = panel_t.shape[0]
    tile = width // TILES
    block = pl.BlockSpec((rows, tile), lambda t: (0, t))
    return pl.pallas_call(
        functools.partial(mirror_kernel, width),
        grid=(TILES,),
        in_specs=[whole_smem()] * 2 + [block, block, whole_vmem()],
        out_specs=pl.BlockSpec((tile // rows, double, rows), lambda t: (t, 0, 0)),
        out_shape=jax.ShapeDtypeStruct((width // rows, double, rows), F32),
        compiler_params=params(32),
        cost_estimate=cost(4 * rows * width * double, 4 * rows * width + 2 * double * width),
        name="mirror_term",
    )(me, counts, data_real, data_imag, panel_t)


def direct_kernel(width, me_ref, counts_ref, real_ref, imag_ref, panel_ref, out_ref):
    rows, tile = real_ref.shape
    mine = me_ref[0] * rows // tile
    t = pl.program_id(0)

    @pl.when(t == 0)
    def _():
        out_ref[...] = jnp.zeros_like(out_ref)

    found = direct_block(real_ref[...], imag_ref[...], panel_ref[...])
    out_ref[...] += found * weight(counts_ref, mine, t, (1, out_ref.shape[1]))


def direct_term(me, counts, data_real, data_imag, panel):
    rows, width = data_real.shape
    double = panel.shape[1]
    tile = width // TILES
    block = pl.BlockSpec((rows, tile), lambda t: (0, t))
    return pl.pallas_call(
        functools.partial(direct_kernel, width),
        grid=(TILES,),
        in_specs=[whole_smem()] * 2 + [block, block, pl.BlockSpec((tile, double), lambda t: (t, 0))],
        out_specs=pl.BlockSpec((rows, double), lambda t: (0, 0)),
        out_shape=jax.ShapeDtypeStruct((rows, double), F32),
        compiler_params=params(),
        cost_estimate=cost(4 * rows * width * double, 4 * rows * width + 2 * double * width),
        name="direct_term",
    )(me, counts, data_real, data_imag, panel)


def swap(value, mask):
    return lax.ppermute(value, AXIS, [(i, i ^ mask) for i in range(lax.axis_size(AXIS))])


def picked(masks, i):
    mask = masks[0]
    for at in range(1, len(masks)):
        mask = jnp.where(i == at, masks[at], mask)
    return mask


def mirror_part_kernel(width, masks, first, me_ref, counts_ref, real_ref, imag_ref, *refs):
    other_ref, near_ref, far_ref, held_ref, sems = refs[-5:]
    panel_t_ref = refs[4] if first else refs[0]
    rows = real_ref.shape[0]
    tile = width // TILES
    me = me_ref[0]
    dy, i = pl.program_id(0), pl.program_id(1)
    some = len(masks)
    mine = me * rows // tile

    def copies(at, mask):
        columns = pl.ds(pl.multiple_of((me ^ mask) // 2 * (2 * rows), 2 * rows), 2 * rows)
        return [
            pltpu.make_async_copy(
                ref.at[:, columns], held_ref.at[at, pl.ds(part * rows, rows)], sems.at[at, part]
            )
            for part, ref in enumerate((real_ref, imag_ref))
        ]

    @pl.when((dy == 0) & (i == 0))
    def _():
        for at in range(2 * some):
            for copy in copies(at, masks[at % some] ^ (2 * (at // some))):
                copy.start()
        if first:
            store_panel(own_panel(width, mine, counts_ref, *refs[:3]), refs[3], panel_t_ref)

    panel_t = panel_t_ref[...]
    at = dy * some + i
    mask = picked(masks, i) ^ (2 * dy)
    for copy in copies(at, mask):
        copy.wait()

    def term(turn):
        block = me ^ mask ^ turn
        scale = weight(counts_ref, mine, block * rows // tile, (1, rows))
        columns = pl.ds(pl.multiple_of(block % 2 * rows, rows), rows)
        return dot(panel_t, held_ref[at, :, columns]) * scale

    other_ref[0] = term(1).astype(BF16)

    @pl.when(dy == 0)
    def _():
        near_ref[0] = term(0)

    @pl.when(dy == 1)
    def _():
        far_ref[0] = term(0)


def mirror_part(me, counts, data_real, data_imag, panel, masks, after):
    rows, width = data_real.shape
    first = len(panel) == 3
    double = panel[0].shape[0]
    some = len(masks)
    shape = (1, double, rows)
    whole = lambda *dims: pl.BlockSpec(dims, lambda dy, i, me: (0,) * len(dims))
    spec = pltpu.PrefetchScalarGridSpec(
        num_scalar_prefetch=1,
        grid=(2, some),
        in_specs=[whole_smem(), anywhere(), anywhere()]
        + [whole_vmem()] * len(panel)
        + [anywhere()] * len(after),
        out_specs=([whole(rows, double), whole(double, 2 * rows)] if first else [])
        + [
            pl.BlockSpec(shape, lambda dy, i, me: (dy * some + i, 0, 0)),
            pl.BlockSpec(shape, lambda dy, i, me: (jnp.where(dy == 0, i, some - 1), 0, 0)),
            pl.BlockSpec(shape, lambda dy, i, me: (jnp.where(dy == 0, 0, i), 0, 0)),
        ],
        scratch_shapes=[
            pltpu.VMEM((2 * some, 2 * rows, 2 * rows), BF16),
            pltpu.SemaphoreType.DMA((2 * some, 2)),
        ],
    )
    panel_shapes = [
        jax.ShapeDtypeStruct((rows, double), BF16),
        jax.ShapeDtypeStruct((double, 2 * rows), BF16),
    ]
    return pl.pallas_call(
        functools.partial(mirror_part_kernel, width, masks, first),
        grid_spec=spec,
        out_shape=(panel_shapes if first else [])
        + [
            jax.ShapeDtypeStruct((2 * some, double, rows), BF16),
            jax.ShapeDtypeStruct((some, double, rows), F32),
            jax.ShapeDtypeStruct((some, double, rows), F32),
        ],
        compiler_params=params(24),
        cost_estimate=cost(MIRROR_COST, 0),
        name="mirror_part",
    )(me, counts, data_real, data_imag, *panel, *after)


def ordered(value, after):
    return lax.optimization_barrier((value, after))[0]


def direct_part_kernel(
    width, masks, mirrors, me_ref, counts_ref, real_ref, imag_ref, panel_ref, *refs
):
    rows = real_ref.shape[0]
    tile = width // TILES
    k = pl.program_id(0)
    mine = me_ref[0] * rows // tile
    block = me_ref[0] ^ picked(masks, k)
    scale = weight(counts_ref, mine, block * rows // tile, (1, panel_ref.shape[2]))
    found = direct_block(real_ref[...], imag_ref[...], panel_ref[0]) * scale
    sum_refs, (total_ref, *out_refs) = (refs[:-3], refs[-1:] + refs[-3:-1]) if mirrors else (
        refs[:-1],
        refs[-1:],
    )

    @pl.when(k == 0)
    def _():
        total = found
        if mirrors:
            mirror = sum_refs[-1][...].astype(F32)
            for ref in sum_refs[1:-1]:
                mirror += ref[...].astype(F32)
            total += jnp.transpose(mirror)
        total_ref[...] = total + sum_refs[0][...] if sum_refs else total

    @pl.when(k > 0)
    def _():
        total_ref[...] += found

    if mirrors:
        factor = -1.0 / math.sqrt(width)
        count = panel_ref.shape[2] // 2

        @pl.when(k == len(masks) - 1)
        def _():
            out_refs[0][...] = factor * total_ref[:, :count]
            out_refs[1][...] = factor * total_ref[:, count:]


def direct_part(me, counts, data_real, data_imag, panels, before, masks, mirrors=()):
    rows, width = data_real.shape
    double = panels.shape[2]
    block = pl.BlockSpec((rows, rows), lambda k, me: (0, me[0] ^ picked(masks, k)))
    outs = [(rows, double // 2)] * 2 if mirrors else [(rows, double)]
    spec = pltpu.PrefetchScalarGridSpec(
        num_scalar_prefetch=1,
        grid=(len(masks),),
        in_specs=[whole_smem(), block, block, pl.BlockSpec((1, rows, double), lambda k, me: (k, 0, 0))]
        + [whole_vmem()] * (len(before) + len(mirrors)),
        out_specs=[pl.BlockSpec(shape, lambda k, me: (0, 0)) for shape in outs],
        scratch_shapes=[pltpu.VMEM((rows, double), F32)] if mirrors else [],
    )
    return pl.pallas_call(
        functools.partial(direct_part_kernel, width, masks, bool(mirrors)),
        grid_spec=spec,
        out_shape=[jax.ShapeDtypeStruct(shape, F32) for shape in outs],
        compiler_params=params(),
        cost_estimate=cost(DIRECT_COST, 0),
        name="direct_part",
    )(me, counts, data_real, data_imag, panels, *before, *mirrors)


def levels(me, counts, data_real, data_imag, rowpart, colpart, col):
    data = (in_hbm(data_real), in_hbm(data_imag))
    panel, panel_t, other, own, own_far = mirror_part(
        me, counts, *data, [rowpart, colpart, col], (HIGH, HIGH | LOW), []
    )
    high, low, beside = swap(panel, HIGH), swap(panel, LOW), swap(panel, Y)

    def to_y(other, own):
        got = swap(other, CORE)
        some = own.shape[0]
        return (own + got[some:].astype(F32)).astype(BF16), got[:some]

    def over_y(sent, own, got):
        return own + got.astype(F32) + swap(sent, Y).astype(F32)

    sent, got = to_y(other, own_far)
    other_here, own_here, own_here_far = mirror_part(me, counts, *data, [panel_t], (0, LOW), [sent])
    total = over_y(sent, own, got)
    to_low = total[1].astype(BF16)

    low, high, beside = ordered([low, high, beside], [sent, own_here])
    direct = []

    def add(panels, masks, mirrors=()):
        direct[:] = direct_part(me, counts, *data, panels, direct, masks, mirrors)

    add(ordered(panel[None], high), (0,))
    sent, got = to_y(ordered(other_here, high), ordered(own_here_far, high))
    total = total[0] + ordered(swap(to_low, LOW), [sent]).astype(F32)
    mirrors = [swap(total.astype(BF16), HIGH)]
    low_beside = ordered(swap(low, Y), [sent, total])
    both = ordered(swap(high, LOW), [sent, to_low])
    column = jnp.stack([panel, low, high, both])
    late = swap(ordered(jnp.stack([high, both]), [sent]), Y)
    early = jnp.stack([beside, low_beside])
    add(jnp.concatenate([column[1:], early]), (LOW, HIGH, HIGH | LOW, Y, Y | LOW))
    add(swap(column, CORE), (CORE, CORE | LOW, CORE | HIGH, CORE | HIGH | LOW))
    total = own_here + got.astype(F32) + swap(sent, Y).astype(F32)
    mirrors += [total[0], swap(total[1].astype(BF16), LOW)]
    add(swap(early, CORE), (Y | CORE, Y | CORE | LOW))
    late = ordered(late, direct + mirrors)
    add(late, (Y | HIGH, Y | HIGH | LOW))
    add(swap(late, CORE), (Y | CORE | HIGH, Y | CORE | HIGH | LOW), mirrors)
    return tuple(direct)


def finish_kernel(factor, direct_ref, mirror_ref, real_ref, imag_ref):
    count = real_ref.shape[1]
    total = factor * (direct_ref[...] + jnp.transpose(mirror_ref[...]))
    real_ref[...] = total[:, :count]
    imag_ref[...] = total[:, count:]


def finish(direct, mirror, width):
    rows, double = direct.shape
    shape = jax.ShapeDtypeStruct((rows, double // 2), F32)
    return pl.pallas_call(
        functools.partial(finish_kernel, -1.0 / math.sqrt(width)),
        in_specs=[whole_vmem()] * 2,
        out_specs=[whole_vmem()] * 2,
        out_shape=[shape, shape],
        compiler_params=params(),
        cost_estimate=cost(4 * rows * double, 10 * rows * double),
        name="finish",
    )(direct, mirror)


def shards(data_real, data_imag, counts, source_cols):
    rows, width = data_real.shape
    groups = width // rows
    count = source_cols.shape[0]
    cap = min(rows, count, -(-2 * count // groups // 8) * 8)
    col = source_cols.reshape(count, 1)
    row = source_cols.reshape(1, count)
    me = lax.axis_index(AXIS).reshape(1)

    def exchange(which):
        sent = own_source_rows(me, data_real, data_imag, source_cols, which, cap)
        return lax.all_to_all(sent, AXIS, split_axis=0, concat_axis=0)

    first = jnp.zeros((1,), jnp.int32)
    got = exchange(first)
    colpart = own_source_cols(data_real, data_imag, row, width // TILES)
    rowpart = select_rows(got, col, first, cap)

    owner = source_cols // rows
    most = jnp.max(jnp.sum(owner[:, None] == jnp.arange(groups)[None, :], axis=0, dtype=jnp.int32))

    def further(rowpart):
        def body(which, held):
            one = which.reshape(1)
            return held + select_rows(exchange(one), col, one, cap)

        return lax.fori_loop(1, (most + cap - 1) // cap, body, rowpart)

    rowpart = lax.cond(most > cap, further, lambda rowpart: rowpart, rowpart)
    if rows % 128 == 0 and groups == 16:
        return levels(me, counts, data_real, data_imag, rowpart, colpart, col)
    panel, panel_t = panel_only(me, counts, rowpart, colpart, col, width)
    full = lax.all_gather(panel, AXIS, axis=0, tiled=True)
    partial = mirror_term(me, counts, data_real, data_imag, panel_t)
    mirror = lax.psum_scatter(partial, AXIS, scatter_dimension=0, tiled=False)
    direct = direct_term(me, counts, data_real, data_imag, full)
    return tuple(finish(direct, mirror, width))


def solution(mesh):
    placed = (P(("freq", "row"), None), P(("freq", "row"), None), P(), P())
    return jax.shard_map(
        shards,
        mesh=mesh,
        in_specs=placed,
        out_specs=(P(("freq", "row"), None), P(("freq", "row"), None)),
        check_vma=False,
    )
```

```python
import functools
import math

import jax
import jax.numpy as jnp
from jax import lax
from jax.experimental import pallas as pl
from jax.experimental.pallas import tpu as pltpu
from jax.sharding import PartitionSpec as P

TILES = 8
AXIS = "row"
CORE, Y, LOW, HIGH = 1, 2, 4, 8
GROUP = 16
MIRROR_COST = 10000000000
DIRECT_COST = 2000000000
PIECE = 1024
F32 = jnp.float32
BF16 = jnp.bfloat16


def params(mib=16):
    return pltpu.CompilerParams(vmem_limit_bytes=mib * 1024 * 1024)


def whole_vmem():
    return pl.BlockSpec(memory_space=pltpu.VMEM)


def anywhere():
    return pl.BlockSpec(memory_space=pl.ANY)


def in_hbm(value):
    return pltpu.with_memory_space_constraint(value, pltpu.HBM)


def whole_smem():
    return pl.BlockSpec(memory_space=pltpu.SMEM)


def cost(flops, size):
    return pl.CostEstimate(flops=flops, bytes_accessed=size, transcendentals=0)


def dot(left, right):
    return jnp.dot(left, right, preferred_element_type=F32)


def ranks_of(col, rows):
    count = col.shape[0]
    owner = col // rows
    owner_row = jnp.transpose(jnp.broadcast_to(owner.astype(F32), (count, count))).astype(jnp.int32)
    before = lax.broadcasted_iota(jnp.int32, (count, count), 1) < lax.broadcasted_iota(
        jnp.int32, (count, count), 0
    )
    same = (owner_row == owner) & before
    return jnp.sum(same.astype(F32), axis=1, keepdims=True).astype(jnp.int32)


def rows_kernel(cap, round_ref, me_ref, col_ref, real_ref, imag_ref, out_ref, list_ref, near_ref, held_ref, sems):
    rows, width = real_ref.shape
    groups = out_ref.shape[0]
    count = col_ref.shape[0]
    base = me_ref[0] * rows
    skip = round_ref[0] * cap

    def copies(slot, local):
        group = pl.ds(pl.multiple_of(local // GROUP * GROUP, GROUP), GROUP)
        return [
            pltpu.make_async_copy(ref.at[group], near_ref.at[slot, part], sems.at[slot, part])
            for part, ref in enumerate((real_ref, imag_ref))
        ]

    def begin(s, found):
        local = col_ref[s] - base
        own = (local >= 0) & (local < rows)
        slot = found - skip

        @pl.when(own & (slot >= 0) & (slot < cap))
        def _():
            list_ref[slot] = local
            for copy in copies(slot, local):
                copy.start()

        return found + own.astype(jnp.int32)

    def pick(slot, _):
        local = list_ref[slot]
        chosen = lax.broadcasted_iota(jnp.int32, (GROUP, PIECE), 0) == local % GROUP
        for part, copy in enumerate(copies(slot, local)):
            copy.wait()
            for at in range(0, width, PIECE):
                group = near_ref[slot, part, :, at : at + PIECE].astype(F32)
                held_ref[pl.ds(part * cap + slot, 1), at : at + PIECE] = jnp.sum(
                    jnp.where(chosen, group, 0.0), axis=0, keepdims=True
                )
        return 0

    found = lax.fori_loop(0, count, begin, jnp.int32(0))
    held_ref[...] = jnp.zeros_like(held_ref)
    lax.fori_loop(0, jnp.clip(found - skip, 0, cap), pick, 0)
    for g in range(groups):
        out_ref[g] = held_ref[:, g * rows : (g + 1) * rows].astype(BF16)


def own_source_rows(me, data_real, data_imag, source_cols, which, cap):
    rows, width = data_real.shape
    return pl.pallas_call(
        functools.partial(rows_kernel, cap),
        in_specs=[whole_smem()] * 3 + [anywhere()] * 2,
        out_specs=whole_vmem(),
        out_shape=jax.ShapeDtypeStruct((width // rows, 2 * cap, rows), BF16),
        scratch_shapes=[
            pltpu.SMEM((cap,), jnp.int32),
            pltpu.VMEM((cap, 2, GROUP, width), BF16),
            pltpu.VMEM((2 * cap, width), F32),
            pltpu.SemaphoreType.DMA((cap, 2)),
        ],
        compiler_params=params(24),
        cost_estimate=cost(0, 2 * cap * width),
        name="own_source_rows",
    )(which, me, source_cols, data_real, data_imag)


def cols_kernel(real_ref, imag_ref, row_ref, out_ref, acc_ref):
    rows, step = real_ref.shape
    count = row_ref.shape[1]
    t = pl.program_id(0)

    @pl.when(t == 0)
    def _():
        acc_ref[...] = jnp.zeros_like(acc_ref)

    place = lax.broadcasted_iota(jnp.int32, (step, count), 0) + t * step
    pick = (place == row_ref[...]).astype(F32).astype(BF16)
    acc_ref[:, :count] += dot(real_ref[...], pick)
    acc_ref[:, count:] += dot(imag_ref[...], pick)

    @pl.when(t == pl.num_programs(0) - 1)
    def _():
        out_ref[...] = jnp.transpose(acc_ref[...]).astype(BF16)


def own_source_cols(data_real, data_imag, row, step):
    rows, width = data_real.shape
    count = row.shape[1]
    block = pl.BlockSpec((rows, step), lambda t: (0, t))
    return pl.pallas_call(
        cols_kernel,
        grid=(width // step,),
        in_specs=[block, block, whole_vmem()],
        out_specs=pl.BlockSpec((2 * count, rows), lambda t: (0, 0)),
        out_shape=jax.ShapeDtypeStruct((2 * count, rows), BF16),
        scratch_shapes=[pltpu.VMEM((rows, 2 * count), F32)],
        compiler_params=params(),
        cost_estimate=cost(4 * rows * width * count, 4 * rows * width),
        name="own_source_cols",
    )(data_real, data_imag, row)


def select_kernel(cap, round_ref, got_ref, col_ref, out_ref):
    out_ref[...] = pick_rows(cap, round_ref[0], got_ref, col_ref).astype(BF16)


def select_rows(got, col, which, cap):
    groups, _, rows = got.shape
    count = col.shape[0]
    return pl.pallas_call(
        functools.partial(select_kernel, cap),
        in_specs=[whole_smem(), whole_vmem(), whole_vmem()],
        out_specs=whole_vmem(),
        out_shape=jax.ShapeDtypeStruct((2 * count, rows), BF16),
        compiler_params=params(),
        cost_estimate=cost(8 * count * groups * cap * rows, 4 * groups * cap * rows),
        name="select_rows",
    )(which, got, col)


def pick_rows(cap, which, got_ref, col_ref):
    groups, _, rows = got_ref.shape
    count = col_ref.shape[0]
    col = col_ref[...]
    slot = ranks_of(col, rows) - which * cap
    inside = (slot >= 0) & (slot < cap)
    place = jnp.where(inside, (col // rows) * (2 * cap) + slot, -1)
    lanes = lax.broadcasted_iota(jnp.int32, (count, groups * 2 * cap), 1)
    pick = jnp.concatenate([lanes == place, lanes == jnp.where(inside, place + cap, -1)], axis=0)
    got = got_ref[...].reshape(groups * 2 * cap, rows)
    return dot(pick.astype(F32).astype(BF16), got)


def own_panel(width, mine, counts_ref, rowpart_ref, colpart_ref, col_ref):
    tile = width // TILES
    tiles = col_ref[...] // tile
    forward = jnp.zeros_like(tiles)
    backward = jnp.zeros_like(tiles)
    for t in range(TILES):
        forward = jnp.where(tiles == t, counts_ref[mine, t], forward)
        backward = jnp.where(tiles == t, counts_ref[t, mine], backward)
    forward = jnp.concatenate([forward, forward], axis=0).astype(F32)
    backward = jnp.concatenate([backward, backward], axis=0).astype(F32)
    own = colpart_ref[...].astype(F32)
    mirror = rowpart_ref[...].astype(F32)
    return (forward * own + backward * mirror) / jnp.maximum(forward + backward, 1.0)


def store_panel(panel, panel_ref, panel_t_ref):
    double, rows = panel.shape
    count = double // 2
    panel_t_ref[:, :rows] = panel.astype(BF16)
    panel_t_ref[:count, rows:] = (-panel[count:]).astype(BF16)
    panel_t_ref[count:, rows:] = panel[:count].astype(BF16)
    panel_ref[...] = jnp.transpose(panel).astype(BF16)


def panel_kernel(
    width, me_ref, counts_ref, rowpart_ref, colpart_ref, col_ref, panel_ref, panel_t_ref
):
    mine = me_ref[0] * rowpart_ref.shape[1] // (width // TILES)
    panel = own_panel(width, mine, counts_ref, rowpart_ref, colpart_ref, col_ref)
    store_panel(panel, panel_ref, panel_t_ref)


def panel_only(me, counts, rowpart, colpart, col, width):
    double, rows = colpart.shape
    return pl.pallas_call(
        functools.partial(panel_kernel, width),
        in_specs=[whole_smem()] * 2 + [whole_vmem()] * 3,
        out_specs=[whole_vmem()] * 2,
        out_shape=[
            jax.ShapeDtypeStruct((rows, double), BF16),
            jax.ShapeDtypeStruct((double, 2 * rows), BF16),
        ],
        compiler_params=params(),
        cost_estimate=cost(8 * rows * double, 8 * rows * double),
        name="panel_only",
    )(me, counts, rowpart, colpart, col)


def weight(counts_ref, mine, other, shape):
    forward = jnp.full(shape, counts_ref[mine, other], jnp.int32).astype(F32)
    backward = jnp.full(shape, counts_ref[other, mine], jnp.int32).astype(F32)
    return forward / jnp.maximum(forward + backward, 1.0)


def mirror_block(real, imag, panel_t):
    rows = real.shape[0]
    return dot(panel_t[:, :rows], real) + dot(panel_t[:, rows:], imag)


def direct_block(real, imag, panel):
    count = panel.shape[1] // 2
    turned = jnp.concatenate([-panel[:, count:], panel[:, :count]], axis=1)
    return dot(real, panel) + dot(imag, turned)


def mirror_kernel(width, me_ref, counts_ref, real_ref, imag_ref, panel_t_ref, out_ref):
    rows, tile = real_ref.shape
    mine = me_ref[0] * rows // tile
    found = mirror_block(real_ref[...], imag_ref[...], panel_t_ref[...])
    found = found * weight(counts_ref, mine, pl.program_id(0), (1, tile))
    for g in range(out_ref.shape[0]):
        out_ref[g] = found[:, g * rows : (g + 1) * rows]


def mirror_term(me, counts, data_real, data_imag, panel_t):
    rows, width = data_real.shape
    double = panel_t.shape[0]
    tile = width // TILES
    block = pl.BlockSpec((rows, tile), lambda t: (0, t))
    return pl.pallas_call(
        functools.partial(mirror_kernel, width),
        grid=(TILES,),
        in_specs=[whole_smem()] * 2 + [block, block, whole_vmem()],
        out_specs=pl.BlockSpec((tile // rows, double, rows), lambda t: (t, 0, 0)),
        out_shape=jax.ShapeDtypeStruct((width // rows, double, rows), F32),
        compiler_params=params(32),
        cost_estimate=cost(4 * rows * width * double, 4 * rows * width + 2 * double * width),
        name="mirror_term",
    )(me, counts, data_real, data_imag, panel_t)


def direct_kernel(width, me_ref, counts_ref, real_ref, imag_ref, panel_ref, out_ref):
    rows, tile = real_ref.shape
    mine = me_ref[0] * rows // tile
    t = pl.program_id(0)

    @pl.when(t == 0)
    def _():
        out_ref[...] = jnp.zeros_like(out_ref)

    found = direct_block(real_ref[...], imag_ref[...], panel_ref[...])
    out_ref[...] += found * weight(counts_ref, mine, t, (1, out_ref.shape[1]))


def direct_term(me, counts, data_real, data_imag, panel):
    rows, width = data_real.shape
    double = panel.shape[1]
    tile = width // TILES
    block = pl.BlockSpec((rows, tile), lambda t: (0, t))
    return pl.pallas_call(
        functools.partial(direct_kernel, width),
        grid=(TILES,),
        in_specs=[whole_smem()] * 2 + [block, block, pl.BlockSpec((tile, double), lambda t: (t, 0))],
        out_specs=pl.BlockSpec((rows, double), lambda t: (0, 0)),
        out_shape=jax.ShapeDtypeStruct((rows, double), F32),
        compiler_params=params(),
        cost_estimate=cost(4 * rows * width * double, 4 * rows * width + 2 * double * width),
        name="direct_term",
    )(me, counts, data_real, data_imag, panel)


def swap(value, mask):
    return lax.ppermute(value, AXIS, [(i, i ^ mask) for i in range(lax.axis_size(AXIS))])


def picked(masks, i):
    mask = masks[0]
    for at in range(1, len(masks)):
        mask = jnp.where(i == at, masks[at], mask)
    return mask


def mirror_part_kernel(width, masks, first, me_ref, counts_ref, real_ref, imag_ref, *refs):
    other_ref, near_ref, far_ref, held_ref, sems = refs[-5:]
    panel_t_ref = refs[4] if first else refs[0]
    rows = real_ref.shape[0]
    tile = width // TILES
    me = me_ref[0]
    dy, i = pl.program_id(0), pl.program_id(1)
    some = len(masks)
    mine = me * rows // tile

    def copies(at, mask):
        columns = pl.ds(pl.multiple_of((me ^ mask) // 2 * (2 * rows), 2 * rows), 2 * rows)
        return [
            pltpu.make_async_copy(
                ref.at[:, columns], held_ref.at[at, pl.ds(part * rows, rows)], sems.at[at, part]
            )
            for part, ref in enumerate((real_ref, imag_ref))
        ]

    @pl.when((dy == 0) & (i == 0))
    def _():
        for at in range(2 * some):
            for copy in copies(at, masks[at % some] ^ (2 * (at // some))):
                copy.start()
        if first:
            store_panel(own_panel(width, mine, counts_ref, *refs[:3]), refs[3], panel_t_ref)

    panel_t = panel_t_ref[...]
    at = dy * some + i
    mask = picked(masks, i) ^ (2 * dy)
    for copy in copies(at, mask):
        copy.wait()

    def term(turn):
        block = me ^ mask ^ turn
        scale = weight(counts_ref, mine, block * rows // tile, (1, rows))
        columns = pl.ds(pl.multiple_of(block % 2 * rows, rows), rows)
        return dot(panel_t, held_ref[at, :, columns]) * scale

    other_ref[0] = term(1).astype(BF16)

    @pl.when(dy == 0)
    def _():
        near_ref[0] = term(0)

    @pl.when(dy == 1)
    def _():
        far_ref[0] = term(0)


def mirror_part(me, counts, data_real, data_imag, panel, masks, after):
    rows, width = data_real.shape
    first = len(panel) == 3
    double = panel[0].shape[0]
    some = len(masks)
    shape = (1, double, rows)
    whole = lambda *dims: pl.BlockSpec(dims, lambda dy, i, me: (0,) * len(dims))
    spec = pltpu.PrefetchScalarGridSpec(
        num_scalar_prefetch=1,
        grid=(2, some),
        in_specs=[whole_smem(), anywhere(), anywhere()]
        + [whole_vmem()] * len(panel)
        + [anywhere()] * len(after),
        out_specs=([whole(rows, double), whole(double, 2 * rows)] if first else [])
        + [
            pl.BlockSpec(shape, lambda dy, i, me: (dy * some + i, 0, 0)),
            pl.BlockSpec(shape, lambda dy, i, me: (jnp.where(dy == 0, i, some - 1), 0, 0)),
            pl.BlockSpec(shape, lambda dy, i, me: (jnp.where(dy == 0, 0, i), 0, 0)),
        ],
        scratch_shapes=[
            pltpu.VMEM((2 * some, 2 * rows, 2 * rows), BF16),
            pltpu.SemaphoreType.DMA((2 * some, 2)),
        ],
    )
    panel_shapes = [
        jax.ShapeDtypeStruct((rows, double), BF16),
        jax.ShapeDtypeStruct((double, 2 * rows), BF16),
    ]
    return pl.pallas_call(
        functools.partial(mirror_part_kernel, width, masks, first),
        grid_spec=spec,
        out_shape=(panel_shapes if first else [])
        + [
            jax.ShapeDtypeStruct((2 * some, double, rows), BF16),
            jax.ShapeDtypeStruct((some, double, rows), F32),
            jax.ShapeDtypeStruct((some, double, rows), F32),
        ],
        compiler_params=params(24),
        cost_estimate=cost(MIRROR_COST, 0),
        name="mirror_part",
    )(me, counts, data_real, data_imag, *panel, *after)


def ordered(value, after):
    return lax.optimization_barrier((value, after))[0]


def direct_part_kernel(
    width, masks, mirrors, me_ref, counts_ref, real_ref, imag_ref, panel_ref, *refs
):
    rows = real_ref.shape[0]
    tile = width // TILES
    k = pl.program_id(0)
    mine = me_ref[0] * rows // tile
    block = me_ref[0] ^ picked(masks, k)
    scale = weight(counts_ref, mine, block * rows // tile, (1, panel_ref.shape[2]))
    found = direct_block(real_ref[...], imag_ref[...], panel_ref[0]) * scale
    sum_refs, (total_ref, *out_refs) = (refs[:-3], refs[-1:] + refs[-3:-1]) if mirrors else (
        refs[:-1],
        refs[-1:],
    )

    @pl.when(k == 0)
    def _():
        total = found
        if mirrors:
            mirror = sum_refs[-1][...].astype(F32)
            for ref in sum_refs[1:-1]:
                mirror += ref[...].astype(F32)
            total += jnp.transpose(mirror)
        total_ref[...] = total + sum_refs[0][...] if sum_refs else total

    @pl.when(k > 0)
    def _():
        total_ref[...] += found

    if mirrors:
        factor = -1.0 / math.sqrt(width)
        count = panel_ref.shape[2] // 2

        @pl.when(k == len(masks) - 1)
        def _():
            out_refs[0][...] = factor * total_ref[:, :count]
            out_refs[1][...] = factor * total_ref[:, count:]


def direct_part(me, counts, data_real, data_imag, panels, before, masks, mirrors=()):
    rows, width = data_real.shape
    double = panels.shape[2]
    block = pl.BlockSpec((rows, rows), lambda k, me: (0, me[0] ^ picked(masks, k)))
    outs = [(rows, double // 2)] * 2 if mirrors else [(rows, double)]
    spec = pltpu.PrefetchScalarGridSpec(
        num_scalar_prefetch=1,
        grid=(len(masks),),
        in_specs=[whole_smem(), block, block, pl.BlockSpec((1, rows, double), lambda k, me: (k, 0, 0))]
        + [whole_vmem()] * (len(before) + len(mirrors)),
        out_specs=[pl.BlockSpec(shape, lambda k, me: (0, 0)) for shape in outs],
        scratch_shapes=[pltpu.VMEM((rows, double), F32)] if mirrors else [],
    )
    return pl.pallas_call(
        functools.partial(direct_part_kernel, width, masks, bool(mirrors)),
        grid_spec=spec,
        out_shape=[jax.ShapeDtypeStruct(shape, F32) for shape in outs],
        compiler_params=params(),
        cost_estimate=cost(DIRECT_COST, 0),
        name="direct_part",
    )(me, counts, data_real, data_imag, panels, *before, *mirrors)


def levels(me, counts, data_real, data_imag, rowpart, colpart, col):
    data = (in_hbm(data_real), in_hbm(data_imag))
    panel, panel_t, other, own, own_far = mirror_part(
        me, counts, *data, [rowpart, colpart, col], (HIGH, HIGH | LOW), []
    )
    high, low, beside = swap(panel, HIGH), swap(panel, LOW), swap(panel, Y)

    def to_y(other, own):
        got = swap(other, CORE)
        some = own.shape[0]
        return (own + got[some:].astype(F32)).astype(BF16), got[:some]

    def over_y(sent, own, got):
        return own + got.astype(F32) + swap(sent, Y).astype(F32)

    sent, got = to_y(other, own_far)
    other_here, own_here, own_here_far = mirror_part(me, counts, *data, [panel_t], (0, LOW), [sent])
    total = over_y(sent, own, got)
    to_low = total[1].astype(BF16)

    low, high, beside = ordered([low, high, beside], [sent, own_here])
    direct = []

    def add(panels, masks, mirrors=()):
        direct[:] = direct_part(me, counts, *data, panels, direct, masks, mirrors)

    add(ordered(panel[None], high), (0,))
    sent, got = to_y(ordered(other_here, high), ordered(own_here_far, high))
    total = total[0] + ordered(swap(to_low, LOW), [sent]).astype(F32)
    mirrors = [swap(total.astype(BF16), HIGH)]
    beside_two = ordered(swap(jnp.stack([low, high]), Y), [sent, total])
    both = ordered(swap(high, LOW), [sent, to_low])
    column = jnp.stack([panel, low, high, both])
    late = swap(ordered(both[None], [sent]), Y)
    early = jnp.concatenate([beside[None], beside_two])
    add(
        jnp.concatenate([column[1:], early]),
        (LOW, HIGH, HIGH | LOW, Y, Y | LOW, Y | HIGH),
    )
    total = own_here + got.astype(F32) + swap(sent, Y).astype(F32)
    mirrors += [total[0], swap(total[1].astype(BF16), LOW)]
    add(swap(column, CORE), (CORE, CORE | LOW, CORE | HIGH, CORE | HIGH | LOW))
    add(swap(early, CORE), (Y | CORE, Y | CORE | LOW, Y | CORE | HIGH))
    late = ordered(late, direct + mirrors)
    add(late, (Y | HIGH | LOW,))
    add(swap(late, CORE), (Y | CORE | HIGH | LOW,), mirrors)
    return tuple(direct)


def finish_kernel(factor, direct_ref, mirror_ref, real_ref, imag_ref):
    count = real_ref.shape[1]
    total = factor * (direct_ref[...] + jnp.transpose(mirror_ref[...]))
    real_ref[...] = total[:, :count]
    imag_ref[...] = total[:, count:]


def finish(direct, mirror, width):
    rows, double = direct.shape
    shape = jax.ShapeDtypeStruct((rows, double // 2), F32)
    return pl.pallas_call(
        functools.partial(finish_kernel, -1.0 / math.sqrt(width)),
        in_specs=[whole_vmem()] * 2,
        out_specs=[whole_vmem()] * 2,
        out_shape=[shape, shape],
        compiler_params=params(),
        cost_estimate=cost(4 * rows * double, 10 * rows * double),
        name="finish",
    )(direct, mirror)


def shards(data_real, data_imag, counts, source_cols):
    rows, width = data_real.shape
    groups = width // rows
    count = source_cols.shape[0]
    cap = min(rows, count, -(-2 * count // groups // 8) * 8)
    col = source_cols.reshape(count, 1)
    row = source_cols.reshape(1, count)
    me = lax.axis_index(AXIS).reshape(1)

    def exchange(which):
        sent = own_source_rows(me, data_real, data_imag, source_cols, which, cap)
        return lax.all_to_all(sent, AXIS, split_axis=0, concat_axis=0)

    first = jnp.zeros((1,), jnp.int32)
    got = exchange(first)
    colpart = own_source_cols(data_real, data_imag, row, width // TILES)
    rowpart = select_rows(got, col, first, cap)

    owner = source_cols // rows
    most = jnp.max(jnp.sum(owner[:, None] == jnp.arange(groups)[None, :], axis=0, dtype=jnp.int32))

    def further(rowpart):
        def body(which, held):
            one = which.reshape(1)
            return held + select_rows(exchange(one), col, one, cap)

        return lax.fori_loop(1, (most + cap - 1) // cap, body, rowpart)

    rowpart = lax.cond(most > cap, further, lambda rowpart: rowpart, rowpart)
    if rows % 128 == 0 and groups == 16:
        return levels(me, counts, data_real, data_imag, rowpart, colpart, col)
    panel, panel_t = panel_only(me, counts, rowpart, colpart, col, width)
    full = lax.all_gather(panel, AXIS, axis=0, tiled=True)
    partial = mirror_term(me, counts, data_real, data_imag, panel_t)
    mirror = lax.psum_scatter(partial, AXIS, scatter_dimension=0, tiled=False)
    direct = direct_term(me, counts, data_real, data_imag, full)
    return tuple(finish(direct, mirror, width))


def solution(mesh):
    placed = (P(("freq", "row"), None), P(("freq", "row"), None), P(), P())
    return jax.shard_map(
        shards,
        mesh=mesh,
        in_specs=placed,
        out_specs=(P(("freq", "row"), None), P(("freq", "row"), None)),
        check_vma=False,
    )
```

```python
import functools
import math

import jax
import jax.numpy as jnp
from jax import lax
from jax.experimental import pallas as pl
from jax.experimental.pallas import tpu as pltpu
from jax.sharding import PartitionSpec as P

TILES = 8
AXIS = "row"
CORE, Y, LOW, HIGH = 1, 2, 4, 8
GROUP = 16
MIRROR_COST = 10000000000
DIRECT_COST = 2000000000
PIECE = 1024
F32 = jnp.float32
BF16 = jnp.bfloat16


def params(mib=16):
    return pltpu.CompilerParams(vmem_limit_bytes=mib * 1024 * 1024)


def whole_vmem():
    return pl.BlockSpec(memory_space=pltpu.VMEM)


def anywhere():
    return pl.BlockSpec(memory_space=pl.ANY)


def in_hbm(value):
    return pltpu.with_memory_space_constraint(value, pltpu.HBM)


def whole_smem():
    return pl.BlockSpec(memory_space=pltpu.SMEM)


def cost(flops, size):
    return pl.CostEstimate(flops=flops, bytes_accessed=size, transcendentals=0)


def dot(left, right):
    return jnp.dot(left, right, preferred_element_type=F32)


def ranks_of(col, rows):
    count = col.shape[0]
    owner = col // rows
    owner_row = jnp.transpose(jnp.broadcast_to(owner.astype(F32), (count, count))).astype(jnp.int32)
    before = lax.broadcasted_iota(jnp.int32, (count, count), 1) < lax.broadcasted_iota(
        jnp.int32, (count, count), 0
    )
    same = (owner_row == owner) & before
    return jnp.sum(same.astype(F32), axis=1, keepdims=True).astype(jnp.int32)


def rows_kernel(cap, round_ref, me_ref, col_ref, real_ref, imag_ref, out_ref, list_ref, near_ref, held_ref, sems):
    rows, width = real_ref.shape
    groups = out_ref.shape[0]
    count = col_ref.shape[0]
    base = me_ref[0] * rows
    skip = round_ref[0] * cap

    def copies(slot, local):
        group = pl.ds(pl.multiple_of(local // GROUP * GROUP, GROUP), GROUP)
        return [
            pltpu.make_async_copy(ref.at[group], near_ref.at[slot, part], sems.at[slot, part])
            for part, ref in enumerate((real_ref, imag_ref))
        ]

    def begin(s, found):
        local = col_ref[s] - base
        own = (local >= 0) & (local < rows)
        slot = found - skip

        @pl.when(own & (slot >= 0) & (slot < cap))
        def _():
            list_ref[slot] = local
            for copy in copies(slot, local):
                copy.start()

        return found + own.astype(jnp.int32)

    def pick(slot, _):
        local = list_ref[slot]
        chosen = lax.broadcasted_iota(jnp.int32, (GROUP, PIECE), 0) == local % GROUP
        for part, copy in enumerate(copies(slot, local)):
            copy.wait()
            for at in range(0, width, PIECE):
                group = near_ref[slot, part, :, at : at + PIECE].astype(F32)
                held_ref[pl.ds(part * cap + slot, 1), at : at + PIECE] = jnp.sum(
                    jnp.where(chosen, group, 0.0), axis=0, keepdims=True
                )
        return 0

    found = lax.fori_loop(0, count, begin, jnp.int32(0))
    held_ref[...] = jnp.zeros_like(held_ref)
    lax.fori_loop(0, jnp.clip(found - skip, 0, cap), pick, 0)
    for g in range(groups):
        out_ref[g] = held_ref[:, g * rows : (g + 1) * rows].astype(BF16)


def own_source_rows(me, data_real, data_imag, source_cols, which, cap):
    rows, width = data_real.shape
    return pl.pallas_call(
        functools.partial(rows_kernel, cap),
        in_specs=[whole_smem()] * 3 + [anywhere()] * 2,
        out_specs=whole_vmem(),
        out_shape=jax.ShapeDtypeStruct((width // rows, 2 * cap, rows), BF16),
        scratch_shapes=[
            pltpu.SMEM((cap,), jnp.int32),
            pltpu.VMEM((cap, 2, GROUP, width), BF16),
            pltpu.VMEM((2 * cap, width), F32),
            pltpu.SemaphoreType.DMA((cap, 2)),
        ],
        compiler_params=params(24),
        cost_estimate=cost(0, 2 * cap * width),
        name="own_source_rows",
    )(which, me, source_cols, data_real, data_imag)


def cols_kernel(real_ref, imag_ref, row_ref, out_ref, acc_ref):
    rows, step = real_ref.shape
    count = row_ref.shape[1]
    t = pl.program_id(0)

    @pl.when(t == 0)
    def _():
        acc_ref[...] = jnp.zeros_like(acc_ref)

    place = lax.broadcasted_iota(jnp.int32, (step, count), 0) + t * step
    pick = (place == row_ref[...]).astype(F32).astype(BF16)
    acc_ref[:, :count] += dot(real_ref[...], pick)
    acc_ref[:, count:] += dot(imag_ref[...], pick)

    @pl.when(t == pl.num_programs(0) - 1)
    def _():
        out_ref[...] = jnp.transpose(acc_ref[...]).astype(BF16)


def own_source_cols(data_real, data_imag, row, step):
    rows, width = data_real.shape
    count = row.shape[1]
    block = pl.BlockSpec((rows, step), lambda t: (0, t))
    return pl.pallas_call(
        cols_kernel,
        grid=(width // step,),
        in_specs=[block, block, whole_vmem()],
        out_specs=pl.BlockSpec((2 * count, rows), lambda t: (0, 0)),
        out_shape=jax.ShapeDtypeStruct((2 * count, rows), BF16),
        scratch_shapes=[pltpu.VMEM((rows, 2 * count), F32)],
        compiler_params=params(),
        cost_estimate=cost(4 * rows * width * count, 4 * rows * width),
        name="own_source_cols",
    )(data_real, data_imag, row)


def select_kernel(cap, round_ref, got_ref, col_ref, out_ref):
    out_ref[...] = pick_rows(cap, round_ref[0], got_ref, col_ref).astype(BF16)


def select_rows(got, col, which, cap):
    groups, _, rows = got.shape
    count = col.shape[0]
    return pl.pallas_call(
        functools.partial(select_kernel, cap),
        in_specs=[whole_smem(), whole_vmem(), whole_vmem()],
        out_specs=whole_vmem(),
        out_shape=jax.ShapeDtypeStruct((2 * count, rows), BF16),
        compiler_params=params(),
        cost_estimate=cost(8 * count * groups * cap * rows, 4 * groups * cap * rows),
        name="select_rows",
    )(which, got, col)


def pick_rows(cap, which, got_ref, col_ref):
    groups, _, rows = got_ref.shape
    count = col_ref.shape[0]
    col = col_ref[...]
    slot = ranks_of(col, rows) - which * cap
    inside = (slot >= 0) & (slot < cap)
    place = jnp.where(inside, (col // rows) * (2 * cap) + slot, -1)
    lanes = lax.broadcasted_iota(jnp.int32, (count, groups * 2 * cap), 1)
    pick = jnp.concatenate([lanes == place, lanes == jnp.where(inside, place + cap, -1)], axis=0)
    got = got_ref[...].reshape(groups * 2 * cap, rows)
    return dot(pick.astype(F32).astype(BF16), got)


def own_panel(width, mine, counts_ref, rowpart_ref, colpart_ref, col_ref):
    tile = width // TILES
    tiles = col_ref[...] // tile
    forward = jnp.zeros_like(tiles)
    backward = jnp.zeros_like(tiles)
    for t in range(TILES):
        forward = jnp.where(tiles == t, counts_ref[mine, t], forward)
        backward = jnp.where(tiles == t, counts_ref[t, mine], backward)
    forward = jnp.concatenate([forward, forward], axis=0).astype(F32)
    backward = jnp.concatenate([backward, backward], axis=0).astype(F32)
    own = colpart_ref[...].astype(F32)
    mirror = rowpart_ref[...].astype(F32)
    return (forward * own + backward * mirror) / jnp.maximum(forward + backward, 1.0)


def store_panel(panel, panel_ref, panel_t_ref):
    double, rows = panel.shape
    count = double // 2
    panel_t_ref[:, :rows] = panel.astype(BF16)
    panel_t_ref[:count, rows:] = (-panel[count:]).astype(BF16)
    panel_t_ref[count:, rows:] = panel[:count].astype(BF16)
    panel_ref[...] = jnp.transpose(panel).astype(BF16)


def panel_kernel(
    width, me_ref, counts_ref, rowpart_ref, colpart_ref, col_ref, panel_ref, panel_t_ref
):
    mine = me_ref[0] * rowpart_ref.shape[1] // (width // TILES)
    panel = own_panel(width, mine, counts_ref, rowpart_ref, colpart_ref, col_ref)
    store_panel(panel, panel_ref, panel_t_ref)


def panel_only(me, counts, rowpart, colpart, col, width):
    double, rows = colpart.shape
    return pl.pallas_call(
        functools.partial(panel_kernel, width),
        in_specs=[whole_smem()] * 2 + [whole_vmem()] * 3,
        out_specs=[whole_vmem()] * 2,
        out_shape=[
            jax.ShapeDtypeStruct((rows, double), BF16),
            jax.ShapeDtypeStruct((double, 2 * rows), BF16),
        ],
        compiler_params=params(),
        cost_estimate=cost(8 * rows * double, 8 * rows * double),
        name="panel_only",
    )(me, counts, rowpart, colpart, col)


def weight(counts_ref, mine, other, shape):
    forward = jnp.full(shape, counts_ref[mine, other], jnp.int32).astype(F32)
    backward = jnp.full(shape, counts_ref[other, mine], jnp.int32).astype(F32)
    return forward / jnp.maximum(forward + backward, 1.0)


def mirror_block(real, imag, panel_t):
    rows = real.shape[0]
    return dot(panel_t[:, :rows], real) + dot(panel_t[:, rows:], imag)


def direct_block(real, imag, panel):
    count = panel.shape[1] // 2
    turned = jnp.concatenate([-panel[:, count:], panel[:, :count]], axis=1)
    return dot(real, panel) + dot(imag, turned)


def mirror_kernel(width, me_ref, counts_ref, real_ref, imag_ref, panel_t_ref, out_ref):
    rows, tile = real_ref.shape
    mine = me_ref[0] * rows // tile
    found = mirror_block(real_ref[...], imag_ref[...], panel_t_ref[...])
    found = found * weight(counts_ref, mine, pl.program_id(0), (1, tile))
    for g in range(out_ref.shape[0]):
        out_ref[g] = found[:, g * rows : (g + 1) * rows]


def mirror_term(me, counts, data_real, data_imag, panel_t):
    rows, width = data_real.shape
    double = panel_t.shape[0]
    tile = width // TILES
    block = pl.BlockSpec((rows, tile), lambda t: (0, t))
    return pl.pallas_call(
        functools.partial(mirror_kernel, width),
        grid=(TILES,),
        in_specs=[whole_smem()] * 2 + [block, block, whole_vmem()],
        out_specs=pl.BlockSpec((tile // rows, double, rows), lambda t: (t, 0, 0)),
        out_shape=jax.ShapeDtypeStruct((width // rows, double, rows), F32),
        compiler_params=params(32),
        cost_estimate=cost(4 * rows * width * double, 4 * rows * width + 2 * double * width),
        name="mirror_term",
    )(me, counts, data_real, data_imag, panel_t)


def direct_kernel(width, me_ref, counts_ref, real_ref, imag_ref, panel_ref, out_ref):
    rows, tile = real_ref.shape
    mine = me_ref[0] * rows // tile
    t = pl.program_id(0)

    @pl.when(t == 0)
    def _():
        out_ref[...] = jnp.zeros_like(out_ref)

    found = direct_block(real_ref[...], imag_ref[...], panel_ref[...])
    out_ref[...] += found * weight(counts_ref, mine, t, (1, out_ref.shape[1]))


def direct_term(me, counts, data_real, data_imag, panel):
    rows, width = data_real.shape
    double = panel.shape[1]
    tile = width // TILES
    block = pl.BlockSpec((rows, tile), lambda t: (0, t))
    return pl.pallas_call(
        functools.partial(direct_kernel, width),
        grid=(TILES,),
        in_specs=[whole_smem()] * 2 + [block, block, pl.BlockSpec((tile, double), lambda t: (t, 0))],
        out_specs=pl.BlockSpec((rows, double), lambda t: (0, 0)),
        out_shape=jax.ShapeDtypeStruct((rows, double), F32),
        compiler_params=params(),
        cost_estimate=cost(4 * rows * width * double, 4 * rows * width + 2 * double * width),
        name="direct_term",
    )(me, counts, data_real, data_imag, panel)


def swap(value, mask):
    return lax.ppermute(value, AXIS, [(i, i ^ mask) for i in range(lax.axis_size(AXIS))])


def picked(masks, i):
    mask = masks[0]
    for at in range(1, len(masks)):
        mask = jnp.where(i == at, masks[at], mask)
    return mask


def mirror_part_kernel(width, masks, first, me_ref, counts_ref, real_ref, imag_ref, *refs):
    other_ref, own_ref, held_ref, sems = refs[-4:]
    panel_t_ref = refs[4] if first else refs[0]
    rows = real_ref.shape[0]
    tile = width // TILES
    me = me_ref[0]
    i = pl.program_id(0)
    mine = me * rows // tile

    def copies(at, mask):
        columns = pl.ds(pl.multiple_of((me ^ mask) // 2 * (2 * rows), 2 * rows), 2 * rows)
        return [
            pltpu.make_async_copy(
                ref.at[:, columns], held_ref.at[at, pl.ds(part * rows, rows)], sems.at[at, part]
            )
            for part, ref in enumerate((real_ref, imag_ref))
        ]

    @pl.when(i == 0)
    def _():
        for at, mask in enumerate(masks):
            for copy in copies(at, mask):
                copy.start()
        if first:
            store_panel(own_panel(width, mine, counts_ref, *refs[:3]), refs[3], panel_t_ref)

    panel_t = panel_t_ref[...]
    mask = picked(masks, i)
    for copy in copies(i, mask):
        copy.wait()

    def term(turn):
        block = me ^ mask ^ turn
        scale = weight(counts_ref, mine, block * rows // tile, (1, rows))
        columns = pl.ds(pl.multiple_of(block % 2 * rows, rows), rows)
        return dot(panel_t, held_ref[i, :, columns]) * scale

    other_ref[0] = term(1).astype(BF16)
    own_ref[0] = term(0)


def mirror_part(me, counts, data_real, data_imag, panel, masks, after):
    rows, width = data_real.shape
    first = len(panel) == 3
    double = panel[0].shape[0]
    blocks = len(masks)
    shape = (1, double, rows)
    whole = lambda *dims: pl.BlockSpec(dims, lambda i, me: (0,) * len(dims))
    spec = pltpu.PrefetchScalarGridSpec(
        num_scalar_prefetch=1,
        grid=(blocks,),
        in_specs=[whole_smem(), anywhere(), anywhere()]
        + [whole_vmem()] * len(panel)
        + [anywhere()] * len(after),
        out_specs=([whole(rows, double), whole(double, 2 * rows)] if first else [])
        + [
            pl.BlockSpec(shape, lambda i, me: (i, 0, 0)),
            pl.BlockSpec(shape, lambda i, me: (i, 0, 0)),
        ],
        scratch_shapes=[
            pltpu.VMEM((blocks, 2 * rows, 2 * rows), BF16),
            pltpu.SemaphoreType.DMA((blocks, 2)),
        ],
    )
    panel_shapes = [
        jax.ShapeDtypeStruct((rows, double), BF16),
        jax.ShapeDtypeStruct((double, 2 * rows), BF16),
    ]
    return pl.pallas_call(
        functools.partial(mirror_part_kernel, width, masks, first),
        grid_spec=spec,
        out_shape=(panel_shapes if first else [])
        + [
            jax.ShapeDtypeStruct((blocks, double, rows), BF16),
            jax.ShapeDtypeStruct((blocks, double, rows), F32),
        ],
        compiler_params=params(32),
        cost_estimate=cost(MIRROR_COST, 0),
        name="mirror_part",
    )(me, counts, data_real, data_imag, *panel, *after)


def ordered(value, after):
    return lax.optimization_barrier((value, after))[0]


def direct_part_kernel(
    width, masks, mirrors, me_ref, counts_ref, real_ref, imag_ref, panel_ref, *refs
):
    rows = real_ref.shape[0]
    tile = width // TILES
    k = pl.program_id(0)
    mine = me_ref[0] * rows // tile
    block = me_ref[0] ^ picked(masks, k)
    scale = weight(counts_ref, mine, block * rows // tile, (1, panel_ref.shape[2]))
    found = direct_block(real_ref[...], imag_ref[...], panel_ref[0]) * scale
    sum_refs, (total_ref, *out_refs) = (refs[:-3], refs[-1:] + refs[-3:-1]) if mirrors else (
        refs[:-1],
        refs[-1:],
    )

    @pl.when(k == 0)
    def _():
        total = found
        if mirrors:
            mirror = sum_refs[-1][...].astype(F32)
            for ref in sum_refs[1:-1]:
                mirror += ref[...].astype(F32)
            total += jnp.transpose(mirror)
        total_ref[...] = total + sum_refs[0][...] if sum_refs else total

    @pl.when(k > 0)
    def _():
        total_ref[...] += found

    if mirrors:
        factor = -1.0 / math.sqrt(width)
        count = panel_ref.shape[2] // 2

        @pl.when(k == len(masks) - 1)
        def _():
            out_refs[0][...] = factor * total_ref[:, :count]
            out_refs[1][...] = factor * total_ref[:, count:]


def direct_part(me, counts, data_real, data_imag, panels, before, masks, mirrors=()):
    rows, width = data_real.shape
    double = panels.shape[2]
    block = pl.BlockSpec((rows, rows), lambda k, me: (0, me[0] ^ picked(masks, k)))
    outs = [(rows, double // 2)] * 2 if mirrors else [(rows, double)]
    spec = pltpu.PrefetchScalarGridSpec(
        num_scalar_prefetch=1,
        grid=(len(masks),),
        in_specs=[whole_smem(), block, block, pl.BlockSpec((1, rows, double), lambda k, me: (k, 0, 0))]
        + [whole_vmem()] * (len(before) + len(mirrors)),
        out_specs=[pl.BlockSpec(shape, lambda k, me: (0, 0)) for shape in outs],
        scratch_shapes=[pltpu.VMEM((rows, double), F32)] if mirrors else [],
    )
    return pl.pallas_call(
        functools.partial(direct_part_kernel, width, masks, bool(mirrors)),
        grid_spec=spec,
        out_shape=[jax.ShapeDtypeStruct(shape, F32) for shape in outs],
        compiler_params=params(),
        cost_estimate=cost(DIRECT_COST, 0),
        name="direct_part",
    )(me, counts, data_real, data_imag, panels, *before, *mirrors)


def levels(me, counts, data_real, data_imag, rowpart, colpart, col):
    data = (in_hbm(data_real), in_hbm(data_imag))
    panel, panel_t, other, own = mirror_part(
        me, counts, *data, [rowpart, colpart, col], (Y | HIGH, Y | HIGH | LOW), []
    )
    high, low, beside = swap(panel, HIGH), swap(panel, LOW), swap(panel, Y)
    far_sent = (own + swap(other, CORE).astype(F32)).astype(BF16)
    def part(masks, after):
        return mirror_part(me, counts, *data, [panel_t], masks, after)

    far_other, far_own = part((HIGH, HIGH | LOW), [far_sent])
    other, own = part((0, LOW, Y, Y | LOW), [far_own])
    arrived = swap(far_sent, Y).astype(F32)

    low, high, beside = ordered([low, high, beside], [far_sent, own])
    direct = []

    def add(panels, masks, mirrors=()):
        direct[:] = direct_part(me, counts, *data, panels, direct, masks, mirrors)

    add(ordered(panel[None], high), (0,))
    own = ordered(own, high)
    got = swap(ordered(other, high), CORE)
    sent = (own[2:] + got[2:].astype(F32)).astype(BF16)
    total = far_own + swap(far_other, CORE).astype(F32) + arrived
    to_low = total[1].astype(BF16)
    total = total[0] + ordered(swap(to_low, LOW), [sent]).astype(F32)
    mirrors = [swap(total.astype(BF16), HIGH)]

    low_beside = ordered(swap(low, Y), [sent, total])
    both = ordered(swap(high, LOW), [sent, to_low])
    column = jnp.stack([panel, low, high, both])
    late = swap(ordered(jnp.stack([high, both]), [sent]), Y)
    early = jnp.stack([beside, low_beside])
    add(jnp.concatenate([column[1:], early]), (LOW, HIGH, HIGH | LOW, Y, Y | LOW))
    add(swap(column, CORE), (CORE, CORE | LOW, CORE | HIGH, CORE | HIGH | LOW))
    total = own[:2] + got[:2].astype(F32) + swap(sent, Y).astype(F32)
    mirrors += [total[0], swap(total[1].astype(BF16), LOW)]
    add(swap(early, CORE), (Y | CORE, Y | CORE | LOW))
    late = ordered(late, direct + mirrors)
    add(late, (Y | HIGH, Y | HIGH | LOW))
    add(swap(late, CORE), (Y | CORE | HIGH, Y | CORE | HIGH | LOW), mirrors)
    return tuple(direct)


def finish_kernel(factor, direct_ref, mirror_ref, real_ref, imag_ref):
    count = real_ref.shape[1]
    total = factor * (direct_ref[...] + jnp.transpose(mirror_ref[...]))
    real_ref[...] = total[:, :count]
    imag_ref[...] = total[:, count:]


def finish(direct, mirror, width):
    rows, double = direct.shape
    shape = jax.ShapeDtypeStruct((rows, double // 2), F32)
    return pl.pallas_call(
        functools.partial(finish_kernel, -1.0 / math.sqrt(width)),
        in_specs=[whole_vmem()] * 2,
        out_specs=[whole_vmem()] * 2,
        out_shape=[shape, shape],
        compiler_params=params(),
        cost_estimate=cost(4 * rows * double, 10 * rows * double),
        name="finish",
    )(direct, mirror)


def shards(data_real, data_imag, counts, source_cols):
    rows, width = data_real.shape
    groups = width // rows
    count = source_cols.shape[0]
    cap = min(rows, count, -(-2 * count // groups // 8) * 8)
    col = source_cols.reshape(count, 1)
    row = source_cols.reshape(1, count)
    me = lax.axis_index(AXIS).reshape(1)

    def exchange(which):
        sent = own_source_rows(me, data_real, data_imag, source_cols, which, cap)
        return lax.all_to_all(sent, AXIS, split_axis=0, concat_axis=0)

    first = jnp.zeros((1,), jnp.int32)
    got = exchange(first)
    colpart = own_source_cols(data_real, data_imag, row, width // TILES)
    rowpart = select_rows(got, col, first, cap)

    owner = source_cols // rows
    most = jnp.max(jnp.sum(owner[:, None] == jnp.arange(groups)[None, :], axis=0, dtype=jnp.int32))

    def further(rowpart):
        def body(which, held):
            one = which.reshape(1)
            return held + select_rows(exchange(one), col, one, cap)

        return lax.fori_loop(1, (most + cap - 1) // cap, body, rowpart)

    rowpart = lax.cond(most > cap, further, lambda rowpart: rowpart, rowpart)
    if rows % 128 == 0 and groups == 16:
        return levels(me, counts, data_real, data_imag, rowpart, colpart, col)
    panel, panel_t = panel_only(me, counts, rowpart, colpart, col, width)
    full = lax.all_gather(panel, AXIS, axis=0, tiled=True)
    partial = mirror_term(me, counts, data_real, data_imag, panel_t)
    mirror = lax.psum_scatter(partial, AXIS, scatter_dimension=0, tiled=False)
    direct = direct_term(me, counts, data_real, data_imag, full)
    return tuple(finish(direct, mirror, width))


def solution(mesh):
    placed = (P(("freq", "row"), None), P(("freq", "row"), None), P(), P())
    return jax.shard_map(
        shards,
        mesh=mesh,
        in_specs=placed,
        out_specs=(P(("freq", "row"), None), P(("freq", "row"), None)),
        check_vma=False,
    )
```

```python
import functools
import math

import jax
import jax.numpy as jnp
from jax import lax
from jax.experimental import pallas as pl
from jax.experimental.pallas import tpu as pltpu
from jax.sharding import PartitionSpec as P

TILES = 8
AXIS = "row"
CORE, Y, LOW, HIGH = 1, 2, 4, 8
GROUP = 16
MIRROR_COST = 10000000000
DIRECT_COST = 2000000000
PIECE = 1024
F32 = jnp.float32
BF16 = jnp.bfloat16


def params(mib=16):
    return pltpu.CompilerParams(vmem_limit_bytes=mib * 1024 * 1024)


def whole_vmem():
    return pl.BlockSpec(memory_space=pltpu.VMEM)


def anywhere():
    return pl.BlockSpec(memory_space=pl.ANY)


def in_hbm(value):
    return pltpu.with_memory_space_constraint(value, pltpu.HBM)


def whole_smem():
    return pl.BlockSpec(memory_space=pltpu.SMEM)


def cost(flops, size):
    return pl.CostEstimate(flops=flops, bytes_accessed=size, transcendentals=0)


def dot(left, right):
    return jnp.dot(left, right, preferred_element_type=F32)


def ranks_of(col, rows):
    count = col.shape[0]
    owner = col // rows
    owner_row = jnp.transpose(jnp.broadcast_to(owner.astype(F32), (count, count))).astype(jnp.int32)
    before = lax.broadcasted_iota(jnp.int32, (count, count), 1) < lax.broadcasted_iota(
        jnp.int32, (count, count), 0
    )
    same = (owner_row == owner) & before
    return jnp.sum(same.astype(F32), axis=1, keepdims=True).astype(jnp.int32)


def rows_kernel(cap, round_ref, me_ref, col_ref, real_ref, imag_ref, out_ref, list_ref, near_ref, held_ref, sems):
    rows, width = real_ref.shape
    groups = out_ref.shape[0]
    count = col_ref.shape[0]
    base = me_ref[0] * rows
    skip = round_ref[0] * cap

    def copies(slot, local):
        group = pl.ds(pl.multiple_of(local // GROUP * GROUP, GROUP), GROUP)
        return [
            pltpu.make_async_copy(ref.at[group], near_ref.at[slot, part], sems.at[slot, part])
            for part, ref in enumerate((real_ref, imag_ref))
        ]

    def begin(s, found):
        local = col_ref[s] - base
        own = (local >= 0) & (local < rows)
        slot = found - skip

        @pl.when(own & (slot >= 0) & (slot < cap))
        def _():
            list_ref[slot] = local
            for copy in copies(slot, local):
                copy.start()

        return found + own.astype(jnp.int32)

    def pick(slot, _):
        local = list_ref[slot]
        chosen = lax.broadcasted_iota(jnp.int32, (GROUP, PIECE), 0) == local % GROUP
        for part, copy in enumerate(copies(slot, local)):
            copy.wait()
            for at in range(0, width, PIECE):
                group = near_ref[slot, part, :, at : at + PIECE].astype(F32)
                held_ref[pl.ds(part * cap + slot, 1), at : at + PIECE] = jnp.sum(
                    jnp.where(chosen, group, 0.0), axis=0, keepdims=True
                )
        return 0

    found = lax.fori_loop(0, count, begin, jnp.int32(0))
    held_ref[...] = jnp.zeros_like(held_ref)
    lax.fori_loop(0, jnp.clip(found - skip, 0, cap), pick, 0)
    for g in range(groups):
        out_ref[g] = held_ref[:, g * rows : (g + 1) * rows].astype(BF16)


def own_source_rows(me, data_real, data_imag, source_cols, which, cap):
    rows, width = data_real.shape
    return pl.pallas_call(
        functools.partial(rows_kernel, cap),
        in_specs=[whole_smem()] * 3 + [anywhere()] * 2,
        out_specs=whole_vmem(),
        out_shape=jax.ShapeDtypeStruct((width // rows, 2 * cap, rows), BF16),
        scratch_shapes=[
            pltpu.SMEM((cap,), jnp.int32),
            pltpu.VMEM((cap, 2, GROUP, width), BF16),
            pltpu.VMEM((2 * cap, width), F32),
            pltpu.SemaphoreType.DMA((cap, 2)),
        ],
        compiler_params=params(24),
        cost_estimate=cost(0, 2 * cap * width),
        name="own_source_rows",
    )(which, me, source_cols, data_real, data_imag)


def cols_kernel(real_ref, imag_ref, row_ref, out_ref, acc_ref):
    rows, step = real_ref.shape
    count = row_ref.shape[1]
    t = pl.program_id(0)

    @pl.when(t == 0)
    def _():
        acc_ref[...] = jnp.zeros_like(acc_ref)

    place = lax.broadcasted_iota(jnp.int32, (step, count), 0) + t * step
    pick = (place == row_ref[...]).astype(F32).astype(BF16)
    acc_ref[:, :count] += dot(real_ref[...], pick)
    acc_ref[:, count:] += dot(imag_ref[...], pick)

    @pl.when(t == pl.num_programs(0) - 1)
    def _():
        out_ref[...] = jnp.transpose(acc_ref[...]).astype(BF16)


def own_source_cols(data_real, data_imag, row, step):
    rows, width = data_real.shape
    count = row.shape[1]
    block = pl.BlockSpec((rows, step), lambda t: (0, t))
    return pl.pallas_call(
        cols_kernel,
        grid=(width // step,),
        in_specs=[block, block, whole_vmem()],
        out_specs=pl.BlockSpec((2 * count, rows), lambda t: (0, 0)),
        out_shape=jax.ShapeDtypeStruct((2 * count, rows), BF16),
        scratch_shapes=[pltpu.VMEM((rows, 2 * count), F32)],
        compiler_params=params(),
        cost_estimate=cost(4 * rows * width * count, 4 * rows * width),
        name="own_source_cols",
    )(data_real, data_imag, row)


def select_kernel(cap, round_ref, got_ref, col_ref, out_ref):
    out_ref[...] = pick_rows(cap, round_ref[0], got_ref, col_ref).astype(BF16)


def select_rows(got, col, which, cap):
    groups, _, rows = got.shape
    count = col.shape[0]
    return pl.pallas_call(
        functools.partial(select_kernel, cap),
        in_specs=[whole_smem(), whole_vmem(), whole_vmem()],
        out_specs=whole_vmem(),
        out_shape=jax.ShapeDtypeStruct((2 * count, rows), BF16),
        compiler_params=params(),
        cost_estimate=cost(8 * count * groups * cap * rows, 4 * groups * cap * rows),
        name="select_rows",
    )(which, got, col)


def pick_rows(cap, which, got_ref, col_ref):
    groups, _, rows = got_ref.shape
    count = col_ref.shape[0]
    col = col_ref[...]
    slot = ranks_of(col, rows) - which * cap
    inside = (slot >= 0) & (slot < cap)
    place = jnp.where(inside, (col // rows) * (2 * cap) + slot, -1)
    lanes = lax.broadcasted_iota(jnp.int32, (count, groups * 2 * cap), 1)
    pick = jnp.concatenate([lanes == place, lanes == jnp.where(inside, place + cap, -1)], axis=0)
    got = got_ref[...].reshape(groups * 2 * cap, rows)
    return dot(pick.astype(F32).astype(BF16), got)


def own_panel(width, mine, counts_ref, rowpart_ref, colpart_ref, col_ref):
    tile = width // TILES
    tiles = col_ref[...] // tile
    forward = jnp.zeros_like(tiles)
    backward = jnp.zeros_like(tiles)
    for t in range(TILES):
        forward = jnp.where(tiles == t, counts_ref[mine, t], forward)
        backward = jnp.where(tiles == t, counts_ref[t, mine], backward)
    forward = jnp.concatenate([forward, forward], axis=0).astype(F32)
    backward = jnp.concatenate([backward, backward], axis=0).astype(F32)
    own = colpart_ref[...].astype(F32)
    mirror = rowpart_ref[...].astype(F32)
    return (forward * own + backward * mirror) / jnp.maximum(forward + backward, 1.0)


def store_panel(panel, panel_ref, panel_t_ref):
    double, rows = panel.shape
    count = double // 2
    panel_t_ref[:, :rows] = panel.astype(BF16)
    panel_t_ref[:count, rows:] = (-panel[count:]).astype(BF16)
    panel_t_ref[count:, rows:] = panel[:count].astype(BF16)
    panel_ref[...] = jnp.transpose(panel).astype(BF16)


def panel_kernel(
    width, me_ref, counts_ref, rowpart_ref, colpart_ref, col_ref, panel_ref, panel_t_ref
):
    mine = me_ref[0] * rowpart_ref.shape[1] // (width // TILES)
    panel = own_panel(width, mine, counts_ref, rowpart_ref, colpart_ref, col_ref)
    store_panel(panel, panel_ref, panel_t_ref)


def panel_only(me, counts, rowpart, colpart, col, width):
    double, rows = colpart.shape
    return pl.pallas_call(
        functools.partial(panel_kernel, width),
        in_specs=[whole_smem()] * 2 + [whole_vmem()] * 3,
        out_specs=[whole_vmem()] * 2,
        out_shape=[
            jax.ShapeDtypeStruct((rows, double), BF16),
            jax.ShapeDtypeStruct((double, 2 * rows), BF16),
        ],
        compiler_params=params(),
        cost_estimate=cost(8 * rows * double, 8 * rows * double),
        name="panel_only",
    )(me, counts, rowpart, colpart, col)


def weight(counts_ref, mine, other, shape):
    forward = jnp.full(shape, counts_ref[mine, other], jnp.int32).astype(F32)
    backward = jnp.full(shape, counts_ref[other, mine], jnp.int32).astype(F32)
    return forward / jnp.maximum(forward + backward, 1.0)


def mirror_block(real, imag, panel_t):
    rows = real.shape[0]
    return dot(panel_t[:, :rows], real) + dot(panel_t[:, rows:], imag)


def direct_block(real, imag, panel):
    count = panel.shape[1] // 2
    turned = jnp.concatenate([-panel[:, count:], panel[:, :count]], axis=1)
    return dot(real, panel) + dot(imag, turned)


def mirror_kernel(width, me_ref, counts_ref, real_ref, imag_ref, panel_t_ref, out_ref):
    rows, tile = real_ref.shape
    mine = me_ref[0] * rows // tile
    found = mirror_block(real_ref[...], imag_ref[...], panel_t_ref[...])
    found = found * weight(counts_ref, mine, pl.program_id(0), (1, tile))
    for g in range(out_ref.shape[0]):
        out_ref[g] = found[:, g * rows : (g + 1) * rows]


def mirror_term(me, counts, data_real, data_imag, panel_t):
    rows, width = data_real.shape
    double = panel_t.shape[0]
    tile = width // TILES
    block = pl.BlockSpec((rows, tile), lambda t: (0, t))
    return pl.pallas_call(
        functools.partial(mirror_kernel, width),
        grid=(TILES,),
        in_specs=[whole_smem()] * 2 + [block, block, whole_vmem()],
        out_specs=pl.BlockSpec((tile // rows, double, rows), lambda t: (t, 0, 0)),
        out_shape=jax.ShapeDtypeStruct((width // rows, double, rows), F32),
        compiler_params=params(32),
        cost_estimate=cost(4 * rows * width * double, 4 * rows * width + 2 * double * width),
        name="mirror_term",
    )(me, counts, data_real, data_imag, panel_t)


def direct_kernel(width, me_ref, counts_ref, real_ref, imag_ref, panel_ref, out_ref):
    rows, tile = real_ref.shape
    mine = me_ref[0] * rows // tile
    t = pl.program_id(0)

    @pl.when(t == 0)
    def _():
        out_ref[...] = jnp.zeros_like(out_ref)

    found = direct_block(real_ref[...], imag_ref[...], panel_ref[...])
    out_ref[...] += found * weight(counts_ref, mine, t, (1, out_ref.shape[1]))


def direct_term(me, counts, data_real, data_imag, panel):
    rows, width = data_real.shape
    double = panel.shape[1]
    tile = width // TILES
    block = pl.BlockSpec((rows, tile), lambda t: (0, t))
    return pl.pallas_call(
        functools.partial(direct_kernel, width),
        grid=(TILES,),
        in_specs=[whole_smem()] * 2 + [block, block, pl.BlockSpec((tile, double), lambda t: (t, 0))],
        out_specs=pl.BlockSpec((rows, double), lambda t: (0, 0)),
        out_shape=jax.ShapeDtypeStruct((rows, double), F32),
        compiler_params=params(),
        cost_estimate=cost(4 * rows * width * double, 4 * rows * width + 2 * double * width),
        name="direct_term",
    )(me, counts, data_real, data_imag, panel)


def swap(value, mask):
    return lax.ppermute(value, AXIS, [(i, i ^ mask) for i in range(lax.axis_size(AXIS))])


def picked(masks, i):
    mask = masks[0]
    for at in range(1, len(masks)):
        mask = jnp.where(i == at, masks[at], mask)
    return mask


def mirror_part_kernel(width, masks, first, me_ref, counts_ref, real_ref, imag_ref, *refs):
    other_ref, own_ref, held_ref, sems = refs[-4:]
    panel_t_ref = refs[4] if first else refs[0]
    rows = real_ref.shape[0]
    tile = width // TILES
    me = me_ref[0]
    i = pl.program_id(0)
    mine = me * rows // tile

    def copies(at, mask):
        columns = pl.ds(pl.multiple_of((me ^ mask) // 2 * (2 * rows), 2 * rows), 2 * rows)
        return [
            pltpu.make_async_copy(
                ref.at[:, columns], held_ref.at[at, pl.ds(part * rows, rows)], sems.at[at, part]
            )
            for part, ref in enumerate((real_ref, imag_ref))
        ]

    @pl.when(i == 0)
    def _():
        for at, mask in enumerate(masks):
            for copy in copies(at, mask):
                copy.start()
        if first:
            store_panel(own_panel(width, mine, counts_ref, *refs[:3]), refs[3], panel_t_ref)

    panel_t = panel_t_ref[...]
    mask = picked(masks, i)
    for copy in copies(i, mask):
        copy.wait()

    def term(turn):
        block = me ^ mask ^ turn
        scale = weight(counts_ref, mine, block * rows // tile, (1, rows))
        columns = pl.ds(pl.multiple_of(block % 2 * rows, rows), rows)
        return dot(panel_t, held_ref[i, :, columns]) * scale

    other_ref[0] = term(1).astype(BF16)
    own_ref[0] = term(0)


def mirror_part(me, counts, data_real, data_imag, panel, masks, after):
    rows, width = data_real.shape
    first = len(panel) == 3
    double = panel[0].shape[0]
    blocks = len(masks)
    shape = (1, double, rows)
    whole = lambda *dims: pl.BlockSpec(dims, lambda i, me: (0,) * len(dims))
    spec = pltpu.PrefetchScalarGridSpec(
        num_scalar_prefetch=1,
        grid=(blocks,),
        in_specs=[whole_smem(), anywhere(), anywhere()]
        + [whole_vmem()] * len(panel)
        + [anywhere()] * len(after),
        out_specs=([whole(rows, double), whole(double, 2 * rows)] if first else [])
        + [
            pl.BlockSpec(shape, lambda i, me: (i, 0, 0)),
            pl.BlockSpec(shape, lambda i, me: (i, 0, 0)),
        ],
        scratch_shapes=[
            pltpu.VMEM((blocks, 2 * rows, 2 * rows), BF16),
            pltpu.SemaphoreType.DMA((blocks, 2)),
        ],
    )
    panel_shapes = [
        jax.ShapeDtypeStruct((rows, double), BF16),
        jax.ShapeDtypeStruct((double, 2 * rows), BF16),
    ]
    return pl.pallas_call(
        functools.partial(mirror_part_kernel, width, masks, first),
        grid_spec=spec,
        out_shape=(panel_shapes if first else [])
        + [
            jax.ShapeDtypeStruct((blocks, double, rows), BF16),
            jax.ShapeDtypeStruct((blocks, double, rows), F32),
        ],
        compiler_params=params(32),
        cost_estimate=cost(MIRROR_COST, 0),
        name="mirror_part",
    )(me, counts, data_real, data_imag, *panel, *after)


def ordered(value, after):
    return lax.optimization_barrier((value, after))[0]


def direct_part_kernel(
    width, masks, mirrors, me_ref, counts_ref, real_ref, imag_ref, panel_ref, *refs
):
    rows = real_ref.shape[0]
    tile = width // TILES
    k = pl.program_id(0)
    mine = me_ref[0] * rows // tile
    block = me_ref[0] ^ picked(masks, k)
    scale = weight(counts_ref, mine, block * rows // tile, (1, panel_ref.shape[2]))
    found = direct_block(real_ref[...], imag_ref[...], panel_ref[0]) * scale
    sum_refs, (total_ref, *out_refs) = (refs[:-3], refs[-1:] + refs[-3:-1]) if mirrors else (
        refs[:-1],
        refs[-1:],
    )

    @pl.when(k == 0)
    def _():
        total = found
        if mirrors:
            mirror = sum_refs[-1][...].astype(F32)
            for ref in sum_refs[1:-1]:
                mirror += ref[...].astype(F32)
            total += jnp.transpose(mirror)
        total_ref[...] = total + sum_refs[0][...] if sum_refs else total

    @pl.when(k > 0)
    def _():
        total_ref[...] += found

    if mirrors:
        factor = -1.0 / math.sqrt(width)
        count = panel_ref.shape[2] // 2

        @pl.when(k == len(masks) - 1)
        def _():
            out_refs[0][...] = factor * total_ref[:, :count]
            out_refs[1][...] = factor * total_ref[:, count:]


def direct_part(me, counts, data_real, data_imag, panels, before, masks, mirrors=()):
    rows, width = data_real.shape
    double = panels.shape[2]
    block = pl.BlockSpec((rows, rows), lambda k, me: (0, me[0] ^ picked(masks, k)))
    outs = [(rows, double // 2)] * 2 if mirrors else [(rows, double)]
    spec = pltpu.PrefetchScalarGridSpec(
        num_scalar_prefetch=1,
        grid=(len(masks),),
        in_specs=[whole_smem(), block, block, pl.BlockSpec((1, rows, double), lambda k, me: (k, 0, 0))]
        + [whole_vmem()] * (len(before) + len(mirrors)),
        out_specs=[pl.BlockSpec(shape, lambda k, me: (0, 0)) for shape in outs],
        scratch_shapes=[pltpu.VMEM((rows, double), F32)] if mirrors else [],
    )
    return pl.pallas_call(
        functools.partial(direct_part_kernel, width, masks, bool(mirrors)),
        grid_spec=spec,
        out_shape=[jax.ShapeDtypeStruct(shape, F32) for shape in outs],
        compiler_params=params(),
        cost_estimate=cost(DIRECT_COST, 0),
        name="direct_part",
    )(me, counts, data_real, data_imag, panels, *before, *mirrors)


def levels(me, counts, data_real, data_imag, rowpart, colpart, col):
    data = (in_hbm(data_real), in_hbm(data_imag))
    panel, panel_t, other, own = mirror_part(
        me, counts, *data, [rowpart, colpart, col], (Y | HIGH, Y | HIGH | LOW), []
    )
    high, low, beside = swap(panel, HIGH), swap(panel, LOW), swap(panel, Y)
    far_sent = (own + swap(other, CORE).astype(F32)).astype(BF16)
    def part(masks, after):
        return mirror_part(me, counts, *data, [panel_t], masks, after)

    far_other, far_own = part((HIGH, HIGH | LOW), [far_sent])
    other, own = part((0, LOW, Y, Y | LOW), [far_own, beside])
    arrived = swap(far_sent, Y).astype(F32)

    low_beside = swap(beside, LOW)
    low, high, beside = ordered([low, high, beside], [far_sent, own])
    direct = []

    def add(panels, masks, mirrors=()):
        direct[:] = direct_part(me, counts, *data, panels, direct, masks, mirrors)

    add(ordered(panel[None], high), (0,))
    own = ordered(own, high)
    got = swap(ordered(other, high), CORE)
    sent = (own[2:] + got[2:].astype(F32)).astype(BF16)
    total = far_own + swap(far_other, CORE).astype(F32) + arrived
    to_low = total[1].astype(BF16)
    total = total[0] + ordered(swap(to_low, LOW), [sent]).astype(F32)
    mirrors = [swap(total.astype(BF16), HIGH)]

    low_beside = ordered(low_beside, [sent, total])
    both = ordered(swap(high, LOW), [sent, to_low])
    column = jnp.stack([panel, low, high, both])
    late = swap(ordered(jnp.stack([high, both]), [sent]), Y)
    early = jnp.stack([beside, low_beside])
    add(jnp.concatenate([column[1:], early]), (LOW, HIGH, HIGH | LOW, Y, Y | LOW))
    add(swap(column, CORE), (CORE, CORE | LOW, CORE | HIGH, CORE | HIGH | LOW))
    total = own[:2] + got[:2].astype(F32) + swap(sent, Y).astype(F32)
    mirrors += [total[0], swap(total[1].astype(BF16), LOW)]
    add(swap(early, CORE), (Y | CORE, Y | CORE | LOW))
    late = ordered(late, direct + mirrors)
    add(late, (Y | HIGH, Y | HIGH | LOW))
    add(swap(late, CORE), (Y | CORE | HIGH, Y | CORE | HIGH | LOW), mirrors)
    return tuple(direct)


def finish_kernel(factor, direct_ref, mirror_ref, real_ref, imag_ref):
    count = real_ref.shape[1]
    total = factor * (direct_ref[...] + jnp.transpose(mirror_ref[...]))
    real_ref[...] = total[:, :count]
    imag_ref[...] = total[:, count:]


def finish(direct, mirror, width):
    rows, double = direct.shape
    shape = jax.ShapeDtypeStruct((rows, double // 2), F32)
    return pl.pallas_call(
        functools.partial(finish_kernel, -1.0 / math.sqrt(width)),
        in_specs=[whole_vmem()] * 2,
        out_specs=[whole_vmem()] * 2,
        out_shape=[shape, shape],
        compiler_params=params(),
        cost_estimate=cost(4 * rows * double, 10 * rows * double),
        name="finish",
    )(direct, mirror)


def shards(data_real, data_imag, counts, source_cols):
    rows, width = data_real.shape
    groups = width // rows
    count = source_cols.shape[0]
    cap = min(rows, count, -(-2 * count // groups // 8) * 8)
    col = source_cols.reshape(count, 1)
    row = source_cols.reshape(1, count)
    me = lax.axis_index(AXIS).reshape(1)

    def exchange(which):
        sent = own_source_rows(me, data_real, data_imag, source_cols, which, cap)
        return lax.all_to_all(sent, AXIS, split_axis=0, concat_axis=0)

    first = jnp.zeros((1,), jnp.int32)
    got = exchange(first)
    colpart = own_source_cols(data_real, data_imag, row, width // TILES)
    rowpart = select_rows(got, col, first, cap)

    owner = source_cols // rows
    most = jnp.max(jnp.sum(owner[:, None] == jnp.arange(groups)[None, :], axis=0, dtype=jnp.int32))

    def further(rowpart):
        def body(which, held):
            one = which.reshape(1)
            return held + select_rows(exchange(one), col, one, cap)

        return lax.fori_loop(1, (most + cap - 1) // cap, body, rowpart)

    rowpart = lax.cond(most > cap, further, lambda rowpart: rowpart, rowpart)
    if rows % 128 == 0 and groups == 16:
        return levels(me, counts, data_real, data_imag, rowpart, colpart, col)
    panel, panel_t = panel_only(me, counts, rowpart, colpart, col, width)
    full = lax.all_gather(panel, AXIS, axis=0, tiled=True)
    partial = mirror_term(me, counts, data_real, data_imag, panel_t)
    mirror = lax.psum_scatter(partial, AXIS, scatter_dimension=0, tiled=False)
    direct = direct_term(me, counts, data_real, data_imag, full)
    return tuple(finish(direct, mirror, width))


def solution(mesh):
    placed = (P(("freq", "row"), None), P(("freq", "row"), None), P(), P())
    return jax.shard_map(
        shards,
        mesh=mesh,
        in_specs=placed,
        out_specs=(P(("freq", "row"), None), P(("freq", "row"), None)),
        check_vma=False,
    )
```

```python
import functools
import math

import jax
import jax.numpy as jnp
from jax import lax
from jax.experimental import pallas as pl
from jax.experimental.pallas import tpu as pltpu
from jax.sharding import PartitionSpec as P

TILES = 8
AXIS = "row"
CORE, Y, LOW, HIGH = 1, 2, 4, 8
GROUP = 16
MIRROR_COST = 10000000000
DIRECT_COST = 2000000000
PIECE = 1024
F32 = jnp.float32
BF16 = jnp.bfloat16


def params(mib=16):
    return pltpu.CompilerParams(vmem_limit_bytes=mib * 1024 * 1024)


def whole_vmem():
    return pl.BlockSpec(memory_space=pltpu.VMEM)


def anywhere():
    return pl.BlockSpec(memory_space=pl.ANY)


def in_hbm(value):
    return pltpu.with_memory_space_constraint(value, pltpu.HBM)


def whole_smem():
    return pl.BlockSpec(memory_space=pltpu.SMEM)


def cost(flops, size):
    return pl.CostEstimate(flops=flops, bytes_accessed=size, transcendentals=0)


def dot(left, right):
    return jnp.dot(left, right, preferred_element_type=F32)


def ranks_of(col, rows):
    count = col.shape[0]
    owner = col // rows
    owner_row = jnp.transpose(jnp.broadcast_to(owner.astype(F32), (count, count))).astype(jnp.int32)
    before = lax.broadcasted_iota(jnp.int32, (count, count), 1) < lax.broadcasted_iota(
        jnp.int32, (count, count), 0
    )
    same = (owner_row == owner) & before
    return jnp.sum(same.astype(F32), axis=1, keepdims=True).astype(jnp.int32)


def rows_kernel(cap, round_ref, me_ref, col_ref, real_ref, imag_ref, out_ref, list_ref, near_ref, held_ref, sems):
    rows, width = real_ref.shape
    groups = out_ref.shape[0]
    count = col_ref.shape[0]
    base = me_ref[0] * rows
    skip = round_ref[0] * cap

    def copies(slot, local):
        group = pl.ds(pl.multiple_of(local // GROUP * GROUP, GROUP), GROUP)
        return [
            pltpu.make_async_copy(ref.at[group], near_ref.at[slot, part], sems.at[slot, part])
            for part, ref in enumerate((real_ref, imag_ref))
        ]

    def begin(s, found):
        local = col_ref[s] - base
        own = (local >= 0) & (local < rows)
        slot = found - skip

        @pl.when(own & (slot >= 0) & (slot < cap))
        def _():
            list_ref[slot] = local
            for copy in copies(slot, local):
                copy.start()

        return found + own.astype(jnp.int32)

    def pick(slot, _):
        local = list_ref[slot]
        chosen = lax.broadcasted_iota(jnp.int32, (GROUP, PIECE), 0) == local % GROUP
        for part, copy in enumerate(copies(slot, local)):
            copy.wait()
            for at in range(0, width, PIECE):
                group = near_ref[slot, part, :, at : at + PIECE].astype(F32)
                held_ref[pl.ds(part * cap + slot, 1), at : at + PIECE] = jnp.sum(
                    jnp.where(chosen, group, 0.0), axis=0, keepdims=True
                )
        return 0

    found = lax.fori_loop(0, count, begin, jnp.int32(0), unroll=8)
    held_ref[...] = jnp.zeros_like(held_ref)
    lax.fori_loop(0, jnp.clip(found - skip, 0, cap), pick, 0)
    for g in range(groups):
        out_ref[g] = held_ref[:, g * rows : (g + 1) * rows].astype(BF16)


def own_source_rows(me, data_real, data_imag, source_cols, which, cap):
    rows, width = data_real.shape
    return pl.pallas_call(
        functools.partial(rows_kernel, cap),
        in_specs=[whole_smem()] * 3 + [anywhere()] * 2,
        out_specs=whole_vmem(),
        out_shape=jax.ShapeDtypeStruct((width // rows, 2 * cap, rows), BF16),
        scratch_shapes=[
            pltpu.SMEM((cap,), jnp.int32),
            pltpu.VMEM((cap, 2, GROUP, width), BF16),
            pltpu.VMEM((2 * cap, width), F32),
            pltpu.SemaphoreType.DMA((cap, 2)),
        ],
        compiler_params=params(24),
        cost_estimate=cost(0, 2 * cap * width),
        name="own_source_rows",
    )(which, me, source_cols, data_real, data_imag)


def cols_kernel(real_ref, imag_ref, row_ref, out_ref, acc_ref):
    rows, step = real_ref.shape
    count = row_ref.shape[1]
    t = pl.program_id(0)

    @pl.when(t == 0)
    def _():
        acc_ref[...] = jnp.zeros_like(acc_ref)

    place = lax.broadcasted_iota(jnp.int32, (step, count), 0) + t * step
    pick = (place == row_ref[...]).astype(F32).astype(BF16)
    acc_ref[:, :count] += dot(real_ref[...], pick)
    acc_ref[:, count:] += dot(imag_ref[...], pick)

    @pl.when(t == pl.num_programs(0) - 1)
    def _():
        out_ref[...] = jnp.transpose(acc_ref[...]).astype(BF16)


def own_source_cols(data_real, data_imag, row, step):
    rows, width = data_real.shape
    count = row.shape[1]
    block = pl.BlockSpec((rows, step), lambda t: (0, t))
    return pl.pallas_call(
        cols_kernel,
        grid=(width // step,),
        in_specs=[block, block, whole_vmem()],
        out_specs=pl.BlockSpec((2 * count, rows), lambda t: (0, 0)),
        out_shape=jax.ShapeDtypeStruct((2 * count, rows), BF16),
        scratch_shapes=[pltpu.VMEM((rows, 2 * count), F32)],
        compiler_params=params(),
        cost_estimate=cost(4 * rows * width * count, 4 * rows * width),
        name="own_source_cols",
    )(data_real, data_imag, row)


def select_kernel(cap, round_ref, got_ref, col_ref, out_ref):
    out_ref[...] = pick_rows(cap, round_ref[0], got_ref, col_ref).astype(BF16)


def select_rows(got, col, which, cap):
    groups, _, rows = got.shape
    count = col.shape[0]
    return pl.pallas_call(
        functools.partial(select_kernel, cap),
        in_specs=[whole_smem(), whole_vmem(), whole_vmem()],
        out_specs=whole_vmem(),
        out_shape=jax.ShapeDtypeStruct((2 * count, rows), BF16),
        compiler_params=params(),
        cost_estimate=cost(8 * count * groups * cap * rows, 4 * groups * cap * rows),
        name="select_rows",
    )(which, got, col)


def pick_rows(cap, which, got_ref, col_ref):
    groups, _, rows = got_ref.shape
    count = col_ref.shape[0]
    col = col_ref[...]
    slot = ranks_of(col, rows) - which * cap
    inside = (slot >= 0) & (slot < cap)
    place = jnp.where(inside, (col // rows) * (2 * cap) + slot, -1)
    lanes = lax.broadcasted_iota(jnp.int32, (count, groups * 2 * cap), 1)
    pick = jnp.concatenate([lanes == place, lanes == jnp.where(inside, place + cap, -1)], axis=0)
    got = got_ref[...].reshape(groups * 2 * cap, rows)
    return dot(pick.astype(F32).astype(BF16), got)


def own_panel(width, mine, counts_ref, rowpart_ref, colpart_ref, col_ref):
    tile = width // TILES
    tiles = col_ref[...] // tile
    forward = jnp.zeros_like(tiles)
    backward = jnp.zeros_like(tiles)
    for t in range(TILES):
        forward = jnp.where(tiles == t, counts_ref[mine, t], forward)
        backward = jnp.where(tiles == t, counts_ref[t, mine], backward)
    forward = jnp.concatenate([forward, forward], axis=0).astype(F32)
    backward = jnp.concatenate([backward, backward], axis=0).astype(F32)
    own = colpart_ref[...].astype(F32)
    mirror = rowpart_ref[...].astype(F32)
    return (forward * own + backward * mirror) / jnp.maximum(forward + backward, 1.0)


def store_panel(panel, panel_ref, panel_t_ref):
    double, rows = panel.shape
    count = double // 2
    panel_t_ref[:, :rows] = panel.astype(BF16)
    panel_t_ref[:count, rows:] = (-panel[count:]).astype(BF16)
    panel_t_ref[count:, rows:] = panel[:count].astype(BF16)
    panel_ref[...] = jnp.transpose(panel).astype(BF16)


def panel_kernel(
    width, me_ref, counts_ref, rowpart_ref, colpart_ref, col_ref, panel_ref, panel_t_ref
):
    mine = me_ref[0] * rowpart_ref.shape[1] // (width // TILES)
    panel = own_panel(width, mine, counts_ref, rowpart_ref, colpart_ref, col_ref)
    store_panel(panel, panel_ref, panel_t_ref)


def panel_only(me, counts, rowpart, colpart, col, width):
    double, rows = colpart.shape
    return pl.pallas_call(
        functools.partial(panel_kernel, width),
        in_specs=[whole_smem()] * 2 + [whole_vmem()] * 3,
        out_specs=[whole_vmem()] * 2,
        out_shape=[
            jax.ShapeDtypeStruct((rows, double), BF16),
            jax.ShapeDtypeStruct((double, 2 * rows), BF16),
        ],
        compiler_params=params(),
        cost_estimate=cost(8 * rows * double, 8 * rows * double),
        name="panel_only",
    )(me, counts, rowpart, colpart, col)


def weight(counts_ref, mine, other, shape):
    forward = jnp.full(shape, counts_ref[mine, other], jnp.int32).astype(F32)
    backward = jnp.full(shape, counts_ref[other, mine], jnp.int32).astype(F32)
    return forward / jnp.maximum(forward + backward, 1.0)


def mirror_block(real, imag, panel_t):
    rows = real.shape[0]
    return dot(panel_t[:, :rows], real) + dot(panel_t[:, rows:], imag)


def direct_block(real, imag, panel):
    count = panel.shape[1] // 2
    turned = jnp.concatenate([-panel[:, count:], panel[:, :count]], axis=1)
    return dot(real, panel) + dot(imag, turned)


def mirror_kernel(width, me_ref, counts_ref, real_ref, imag_ref, panel_t_ref, out_ref):
    rows, tile = real_ref.shape
    mine = me_ref[0] * rows // tile
    found = mirror_block(real_ref[...], imag_ref[...], panel_t_ref[...])
    found = found * weight(counts_ref, mine, pl.program_id(0), (1, tile))
    for g in range(out_ref.shape[0]):
        out_ref[g] = found[:, g * rows : (g + 1) * rows]


def mirror_term(me, counts, data_real, data_imag, panel_t):
    rows, width = data_real.shape
    double = panel_t.shape[0]
    tile = width // TILES
    block = pl.BlockSpec((rows, tile), lambda t: (0, t))
    return pl.pallas_call(
        functools.partial(mirror_kernel, width),
        grid=(TILES,),
        in_specs=[whole_smem()] * 2 + [block, block, whole_vmem()],
        out_specs=pl.BlockSpec((tile // rows, double, rows), lambda t: (t, 0, 0)),
        out_shape=jax.ShapeDtypeStruct((width // rows, double, rows), F32),
        compiler_params=params(32),
        cost_estimate=cost(4 * rows * width * double, 4 * rows * width + 2 * double * width),
        name="mirror_term",
    )(me, counts, data_real, data_imag, panel_t)


def direct_kernel(width, me_ref, counts_ref, real_ref, imag_ref, panel_ref, out_ref):
    rows, tile = real_ref.shape
    mine = me_ref[0] * rows // tile
    t = pl.program_id(0)

    @pl.when(t == 0)
    def _():
        out_ref[...] = jnp.zeros_like(out_ref)

    found = direct_block(real_ref[...], imag_ref[...], panel_ref[...])
    out_ref[...] += found * weight(counts_ref, mine, t, (1, out_ref.shape[1]))


def direct_term(me, counts, data_real, data_imag, panel):
    rows, width = data_real.shape
    double = panel.shape[1]
    tile = width // TILES
    block = pl.BlockSpec((rows, tile), lambda t: (0, t))
    return pl.pallas_call(
        functools.partial(direct_kernel, width),
        grid=(TILES,),
        in_specs=[whole_smem()] * 2 + [block, block, pl.BlockSpec((tile, double), lambda t: (t, 0))],
        out_specs=pl.BlockSpec((rows, double), lambda t: (0, 0)),
        out_shape=jax.ShapeDtypeStruct((rows, double), F32),
        compiler_params=params(),
        cost_estimate=cost(4 * rows * width * double, 4 * rows * width + 2 * double * width),
        name="direct_term",
    )(me, counts, data_real, data_imag, panel)


def swap(value, mask):
    return lax.ppermute(value, AXIS, [(i, i ^ mask) for i in range(lax.axis_size(AXIS))])


def picked(masks, i):
    mask = masks[0]
    for at in range(1, len(masks)):
        mask = jnp.where(i == at, masks[at], mask)
    return mask


def mirror_part_kernel(width, masks, first, me_ref, counts_ref, real_ref, imag_ref, *refs):
    other_ref, own_ref, held_ref, sems = refs[-4:]
    panel_t_ref = refs[4] if first else refs[0]
    rows = real_ref.shape[0]
    tile = width // TILES
    me = me_ref[0]
    i = pl.program_id(0)
    mine = me * rows // tile

    def copies(at, mask):
        columns = pl.ds(pl.multiple_of((me ^ mask) // 2 * (2 * rows), 2 * rows), 2 * rows)
        return [
            pltpu.make_async_copy(
                ref.at[:, columns], held_ref.at[at, pl.ds(part * rows, rows)], sems.at[at, part]
            )
            for part, ref in enumerate((real_ref, imag_ref))
        ]

    @pl.when(i == 0)
    def _():
        for at, mask in enumerate(masks):
            for copy in copies(at, mask):
                copy.start()
        if first:
            store_panel(own_panel(width, mine, counts_ref, *refs[:3]), refs[3], panel_t_ref)

    panel_t = panel_t_ref[...]
    mask = picked(masks, i)
    for copy in copies(i, mask):
        copy.wait()

    def term(turn):
        block = me ^ mask ^ turn
        scale = weight(counts_ref, mine, block * rows // tile, (1, rows))
        columns = pl.ds(pl.multiple_of(block % 2 * rows, rows), rows)
        return dot(panel_t, held_ref[i, :, columns]) * scale

    other_ref[0] = term(1).astype(BF16)
    own_ref[0] = term(0)


def mirror_part(me, counts, data_real, data_imag, panel, masks, after):
    rows, width = data_real.shape
    first = len(panel) == 3
    double = panel[0].shape[0]
    blocks = len(masks)
    shape = (1, double, rows)
    whole = lambda *dims: pl.BlockSpec(dims, lambda i, me: (0,) * len(dims))
    spec = pltpu.PrefetchScalarGridSpec(
        num_scalar_prefetch=1,
        grid=(blocks,),
        in_specs=[whole_smem(), anywhere(), anywhere()]
        + [whole_vmem()] * len(panel)
        + [anywhere()] * len(after),
        out_specs=([whole(rows, double), whole(double, 2 * rows)] if first else [])
        + [
            pl.BlockSpec(shape, lambda i, me: (i, 0, 0)),
            pl.BlockSpec(shape, lambda i, me: (i, 0, 0)),
        ],
        scratch_shapes=[
            pltpu.VMEM((blocks, 2 * rows, 2 * rows), BF16),
            pltpu.SemaphoreType.DMA((blocks, 2)),
        ],
    )
    panel_shapes = [
        jax.ShapeDtypeStruct((rows, double), BF16),
        jax.ShapeDtypeStruct((double, 2 * rows), BF16),
    ]
    return pl.pallas_call(
        functools.partial(mirror_part_kernel, width, masks, first),
        grid_spec=spec,
        out_shape=(panel_shapes if first else [])
        + [
            jax.ShapeDtypeStruct((blocks, double, rows), BF16),
            jax.ShapeDtypeStruct((blocks, double, rows), F32),
        ],
        compiler_params=params(32),
        cost_estimate=cost(MIRROR_COST, 0),
        name="mirror_part",
    )(me, counts, data_real, data_imag, *panel, *after)


def ordered(value, after):
    return lax.optimization_barrier((value, after))[0]


def direct_part_kernel(
    width, masks, mirrors, me_ref, counts_ref, real_ref, imag_ref, panel_ref, *refs
):
    rows = real_ref.shape[0]
    tile = width // TILES
    k = pl.program_id(0)
    mine = me_ref[0] * rows // tile
    block = me_ref[0] ^ picked(masks, k)
    scale = weight(counts_ref, mine, block * rows // tile, (1, panel_ref.shape[2]))
    found = direct_block(real_ref[...], imag_ref[...], panel_ref[0]) * scale
    sum_refs, (total_ref, *out_refs) = (refs[:-3], refs[-1:] + refs[-3:-1]) if mirrors else (
        refs[:-1],
        refs[-1:],
    )

    @pl.when(k == 0)
    def _():
        total = found
        if mirrors:
            mirror = sum_refs[-1][...].astype(F32)
            for ref in sum_refs[1:-1]:
                mirror += ref[...].astype(F32)
            total += jnp.transpose(mirror)
        total_ref[...] = total + sum_refs[0][...] if sum_refs else total

    @pl.when(k > 0)
    def _():
        total_ref[...] += found

    if mirrors:
        factor = -1.0 / math.sqrt(width)
        count = panel_ref.shape[2] // 2

        @pl.when(k == len(masks) - 1)
        def _():
            out_refs[0][...] = factor * total_ref[:, :count]
            out_refs[1][...] = factor * total_ref[:, count:]


def direct_part(me, counts, data_real, data_imag, panels, before, masks, mirrors=()):
    rows, width = data_real.shape
    double = panels.shape[2]
    block = pl.BlockSpec((rows, rows), lambda k, me: (0, me[0] ^ picked(masks, k)))
    outs = [(rows, double // 2)] * 2 if mirrors else [(rows, double)]
    spec = pltpu.PrefetchScalarGridSpec(
        num_scalar_prefetch=1,
        grid=(len(masks),),
        in_specs=[whole_smem(), block, block, pl.BlockSpec((1, rows, double), lambda k, me: (k, 0, 0))]
        + [whole_vmem()] * (len(before) + len(mirrors)),
        out_specs=[pl.BlockSpec(shape, lambda k, me: (0, 0)) for shape in outs],
        scratch_shapes=[pltpu.VMEM((rows, double), F32)] if mirrors else [],
    )
    return pl.pallas_call(
        functools.partial(direct_part_kernel, width, masks, bool(mirrors)),
        grid_spec=spec,
        out_shape=[jax.ShapeDtypeStruct(shape, F32) for shape in outs],
        compiler_params=params(),
        cost_estimate=cost(DIRECT_COST, 0),
        name="direct_part",
    )(me, counts, data_real, data_imag, panels, *before, *mirrors)


def levels(me, counts, data_real, data_imag, rowpart, colpart, col):
    data = (in_hbm(data_real), in_hbm(data_imag))
    panel, panel_t, other, own = mirror_part(
        me, counts, *data, [rowpart, colpart, col], (Y | HIGH, Y | HIGH | LOW), []
    )
    high, low, beside = swap(panel, HIGH), swap(panel, LOW), swap(panel, Y)
    far_sent = (own + swap(other, CORE).astype(F32)).astype(BF16)
    def part(masks, after):
        return mirror_part(me, counts, *data, [panel_t], masks, after)

    far_other, far_own = part((HIGH, HIGH | LOW), [far_sent])
    other, own = part((0, LOW, Y, Y | LOW), [far_own])
    arrived = swap(far_sent, Y).astype(F32)

    low, high, beside = ordered([low, high, beside], [far_sent, own])
    direct = []

    def add(panels, masks, mirrors=()):
        direct[:] = direct_part(me, counts, *data, panels, direct, masks, mirrors)

    add(ordered(panel[None], high), (0,))
    own = ordered(own, high)
    got = swap(ordered(other, high), CORE)
    sent = (own[2:] + got[2:].astype(F32)).astype(BF16)
    total = far_own + swap(far_other, CORE).astype(F32) + arrived
    to_low = total[1].astype(BF16)
    total = total[0] + ordered(swap(to_low, LOW), [sent]).astype(F32)
    mirrors = [swap(total.astype(BF16), HIGH)]

    low_beside = ordered(swap(low, Y), [sent, total])
    both = ordered(swap(high, LOW), [sent, to_low])
    column = jnp.stack([panel, low, high, both])
    late = swap(ordered(jnp.stack([high, both]), [sent]), Y)
    early = jnp.stack([beside, low_beside])
    add(jnp.concatenate([column[1:], early]), (LOW, HIGH, HIGH | LOW, Y, Y | LOW))
    add(swap(column, CORE), (CORE, CORE | LOW, CORE | HIGH, CORE | HIGH | LOW))
    total = own[:2] + got[:2].astype(F32) + swap(sent, Y).astype(F32)
    mirrors += [total[0], swap(total[1].astype(BF16), LOW)]
    add(swap(early, CORE), (Y | CORE, Y | CORE | LOW))
    late = ordered(late, direct + mirrors)
    add(late, (Y | HIGH, Y | HIGH | LOW))
    add(swap(late, CORE), (Y | CORE | HIGH, Y | CORE | HIGH | LOW), mirrors)
    return tuple(direct)


def finish_kernel(factor, direct_ref, mirror_ref, real_ref, imag_ref):
    count = real_ref.shape[1]
    total = factor * (direct_ref[...] + jnp.transpose(mirror_ref[...]))
    real_ref[...] = total[:, :count]
    imag_ref[...] = total[:, count:]


def finish(direct, mirror, width):
    rows, double = direct.shape
    shape = jax.ShapeDtypeStruct((rows, double // 2), F32)
    return pl.pallas_call(
        functools.partial(finish_kernel, -1.0 / math.sqrt(width)),
        in_specs=[whole_vmem()] * 2,
        out_specs=[whole_vmem()] * 2,
        out_shape=[shape, shape],
        compiler_params=params(),
        cost_estimate=cost(4 * rows * double, 10 * rows * double),
        name="finish",
    )(direct, mirror)


def shards(data_real, data_imag, counts, source_cols):
    rows, width = data_real.shape
    groups = width // rows
    count = source_cols.shape[0]
    cap = min(rows, count, -(-2 * count // groups // 8) * 8)
    col = source_cols.reshape(count, 1)
    row = source_cols.reshape(1, count)
    me = lax.axis_index(AXIS).reshape(1)

    def exchange(which):
        sent = own_source_rows(me, data_real, data_imag, source_cols, which, cap)
        return lax.all_to_all(sent, AXIS, split_axis=0, concat_axis=0)

    first = jnp.zeros((1,), jnp.int32)
    got = exchange(first)
    colpart = own_source_cols(data_real, data_imag, row, width // TILES)
    rowpart = select_rows(got, col, first, cap)

    owner = source_cols // rows
    most = jnp.max(jnp.sum(owner[:, None] == jnp.arange(groups)[None, :], axis=0, dtype=jnp.int32))

    def further(rowpart):
        def body(which, held):
            one = which.reshape(1)
            return held + select_rows(exchange(one), col, one, cap)

        return lax.fori_loop(1, (most + cap - 1) // cap, body, rowpart)

    rowpart = lax.cond(most > cap, further, lambda rowpart: rowpart, rowpart)
    if rows % 128 == 0 and groups == 16:
        return levels(me, counts, data_real, data_imag, rowpart, colpart, col)
    panel, panel_t = panel_only(me, counts, rowpart, colpart, col, width)
    full = lax.all_gather(panel, AXIS, axis=0, tiled=True)
    partial = mirror_term(me, counts, data_real, data_imag, panel_t)
    mirror = lax.psum_scatter(partial, AXIS, scatter_dimension=0, tiled=False)
    direct = direct_term(me, counts, data_real, data_imag, full)
    return tuple(finish(direct, mirror, width))


def solution(mesh):
    placed = (P(("freq", "row"), None), P(("freq", "row"), None), P(), P())
    return jax.shard_map(
        shards,
        mesh=mesh,
        in_specs=placed,
        out_specs=(P(("freq", "row"), None), P(("freq", "row"), None)),
        check_vma=False,
    )
```
